32 devices in a mesh: expert: 8 (over z, x), tensor: 4 (over y, core).
Axes of the slice: x: 2, y: 2, z: 4, core: 2. Of those that a mesh axis runs over, the one named last changes fastest.
Arguments:
- inputs: bfloat16 [16384, 768], P(('expert', 'tensor')), may hold values from -6 to 6
- lengths: int32 [16], P('expert'), may hold values from 512 to 1024, as said below
- routes: int32 [16384, 2], P(('expert', 'tensor')), may hold values from 0 to 7, all different within a row; in each aligned block of 512 rows (0 to 511, 512 to 1023, ...) at most 256 rows name the same one
- attn_gain: float32 [768], replicated, may hold values from 0.25 to 1.75
- qkv_weight: bfloat16 [768, 3, 768], P(None, None, 'tensor'), may hold values from -0.21875 to 0.21875
- out_weight: bfloat16 [768, 768], P('tensor'), may hold values from -1.5 to 1.5
- rel_bias: float32 [32, 12], P(None, 'tensor'), may hold values from -4 to 4
- moe_gain: float32 [768], replicated, may hold values from 0.25 to 1.75
- router_weight: bfloat16 [768, 8], replicated, may hold values from -0.15625 to 0.15625
- up_weight: bfloat16 [8, 768, 3072], P('expert', None, 'tensor'), may hold values from -0.21875 to 0.21875
- down_weight: bfloat16 [8, 3072, 768], P('expert', 'tensor'), may hold values from -0.109375 to 0.109375
- out_grad: bfloat16 [16384, 768], P(('expert', 'tensor')), may hold values from -6 to 6
Outputs:
- outputs: bfloat16 [16384, 768], P(('expert', 'tensor'))
- grad_inputs: bfloat16 [16384, 768], P(('expert', 'tensor'))
- grad_attn_gain: float32 [768], replicated
- grad_qkv_weight: float32 [768, 3, 768], P(None, None, 'tensor')
- grad_out_weight: float32 [768, 768], P('tensor')
- grad_rel_bias: float32 [32, 12], P(None, 'tensor')
- grad_moe_gain: float32 [768], replicated
- grad_router: float32 [768, 8], replicated
- grad_up: float32 [8, 768, 3072], P('expert', None, 'tensor')
- grad_down: float32 [8, 3072, 768], P('expert', 'tensor')
The draws below stay inside these ranges and needn't reach their ends.
Inputs may be any that keep to these rules, and one draw needn't show every extreme that they name: `lengths`: each sequence's real tokens come first, the rest of its 1024 slots are padding; some sequence fills all 1024 slots. `routes`: A token names two different experts. Among the rows of one device no expert is named more than 256 times, and in every draw some device names some expert exactly 256 times.
All inputs are finite; a program needn't handle non-finite values.
Results may differ from the reference program's by a relative error of at most 0.017.
Values may be sent and summed in bfloat16 or wider, within the bound.
A program may use at most 192 MiB of HBM per device.

```python
import math
import jax
import jax.numpy as jnp
import numpy as np
from jax import lax

D = 768
HEADS = 12
HD = 64
FF = 3072
NB = 32
MAXDIST = 128
SEQ = 1024
TOK_DEV = 512
INNER = 768
EXPERTS = 8
TOKENS = 16384
NSEQ = 16
CAP = 256
N_EXPERT = 8
N_TENSOR = 4


def draw_lengths(key, part):
    key_left, key_right = jax.random.split(key)
    spread = jax.random.randint(key_left, (NSEQ,), SEQ // 2, SEQ + 1, dtype=jnp.int32)
    widest = jax.random.randint(key_right, (), 0, NSEQ, dtype=jnp.int32)
    return spread.at[widest].set(SEQ)


def level_of(own_key, dims, cuts, low, high):
    def one(dim, blocks):
        heights = jax.random.uniform(jax.random.fold_in(jax.random.fold_in(own_key, 6), dim), (blocks,), jnp.float32, low / len(cuts), high / len(cuts))
        return jnp.repeat(jnp.exp(heights), dims[dim] // blocks).reshape((-1,) + (1,) * (len(dims) - dim - 1))

    loudness = one(*cuts[0])
    for cut in cuts[1:]:
        loudness = loudness * one(*cut)
    return loudness


def assign_block(key, own, number, rows, count, top, limit, slope):
    sequence = jax.random.permutation(key, count)
    heavy_load, common = shares(count, rows * top, limit, slope, True), shares(count, rows * top, limit, slope, False)
    places = jnp.arange(count)

    def named(sizes, turn):
        used = int((sizes > 0).sum())
        fixed = max(1, used // 4)
        moved = fixed + (places - fixed + turn * (used - fixed)) % max(1, count - fixed)
        return jnp.zeros((count,), jnp.int32).at[sequence[jnp.where(places < fixed, places, moved)]].set(jnp.asarray(sizes, jnp.int32))

    sizes = jnp.where(number % 4 == 0, named(heavy_load, number // 4), named(common, number - number // 4 - 1))
    mixed = jax.random.permutation(jax.random.fold_in(own, 3), count)
    donor, taker = mixed[0:count // 2 * 2:2], mixed[1:count // 2 * 2:2]
    slack = jnp.minimum(sizes[donor] - 1, limit - sizes[taker]) // 2
    slack = jnp.where((donor == sequence[0]) | (taker == sequence[0]) | (sizes[taker] == 0), 0, jnp.maximum(slack, 0))
    moved = jax.random.randint(jax.random.fold_in(own, 4), (count // 2,), 0, 1 << 20) % (slack + 1)
    sizes = sizes.at[donor].add(-moved).at[taker].add(moved)
    labels = jnp.searchsorted(jnp.cumsum(sizes), jnp.arange(rows * top), side="right").astype(jnp.int32)
    listing = labels.reshape(top, rows).T
    listing = listing[jax.random.permutation(jax.random.fold_in(own, 1), rows)]
    turn = jax.random.randint(jax.random.fold_in(own, 2), (rows, 1), 0, top)
    return jnp.take_along_axis(listing, (jnp.arange(top)[None, :] + turn) % top, axis=1)


def shares(count, total, bound, slope, full):
    loads = [(1 << 20) // math.isqrt(grade ** slope) + 1 for grade in range(1, count + 1)]
    largest = bound if full else min(bound, max(-(-total // count), total * loads[0] // sum(loads)))
    least = 1 if total - largest >= count - 1 else 0
    given, rest = [largest] + [least] * (count - 1), total - largest - least * (count - 1)
    while rest > 0:
        free = [i for i in range(1, count) if given[i] < largest] or [i for i in range(1, count) if given[i] < bound]
        mass, left = sum([loads[i] for i in free]), rest
        for i in free:
            extra = min(bound - given[i], max(1, left * loads[i] // mass), rest)
            given[i] = given[i] + extra
            rest = rest - extra
    return np.array(given)


def bell_draw(stream_key, shape, scale, limit, cuts=(), kind=jnp.bfloat16):
    level = level_of(stream_key, shape, cuts, -0.22, 0.18) if cuts else 1.0
    drawn = jax.random.normal(stream_key, shape, jnp.float32) * scale * level
    return jnp.minimum(jnp.maximum(drawn, -limit), limit).astype(kind)


def setup_inputs(seed: int = 0) -> dict:
    key_list = jax.random.split(jax.random.key(seed), 13)
    inputs = bell_draw(key_list[0], (TOKENS, D), 1.0, 6.0, ((0, 32),))
    lengths = draw_lengths(jax.random.fold_in(key_list[12], 71), 0)
    routes_keys = jax.random.split(jax.random.fold_in(key_list[2], 1), TOKENS // TOK_DEV)
    routes_turns = jax.random.permutation(jax.random.fold_in(key_list[2], 3), TOKENS // TOK_DEV)
    routes = jax.vmap(lambda own, number: assign_block(jax.random.fold_in(key_list[2], 2), own, number, TOK_DEV, EXPERTS, 2, CAP, 1))(routes_keys, routes_turns).reshape((TOKENS, 2))
    attn_gain = jnp.clip(1.0 + 0.15 * jax.random.normal(key_list[3], (D,), jnp.float32), 0.25, 1.75)
    qkv_weight = bell_draw(key_list[4], (D, 3, INNER), D ** -0.5, 0.21875, ((2, 4),))
    out_weight = bell_draw(key_list[5], (INNER, D), (HD // 4) ** -0.5, 1.5, ((0, 4),))
    rel_bias = bell_draw(key_list[6], (NB, HEADS), 1.0, 4.0, ((1, 4),), jnp.float32)
    moe_gain = jnp.clip(1.0 + 0.15 * jax.random.normal(key_list[7], (D,), jnp.float32), 0.25, 1.75)
    router_weight = bell_draw(key_list[8], (D, EXPERTS), (2 * D) ** -0.5, 0.15625)
    up_weight = bell_draw(key_list[9], (EXPERTS, D, FF), D ** -0.5, 0.21875, ((0, 8), (2, 4)))
    down_weight = bell_draw(key_list[10], (EXPERTS, FF, D), FF ** -0.5, 0.109375, ((0, 8), (1, 4)))
    out_grad = bell_draw(key_list[11], (TOKENS, D), 1.0, 6.0, ((0, 32),))
    return {"inputs": inputs, "lengths": lengths, "routes": routes, "attn_gain": attn_gain, "qkv_weight": qkv_weight, "out_weight": out_weight, "rel_bias": rel_bias, "moe_gain": moe_gain, "router_weight": router_weight, "up_weight": up_weight, "down_weight": down_weight, "out_grad": out_grad}


EPSILON = 1e-06
NEGATIVE = -1e+30
HIGHEST = lax.Precision.HIGHEST

@jax.custom_vjp
def low(v):
    return lax.optimization_barrier(v.astype(jnp.bfloat16)).astype(jnp.float32)

@jax.custom_vjp
def low_back(v):
    return v

def low_keep(v):
    return (low(v), None)

def low_pass(kept, grad):
    return (grad,)

def back_keep(v):
    return (v, None)

def back_low(kept, grad):
    return (low(grad),)
low.defvjp(low_keep, low_pass)
low_back.defvjp(back_keep, back_low)

def bucket_edges():
    half_count = NB // 2
    short_edges = list(range(1, half_count))
    long_edges = [int(half_count * (MAXDIST / half_count) ** (step_index / half_count)) for step_index in range(half_count)]
    return short_edges + long_edges

def bucket_table(seq_span):
    positions = jnp.arange(seq_span, dtype=jnp.int32)
    distance = positions[:, None] - positions[None, :]
    bucket = jnp.zeros((seq_span, seq_span), jnp.int32)
    for edge_value in bucket_edges():
        bucket = bucket + (distance >= edge_value).astype(jnp.int32)
    return bucket

def rms_scale(values):
    return lax.rsqrt(lax.optimization_barrier(jnp.mean(values * values, axis=-1, keepdims=True)) + EPSILON)

def forward(inputs, attn_gain, qkv_weight, out_weight, rel_bias, moe_gain, router_weight, up_weight, down_weight, lengths, routes):
    score_scale = HD ** (-0.5)
    normed = low(inputs * rms_scale(inputs) * attn_gain)
    qkv_rows = low(low_back(jnp.dot(normed, qkv_weight.reshape(D, 3 * INNER), precision=HIGHEST)))
    bias_full = jnp.transpose(rel_bias[bucket_table(SEQ)], (2, 0, 1))
    positions = jnp.arange(SEQ, dtype=jnp.int32)

    def one_sequence(packed):
        sequence_rows, length = packed
        pieces = sequence_rows.reshape(SEQ, 3, HEADS, HD)
        raw_scores = jnp.einsum('qhd,khd->hqk', pieces[:, 0], pieces[:, 1], precision=HIGHEST) * score_scale + bias_full
        scores = low_back(raw_scores)
        allowed = (positions[None, :] <= positions[:, None]) & (positions[None, :] < length)
        scores = jnp.where(allowed[None], scores, NEGATIVE)
        attn_probs = low(jax.nn.softmax(scores, axis=-1))
        return jnp.einsum('hqk,khd->qhd', attn_probs, pieces[:, 2], precision=HIGHEST).reshape(SEQ, INNER)
    mixed_heads = lax.map(jax.checkpoint(one_sequence), (qkv_rows.reshape(NSEQ, SEQ, 3 * INNER), lengths))
    mixed_heads = low(low_back(mixed_heads.reshape(TOKENS, INNER)))
    attended = low_back(jnp.dot(mixed_heads, out_weight, precision=HIGHEST))
    hidden = inputs + attended
    normed_two = low(hidden * rms_scale(hidden) * moe_gain)
    logits = low_back(jnp.dot(normed_two, router_weight, precision=HIGHEST))
    gate_weights = jax.nn.softmax(jnp.take_along_axis(logits, routes, axis=1), axis=-1)
    flat_routes = routes.reshape(-1)
    pair_order = jnp.argsort(flat_routes, stable=True).astype(jnp.int32)
    counts = lax.optimization_barrier(jnp.sum((flat_routes[:, None] == jnp.arange(EXPERTS, dtype=jnp.int32)[None, :]).astype(jnp.int32), axis=0))
    starts = jnp.cumsum(counts) - counts
    most_rows = N_EXPERT * N_TENSOR * CAP
    padded = jnp.concatenate([normed_two, jnp.zeros((1, D), jnp.float32)], axis=0)

    def one_expert(packed):
        expert_id, weight_up, weight_down = packed
        slot_ids = jnp.arange(most_rows, dtype=jnp.int32)
        live_slot = slot_ids < counts[expert_id]
        pair_ids = pair_order[jnp.minimum(starts[expert_id] + slot_ids, 2 * TOKENS - 1)]
        expert_rows = low_back(padded[jnp.where(live_slot, pair_ids // 2, TOKENS)])
        inner_act = low_back(jnp.dot(expert_rows, weight_up, precision=HIGHEST))
        active = low(jax.nn.gelu(inner_act))
        result = low(low_back(jnp.dot(active, weight_down, precision=HIGHEST)))
        return (result, jnp.where(live_slot, pair_ids, 2 * TOKENS))
    results, targets = lax.map(jax.checkpoint(one_expert), (jnp.arange(EXPERTS, dtype=jnp.int32), up_weight, down_weight))
    per_pair = jnp.zeros((2 * TOKENS + 1, D), jnp.float32).at[targets.reshape(-1)].add(results.reshape(-1, D))
    expert_out = per_pair[:2 * TOKENS].reshape(TOKENS, 2, D)
    mixture = lax.optimization_barrier(jnp.sum(gate_weights[:, :, None] * expert_out, axis=1))
    token_ids = jnp.arange(TOKENS, dtype=jnp.int32)
    valid_mask = (token_ids % SEQ < lengths[token_ids // SEQ]).astype(jnp.float32)
    return valid_mask[:, None] * (hidden + mixture)

def reference(inputs, lengths, routes, attn_gain, qkv_weight, out_weight, rel_bias, moe_gain, router_weight, up_weight, down_weight, out_grad):

    def layer_pass(layer_in, gain_one, qkv_float, out_float, table_float, gain_two, router_float, up_float, down_float):
        return forward(layer_in, gain_one, qkv_float, out_float, table_float, gain_two, router_float, up_float, down_float, lengths, routes)
    outputs, pullback = jax.vjp(layer_pass, inputs.astype(jnp.float32), attn_gain, qkv_weight.astype(jnp.float32), out_weight.astype(jnp.float32), rel_bias, moe_gain, router_weight.astype(jnp.float32), up_weight.astype(jnp.float32), down_weight.astype(jnp.float32))
    gradients = pullback(out_grad.astype(jnp.float32))
    return (outputs.astype(jnp.bfloat16), gradients[0].astype(jnp.bfloat16), gradients[1], gradients[2], gradients[3], gradients[4], gradients[5], gradients[6], gradients[7], gradients[8])
```

```python
import functools

import jax
import jax.numpy as jnp
from jax import lax
from jax.experimental import pallas as pl
from jax.experimental.pallas import tpu as pltpu
from jax.sharding import PartitionSpec as P

D = 768
HD = 64
NB = 32
MAXDIST = 128
SEQ = 1024
EPSILON = 1e-06
NEGATIVE = -1e30
TILE = 256
BF = jnp.bfloat16
F32 = jnp.float32
MIB = 2**20


def bucket_edges():
    half_count = NB // 2
    short_edges = list(range(1, half_count))
    long_edges = [
        int(half_count * (MAXDIST / half_count) ** (step_index / half_count))
        for step_index in range(half_count)
    ]
    return short_edges + long_edges


EDGES = bucket_edges()


def dot(a, b, ca=1, cb=0, precision=None):
    return lax.dot_general(
        a, b, (((ca,), (cb,)), ((), ())), preferred_element_type=F32, precision=precision
    )


def iota(shape, dim):
    return lax.broadcasted_iota(jnp.int32, shape, dim)


def rms(v):
    return lax.rsqrt(jnp.mean(v * v, axis=-1, keepdims=True) + EPSILON)


def call(kernel, outs, args, specs=None, scratch=(), flops=0, moved=0, exps=0, vmem=56, name=None):
    vm = pl.BlockSpec(memory_space=pltpu.VMEM)
    return pl.pallas_call(
        kernel,
        out_shape=[jax.ShapeDtypeStruct(s, d) for s, d in outs],
        in_specs=specs or [vm] * len(args),
        out_specs=[vm] * len(outs),
        scratch_shapes=list(scratch),
        compiler_params=pltpu.CompilerParams(vmem_limit_bytes=vmem * MIB),
        cost_estimate=pl.CostEstimate(flops=flops, bytes_accessed=moved, transcendentals=exps),
        name=name,
    )(*args)


VM = pl.BlockSpec(memory_space=pltpu.VMEM)
SM = pl.BlockSpec(memory_space=pltpu.SMEM)


def route_kernel(experts, cap, nv_ref, routes_ref, grad_ref, packed_ref, slots_ref, meta_ref):
    rows = grad_ref.shape[0]
    routes = routes_ref[...]
    first, second = routes[0:1], routes[1:2]
    valid = iota((1, rows), 1) < nv_ref[0]
    ids = iota((experts, rows), 0)
    hot0 = ((ids == first) & valid).astype(F32)
    hot1 = ((ids == second) & valid).astype(F32)
    before = (iota((rows, rows), 0) < iota((rows, rows), 1)).astype(BF)
    rank = dot((hot0 + hot1).astype(BF), before)
    place = ids.astype(F32) * cap + rank
    bad = jnp.where(valid, 0.0, 1.0)
    slot0 = jnp.sum(hot0 * place, axis=0, keepdims=True) - bad
    slot1 = jnp.sum(hot1 * place, axis=0, keepdims=True) - bad
    spots = iota((experts * cap, rows), 0)
    pick0 = spots == slot0.astype(jnp.int32)
    pick1 = spots == slot1.astype(jnp.int32)
    packed_ref[...] = dot((pick0 | pick1).astype(BF), grad_ref[...]).astype(BF)
    code0 = jnp.broadcast_to((second + 1).astype(F32), (8, rows)).astype(BF)
    code1 = jnp.broadcast_to((first + 1).astype(F32), (8, rows)).astype(BF)
    meta_ref[...] = dot(code0, pick0.astype(BF), 1, 1) + dot(code1, pick1.astype(BF), 1, 1)
    slots_ref[...] = jnp.concatenate([slot0, slot1, jnp.zeros((6, rows), F32)], axis=0)


def pick_matrix(slots_ref, spots):
    rows = slots_ref.shape[1]
    where = iota((spots, rows), 0)
    slots = slots_ref[...].astype(jnp.int32)
    return ((where == slots[0:1]) | (where == slots[1:2])).astype(BF)


def back_matrix(slots_ref, spots):
    rows = slots_ref.shape[1]
    where = iota((rows, spots), 1)
    slots = slots_ref[...].T.astype(jnp.int32)
    return ((where == slots[:, 0:1]) | (where == slots[:, 1:2])).astype(BF)


def bias_tiles(table_ref, head):
    dist = iota((8, TILE), 1)
    far = table_ref[NB - 1, head]
    curve = jnp.full((8, TILE), table_ref[0, head] - far, F32)
    for number, edge in enumerate(EDGES):
        curve = jnp.where(dist >= edge, table_ref[number + 1, head] - far, curve)
    spread = jnp.broadcast_to(curve[0:1], (TILE, TILE))
    ring = pltpu.roll(spread, 0, 1, stride=1, stride_axis=0)
    ahead = iota((TILE, TILE), 1) >= iota((TILE, TILE), 0)
    return jnp.where(ahead, ring, NEGATIVE), jnp.where(ahead, 0.0, ring)


def head_pieces(qkvt_ref, mask_rows, head, local_inner):
    start = pl.multiple_of(head * HD, HD)
    q = qkvt_ref[pl.ds(start, HD), :] * jnp.asarray(HD**-0.5, BF)
    k = qkvt_ref[pl.ds(local_inner + start, HD), :]
    v = qkvt_ref[pl.ds(2 * local_inner + start, HD), :]
    ones = jnp.ones((16, SEQ), BF)
    return jnp.concatenate([q, ones], 0), jnp.concatenate([k, mask_rows], 0), v, ones


def mask_block(length):
    keep = (iota((16, SEQ), 1) < length) | (iota((16, SEQ), 0) > 0)
    return jnp.where(keep, 0.0, NEGATIVE).astype(BF)


def score_pieces(k, q, block, near, below):
    cols = slice(block * TILE, (block + 1) * TILE)
    qb = q[:, cols]
    pieces = []
    if block >= 2:
        pieces.append((0, (block - 1) * TILE, dot(k[: (block - 1) * TILE], qb)))
    if block >= 1:
        lo = (block - 1) * TILE
        pieces.append((lo, block * TILE, dot(k[lo : lo + TILE], qb) + below))
    lo = block * TILE
    pieces.append((lo, lo + TILE, dot(k[lo : lo + TILE], qb) + near))
    return cols, pieces


def attn_fwd_kernel(first, heads, scal_ref, table_ref, *refs):
    if first:
        own_ref, other_ref, gain_ref, w_ref, ow_ref = refs[:5]
        normed_ref, qkvt_ref, mixt_ref, lse_ref, part_ref = refs[5:]
        half = own_ref.shape[0]
        core = scal_ref[0]
        for source, place in ((own_ref, core), (other_ref, 1 - core)):
            x = source[...].astype(F32)
            normed_ref[pl.ds(pl.multiple_of(place * half, half), half), :] = (
                x * rms(x) * gain_ref[...]
            ).astype(BF)
    else:
        normed_ref, w_ref, ow_ref, part_in = refs[:4]
        qkvt_ref, mixt_ref, lse_ref, keep_ref, send_ref, part_ref = refs[4:]
    local_inner = heads * HD
    qkvt_ref[...] = dot(w_ref[...], normed_ref[...], 1, 1).astype(BF)
    masks = mask_block(scal_ref[1])
    lse_ref[...] = jnp.zeros_like(lse_ref)

    for head in range(heads):
        near, below = bias_tiles(table_ref, head)
        q, kt, v, ones = head_pieces(qkvt_ref, masks, head, local_inner)
        k = kt.T
        vx = jnp.concatenate([v, ones], 0)
        for block in range(SEQ // TILE):
            cols, pieces = score_pieces(k, q, block, near, below)
            top = functools.reduce(
                jnp.maximum, [jnp.max(s, axis=0, keepdims=True) for _, _, s in pieces]
            )
            total = None
            for lo, hi, s in pieces:
                term = dot(vx[:, lo:hi], jnp.exp(s - top).astype(BF))
                total = term if total is None else total + term
            weight = total[HD : HD + 1]
            mixt_ref[head * HD : (head + 1) * HD, cols] = (total[:HD] / weight).astype(BF)
            lse_ref[head : head + 1, cols] = top + jnp.log(weight)
    part = dot(mixt_ref[...], ow_ref[...], 0, 0)
    if first:
        part_ref[...] = part
    else:
        part_ref[...] = part + part_in[...]
        half = keep_ref.shape[0]
        core = scal_ref[0]
        keep_ref[...] = part_ref[pl.ds(pl.multiple_of(core * half, half), half), :]
        send_ref[...] = part_ref[pl.ds(pl.multiple_of((1 - core) * half, half), half), :].astype(BF)


def attn_bwd_kernel(last, heads, scal_ref, table_ref, *refs):
    if last:
        (normed_ref, w_ref, ow_ref, qkvt_ref, mixt_ref, lse_ref, own_ref, other_ref, part_in) = refs[:9]
        gw_ref, gow_ref, gbias_ref, keep_ref, send_ref, ga_ref, got_ref, gt_ref, d0_ref, d1_ref, part_ref = refs[9:]
    else:
        (normed_ref, w_ref, ow_ref, qkvt_ref, mixt_ref, lse_ref, own_ref, other_ref) = refs[:8]
        gw_ref, gow_ref, gbias_ref, part_ref, ga_ref, got_ref, gt_ref, d0_ref, d1_ref = refs[8:]
    local_inner = heads * HD
    half = own_ref.shape[0]
    core = scal_ref[0]
    ga_ref[pl.ds(pl.multiple_of(core * half, half), half), :] = own_ref[...]
    ga_ref[pl.ds(pl.multiple_of((1 - core) * half, half), half), :] = other_ref[...]
    got_ref[...] = dot(ow_ref[...], ga_ref[...], 1, 1).astype(BF)
    gow_ref[...] = dot(mixt_ref[...], ga_ref[...]).astype(gow_ref.dtype)
    masks = mask_block(scal_ref[1])
    gbias_ref[...] = jnp.zeros_like(gbias_ref)
    ahead = iota((TILE, TILE), 1) >= iota((TILE, TILE), 0)
    spot = (iota((TILE, 128), 0) + 1) % TILE
    flip = (iota((TILE, TILE), 0) + iota((TILE, TILE), 1) == TILE - 1).astype(F32)
    bucket = jnp.zeros((TILE, 128), jnp.int32)
    for edge in EDGES:
        bucket = bucket + (spot >= edge).astype(jnp.int32)
    hot = (bucket == iota((TILE, 128), 1)).astype(F32)

    for head in range(heads):
        near, below = bias_tiles(table_ref, head)
        q, kt, vt, _ = head_pieces(qkvt_ref, masks, head, local_inner)
        k = kt.T
        v = vt.T
        rows = slice(head * HD, (head + 1) * HD)
        gt = got_ref[rows, :]
        delta = jnp.sum(gt.astype(F32) * mixt_ref[rows, :].astype(F32), axis=0, keepdims=True)
        gk = [None] * (SEQ // TILE)
        gv = [None] * (SEQ // TILE)
        far = jnp.zeros((8, TILE), F32)
        for block in range(SEQ // TILE):
            cols, pieces = score_pieces(k, q, block, near, below)
            gb = gt[:, cols]
            qb = q[:HD, cols]
            lse = lse_ref[head : head + 1, cols]
            db = delta[:, cols]
            gq = None
            for lo, hi, s in pieces:
                p = jnp.exp(s - lse)
                ds = p * (dot(v[lo:hi], gb) - db)
                pb = p.astype(BF)
                dsb = ds.astype(BF)
                term = dot(kt[:HD, lo:hi], dsb)
                gq = term if gq is None else gq + term
                tv = dot(pb, gb, 1, 1)
                tk = dot(dsb, qb, 1, 1)
                for tile in range(lo // TILE, hi // TILE):
                    part = slice(tile * TILE - lo, (tile + 1) * TILE - lo)
                    gv[tile] = tv[part] if gv[tile] is None else gv[tile] + tv[part]
                    gk[tile] = tk[part] if gk[tile] is None else gk[tile] + tk[part]
                if hi == (block + 1) * TILE:
                    d0_ref[...] = ds if block == 0 else d0_ref[...] + ds
                elif hi == block * TILE and lo == (block - 1) * TILE:
                    d1_ref[...] = ds if block == 1 else d1_ref[...] + ds
                else:
                    far = far + jnp.sum(ds.reshape((hi - lo) // 8, 8, TILE), axis=0)
            gt_ref[rows, cols] = (gq * HD**-0.5).astype(BF)
        for tile in range(SEQ // TILE):
            cols = slice(tile * TILE, (tile + 1) * TILE)
            gt_ref[local_inner + head * HD : local_inner + (head + 1) * HD, cols] = (
                gk[tile].T.astype(BF)
            )
            gt_ref[2 * local_inner + head * HD : 2 * local_inner + (head + 1) * HD, cols] = (
                gv[tile].T.astype(BF)
            )
        d1 = d1_ref[...]
        ring = jnp.where(ahead, d0_ref[...], d1)
        turned = pltpu.roll(
            dot(flip, ring, 1, 0, lax.Precision.HIGHEST), 0, 1, stride=1, stride_axis=0
        )
        far = far + jnp.sum(jnp.where(ahead, d1, 0.0).reshape(TILE // 8, 8, TILE), axis=0)
        line = jnp.sum(turned, axis=0, keepdims=True)
        sums = dot(
            jnp.broadcast_to(line, (8, TILE)), hot, 1, 0, lax.Precision.HIGHEST
        )
        sums = sums + jnp.where(iota((8, 128), 1) == NB - 1, jnp.sum(far), 0.0)
        gbias_ref[head : head + 1, :] = sums[0:1]
    gw_ref[...] = dot(gt_ref[...], normed_ref[...]).astype(gw_ref.dtype)
    part = dot(gt_ref[...], w_ref[...], 0, 0)
    if last:
        part_ref[...] = part + part_in[...]
        keep_ref[...] = part_ref[pl.ds(pl.multiple_of(core * half, half), half), :]
        send_ref[...] = part_ref[pl.ds(pl.multiple_of((1 - core) * half, half), half), :].astype(BF)
    else:
        part_ref[...] = part


def middle_kernel(x_ref, keep_ref, got_ref, gain_ref, slots_ref, hidden_ref, packed_ref):
    hidden = x_ref[...].astype(F32) + keep_ref[...] + got_ref[...].astype(F32)
    hidden_ref[...] = hidden
    normed = (hidden * rms(hidden) * gain_ref[...]).astype(BF)
    packed_ref[...] = dot(pick_matrix(slots_ref, packed_ref.shape[0]), normed).astype(BF)


def turn_kernel(nv_ref, came_ref, slots_ref, hidden_ref, gain_ref, grad_ref, gh_ref, ga_ref, gain_out):
    gn = dot(back_matrix(slots_ref, came_ref.shape[0]), came_ref[...])
    hidden = hidden_ref[...]
    scale = rms(hidden)
    unit = hidden * scale
    gain_out[...] = jnp.broadcast_to(jnp.sum(gn * unit, axis=0, keepdims=True), gain_out.shape)
    g = gn * gain_ref[...]
    valid = (iota((hidden.shape[0], 1), 0) < nv_ref[0]).astype(F32)
    gh = scale * (g - unit * jnp.mean(g * unit, axis=1, keepdims=True)) + valid * grad_ref[...].astype(F32)
    gh_ref[...] = gh
    ga_ref[...] = gh.astype(BF)


def output_kernel(nv_ref, came_ref, slots_ref, hidden_ref, out_ref):
    mix = dot(back_matrix(slots_ref, came_ref.shape[0]), came_ref[...])
    hidden = hidden_ref[...]
    valid = (iota((hidden.shape[0], 1), 0) < nv_ref[0]).astype(F32)
    out_ref[...] = (valid * (hidden + mix)).astype(BF)


def last_kernel(x_ref, keep_ref, got_ref, gain_ref, gh_ref, out_ref, gain_out):
    x = x_ref[...].astype(F32)
    scale = rms(x)
    unit = x * scale
    gn = keep_ref[...] + got_ref[...].astype(F32)
    gain_out[...] = jnp.broadcast_to(jnp.sum(gn * unit, axis=0, keepdims=True), gain_out.shape)
    g = gn * gain_ref[...]
    out_ref[...] = (
        gh_ref[...] + scale * (g - unit * jnp.mean(g * unit, axis=1, keepdims=True))
    ).astype(BF)


def shards(
    inputs,
    lengths,
    routes,
    attn_gain,
    qkv_weight,
    out_weight,
    rel_bias,
    moe_gain,
    router_weight,
    up_weight,
    down_weight,
    out_grad,
):
    rows = inputs.shape[0]
    rank = lax.axis_index("tensor")
    expert = lax.axis_index("expert")
    heads = rel_bias.shape[1]
    inner = heads * HD
    experts = router_weight.shape[1]
    cap = 4 * rows // experts
    spots = experts * cap
    core = rank % 2
    length = lengths[rank // 2]
    nvalid = jnp.clip(length - core * rows, 0, rows).astype(jnp.int32).reshape(1)
    scal = jnp.stack([core, length]).astype(jnp.int32)

    def swap(x, bit):
        return lax.ppermute(x, "tensor", [(i, i ^ bit) for i in range(4)])

    gain1 = attn_gain.reshape(1, D)
    gain2 = moe_gain.reshape(1, D)
    other = swap(inputs, 1)
    wt = jnp.transpose(qkv_weight.reshape(D, 3 * inner))
    pair_w = swap(jnp.concatenate([wt, out_weight], axis=0), 2)
    pair_table = swap(rel_bias, 2)

    packed_grad, slots, meta = call(
        functools.partial(route_kernel, experts, cap),
        [((spots, D), BF), ((8, rows), F32), ((8, spots), F32)],
        (nvalid, jnp.transpose(routes), out_grad),
        [SM, VM, VM],
        flops=2 * spots * rows * D,
        moved=4 * MIB,
        name="route",
    )

    def exchange(x):
        return lax.all_to_all(
            x.reshape(experts, cap, x.shape[-1]), "expert", split_axis=0, concat_axis=0, tiled=True
        ).reshape(x.shape)

    grads_in = exchange(packed_grad)
    partner = lax.all_to_all(
        meta[0].reshape(experts, cap), "expert", split_axis=0, concat_axis=0, tiled=True
    ).reshape(spots, 1)

    mine = jnp.concatenate([up_weight[0], down_weight[0]], axis=0)
    far = swap(mine, 2)
    side = swap(mine, 1)
    cross = swap(far, 1)
    quarters = [mine, side, far, cross]

    attn_cost = dict(
        flops=2 * SEQ * D * 4 * inner + heads * SEQ * SEQ * 160, moved=6 * MIB, exps=heads * SEQ * SEQ
    )
    normed, qkvt0, mixt0, lse0, part0 = call(
        functools.partial(attn_fwd_kernel, True, heads),
        [((SEQ, D), BF), ((3 * inner, SEQ), BF), ((inner, SEQ), BF), ((8, SEQ), F32), ((SEQ, D), F32)],
        (scal, rel_bias, inputs, other, gain1, wt, out_weight),
        [SM, SM] + [VM] * 5,
        name="attend_own",
        **attn_cost,
    )
    wt1, ow1 = pair_w[: 3 * inner], pair_w[3 * inner :]
    qkvt1, mixt1, lse1, keep, send = call(
        functools.partial(attn_fwd_kernel, False, heads),
        [((3 * inner, SEQ), BF), ((inner, SEQ), BF), ((8, SEQ), F32), ((rows, D), F32), ((rows, D), BF)],
        (scal, pair_table, normed, wt1, ow1, part0),
        [SM, SM] + [VM] * 4,
        scratch=[pltpu.VMEM((SEQ, D), F32)],
        name="attend_pair",
        **attn_cost,
    )
    got = swap(send, 1)
    hidden, packed_rows = call(
        middle_kernel,
        [((rows, D), F32), ((spots, D), BF)],
        (inputs, keep, got, gain2, slots),
        flops=2 * spots * rows * D,
        moved=8 * MIB,
        name="middle",
    )
    arrived = exchange(packed_rows)

    logits = jnp.dot(arrived, router_weight, preferred_element_type=F32)
    ids = jnp.arange(experts, dtype=jnp.int32)
    own_hot = (ids[None, :] == expert).astype(F32)
    other_hot = (ids[None, :] + 1 == partner.astype(jnp.int32)).astype(F32)
    gap = jnp.sum(logits * (own_hot - other_hot), axis=1, keepdims=True)
    gate = jax.nn.sigmoid(gap)
    geo = (gate * grads_in.astype(F32)).astype(BF)
    up_grads, down_grads = [], []
    back = jnp.zeros((spots, D), F32)
    result = jnp.zeros((spots, D), F32)
    worth = jnp.zeros((spots, 1), F32)
    for quarter in quarters:
        up, down = quarter[:D], quarter[D:]
        inner_act = jnp.dot(arrived, up, preferred_element_type=F32)
        active = jax.nn.gelu(inner_act).astype(BF)
        grad_active = dot(geo, down, 1, 1)
        _, gelu_back = jax.vjp(jax.nn.gelu, inner_act)
        grad_inner = gelu_back(grad_active)[0].astype(BF)
        worth = worth + jnp.sum(active.astype(F32) * grad_active, axis=1, keepdims=True)
        back = back + dot(grad_inner, up, 1, 1)
        result = result + jnp.dot(active, down, preferred_element_type=F32)
        up_grads.append(dot(arrived, grad_inner, 0, 0).astype(BF))
        down_grads.append(dot(active, geo, 0, 0).astype(BF))
    share = (1.0 - gate) * worth * (own_hot - other_hot)
    share = jnp.where(partner > 0, share, 0.0)
    share_hi = share.astype(BF)
    share_lo = (share - share_hi.astype(F32)).astype(BF)
    back = back + dot(share_hi, router_weight, 1, 1)
    grad_router = dot(arrived, jnp.concatenate([share_hi, share_lo], axis=1), 0, 0)
    grad_router = grad_router[:, :experts] + grad_router[:, experts:]
    came = exchange(back.astype(BF))
    came_out = exchange((gate * result).astype(BF))

    grads = [jnp.concatenate([u, d], axis=0) for u, d in zip(up_grads, down_grads)]
    near = grads[0].astype(F32) + swap(grads[1], 1).astype(F32)
    away = grads[2].astype(F32) + swap(grads[3], 1).astype(F32)
    grad_weights = near + swap(away.astype(BF), 2).astype(F32)

    grad_hidden, grad_attended, moe_part = call(
        turn_kernel,
        [((rows, D), F32), ((rows, D), BF), ((8, D), F32)],
        (nvalid, came, slots, hidden, gain2, out_grad),
        [SM] + [VM] * 5,
        flops=2 * spots * rows * D,
        moved=8 * MIB,
        name="turn",
    )
    other_grad = swap(grad_attended, 1)
    bwd_cost = dict(
        flops=2 * SEQ * D * 10 * inner + heads * SEQ * SEQ * 400, moved=9 * MIB, exps=heads * SEQ * SEQ
    )
    work = [
        pltpu.VMEM((SEQ, D), BF),
        pltpu.VMEM((inner, SEQ), BF),
        pltpu.VMEM((3 * inner, SEQ), BF),
        pltpu.VMEM((TILE, TILE), F32),
        pltpu.VMEM((TILE, TILE), F32),
    ]
    gw1, gow1, gbias1, npart = call(
        functools.partial(attn_bwd_kernel, False, heads),
        [((3 * inner, D), BF), ((inner, D), BF), ((8, 128), F32), ((SEQ, D), F32)],
        (scal, pair_table, normed, wt1, ow1, qkvt1, mixt1, lse1, grad_attended, other_grad),
        [SM, SM] + [VM] * 8,
        scratch=work,
        name="attend_pair_back",
        **bwd_cost,
    )
    gpair = swap(jnp.concatenate([gw1, gow1], axis=0), 2)
    gw0, gow0, gbias0, keep_n, send_n = call(
        functools.partial(attn_bwd_kernel, True, heads),
        [((3 * inner, D), F32), ((inner, D), F32), ((8, 128), F32), ((rows, D), F32), ((rows, D), BF)],
        (scal, rel_bias, normed, wt, out_weight, qkvt0, mixt0, lse0, grad_attended, other_grad, npart),
        [SM, SM] + [VM] * 9,
        scratch=work + [pltpu.VMEM((SEQ, D), F32)],
        name="attend_own_back",
        **bwd_cost,
    )
    got_n = swap(send_n, 1)
    grad_inputs, attn_part = call(
        last_kernel,
        [((rows, D), BF), ((8, D), F32)],
        (inputs, keep_n, got_n, gain1, grad_hidden),
        moved=6 * MIB,
        name="last",
    )
    wide = (jnp.concatenate([gw0, gow0], axis=0) + gpair.astype(F32)).astype(BF)
    wide = lax.psum(wide, "expert").astype(F32)
    outputs = call(
        output_kernel,
        [((rows, D), BF)],
        (nvalid, came_out, slots, hidden),
        [SM] + [VM] * 3,
        flops=2 * spots * rows * D,
        moved=8 * MIB,
        name="outputs",
    )[0]

    own_bias = gbias0[:heads, :NB].reshape(1, -1)
    pair_bias = gbias1[:heads, :NB].reshape(1, -1)
    ranks = jnp.arange(4, dtype=jnp.int32)[:, None]
    bias_parts = jnp.where(ranks == rank, own_bias, 0.0) + jnp.where(ranks == (rank ^ 2), pair_bias, 0.0)
    small = jnp.concatenate(
        [attn_part[0], moe_part[0], grad_router.reshape(-1), bias_parts.reshape(-1)]
    )
    small = lax.psum(small, ("expert", "tensor"))
    bias_sum = lax.dynamic_slice(
        small[2 * D + experts * D :].reshape(4, heads * NB), (rank, 0), (1, heads * NB)
    )
    return (
        outputs,
        grad_inputs,
        small[:D],
        jnp.transpose(wide[: 3 * inner]).reshape(D, 3, inner),
        wide[3 * inner :],
        jnp.transpose(bias_sum.reshape(heads, NB)),
        small[D : 2 * D],
        small[2 * D : 2 * D + experts * D].reshape(D, experts),
        grad_weights[:D][None],
        grad_weights[D:][None],
    )


def solution(mesh):
    return jax.shard_map(
        shards,
        mesh=mesh,
        in_specs=(
            P(("expert", "tensor"), None),
            P("expert"),
            P(("expert", "tensor"), None),
            P(),
            P(None, None, "tensor"),
            P("tensor", None),
            P(None, "tensor"),
            P(),
            P(),
            P("expert", None, "tensor"),
            P("expert", "tensor", None),
            P(("expert", "tensor"), None),
        ),
        out_specs=(
            P(("expert", "tensor"), None),
            P(("expert", "tensor"), None),
            P(),
            P(None, None, "tensor"),
            P("tensor", None),
            P(None, "tensor"),
            P(),
            P(),
            P("expert", None, "tensor"),
            P("expert", "tensor", None),
        ),
        check_vma=False,
    )
```

```python
import functools

import jax
import jax.numpy as jnp
from jax import lax
from jax.experimental import pallas as pl
from jax.experimental.pallas import tpu as pltpu
from jax.sharding import PartitionSpec as P

D = 768
HD = 64
NB = 32
MAXDIST = 128
SEQ = 1024
EPSILON = 1e-06
NEGATIVE = -1e30
TILE = 256
BF = jnp.bfloat16
F32 = jnp.float32
MIB = 2**20
CHUNK = 256
GELU = 0.7978845608028654
CUBIC = 0.044715


def bucket_edges():
    half_count = NB // 2
    short_edges = list(range(1, half_count))
    long_edges = [
        int(half_count * (MAXDIST / half_count) ** (step_index / half_count))
        for step_index in range(half_count)
    ]
    return short_edges + long_edges


EDGES = bucket_edges()


def dot(a, b, ca=1, cb=0, precision=None):
    return lax.dot_general(
        a, b, (((ca,), (cb,)), ((), ())), preferred_element_type=F32, precision=precision
    )


def iota(shape, dim):
    return lax.broadcasted_iota(jnp.int32, shape, dim)


def rms(v):
    return lax.rsqrt(jnp.mean(v * v, axis=-1, keepdims=True) + EPSILON)


def call(kernel, outs, args, specs=None, scratch=(), flops=0, moved=0, exps=0, vmem=56, name=None):
    vm = pl.BlockSpec(memory_space=pltpu.VMEM)
    return pl.pallas_call(
        kernel,
        out_shape=[jax.ShapeDtypeStruct(s, d) for s, d in outs],
        in_specs=specs or [vm] * len(args),
        out_specs=[vm] * len(outs),
        scratch_shapes=list(scratch),
        compiler_params=pltpu.CompilerParams(vmem_limit_bytes=vmem * MIB),
        cost_estimate=pl.CostEstimate(flops=flops, bytes_accessed=moved, transcendentals=exps),
        name=name,
    )(*args)


VM = pl.BlockSpec(memory_space=pltpu.VMEM)
SM = pl.BlockSpec(memory_space=pltpu.SMEM)


def route_kernel(experts, cap, nv_ref, routes_ref, grad_ref, packed_ref, slots_ref):
    rows = grad_ref.shape[0]
    routes = routes_ref[...]
    first, second = routes[0:1], routes[1:2]
    valid = iota((1, rows), 1) < nv_ref[0]
    ids = iota((experts, rows), 0)
    hot0 = ((ids == first) & valid).astype(F32)
    hot1 = ((ids == second) & valid).astype(F32)
    before = (iota((rows, rows), 0) < iota((rows, rows), 1)).astype(BF)
    rank = dot((hot0 + hot1).astype(BF), before)
    place = ids.astype(F32) * cap + rank
    bad = jnp.where(valid, 0.0, 1.0)
    slot0 = jnp.sum(hot0 * place, axis=0, keepdims=True) - bad
    slot1 = jnp.sum(hot1 * place, axis=0, keepdims=True) - bad
    spots = iota((experts * cap, rows), 0)
    pick0 = spots == slot0.astype(jnp.int32)
    pick1 = spots == slot1.astype(jnp.int32)
    packed_ref[...] = dot((pick0 | pick1).astype(BF), grad_ref[...]).astype(BF)
    slots_ref[...] = jnp.concatenate([slot0, slot1, jnp.zeros((6, rows), F32)], axis=0)


def pick_matrix(slots_ref, spots):
    rows = slots_ref.shape[1]
    where = iota((spots, rows), 0)
    slots = slots_ref[...].astype(jnp.int32)
    return ((where == slots[0:1]) | (where == slots[1:2])).astype(BF)


def back_matrix(slots_ref, spots):
    rows = slots_ref.shape[1]
    where = iota((rows, spots), 1)
    slots = slots_ref[...].T.astype(jnp.int32)
    return ((where == slots[:, 0:1]) | (where == slots[:, 1:2])).astype(BF)


def bias_tiles(table_ref, head):
    dist = iota((8, TILE), 1)
    far = table_ref[NB - 1, head]
    curve = jnp.full((8, TILE), table_ref[0, head] - far, F32)
    for number, edge in enumerate(EDGES):
        curve = jnp.where(dist >= edge, table_ref[number + 1, head] - far, curve)
    spread = jnp.broadcast_to(curve[0:1], (TILE, TILE))
    ring = pltpu.roll(spread, 0, 1, stride=1, stride_axis=0)
    ahead = iota((TILE, TILE), 1) >= iota((TILE, TILE), 0)
    return jnp.where(ahead, ring, NEGATIVE), jnp.where(ahead, 0.0, ring)


def head_pieces(qkvt_ref, mask_rows, head, local_inner):
    start = pl.multiple_of(head * HD, HD)
    q = qkvt_ref[pl.ds(start, HD), :] * jnp.asarray(HD**-0.5, BF)
    k = qkvt_ref[pl.ds(local_inner + start, HD), :]
    v = qkvt_ref[pl.ds(2 * local_inner + start, HD), :]
    ones = jnp.ones((16, SEQ), BF)
    return jnp.concatenate([q, ones], 0), jnp.concatenate([k, mask_rows], 0), v, ones


def mask_block(length):
    keep = (iota((16, SEQ), 1) < length) | (iota((16, SEQ), 0) > 0)
    return jnp.where(keep, 0.0, NEGATIVE).astype(BF)


def score_pieces(k, q, block, near, below):
    cols = slice(block * TILE, (block + 1) * TILE)
    qb = q[:, cols]
    pieces = []
    if block >= 2:
        pieces.append((0, (block - 1) * TILE, dot(k[: (block - 1) * TILE], qb)))
    if block >= 1:
        lo = (block - 1) * TILE
        pieces.append((lo, block * TILE, dot(k[lo : lo + TILE], qb) + below))
    lo = block * TILE
    pieces.append((lo, lo + TILE, dot(k[lo : lo + TILE], qb) + near))
    return cols, pieces


def attn_fwd_kernel(first, heads, scal_ref, table_ref, *refs):
    if first:
        own_ref, other_ref, gain_ref, w_ref, ow_ref = refs[:5]
        normed_ref, qkvt_ref, mixt_ref, lse_ref, part_ref = refs[5:]
        half = own_ref.shape[0]
        core = scal_ref[0]
        for source, place in ((own_ref, core), (other_ref, 1 - core)):
            x = source[...].astype(F32)
            normed_ref[pl.ds(pl.multiple_of(place * half, half), half), :] = (
                x * rms(x) * gain_ref[...]
            ).astype(BF)
    else:
        normed_ref, w_ref, ow_ref, part_in = refs[:4]
        qkvt_ref, mixt_ref, lse_ref, keep_ref, send_ref, part_ref = refs[4:]
    local_inner = heads * HD
    qkvt_ref[...] = dot(w_ref[...], normed_ref[...], 1, 1).astype(BF)
    masks = mask_block(scal_ref[1])
    lse_ref[...] = jnp.zeros_like(lse_ref)

    for head in range(heads):
        near, below = bias_tiles(table_ref, head)
        q, kt, v, ones = head_pieces(qkvt_ref, masks, head, local_inner)
        k = kt.T
        vx = jnp.concatenate([v, ones], 0)
        for block in range(SEQ // TILE):
            cols, pieces = score_pieces(k, q, block, near, below)
            top = functools.reduce(
                jnp.maximum, [jnp.max(s, axis=0, keepdims=True) for _, _, s in pieces]
            )
            total = None
            for lo, hi, s in pieces:
                term = dot(vx[:, lo:hi], jnp.exp(s - top).astype(BF))
                total = term if total is None else total + term
            weight = total[HD : HD + 1]
            mixt_ref[head * HD : (head + 1) * HD, cols] = (total[:HD] / weight).astype(BF)
            lse_ref[head : head + 1, cols] = top + jnp.log(weight)
    part = dot(mixt_ref[...], ow_ref[...], 0, 0)
    if first:
        part_ref[...] = part
    else:
        part_ref[...] = part + part_in[...]
        half = keep_ref.shape[0]
        core = scal_ref[0]
        keep_ref[...] = part_ref[pl.ds(pl.multiple_of(core * half, half), half), :]
        send_ref[...] = part_ref[pl.ds(pl.multiple_of((1 - core) * half, half), half), :].astype(BF)


def attn_bwd_kernel(last, heads, scal_ref, table_ref, *refs):
    if last:
        (normed_ref, w_ref, ow_ref, qkvt_ref, mixt_ref, lse_ref, own_ref, other_ref, part_in) = refs[:9]
        gw_ref, gow_ref, gbias_ref, keep_ref, send_ref, ga_ref, got_ref, gt_ref, d0_ref, d1_ref, part_ref = refs[9:]
    else:
        (normed_ref, w_ref, ow_ref, qkvt_ref, mixt_ref, lse_ref, own_ref, other_ref) = refs[:8]
        gw_ref, gow_ref, gbias_ref, part_ref, ga_ref, got_ref, gt_ref, d0_ref, d1_ref = refs[8:]
    local_inner = heads * HD
    half = own_ref.shape[0]
    core = scal_ref[0]
    ga_ref[pl.ds(pl.multiple_of(core * half, half), half), :] = own_ref[...]
    ga_ref[pl.ds(pl.multiple_of((1 - core) * half, half), half), :] = other_ref[...]
    got_ref[...] = dot(ow_ref[...], ga_ref[...], 1, 1).astype(BF)
    gow_ref[...] = dot(mixt_ref[...], ga_ref[...]).astype(gow_ref.dtype)
    masks = mask_block(scal_ref[1])
    gbias_ref[...] = jnp.zeros_like(gbias_ref)
    ahead = iota((TILE, TILE), 1) >= iota((TILE, TILE), 0)
    spot = (iota((TILE, 128), 0) + 1) % TILE
    flip = (iota((TILE, TILE), 0) + iota((TILE, TILE), 1) == TILE - 1).astype(F32)
    bucket = jnp.zeros((TILE, 128), jnp.int32)
    for edge in EDGES:
        bucket = bucket + (spot >= edge).astype(jnp.int32)
    hot = (bucket == iota((TILE, 128), 1)).astype(F32)

    for head in range(heads):
        near, below = bias_tiles(table_ref, head)
        q, kt, vt, _ = head_pieces(qkvt_ref, masks, head, local_inner)
        k = kt.T
        v = vt.T
        rows = slice(head * HD, (head + 1) * HD)
        gt = got_ref[rows, :]
        delta = jnp.sum(gt.astype(F32) * mixt_ref[rows, :].astype(F32), axis=0, keepdims=True)
        gk = [None] * (SEQ // TILE)
        gv = [None] * (SEQ // TILE)
        far = jnp.zeros((8, TILE), F32)
        for block in range(SEQ // TILE):
            cols, pieces = score_pieces(k, q, block, near, below)
            gb = gt[:, cols]
            qb = q[:HD, cols]
            lse = lse_ref[head : head + 1, cols]
            db = delta[:, cols]
            gq = None
            for lo, hi, s in pieces:
                p = jnp.exp(s - lse)
                ds = p * (dot(v[lo:hi], gb) - db)
                pb = p.astype(BF)
                dsb = ds.astype(BF)
                term = dot(kt[:HD, lo:hi], dsb)
                gq = term if gq is None else gq + term
                tv = dot(pb, gb, 1, 1)
                tk = dot(dsb, qb, 1, 1)
                for tile in range(lo // TILE, hi // TILE):
                    part = slice(tile * TILE - lo, (tile + 1) * TILE - lo)
                    gv[tile] = tv[part] if gv[tile] is None else gv[tile] + tv[part]
                    gk[tile] = tk[part] if gk[tile] is None else gk[tile] + tk[part]
                if hi == (block + 1) * TILE:
                    d0_ref[...] = ds if block == 0 else d0_ref[...] + ds
                elif hi == block * TILE and lo == (block - 1) * TILE:
                    d1_ref[...] = ds if block == 1 else d1_ref[...] + ds
                else:
                    far = far + jnp.sum(ds.reshape((hi - lo) // 8, 8, TILE), axis=0)
            gt_ref[rows, cols] = (gq * HD**-0.5).astype(BF)
        for tile in range(SEQ // TILE):
            cols = slice(tile * TILE, (tile + 1) * TILE)
            gt_ref[local_inner + head * HD : local_inner + (head + 1) * HD, cols] = (
                gk[tile].T.astype(BF)
            )
            gt_ref[2 * local_inner + head * HD : 2 * local_inner + (head + 1) * HD, cols] = (
                gv[tile].T.astype(BF)
            )
        d1 = d1_ref[...]
        ring = jnp.where(ahead, d0_ref[...], d1)
        turned = pltpu.roll(
            dot(flip, ring, 1, 0, lax.Precision.HIGHEST), 0, 1, stride=1, stride_axis=0
        )
        far = far + jnp.sum(jnp.where(ahead, d1, 0.0).reshape(TILE // 8, 8, TILE), axis=0)
        line = jnp.sum(turned, axis=0, keepdims=True)
        sums = dot(
            jnp.broadcast_to(line, (8, TILE)), hot, 1, 0, lax.Precision.HIGHEST
        )
        sums = sums + jnp.where(iota((8, 128), 1) == NB - 1, jnp.sum(far), 0.0)
        gbias_ref[head : head + 1, :] = sums[0:1]
    gw_ref[...] = dot(gt_ref[...], normed_ref[...]).astype(gw_ref.dtype)
    part = dot(gt_ref[...], w_ref[...], 0, 0)
    if last:
        part_ref[...] = part + part_in[...]
        keep_ref[...] = part_ref[pl.ds(pl.multiple_of(core * half, half), half), :]
        send_ref[...] = part_ref[pl.ds(pl.multiple_of((1 - core) * half, half), half), :].astype(BF)
    else:
        part_ref[...] = part


def middle_kernel(
    experts, cap, x_ref, keep_ref, got_ref, gain_ref, router_ref, routes_ref, slots_ref, hidden_ref, packed_ref, meta_ref
):
    hidden = x_ref[...].astype(F32) + keep_ref[...] + got_ref[...].astype(F32)
    hidden_ref[...] = hidden
    normed = (hidden * rms(hidden) * gain_ref[...]).astype(BF)
    rows = hidden.shape[0]
    spots = experts * cap
    slots = slots_ref[...].astype(jnp.int32)
    where = iota((spots, rows), 0)
    pick0 = where == slots[0:1]
    pick1 = where == slots[1:2]
    packed_ref[...] = dot((pick0 | pick1).astype(BF), normed).astype(BF)
    logits = dot(router_ref[...], normed, 1, 1)
    routes = routes_ref[...]
    first, second = routes[0:1], routes[1:2]
    ids = iota((experts, rows), 0)
    gap = jnp.sum(
        logits * ((ids == first).astype(F32) - (ids == second).astype(F32)), axis=0, keepdims=True
    )
    gate0 = 1.0 / (1.0 + jnp.exp(-gap))
    gate1 = 1.0 / (1.0 + jnp.exp(gap))
    line = iota((8, rows), 0)

    def lines(gate, code):
        high = gate.astype(BF).astype(F32)
        mid = (gate - high).astype(BF).astype(F32)
        low = gate - high - mid
        picked = jnp.where(line == 0, high, jnp.where(line == 1, mid, jnp.where(line == 2, low, 0.0)))
        return jnp.where(line == 3, (code + 1).astype(F32), picked).astype(BF)

    meta = dot(lines(gate0, second), pick0.astype(BF), 1, 1) + dot(
        lines(gate1, first), pick1.astype(BF), 1, 1
    )
    for number in range(experts):
        meta_ref[number] = meta[:, number * cap : (number + 1) * cap]


def gelu_pair(v):
    squared = v * v
    slope = GELU * (1.0 + 3 * CUBIC * squared)
    t = jnp.tanh(v * (GELU + GELU * CUBIC * squared))
    half = 0.5 + 0.5 * t
    return v * half, half + 0.5 * v * (1.0 - t * t) * slope


def expert_kernel(
    count, cap, packed_ref, send_meta_ref, grads_ref, router_ref, w0, w1, w2, w3,
    came_ref, result_ref, gw_ref, grouter_ref,
    w_ref, x_ref, xt_ref, geot_ref, act_ref, gi_ref, gsend_ref, meta_ref, acc_ref, stage_ref,
    x_send, x_recv, m_send, m_recv, r_send, r_recv, local_sem, w_sem, out_sem,
):
    me = lax.axis_index("expert")
    barrier = pltpu.get_barrier_semaphore()

    def peer(k):
        return lax.rem(me + k, count)

    def source(k):
        return lax.rem(me + count - k, count)

    def greet(k, carry):
        pl.semaphore_signal(
            barrier, inc=1, device_id={"expert": peer(k)}, device_id_type=pl.DeviceIdType.MESH
        )
        return carry

    lax.fori_loop(1, count, greet, 0)
    pl.semaphore_wait(barrier, count - 1)

    def rows_of(k):
        return pl.ds(pl.multiple_of(k * cap, cap), cap)

    def send_rows(k):
        return pltpu.make_async_remote_copy(
            src_ref=packed_ref.at[rows_of(peer(k))],
            dst_ref=x_ref.at[rows_of(k)],
            send_sem=x_send.at[k],
            recv_sem=x_recv.at[k],
            device_id={"expert": peer(k)},
            device_id_type=pl.DeviceIdType.MESH,
        )

    def send_meta(k):
        return pltpu.make_async_remote_copy(
            src_ref=send_meta_ref.at[peer(k)],
            dst_ref=meta_ref.at[k],
            send_sem=m_send.at[k],
            recv_sem=m_recv.at[k],
            device_id={"expert": peer(k)},
            device_id_type=pl.DeviceIdType.MESH,
        )

    def send_back(k):
        return pltpu.make_async_remote_copy(
            src_ref=gsend_ref.at[rows_of(k)],
            dst_ref=came_ref.at[rows_of(me)],
            send_sem=r_send.at[k],
            recv_sem=r_recv.at[k],
            device_id={"expert": source(k)},
            device_id_type=pl.DeviceIdType.MESH,
        )

    def start_sends(k, carry):
        send_meta(k).start()
        send_rows(k).start()
        return carry

    lax.fori_loop(1, count, start_sends, 0)
    own_rows = pltpu.make_async_copy(packed_ref.at[rows_of(me)], x_ref.at[rows_of(0)], local_sem.at[0])
    own_rows.start()
    own_meta = pltpu.make_async_copy(send_meta_ref.at[me], meta_ref.at[0], local_sem.at[1])
    own_meta.start()
    loads = [
        pltpu.make_async_copy(w, w_ref.at[i], w_sem.at[i]) for i, w in enumerate((w0, w1, w2, w3))
    ]
    for load in loads:
        load.start()
    grouter_ref[...] = jnp.zeros_like(grouter_ref)
    experts = router_ref.shape[1]
    own_rows.wait()
    own_meta.wait()
    for load in loads:
        load.wait()
    group = max(1, CHUNK // cap)
    span = group * cap

    def chunk(j, carry):
        for i in range(group):
            k = j * group + i

            @pl.when(k > 0)
            def _():
                send_rows(k).wait_recv()
                send_meta(k).wait_recv()

        here = pl.ds(pl.multiple_of(j * span, span), span)
        meta = jnp.concatenate([meta_ref[j * group + i].T for i in range(group)], axis=0)
        gate = meta[:, 0:1] + meta[:, 1:2] + meta[:, 2:3]
        code = meta[:, 3:4].astype(jnp.int32)
        gy = jnp.concatenate([grads_ref[rows_of(source(j * group + i)), :] for i in range(group)], axis=0)
        geo = (gate * gy.astype(F32)).astype(BF)
        x = x_ref[here, :]
        xt = x.T
        xt_ref[j] = xt
        geot_ref[j] = geo.T
        acc_ref[...] = jnp.zeros_like(acc_ref)

        def quarter(q, worth):
            inner = dot(x, w_ref[q, :D])
            grad_active = dot(geo, w_ref[q, D:], 1, 1)
            act, slope = gelu_pair(inner)
            gi = (slope * grad_active).astype(BF)
            act_ref[q, here] = act.astype(BF)
            gi_ref[q, here] = gi
            acc_ref[...] += dot(gi, w_ref[q, :D], 1, 1)
            return worth + jnp.sum(act * grad_active, axis=1, keepdims=True)

        worth = lax.fori_loop(0, 4, quarter, jnp.zeros((span, 1), F32))
        ids = iota((span, experts), 1)
        signs = (ids == me).astype(F32) - (ids + 1 == code).astype(F32)
        share = jnp.where(code > 0, (1.0 - gate) * worth, 0.0) * signs
        high = share.astype(BF)
        low = (share - high.astype(F32)).astype(BF)
        gsend_ref[here, :] = (acc_ref[...] + dot(high, router_ref[...], 1, 1)).astype(BF)
        grouter_ref[...] += dot(high.T, x) + dot(low.T, x)
        for i in range(group):
            k = j * group + i

            @pl.when(k > 0)
            def _():
                send_back(k).start()

        return carry

    lax.fori_loop(0, count // group, chunk, 0)
    own_back = pltpu.make_async_copy(gsend_ref.at[rows_of(0)], came_ref.at[rows_of(me)], local_sem.at[0])
    own_back.start()

    def results(j, carry):
        here = pl.ds(pl.multiple_of(j * span, span), span)
        meta = jnp.concatenate([meta_ref[j * group + i].T for i in range(group)], axis=0)
        gate = meta[:, 0:1] + meta[:, 1:2] + meta[:, 2:3]
        acc_ref[...] = jnp.zeros_like(acc_ref)

        def quarter(q, c):
            acc_ref[...] += dot(act_ref[q, here], w_ref[q, D:])
            return c

        lax.fori_loop(0, 4, quarter, 0)
        out = (gate * acc_ref[...]).astype(BF)
        for i in range(group):
            result_ref[rows_of(source(j * group + i)), :] = out[i * cap : (i + 1) * cap]
        return carry

    lax.fori_loop(0, count // group, results, 0)

    tiles = D // TILE

    def store(step, slot):
        q = step // (2 * tiles)
        place = lax.rem(step, 2 * tiles)
        return pltpu.make_async_copy(
            stage_ref.at[slot],
            gw_ref.at[q, pl.ds(pl.multiple_of(place * TILE, TILE), TILE)],
            out_sem.at[slot],
        )

    def weights(step, carry):
        q = step // (2 * tiles)
        place = lax.rem(step, 2 * tiles)
        slot = lax.rem(step, 2)

        @pl.when(step >= 2)
        def _():
            store(step - 2, slot).wait()

        def reduce(left_ref, right_ref, tile):
            acc_ref[...] = jnp.zeros_like(acc_ref)

            def one(j, c):
                lines = pl.ds(pl.multiple_of(tile * TILE, TILE), TILE)
                there = pl.ds(pl.multiple_of(j * span, span), span)
                acc_ref[...] += dot(left_ref[j, lines], right_ref[q, there])
                return c

            lax.fori_loop(0, count // group, one, 0)
            stage_ref[slot] = acc_ref[...].astype(BF)

        @pl.when(place < tiles)
        def _():
            reduce(xt_ref, gi_ref, place)

        @pl.when(place >= tiles)
        def _():
            reduce(geot_ref, act_ref, place - tiles)

        store(step, slot).start()
        return carry

    steps = 8 * tiles
    lax.fori_loop(0, steps, weights, 0)
    for step in (steps - 2, steps - 1):
        store(step, step % 2).wait()
    own_back.wait()

    def finish(k, carry):
        send_rows(k).wait_send()
        send_meta(k).wait_send()
        send_back(k).wait()
        return carry

    lax.fori_loop(1, count, finish, 0)


def turn_kernel(nv_ref, came_ref, slots_ref, hidden_ref, gain_ref, grad_ref, gh_ref, ga_ref, gain_out):
    gn = dot(back_matrix(slots_ref, came_ref.shape[0]), came_ref[...])
    hidden = hidden_ref[...]
    scale = rms(hidden)
    unit = hidden * scale
    gain_out[...] = jnp.broadcast_to(jnp.sum(gn * unit, axis=0, keepdims=True), gain_out.shape)
    g = gn * gain_ref[...]
    valid = (iota((hidden.shape[0], 1), 0) < nv_ref[0]).astype(F32)
    gh = scale * (g - unit * jnp.mean(g * unit, axis=1, keepdims=True)) + valid * grad_ref[...].astype(F32)
    gh_ref[...] = gh
    ga_ref[...] = gh.astype(BF)


def output_kernel(nv_ref, came_ref, slots_ref, hidden_ref, out_ref):
    mix = dot(back_matrix(slots_ref, came_ref.shape[0]), came_ref[...])
    hidden = hidden_ref[...]
    valid = (iota((hidden.shape[0], 1), 0) < nv_ref[0]).astype(F32)
    out_ref[...] = (valid * (hidden + mix)).astype(BF)


def last_kernel(x_ref, keep_ref, got_ref, gain_ref, gh_ref, out_ref, gain_out):
    x = x_ref[...].astype(F32)
    scale = rms(x)
    unit = x * scale
    gn = keep_ref[...] + got_ref[...].astype(F32)
    gain_out[...] = jnp.broadcast_to(jnp.sum(gn * unit, axis=0, keepdims=True), gain_out.shape)
    g = gn * gain_ref[...]
    out_ref[...] = (
        gh_ref[...] + scale * (g - unit * jnp.mean(g * unit, axis=1, keepdims=True))
    ).astype(BF)


def moe(experts, cap, packed, meta, grads, router, quarters):
    spots = experts * cap
    groups = spots // CHUNK
    anyspec = pl.BlockSpec(memory_space=pl.ANY)
    dma = pltpu.SemaphoreType.DMA
    return pl.pallas_call(
        functools.partial(expert_kernel, experts, cap),
        out_shape=[
            jax.ShapeDtypeStruct((spots, D), BF),
            jax.ShapeDtypeStruct((spots, D), BF),
            jax.ShapeDtypeStruct((4, 2 * D, D), BF),
            jax.ShapeDtypeStruct((experts, D), F32),
        ],
        in_specs=[anyspec, VM, VM, VM] + [anyspec] * 4,
        out_specs=[anyspec, VM, anyspec, VM],
        scratch_shapes=[
            pltpu.VMEM((4, 2 * D, D), BF),
            pltpu.VMEM((spots, D), BF),
            pltpu.VMEM((groups, D, CHUNK), BF),
            pltpu.VMEM((groups, D, CHUNK), BF),
            pltpu.VMEM((4, spots, D), BF),
            pltpu.VMEM((4, spots, D), BF),
            pltpu.VMEM((spots, D), BF),
            pltpu.VMEM((experts, 8, cap), F32),
            pltpu.VMEM((CHUNK, D), F32),
            pltpu.VMEM((2, CHUNK, D), BF),
            dma((experts,)),
            dma((experts,)),
            dma((experts,)),
            dma((experts,)),
            dma((experts,)),
            dma((experts,)),
            dma((2,)),
            dma((4,)),
            dma((2,)),
        ],
        compiler_params=pltpu.CompilerParams(
            collective_id=1, has_side_effects=True, vmem_limit_bytes=60 * MIB
        ),
        cost_estimate=pl.CostEstimate(flops=12 * spots * D * 4 * D, bytes_accessed=60 * MIB, transcendentals=0),
        name="experts",
    )(packed, meta, grads, router, *quarters)


def shards(
    inputs,
    lengths,
    routes,
    attn_gain,
    qkv_weight,
    out_weight,
    rel_bias,
    moe_gain,
    router_weight,
    up_weight,
    down_weight,
    out_grad,
):
    rows = inputs.shape[0]
    rank = lax.axis_index("tensor")
    expert = lax.axis_index("expert")
    heads = rel_bias.shape[1]
    inner = heads * HD
    experts = router_weight.shape[1]
    cap = 4 * rows // experts
    spots = experts * cap
    core = rank % 2
    length = lengths[rank // 2]
    nvalid = jnp.clip(length - core * rows, 0, rows).astype(jnp.int32).reshape(1)
    scal = jnp.stack([core, length]).astype(jnp.int32)

    def swap(x, bit):
        return lax.ppermute(x, "tensor", [(i, i ^ bit) for i in range(4)])

    gain1 = attn_gain.reshape(1, D)
    gain2 = moe_gain.reshape(1, D)
    other = swap(inputs, 1)
    wt = jnp.transpose(qkv_weight.reshape(D, 3 * inner))
    pair_w = swap(jnp.concatenate([wt, out_weight], axis=0), 2)
    pair_table = swap(rel_bias, 2)

    routes_t = jnp.transpose(routes)
    packed_grad, slots = call(
        functools.partial(route_kernel, experts, cap),
        [((spots, D), BF), ((8, rows), F32)],
        (nvalid, routes_t, out_grad),
        [SM, VM, VM],
        flops=2 * spots * rows * D,
        moved=4 * MIB,
        name="route",
    )

    def exchange(x):
        return lax.all_to_all(
            x.reshape(experts, cap, x.shape[-1]), "expert", split_axis=0, concat_axis=0, tiled=True
        ).reshape(x.shape)

    grads_in = exchange(packed_grad)
    mine = jnp.concatenate([up_weight[0], down_weight[0]], axis=0)
    far = swap(mine, 2)
    side = swap(mine, 1)
    cross = swap(far, 1)
    quarters = [mine, side, far, cross]

    attn_cost = dict(
        flops=2 * SEQ * D * 4 * inner + heads * SEQ * SEQ * 160, moved=6 * MIB, exps=heads * SEQ * SEQ
    )
    normed, qkvt0, mixt0, lse0, part0 = call(
        functools.partial(attn_fwd_kernel, True, heads),
        [((SEQ, D), BF), ((3 * inner, SEQ), BF), ((inner, SEQ), BF), ((8, SEQ), F32), ((SEQ, D), F32)],
        (scal, rel_bias, inputs, other, gain1, wt, out_weight),
        [SM, SM] + [VM] * 5,
        name="attend_own",
        **attn_cost,
    )
    wt1, ow1 = pair_w[: 3 * inner], pair_w[3 * inner :]
    qkvt1, mixt1, lse1, keep, send = call(
        functools.partial(attn_fwd_kernel, False, heads),
        [((3 * inner, SEQ), BF), ((inner, SEQ), BF), ((8, SEQ), F32), ((rows, D), F32), ((rows, D), BF)],
        (scal, pair_table, normed, wt1, ow1, part0),
        [SM, SM] + [VM] * 4,
        scratch=[pltpu.VMEM((SEQ, D), F32)],
        name="attend_pair",
        **attn_cost,
    )
    got = swap(send, 1)
    hidden, packed_rows, meta = call(
        functools.partial(middle_kernel, experts, cap),
        [((rows, D), F32), ((spots, D), BF), ((experts, 8, cap), F32)],
        (inputs, keep, got, gain2, jnp.transpose(router_weight), routes_t, slots),
        flops=2 * spots * rows * D,
        moved=8 * MIB,
        name="middle",
    )
    came, result, weight_grads, grad_router = moe(
        experts, cap, packed_rows, meta, grads_in, router_weight, quarters
    )
    came_out = exchange(result)

    grads = weight_grads
    near = grads[0].astype(F32) + swap(grads[1], 1).astype(F32)
    away = grads[2].astype(F32) + swap(grads[3], 1).astype(F32)
    grad_weights = near + swap(away.astype(BF), 2).astype(F32)

    grad_hidden, grad_attended, moe_part = call(
        turn_kernel,
        [((rows, D), F32), ((rows, D), BF), ((8, D), F32)],
        (nvalid, came, slots, hidden, gain2, out_grad),
        [SM] + [VM] * 5,
        flops=2 * spots * rows * D,
        moved=8 * MIB,
        name="turn",
    )
    other_grad = swap(grad_attended, 1)
    bwd_cost = dict(
        flops=2 * SEQ * D * 10 * inner + heads * SEQ * SEQ * 400, moved=9 * MIB, exps=heads * SEQ * SEQ
    )
    work = [
        pltpu.VMEM((SEQ, D), BF),
        pltpu.VMEM((inner, SEQ), BF),
        pltpu.VMEM((3 * inner, SEQ), BF),
        pltpu.VMEM((TILE, TILE), F32),
        pltpu.VMEM((TILE, TILE), F32),
    ]
    gw1, gow1, gbias1, npart = call(
        functools.partial(attn_bwd_kernel, False, heads),
        [((3 * inner, D), BF), ((inner, D), BF), ((8, 128), F32), ((SEQ, D), F32)],
        (scal, pair_table, normed, wt1, ow1, qkvt1, mixt1, lse1, grad_attended, other_grad),
        [SM, SM] + [VM] * 8,
        scratch=work,
        name="attend_pair_back",
        **bwd_cost,
    )
    gpair = swap(jnp.concatenate([gw1, gow1], axis=0), 2)
    gw0, gow0, gbias0, keep_n, send_n = call(
        functools.partial(attn_bwd_kernel, True, heads),
        [((3 * inner, D), F32), ((inner, D), F32), ((8, 128), F32), ((rows, D), F32), ((rows, D), BF)],
        (scal, rel_bias, normed, wt, out_weight, qkvt0, mixt0, lse0, grad_attended, other_grad, npart),
        [SM, SM] + [VM] * 9,
        scratch=work + [pltpu.VMEM((SEQ, D), F32)],
        name="attend_own_back",
        **bwd_cost,
    )
    got_n = swap(send_n, 1)
    grad_inputs, attn_part = call(
        last_kernel,
        [((rows, D), BF), ((8, D), F32)],
        (inputs, keep_n, got_n, gain1, grad_hidden),
        moved=6 * MIB,
        name="last",
    )
    wide = (jnp.concatenate([gw0, gow0], axis=0) + gpair.astype(F32)).astype(BF)
    wide = lax.psum(wide, "expert").astype(F32)
    outputs = call(
        output_kernel,
        [((rows, D), BF)],
        (nvalid, came_out, slots, hidden),
        [SM] + [VM] * 3,
        flops=2 * spots * rows * D,
        moved=8 * MIB,
        name="outputs",
    )[0]

    own_bias = gbias0[:heads, :NB].reshape(1, -1)
    pair_bias = gbias1[:heads, :NB].reshape(1, -1)
    ranks = jnp.arange(4, dtype=jnp.int32)[:, None]
    bias_parts = jnp.where(ranks == rank, own_bias, 0.0) + jnp.where(ranks == (rank ^ 2), pair_bias, 0.0)
    small = jnp.concatenate(
        [attn_part[0], moe_part[0], jnp.transpose(grad_router).reshape(-1), bias_parts.reshape(-1)]
    )
    small = lax.psum(small, ("expert", "tensor"))
    bias_sum = lax.dynamic_slice(
        small[2 * D + experts * D :].reshape(4, heads * NB), (rank, 0), (1, heads * NB)
    )
    return (
        outputs,
        grad_inputs,
        small[:D],
        jnp.transpose(wide[: 3 * inner]).reshape(D, 3, inner),
        wide[3 * inner :],
        jnp.transpose(bias_sum.reshape(heads, NB)),
        small[D : 2 * D],
        small[2 * D : 2 * D + experts * D].reshape(D, experts),
        grad_weights[:D][None],
        jnp.transpose(grad_weights[D:])[None],
    )


def solution(mesh):
    return jax.shard_map(
        shards,
        mesh=mesh,
        in_specs=(
            P(("expert", "tensor"), None),
            P("expert"),
            P(("expert", "tensor"), None),
            P(),
            P(None, None, "tensor"),
            P("tensor", None),
            P(None, "tensor"),
            P(),
            P(),
            P("expert", None, "tensor"),
            P("expert", "tensor", None),
            P(("expert", "tensor"), None),
        ),
        out_specs=(
            P(("expert", "tensor"), None),
            P(("expert", "tensor"), None),
            P(),
            P(None, None, "tensor"),
            P("tensor", None),
            P(None, "tensor"),
            P(),
            P(),
            P("expert", None, "tensor"),
            P("expert", "tensor", None),
        ),
        check_vma=False,
    )
```

```python
import functools

import jax
import jax.numpy as jnp
from jax import lax
from jax.experimental import pallas as pl
from jax.experimental.pallas import tpu as pltpu
from jax.sharding import PartitionSpec as P

D = 768
HD = 64
NB = 32
MAXDIST = 128
SEQ = 1024
EPSILON = 1e-06
NEGATIVE = -1e30
TILE = 256
BF = jnp.bfloat16
F32 = jnp.float32
MIB = 2**20
CHUNK = 256
GELU = 0.7978845608028654
CUBIC = 0.044715


def bucket_edges():
    half_count = NB // 2
    short_edges = list(range(1, half_count))
    long_edges = [
        int(half_count * (MAXDIST / half_count) ** (step_index / half_count))
        for step_index in range(half_count)
    ]
    return short_edges + long_edges


EDGES = bucket_edges()


def dot(a, b, ca=1, cb=0, precision=None):
    return lax.dot_general(
        a, b, (((ca,), (cb,)), ((), ())), preferred_element_type=F32, precision=precision
    )


def iota(shape, dim):
    return lax.broadcasted_iota(jnp.int32, shape, dim)


def rms(v):
    return lax.rsqrt(jnp.mean(v * v, axis=-1, keepdims=True) + EPSILON)


def call(kernel, outs, args, specs=None, scratch=(), flops=0, moved=0, exps=0, vmem=56, name=None):
    vm = pl.BlockSpec(memory_space=pltpu.VMEM)
    return pl.pallas_call(
        kernel,
        out_shape=[jax.ShapeDtypeStruct(s, d) for s, d in outs],
        in_specs=specs or [vm] * len(args),
        out_specs=[vm] * len(outs),
        scratch_shapes=list(scratch),
        compiler_params=pltpu.CompilerParams(vmem_limit_bytes=vmem * MIB),
        cost_estimate=pl.CostEstimate(flops=flops, bytes_accessed=moved, transcendentals=exps),
        name=name,
    )(*args)


VM = pl.BlockSpec(memory_space=pltpu.VMEM)
SM = pl.BlockSpec(memory_space=pltpu.SMEM)


def slot_lines(experts, cap, valid_count, routes):
    rows = routes.shape[1]
    valid = iota((1, rows), 1) < valid_count
    ids = iota((experts, rows), 0)
    hot0 = ((ids == routes[0:1]) & valid).astype(F32)
    hot1 = ((ids == routes[1:2]) & valid).astype(F32)
    before = (iota((rows, rows), 0) < iota((rows, rows), 1)).astype(BF)
    rank = dot((hot0 + hot1).astype(BF), before)
    place = ids.astype(F32) * cap + rank
    bad = jnp.where(valid, 0.0, 1.0)
    slot0 = jnp.sum(hot0 * place, axis=0, keepdims=True) - bad
    slot1 = jnp.sum(hot1 * place, axis=0, keepdims=True) - bad
    return slot0, slot1


def route_kernel(experts, cap, nv_ref, routes_ref, grad_ref, packed_ref, slots_ref):
    rows = grad_ref.shape[0]
    slot0, slot1 = slot_lines(experts, cap, nv_ref[0], routes_ref[...])
    spots = iota((experts * cap, rows), 0)
    pick0 = spots == slot0.astype(jnp.int32)
    pick1 = spots == slot1.astype(jnp.int32)
    packed_ref[...] = dot((pick0 | pick1).astype(BF), grad_ref[...]).astype(BF)
    slots_ref[...] = jnp.concatenate([slot0, slot1, jnp.zeros((6, rows), F32)], axis=0)


def back_matrix(slots_ref, spots):
    rows = slots_ref.shape[1]
    where = iota((rows, spots), 1)
    slots = slots_ref[...].T.astype(jnp.int32)
    return ((where == slots[:, 0:1]) | (where == slots[:, 1:2])).astype(BF)


def bias_tiles(table_ref, head):
    dist = iota((8, TILE), 1)
    far = table_ref[NB - 1, head]
    curve = jnp.full((8, TILE), table_ref[0, head] - far, F32)
    for number, edge in enumerate(EDGES):
        curve = jnp.where(dist >= edge, table_ref[number + 1, head] - far, curve)
    spread = jnp.broadcast_to(curve[0:1], (TILE, TILE))
    ring = pltpu.roll(spread, 0, 1, stride=1, stride_axis=0)
    ahead = iota((TILE, TILE), 1) >= iota((TILE, TILE), 0)
    return jnp.where(ahead, ring, NEGATIVE), jnp.where(ahead, 0.0, ring)


def head_pieces(qkvt_ref, mask_rows, head, local_inner):
    start = pl.multiple_of(head * HD, HD)
    q = qkvt_ref[pl.ds(start, HD), :] * jnp.asarray(HD**-0.5, BF)
    k = qkvt_ref[pl.ds(local_inner + start, HD), :]
    v = qkvt_ref[pl.ds(2 * local_inner + start, HD), :]
    ones = jnp.ones((16, SEQ), BF)
    return jnp.concatenate([q, ones], 0), jnp.concatenate([k, mask_rows], 0), v, ones


def mask_block(length):
    keep = (iota((16, SEQ), 1) < length) | (iota((16, SEQ), 0) > 0)
    return jnp.where(keep, 0.0, NEGATIVE).astype(BF)


def score_pieces(k, q, block, near, below):
    cols = slice(block * TILE, (block + 1) * TILE)
    qb = q[:, cols]
    pieces = []
    if block >= 2:
        pieces.append((0, (block - 1) * TILE, dot(k[: (block - 1) * TILE], qb)))
    if block >= 1:
        lo = (block - 1) * TILE
        pieces.append((lo, block * TILE, dot(k[lo : lo + TILE], qb) + below))
    lo = block * TILE
    pieces.append((lo, lo + TILE, dot(k[lo : lo + TILE], qb) + near))
    return cols, pieces


def attn_fwd_kernel(first, heads, scal_ref, table_ref, *refs):
    if first:
        own_ref, other_ref, gain_ref, w_ref, ow_ref = refs[:5]
        normed_ref, qkvt_ref, mixt_ref, lse_ref, part_ref = refs[5:]
        half = own_ref.shape[0]
        core = scal_ref[0]
        for source, place in ((own_ref, core), (other_ref, 1 - core)):
            x = source[...].astype(F32)
            normed_ref[pl.ds(pl.multiple_of(place * half, half), half), :] = (
                x * rms(x) * gain_ref[...]
            ).astype(BF)
    else:
        normed_ref, w_ref, ow_ref, part_in = refs[:4]
        qkvt_ref, mixt_ref, lse_ref, keep_ref, send_ref, part_ref = refs[4:]
    local_inner = heads * HD
    qkvt_ref[...] = dot(w_ref[...], normed_ref[...], 1, 1).astype(BF)
    masks = mask_block(scal_ref[1])
    lse_ref[...] = jnp.zeros_like(lse_ref)

    for head in range(heads):
        near, below = bias_tiles(table_ref, head)
        q, kt, v, ones = head_pieces(qkvt_ref, masks, head, local_inner)
        k = kt.T
        vx = jnp.concatenate([v, ones], 0)
        for block in range(SEQ // TILE):
            cols, pieces = score_pieces(k, q, block, near, below)
            top = functools.reduce(
                jnp.maximum, [jnp.max(s, axis=0, keepdims=True) for _, _, s in pieces]
            )
            total = None
            for lo, hi, s in pieces:
                term = dot(vx[:, lo:hi], jnp.exp(s - top).astype(BF))
                total = term if total is None else total + term
            weight = total[HD : HD + 1]
            mixt_ref[head * HD : (head + 1) * HD, cols] = (total[:HD] / weight).astype(BF)
            lse_ref[head : head + 1, cols] = top + jnp.log(weight)
    part = dot(mixt_ref[...], ow_ref[...], 0, 0)
    if first:
        part_ref[...] = part
    else:
        part_ref[...] = part + part_in[...]
        half = keep_ref.shape[0]
        core = scal_ref[0]
        keep_ref[...] = part_ref[pl.ds(pl.multiple_of(core * half, half), half), :]
        send_ref[...] = part_ref[pl.ds(pl.multiple_of((1 - core) * half, half), half), :].astype(BF)


def attn_bwd_kernel(last, heads, scal_ref, table_ref, *refs):
    if last:
        (normed_ref, w_ref, ow_ref, qkvt_ref, mixt_ref, lse_ref, own_ref, other_ref, part_in) = refs[:9]
        gw_ref, gow_ref, gbias_ref, keep_ref, send_ref, ga_ref, got_ref, gt_ref, d0_ref, d1_ref, part_ref = refs[9:]
    else:
        (normed_ref, w_ref, ow_ref, qkvt_ref, mixt_ref, lse_ref, own_ref, other_ref) = refs[:8]
        gw_ref, gow_ref, gbias_ref, part_ref, ga_ref, got_ref, gt_ref, d0_ref, d1_ref = refs[8:]
    local_inner = heads * HD
    half = own_ref.shape[0]
    core = scal_ref[0]
    ga_ref[pl.ds(pl.multiple_of(core * half, half), half), :] = own_ref[...]
    ga_ref[pl.ds(pl.multiple_of((1 - core) * half, half), half), :] = other_ref[...]
    got_ref[...] = dot(ow_ref[...], ga_ref[...], 1, 1).astype(BF)
    gow_ref[...] = dot(mixt_ref[...], ga_ref[...]).astype(gow_ref.dtype)
    masks = mask_block(scal_ref[1])
    gbias_ref[...] = jnp.zeros_like(gbias_ref)
    ahead = iota((TILE, TILE), 1) >= iota((TILE, TILE), 0)
    spot = (iota((TILE, 128), 0) + 1) % TILE
    flip = (iota((TILE, TILE), 0) + iota((TILE, TILE), 1) == TILE - 1).astype(F32)
    bucket = jnp.zeros((TILE, 128), jnp.int32)
    for edge in EDGES:
        bucket = bucket + (spot >= edge).astype(jnp.int32)
    hot = (bucket == iota((TILE, 128), 1)).astype(F32)

    for head in range(heads):
        near, below = bias_tiles(table_ref, head)
        q, kt, vt, _ = head_pieces(qkvt_ref, masks, head, local_inner)
        k = kt.T
        v = vt.T
        rows = slice(head * HD, (head + 1) * HD)
        gt = got_ref[rows, :]
        delta = jnp.sum(gt.astype(F32) * mixt_ref[rows, :].astype(F32), axis=0, keepdims=True)
        gk = [None] * (SEQ // TILE)
        gv = [None] * (SEQ // TILE)
        far = jnp.zeros((8, TILE), F32)
        for block in range(SEQ // TILE):
            cols, pieces = score_pieces(k, q, block, near, below)
            gb = gt[:, cols]
            qb = q[:HD, cols]
            lse = lse_ref[head : head + 1, cols]
            db = delta[:, cols]
            gq = None
            for lo, hi, s in pieces:
                p = jnp.exp(s - lse)
                ds = p * (dot(v[lo:hi], gb) - db)
                pb = p.astype(BF)
                dsb = ds.astype(BF)
                term = dot(kt[:HD, lo:hi], dsb)
                gq = term if gq is None else gq + term
                tv = dot(pb, gb, 1, 1)
                tk = dot(dsb, qb, 1, 1)
                for tile in range(lo // TILE, hi // TILE):
                    part = slice(tile * TILE - lo, (tile + 1) * TILE - lo)
                    gv[tile] = tv[part] if gv[tile] is None else gv[tile] + tv[part]
                    gk[tile] = tk[part] if gk[tile] is None else gk[tile] + tk[part]
                if hi == (block + 1) * TILE:
                    d0_ref[...] = ds if block == 0 else d0_ref[...] + ds
                elif hi == block * TILE and lo == (block - 1) * TILE:
                    d1_ref[...] = ds if block == 1 else d1_ref[...] + ds
                else:
                    far = far + jnp.sum(ds.reshape((hi - lo) // 8, 8, TILE), axis=0)
            gt_ref[rows, cols] = (gq * HD**-0.5).astype(BF)
        for tile in range(SEQ // TILE):
            cols = slice(tile * TILE, (tile + 1) * TILE)
            gt_ref[local_inner + head * HD : local_inner + (head + 1) * HD, cols] = (
                gk[tile].T.astype(BF)
            )
            gt_ref[2 * local_inner + head * HD : 2 * local_inner + (head + 1) * HD, cols] = (
                gv[tile].T.astype(BF)
            )
        d1 = d1_ref[...]
        ring = jnp.where(ahead, d0_ref[...], d1)
        turned = pltpu.roll(
            dot(flip, ring, 1, 0, lax.Precision.HIGHEST), 0, 1, stride=1, stride_axis=0
        )
        far = far + jnp.sum(jnp.where(ahead, d1, 0.0).reshape(TILE // 8, 8, TILE), axis=0)
        line = jnp.sum(turned, axis=0, keepdims=True)
        sums = dot(
            jnp.broadcast_to(line, (8, TILE)), hot, 1, 0, lax.Precision.HIGHEST
        )
        sums = sums + jnp.where(iota((8, 128), 1) == NB - 1, jnp.sum(far), 0.0)
        gbias_ref[head : head + 1, :] = sums[0:1]
    gw_ref[...] = dot(gt_ref[...], normed_ref[...]).astype(gw_ref.dtype)
    part = dot(gt_ref[...], w_ref[...], 0, 0)
    if last:
        part_ref[...] = part + part_in[...]
        keep_ref[...] = part_ref[pl.ds(pl.multiple_of(core * half, half), half), :]
        send_ref[...] = part_ref[pl.ds(pl.multiple_of((1 - core) * half, half), half), :].astype(BF)
    else:
        part_ref[...] = part


def gates_of(experts, normed, router_t, routes):
    rows = normed.shape[0]
    logits = dot(router_t, normed, 1, 1)
    ids = iota((experts, rows), 0)
    signs = (ids == routes[0:1]).astype(F32) - (ids == routes[1:2]).astype(F32)
    gap = jnp.sum(logits * signs, axis=0, keepdims=True)
    return 1.0 / (1.0 + jnp.exp(-gap)), 1.0 / (1.0 + jnp.exp(gap))


def meta_lines(gate, code):
    rows = gate.shape[1]
    line = iota((8, rows), 0)
    high = gate.astype(BF).astype(F32)
    mid = (gate - high).astype(BF).astype(F32)
    low = gate - high - mid
    picked = jnp.where(line == 0, high, jnp.where(line == 1, mid, jnp.where(line == 2, low, 0.0)))
    return jnp.where(line == 3, code, picked).astype(BF)


def hidden_rows(x_ref, keep_ref, got_ref, gain_ref, hidden_ref):
    hidden = x_ref[...].astype(F32) + keep_ref[...] + got_ref[...].astype(F32)
    hidden_ref[...] = hidden
    return (hidden * rms(hidden) * gain_ref[...]).astype(BF)


def middle_kernel(
    experts, cap, x_ref, keep_ref, got_ref, gain_ref, router_ref, routes_ref, slots_ref, hidden_ref, packed_ref, meta_ref
):
    normed = hidden_rows(x_ref, keep_ref, got_ref, gain_ref, hidden_ref)
    slots = slots_ref[...].astype(jnp.int32)
    routes = routes_ref[...]
    where = iota((experts * cap, normed.shape[0]), 0)
    pick0 = where == slots[0:1]
    pick1 = where == slots[1:2]
    packed_ref[...] = dot((pick0 | pick1).astype(BF), normed).astype(BF)
    gate0, gate1 = gates_of(experts, normed, router_ref[...], routes)
    codes = (routes + 1).astype(F32)
    meta = dot(meta_lines(gate0, codes[1:2]), pick0.astype(BF), 1, 1) + dot(
        meta_lines(gate1, codes[0:1]), pick1.astype(BF), 1, 1
    )
    for number in range(experts):
        meta_ref[number] = meta[:, number * cap : (number + 1) * cap]


def middle_line_kernel(
    experts, x_ref, keep_ref, got_ref, gain_ref, router_ref, routes_ref, slots_ref, hidden_ref, normed_ref, info_ref
):
    normed = hidden_rows(x_ref, keep_ref, got_ref, gain_ref, hidden_ref)
    normed_ref[...] = normed
    routes = routes_ref[...]
    gate0, gate1 = gates_of(experts, normed, router_ref[...], routes)
    codes = (routes + 1).astype(F32)
    info_ref[...] = jnp.concatenate(
        [slots_ref[0:2], gate0, gate1, codes, jnp.zeros((2, normed.shape[0]), F32)], axis=0
    )


def gelu_pair(v):
    squared = v * v
    slope = GELU * (1.0 + 3 * CUBIC * squared)
    t = jnp.tanh(v * (GELU + GELU * CUBIC * squared))
    half = 0.5 + 0.5 * t
    return v * half, half + 0.5 * v * (1.0 - t * t) * slope


def flipped(me, k, count):
    total, bit = 0, 1
    while bit < count:
        total = total + lax.rem(me // bit + k // bit, 2) * bit
        bit *= 2
    return total


def weight_grads(chunks, span, xt_ref, geot_ref, act_ref, gi_ref, acc_ref, stage_ref, gw_ref, out_sem):
    tiles = D // TILE

    def store(step, slot):
        q = step // (2 * tiles)
        place = lax.rem(step, 2 * tiles)
        return pltpu.make_async_copy(
            stage_ref.at[slot],
            gw_ref.at[q, pl.ds(pl.multiple_of(place * TILE, TILE), TILE)],
            out_sem.at[slot],
        )

    def weights(step, carry):
        q = step // (2 * tiles)
        place = lax.rem(step, 2 * tiles)
        slot = lax.rem(step, 2)

        @pl.when(step >= 2)
        def _():
            store(step - 2, slot).wait()

        def reduce(left_ref, right_ref, tile):
            acc_ref[...] = jnp.zeros_like(acc_ref)

            def one(j, c):
                lines = pl.ds(pl.multiple_of(tile * TILE, TILE), TILE)
                there = pl.ds(pl.multiple_of(j * span, span), span)
                acc_ref[...] += dot(left_ref[j, lines], right_ref[q, there])
                return c

            lax.fori_loop(0, chunks, one, 0)
            stage_ref[slot] = acc_ref[...].astype(BF)

        @pl.when(place < tiles)
        def _():
            reduce(xt_ref, gi_ref, place)

        @pl.when(place >= tiles)
        def _():
            reduce(geot_ref, act_ref, place - tiles)

        store(step, slot).start()
        return carry

    steps = 8 * tiles
    lax.fori_loop(0, steps, weights, 0)
    for step in (steps - 2, steps - 1):
        store(step, step % 2).wait()


def expert_kernel(
    count, cap, packed_ref, send_meta_ref, grads_ref, router_ref, w0, w1, w2, w3,
    came_ref, result_ref, gw_ref, grouter_ref,
    w_ref, x_ref, xt_ref, geot_ref, act_ref, gi_ref, gsend_ref, meta_ref, acc_ref, stage_ref,
    x_send, x_recv, m_send, m_recv, r_send, r_recv, local_sem, w_sem, out_sem,
):
    me = lax.axis_index("expert")
    barrier = pltpu.get_barrier_semaphore()

    def peer(k):
        return flipped(me, k, count)

    source = peer

    def greet(k, carry):
        pl.semaphore_signal(
            barrier, inc=1, device_id={"expert": peer(k)}, device_id_type=pl.DeviceIdType.MESH
        )
        return carry

    lax.fori_loop(1, count, greet, 0)
    pl.semaphore_wait(barrier, count - 1)

    def rows_of(k):
        return pl.ds(pl.multiple_of(k * cap, cap), cap)

    def send_rows(k):
        return pltpu.make_async_remote_copy(
            src_ref=packed_ref.at[rows_of(peer(k))],
            dst_ref=x_ref.at[rows_of(k)],
            send_sem=x_send.at[k],
            recv_sem=x_recv.at[k],
            device_id={"expert": peer(k)},
            device_id_type=pl.DeviceIdType.MESH,
        )

    def send_meta(k):
        return pltpu.make_async_remote_copy(
            src_ref=send_meta_ref.at[peer(k)],
            dst_ref=meta_ref.at[k],
            send_sem=m_send.at[k],
            recv_sem=m_recv.at[k],
            device_id={"expert": peer(k)},
            device_id_type=pl.DeviceIdType.MESH,
        )

    def send_back(k):
        return pltpu.make_async_remote_copy(
            src_ref=gsend_ref.at[rows_of(k)],
            dst_ref=came_ref.at[rows_of(me)],
            send_sem=r_send.at[k],
            recv_sem=r_recv.at[k],
            device_id={"expert": source(k)},
            device_id_type=pl.DeviceIdType.MESH,
        )

    def start_sends(k, carry):
        send_meta(k).start()
        send_rows(k).start()
        return carry

    lax.fori_loop(count // 2, count, start_sends, 0)
    lax.fori_loop(1, count // 2, start_sends, 0)
    own_rows = pltpu.make_async_copy(packed_ref.at[rows_of(me)], x_ref.at[rows_of(0)], local_sem.at[0])
    own_rows.start()
    own_meta = pltpu.make_async_copy(send_meta_ref.at[me], meta_ref.at[0], local_sem.at[1])
    own_meta.start()
    loads = [
        pltpu.make_async_copy(w, w_ref.at[i], w_sem.at[i]) for i, w in enumerate((w0, w1, w2, w3))
    ]
    for load in loads:
        load.start()
    grouter_ref[...] = jnp.zeros_like(grouter_ref)
    experts = router_ref.shape[1]
    own_rows.wait()
    own_meta.wait()
    for load in loads:
        load.wait()
    group = max(1, CHUNK // cap)
    span = group * cap

    def chunk(j, carry):
        for i in range(group):
            k = j * group + i

            @pl.when(k > 0)
            def _():
                send_rows(k).wait_recv()
                send_meta(k).wait_recv()

        here = pl.ds(pl.multiple_of(j * span, span), span)
        meta = jnp.concatenate([meta_ref[j * group + i].T for i in range(group)], axis=0)
        gate = meta[:, 0:1] + meta[:, 1:2] + meta[:, 2:3]
        code = meta[:, 3:4].astype(jnp.int32)
        gy = jnp.concatenate([grads_ref[rows_of(source(j * group + i)), :] for i in range(group)], axis=0)
        geo = (gate * gy.astype(F32)).astype(BF)
        x = x_ref[here, :]
        xt = x.T
        xt_ref[j] = xt
        geot_ref[j] = geo.T
        acc_ref[...] = jnp.zeros_like(acc_ref)

        def quarter(q, worth):
            inner = dot(x, w_ref[q, :D])
            grad_active = dot(geo, w_ref[q, D:], 1, 1)
            act, slope = gelu_pair(inner)
            gi = (slope * grad_active).astype(BF)
            act_ref[q, here] = act.astype(BF)
            gi_ref[q, here] = gi
            acc_ref[...] += dot(gi, w_ref[q, :D], 1, 1)
            return worth + jnp.sum(act * grad_active, axis=1, keepdims=True)

        worth = lax.fori_loop(0, 4, quarter, jnp.zeros((span, 1), F32))
        ids = iota((span, experts), 1)
        signs = (ids == me).astype(F32) - (ids + 1 == code).astype(F32)
        share = jnp.where(code > 0, (1.0 - gate) * worth, 0.0) * signs
        high = share.astype(BF)
        low = (share - high.astype(F32)).astype(BF)
        gsend_ref[here, :] = (acc_ref[...] + dot(high, router_ref[...], 1, 1)).astype(BF)
        grouter_ref[...] += dot(high.T, x) + dot(low.T, x)
        for i in range(group):
            k = j * group + i

            @pl.when(k > 0)
            def _():
                send_back(k).start()

        return carry

    lax.fori_loop(0, count // group, chunk, 0)
    own_back = pltpu.make_async_copy(gsend_ref.at[rows_of(0)], came_ref.at[rows_of(me)], local_sem.at[0])
    own_back.start()

    def results(j, carry):
        here = pl.ds(pl.multiple_of(j * span, span), span)
        meta = jnp.concatenate([meta_ref[j * group + i].T for i in range(group)], axis=0)
        gate = meta[:, 0:1] + meta[:, 1:2] + meta[:, 2:3]
        acc_ref[...] = jnp.zeros_like(acc_ref)

        def quarter(q, c):
            acc_ref[...] += dot(act_ref[q, here], w_ref[q, D:])
            return c

        lax.fori_loop(0, 4, quarter, 0)
        out = (gate * acc_ref[...]).astype(BF)
        for i in range(group):
            result_ref[rows_of(source(j * group + i)), :] = out[i * cap : (i + 1) * cap]
        return carry

    lax.fori_loop(0, count // group, results, 0)

    weight_grads(count // group, span, xt_ref, geot_ref, act_ref, gi_ref, acc_ref, stage_ref, gw_ref, out_sem)
    own_back.wait()

    def finish(k, carry):
        send_rows(k).wait_send()
        send_meta(k).wait_send()
        send_back(k).wait()
        return carry

    lax.fori_loop(1, count, finish, 0)


def mesh_copy(src, dst, send_sem, recv_sem, target):
    return pltpu.make_async_remote_copy(
        src_ref=src,
        dst_ref=dst,
        send_sem=send_sem,
        recv_sem=recv_sem,
        device_id={"expert": target},
        device_id_type=pl.DeviceIdType.MESH,
    )


LINE = 4


def expert_line_kernel(
    cap, normed_ref, info_in, grads_ref, router_ref, w0, w1, w2, w3,
    came_ref, result_ref, gw_ref, grouter_ref,
    w_ref, block_ref, info_ref, x_ref, xs_ref, meta_ref, ms_ref, xt_ref, geot_ref, act_ref, gi_ref, acc_ref, stage_ref,
    b_send, b_recv, i_send, i_recv, x_send, x_recv, m_send, m_recv, r_send, r_recv, local_sem, w_sem, out_sem,
):
    count = 2 * LINE
    me = lax.axis_index("expert")
    place = me // 2
    side = me - 2 * place
    mate = me + 1 - 2 * side
    barrier = pltpu.get_barrier_semaphore()

    def greet(k, carry):
        pl.semaphore_signal(
            barrier,
            inc=1,
            device_id={"expert": lax.rem(me + k, count)},
            device_id_type=pl.DeviceIdType.MESH,
        )
        return carry

    lax.fori_loop(1, count, greet, 0)
    pl.semaphore_wait(barrier, count - 1)

    def along(block, step):
        return (
            mesh_copy(
                info_ref.at[block],
                info_ref.at[block],
                i_send.at[(step + 1) // 2, block],
                i_recv.at[block],
                me + 2 * step,
            ),
            mesh_copy(
                block_ref.at[block],
                block_ref.at[block],
                b_send.at[(step + 1) // 2, block],
                b_recv.at[block],
                me + 2 * step,
            ),
        )

    def across(block):
        return (
            mesh_copy(ms_ref.at[block], meta_ref.at[1, block], m_send.at[block], m_recv.at[block], mate),
            mesh_copy(xs_ref.at[block], x_ref.at[1, block], x_send.at[block], x_recv.at[block], mate),
        )

    def rows_of(number):
        return pl.ds(pl.multiple_of(number * cap, cap), cap)

    def origin(part, block):
        return 2 * block + side + part * (1 - 2 * side)

    def give_back(part, block):
        return mesh_copy(
            x_ref.at[part, block],
            came_ref.at[rows_of(me)],
            r_send.at[part, block],
            r_recv.at[me],
            origin(part, block),
        )

    def each(pair, act):
        for one in pair:
            act(one)

    own = (
        pltpu.make_async_copy(info_in, info_ref.at[place], local_sem.at[0]),
        pltpu.make_async_copy(normed_ref, block_ref.at[place], local_sem.at[1]),
    )
    each(own, lambda c: c.start())
    loads = [
        pltpu.make_async_copy(w, w_ref.at[i], w_sem.at[i]) for i, w in enumerate((w0, w1, w2, w3))
    ]
    each(loads, lambda c: c.start())
    each(own, lambda c: c.wait())

    @pl.when(place < LINE - 1)
    def _():
        each(along(place, 1), lambda c: c.start())

    @pl.when(place > 0)
    def _():
        each(along(place, -1), lambda c: c.start())

    experts = router_ref.shape[1]
    rows = normed_ref.shape[0]

    def select(block):
        info = info_ref[block]
        slots = info[0:2].astype(jnp.int32)
        lines0 = meta_lines(info[2:3], info[5:6])
        lines1 = meta_lines(info[3:4], info[4:5])
        for part, expert in ((1, mate), (0, me)):
            where = iota((cap, rows), 0) + expert * cap
            pick0 = where == slots[0:1]
            pick1 = where == slots[1:2]
            taken = dot((pick0 | pick1).astype(BF), block_ref[block]).astype(BF)
            meta = dot(lines0, pick0.astype(BF), 1, 1) + dot(lines1, pick1.astype(BF), 1, 1)
            if part:
                xs_ref[block] = taken
                ms_ref[block] = meta
                each(across(block), lambda c: c.start())
            else:
                x_ref[0, block] = taken
                meta_ref[0, block] = meta

    select(place)
    grouter_ref[...] = jnp.zeros_like(grouter_ref)
    each(loads, lambda c: c.wait())
    mirror = place // 2
    inward = place + mirror * (LINE - 1 - 2 * place)

    def block_at(i):
        step = i + inward * (1 - i // 2 - 2 * (i // 2 - i // (LINE - 1)))
        return step + mirror * (LINE - 1 - 2 * step)

    def accept(distance):
        for step in (-1, 1):
            block = place + step * distance
            inside = (block >= 0) & (block < LINE)

            @pl.when(inside)
            def _():
                each(along(block, -step), lambda c: c.wait_recv())
                ahead = place - step

                @pl.when((ahead >= 0) & (ahead < LINE))
                def _():
                    each(along(block, -step), lambda c: c.start())

        for step in (-1, 1):
            block = place + step * distance
            inside = (block >= 0) & (block < LINE)

            @pl.when(inside)
            def _():
                select(block)

    def chunk(c, carry):
        for distance in range(1, LINE):

            @pl.when(c == 2 * distance - 1)
            def _():
                accept(distance)

        part = lax.rem(c + 1, 2) - (7 - c) // 7 + c // 7
        block = block_at((c + 1) // 2 - part * ((c + 1) // 2 - (c - 1) // 2))

        @pl.when(part == 1)
        def _():
            each(across(block), lambda c: c.wait_recv())

        here = pl.ds(pl.multiple_of(c * cap, cap), cap)
        meta = meta_ref[part, block].T
        gate = meta[:, 0:1] + meta[:, 1:2] + meta[:, 2:3]
        code = meta[:, 3:4].astype(jnp.int32)
        geo = (gate * grads_ref[rows_of(origin(part, block)), :].astype(F32)).astype(BF)
        x = x_ref[part, block]
        xt_ref[c] = x.T
        geot_ref[c] = geo.T
        acc_ref[...] = jnp.zeros_like(acc_ref)

        def quarter(q, worth):
            inner = dot(x, w_ref[q, :D])
            grad_active = dot(geo, w_ref[q, D:], 1, 1)
            act, slope = gelu_pair(inner)
            gi = (slope * grad_active).astype(BF)
            act_ref[q, here] = act.astype(BF)
            gi_ref[q, here] = gi
            acc_ref[...] += dot(gi, w_ref[q, :D], 1, 1)
            return worth + jnp.sum(act * grad_active, axis=1, keepdims=True)

        worth = lax.fori_loop(0, 4, quarter, jnp.zeros((cap, 1), F32))
        ids = iota((cap, experts), 1)
        signs = (ids == me).astype(F32) - (ids + 1 == code).astype(F32)
        share = jnp.where(code > 0, (1.0 - gate) * worth, 0.0) * signs
        high = share.astype(BF)
        low = (share - high.astype(F32)).astype(BF)
        grouter_ref[...] += dot(high.T, x) + dot(low.T, x)
        x_ref[part, block] = (acc_ref[...] + dot(high, router_ref[...], 1, 1)).astype(BF)

        @pl.when(origin(part, block) != me)
        def _():
            give_back(part, block).start()

        return carry

    lax.fori_loop(0, count, chunk, 0)
    own_back = pltpu.make_async_copy(x_ref.at[0, place], came_ref.at[rows_of(me)], local_sem.at[0])
    own_back.start()

    def results(c, carry):
        part = lax.rem(c + 1, 2) - (7 - c) // 7 + c // 7
        block = block_at((c + 1) // 2 - part * ((c + 1) // 2 - (c - 1) // 2))
        here = pl.ds(pl.multiple_of(c * cap, cap), cap)
        meta = meta_ref[part, block].T
        gate = meta[:, 0:1] + meta[:, 1:2] + meta[:, 2:3]
        acc_ref[...] = jnp.zeros_like(acc_ref)

        def quarter(q, carry):
            acc_ref[...] += dot(act_ref[q, here], w_ref[q, D:])
            return carry

        lax.fori_loop(0, 4, quarter, 0)
        result_ref[rows_of(origin(part, block)), :] = (gate * acc_ref[...]).astype(BF)
        return carry

    lax.fori_loop(0, count, results, 0)
    weight_grads(count, cap, xt_ref, geot_ref, act_ref, gi_ref, acc_ref, stage_ref, gw_ref, out_sem)
    own_back.wait()

    for block in range(LINE):
        each(across(block), lambda c: c.wait_send())
        for step in (-1, 1):
            @pl.when((place + step >= 0) & (place + step < LINE) & ((place - block) * step >= 0))
            def _():
                each(along(block, step), lambda c: c.wait_send())

        for part in (0, 1):

            @pl.when(origin(part, block) != me)
            def _():
                give_back(part, block).wait_send()

    for number in range(count):

        @pl.when(number != me)
        def _():
            mesh_copy(
                x_ref.at[0, 0], came_ref.at[rows_of(number)], r_send.at[0, 0], r_recv.at[number], mate
            ).wait_recv()


def turn_kernel(nv_ref, came_ref, slots_ref, hidden_ref, gain_ref, grad_ref, gh_ref, ga_ref, gain_out):
    gn = dot(back_matrix(slots_ref, came_ref.shape[0]), came_ref[...])
    hidden = hidden_ref[...]
    scale = rms(hidden)
    unit = hidden * scale
    gain_out[...] = jnp.broadcast_to(jnp.sum(gn * unit, axis=0, keepdims=True), gain_out.shape)
    g = gn * gain_ref[...]
    valid = (iota((hidden.shape[0], 1), 0) < nv_ref[0]).astype(F32)
    gh = scale * (g - unit * jnp.mean(g * unit, axis=1, keepdims=True)) + valid * grad_ref[...].astype(F32)
    gh_ref[...] = gh
    ga_ref[...] = gh.astype(BF)


def output_kernel(nv_ref, came_ref, slots_ref, hidden_ref, out_ref):
    mix = dot(back_matrix(slots_ref, came_ref.shape[0]), came_ref[...])
    hidden = hidden_ref[...]
    valid = (iota((hidden.shape[0], 1), 0) < nv_ref[0]).astype(F32)
    out_ref[...] = (valid * (hidden + mix)).astype(BF)


def last_kernel(x_ref, keep_ref, got_ref, gain_ref, gh_ref, out_ref, gain_out):
    x = x_ref[...].astype(F32)
    scale = rms(x)
    unit = x * scale
    gn = keep_ref[...] + got_ref[...].astype(F32)
    gain_out[...] = jnp.broadcast_to(jnp.sum(gn * unit, axis=0, keepdims=True), gain_out.shape)
    g = gn * gain_ref[...]
    out_ref[...] = (
        gh_ref[...] + scale * (g - unit * jnp.mean(g * unit, axis=1, keepdims=True))
    ).astype(BF)


def moe(experts, cap, packed, meta, grads, router, quarters):
    spots = experts * cap
    groups = spots // CHUNK
    anyspec = pl.BlockSpec(memory_space=pl.ANY)
    dma = pltpu.SemaphoreType.DMA
    return pl.pallas_call(
        functools.partial(expert_kernel, experts, cap),
        out_shape=[
            jax.ShapeDtypeStruct((spots, D), BF),
            jax.ShapeDtypeStruct((spots, D), BF),
            jax.ShapeDtypeStruct((4, 2 * D, D), BF),
            jax.ShapeDtypeStruct((experts, D), F32),
        ],
        in_specs=[anyspec, VM, VM, VM] + [anyspec] * 4,
        out_specs=[anyspec, VM, anyspec, VM],
        scratch_shapes=[
            pltpu.VMEM((4, 2 * D, D), BF),
            pltpu.VMEM((spots, D), BF),
            pltpu.VMEM((groups, D, CHUNK), BF),
            pltpu.VMEM((groups, D, CHUNK), BF),
            pltpu.VMEM((4, spots, D), BF),
            pltpu.VMEM((4, spots, D), BF),
            pltpu.VMEM((spots, D), BF),
            pltpu.VMEM((experts, 8, cap), F32),
            pltpu.VMEM((CHUNK, D), F32),
            pltpu.VMEM((2, CHUNK, D), BF),
            dma((experts,)),
            dma((experts,)),
            dma((experts,)),
            dma((experts,)),
            dma((experts,)),
            dma((experts,)),
            dma((2,)),
            dma((4,)),
            dma((2,)),
        ],
        compiler_params=pltpu.CompilerParams(
            collective_id=1, has_side_effects=True, vmem_limit_bytes=60 * MIB
        ),
        cost_estimate=pl.CostEstimate(flops=12 * spots * D * 4 * D, bytes_accessed=60 * MIB, transcendentals=0),
        name="experts",
    )(packed, meta, grads, router, *quarters)


def moe_line(experts, cap, normed, info, grads, router, quarters):
    rows = normed.shape[0]
    spots = experts * cap
    anyspec = pl.BlockSpec(memory_space=pl.ANY)
    dma = pltpu.SemaphoreType.DMA
    return pl.pallas_call(
        functools.partial(expert_line_kernel, cap),
        out_shape=[
            jax.ShapeDtypeStruct((spots, D), BF),
            jax.ShapeDtypeStruct((spots, D), BF),
            jax.ShapeDtypeStruct((4, 2 * D, D), BF),
            jax.ShapeDtypeStruct((experts, D), F32),
        ],
        in_specs=[VM, VM, VM, VM] + [anyspec] * 4,
        out_specs=[anyspec, VM, anyspec, VM],
        scratch_shapes=[
            pltpu.VMEM((4, 2 * D, D), BF),
            pltpu.VMEM((LINE, rows, D), BF),
            pltpu.VMEM((LINE, 8, rows), F32),
            pltpu.VMEM((2, LINE, cap, D), BF),
            pltpu.VMEM((LINE, cap, D), BF),
            pltpu.VMEM((2, LINE, 8, cap), F32),
            pltpu.VMEM((LINE, 8, cap), F32),
            pltpu.VMEM((experts, D, cap), BF),
            pltpu.VMEM((experts, D, cap), BF),
            pltpu.VMEM((4, spots, D), BF),
            pltpu.VMEM((4, spots, D), BF),
            pltpu.VMEM((cap, D), F32),
            pltpu.VMEM((2, TILE, D), BF),
            dma((2, LINE)),
            dma((LINE,)),
            dma((2, LINE)),
            dma((LINE,)),
            dma((LINE,)),
            dma((LINE,)),
            dma((LINE,)),
            dma((LINE,)),
            dma((2, LINE)),
            dma((experts,)),
            dma((2,)),
            dma((4,)),
            dma((2,)),
        ],
        compiler_params=pltpu.CompilerParams(
            collective_id=2, has_side_effects=True, vmem_limit_bytes=62 * MIB
        ),
        cost_estimate=pl.CostEstimate(flops=12 * spots * D * 4 * D, bytes_accessed=60 * MIB, transcendentals=0),
        name="experts_line",
    )(normed, info, grads, router, *quarters)


def shards(
    inputs,
    lengths,
    routes,
    attn_gain,
    qkv_weight,
    out_weight,
    rel_bias,
    moe_gain,
    router_weight,
    up_weight,
    down_weight,
    out_grad,
):
    rows = inputs.shape[0]
    rank = lax.axis_index("tensor")
    expert = lax.axis_index("expert")
    heads = rel_bias.shape[1]
    inner = heads * HD
    experts = router_weight.shape[1]
    cap = 4 * rows // experts
    spots = experts * cap
    core = rank % 2
    length = lengths[rank // 2]
    nvalid = jnp.clip(length - core * rows, 0, rows).astype(jnp.int32).reshape(1)
    scal = jnp.stack([core, length]).astype(jnp.int32)

    def swap(x, bit):
        return lax.ppermute(x, "tensor", [(i, i ^ bit) for i in range(4)])

    gain1 = attn_gain.reshape(1, D)
    gain2 = moe_gain.reshape(1, D)
    other = swap(inputs, 1)
    wt = jnp.transpose(qkv_weight.reshape(D, 3 * inner))
    pair_w = swap(jnp.concatenate([wt, out_weight], axis=0), 2)
    pair_table = swap(rel_bias, 2)

    routes_t = jnp.transpose(routes)
    packed_grad, slots = call(
        functools.partial(route_kernel, experts, cap),
        [((spots, D), BF), ((8, rows), F32)],
        (nvalid, routes_t, out_grad),
        [SM, VM, VM],
        flops=2 * spots * rows * D,
        moved=4 * MIB,
        name="route",
    )

    def exchange(x):
        return lax.all_to_all(
            x.reshape(experts, cap, x.shape[-1]), "expert", split_axis=0, concat_axis=0, tiled=True
        ).reshape(x.shape)

    grads_in = exchange(packed_grad)
    mine, pair_w = lax.optimization_barrier(
        (jnp.concatenate([up_weight[0], down_weight[0]], axis=0), pair_w)
    )
    far = swap(mine, 2)
    side = swap(mine, 1)

    attn_cost = dict(
        flops=2 * SEQ * D * 4 * inner + heads * SEQ * SEQ * 160, moved=6 * MIB, exps=heads * SEQ * SEQ
    )
    normed, qkvt0, mixt0, lse0, part0 = call(
        functools.partial(attn_fwd_kernel, True, heads),
        [((SEQ, D), BF), ((3 * inner, SEQ), BF), ((inner, SEQ), BF), ((8, SEQ), F32), ((SEQ, D), F32)],
        (scal, rel_bias, inputs, other, gain1, wt, out_weight),
        [SM, SM] + [VM] * 5,
        name="attend_own",
        **attn_cost,
    )
    wt1, ow1 = pair_w[: 3 * inner], pair_w[3 * inner :]
    qkvt1, mixt1, lse1, keep, send = call(
        functools.partial(attn_fwd_kernel, False, heads),
        [((3 * inner, SEQ), BF), ((inner, SEQ), BF), ((8, SEQ), F32), ((rows, D), F32), ((rows, D), BF)],
        (scal, pair_table, normed, wt1, ow1, part0),
        [SM, SM] + [VM] * 4,
        scratch=[pltpu.VMEM((SEQ, D), F32)],
        name="attend_pair",
        **attn_cost,
    )
    got = swap(send, 1)
    far, got = lax.optimization_barrier((far, got))
    quarters = [mine, side, far, swap(far, 1)]
    middle_args = (inputs, keep, got, gain2, jnp.transpose(router_weight), routes_t, slots)
    if experts == 2 * LINE and cap == TILE:
        hidden, normed_two, info = call(
            functools.partial(middle_line_kernel, experts),
            [((rows, D), F32), ((rows, D), BF), ((8, rows), F32)],
            middle_args,
            moved=6 * MIB,
            name="middle",
        )
        came, result, weight_parts, grad_router = moe_line(
            experts, cap, normed_two, info, grads_in, router_weight, quarters
        )
    else:
        hidden, packed_rows, meta = call(
            functools.partial(middle_kernel, experts, cap),
            [((rows, D), F32), ((spots, D), BF), ((experts, 8, cap), F32)],
            middle_args,
            flops=2 * spots * rows * D,
            moved=8 * MIB,
            name="middle",
        )
        came, result, weight_parts, grad_router = moe(
            experts, cap, packed_rows, meta, grads_in, router_weight, quarters
        )
    came_out = exchange(result)

    grads = weight_parts
    near = grads[0].astype(F32) + swap(grads[1], 1).astype(F32)
    away = grads[2].astype(F32) + swap(grads[3], 1).astype(F32)
    grad_weights = near + swap(away.astype(BF), 2).astype(F32)

    grad_hidden, grad_attended, moe_part = call(
        turn_kernel,
        [((rows, D), F32), ((rows, D), BF), ((8, D), F32)],
        (nvalid, came, slots, hidden, gain2, out_grad),
        [SM] + [VM] * 5,
        flops=2 * spots * rows * D,
        moved=8 * MIB,
        name="turn",
    )
    other_grad = swap(grad_attended, 1)
    bwd_cost = dict(
        flops=2 * SEQ * D * 10 * inner + heads * SEQ * SEQ * 400, moved=9 * MIB, exps=heads * SEQ * SEQ
    )
    work = [
        pltpu.VMEM((SEQ, D), BF),
        pltpu.VMEM((inner, SEQ), BF),
        pltpu.VMEM((3 * inner, SEQ), BF),
        pltpu.VMEM((TILE, TILE), F32),
        pltpu.VMEM((TILE, TILE), F32),
    ]
    gw1, gow1, gbias1, npart = call(
        functools.partial(attn_bwd_kernel, False, heads),
        [((3 * inner, D), BF), ((inner, D), BF), ((8, 128), F32), ((SEQ, D), F32)],
        (scal, pair_table, normed, wt1, ow1, qkvt1, mixt1, lse1, grad_attended, other_grad),
        [SM, SM] + [VM] * 8,
        scratch=work,
        name="attend_pair_back",
        **bwd_cost,
    )
    gpair = swap(jnp.concatenate([gw1, gow1], axis=0), 2)
    gw0, gow0, gbias0, keep_n, send_n = call(
        functools.partial(attn_bwd_kernel, True, heads),
        [((3 * inner, D), F32), ((inner, D), F32), ((8, 128), F32), ((rows, D), F32), ((rows, D), BF)],
        (scal, rel_bias, normed, wt, out_weight, qkvt0, mixt0, lse0, grad_attended, other_grad, npart),
        [SM, SM] + [VM] * 9,
        scratch=work + [pltpu.VMEM((SEQ, D), F32)],
        name="attend_own_back",
        **bwd_cost,
    )
    got_n = swap(send_n, 1)
    grad_inputs, attn_part = call(
        last_kernel,
        [((rows, D), BF), ((8, D), F32)],
        (inputs, keep_n, got_n, gain1, grad_hidden),
        moved=6 * MIB,
        name="last",
    )
    wide = (jnp.concatenate([gw0, gow0], axis=0) + gpair.astype(F32)).astype(BF)
    wide = lax.psum(wide, "expert").astype(F32)
    outputs = call(
        output_kernel,
        [((rows, D), BF)],
        (nvalid, came_out, slots, hidden),
        [SM] + [VM] * 3,
        flops=2 * spots * rows * D,
        moved=8 * MIB,
        name="outputs",
    )[0]

    own_bias = gbias0[:heads, :NB].reshape(1, -1)
    pair_bias = gbias1[:heads, :NB].reshape(1, -1)
    ranks = jnp.arange(4, dtype=jnp.int32)[:, None]
    bias_parts = jnp.where(ranks == rank, own_bias, 0.0) + jnp.where(ranks == (rank ^ 2), pair_bias, 0.0)
    small = jnp.concatenate(
        [attn_part[0], moe_part[0], jnp.transpose(grad_router).reshape(-1), bias_parts.reshape(-1)]
    )
    small = lax.psum(small, ("expert", "tensor"))
    bias_sum = lax.dynamic_slice(
        small[2 * D + experts * D :].reshape(4, heads * NB), (rank, 0), (1, heads * NB)
    )
    return (
        outputs,
        grad_inputs,
        small[:D],
        jnp.transpose(wide[: 3 * inner]).reshape(D, 3, inner),
        wide[3 * inner :],
        jnp.transpose(bias_sum.reshape(heads, NB)),
        small[D : 2 * D],
        small[2 * D : 2 * D + experts * D].reshape(D, experts),
        grad_weights[:D][None],
        jnp.transpose(grad_weights[D:])[None],
    )


def solution(mesh):
    return jax.shard_map(
        shards,
        mesh=mesh,
        in_specs=(
            P(("expert", "tensor"), None),
            P("expert"),
            P(("expert", "tensor"), None),
            P(),
            P(None, None, "tensor"),
            P("tensor", None),
            P(None, "tensor"),
            P(),
            P(),
            P("expert", None, "tensor"),
            P("expert", "tensor", None),
            P(("expert", "tensor"), None),
        ),
        out_specs=(
            P(("expert", "tensor"), None),
            P(("expert", "tensor"), None),
            P(),
            P(None, None, "tensor"),
            P("tensor", None),
            P(None, "tensor"),
            P(),
            P(),
            P("expert", None, "tensor"),
            P("expert", "tensor", None),
        ),
        check_vma=False,
    )
```

```python
import functools

import jax
import jax.numpy as jnp
from jax import lax
from jax.experimental import pallas as pl
from jax.experimental.pallas import tpu as pltpu
from jax.sharding import PartitionSpec as P

D = 768
HD = 64
NB = 32
MAXDIST = 128
SEQ = 1024
EPSILON = 1e-06
NEGATIVE = -1e30
TILE = 256
BF = jnp.bfloat16
F32 = jnp.float32
MIB = 2**20
CHUNK = 256
GELU = 0.7978845608028654
CUBIC = 0.044715


def bucket_edges():
    half_count = NB // 2
    short_edges = list(range(1, half_count))
    long_edges = [
        int(half_count * (MAXDIST / half_count) ** (step_index / half_count))
        for step_index in range(half_count)
    ]
    return short_edges + long_edges


EDGES = bucket_edges()


def dot(a, b, ca=1, cb=0, precision=None):
    return lax.dot_general(
        a, b, (((ca,), (cb,)), ((), ())), preferred_element_type=F32, precision=precision
    )


def iota(shape, dim):
    return lax.broadcasted_iota(jnp.int32, shape, dim)


def rms(v):
    return lax.rsqrt(jnp.mean(v * v, axis=-1, keepdims=True) + EPSILON)


def call(kernel, outs, args, specs=None, scratch=(), flops=0, moved=0, exps=0, vmem=56, name=None):
    vm = pl.BlockSpec(memory_space=pltpu.VMEM)
    return pl.pallas_call(
        kernel,
        out_shape=[jax.ShapeDtypeStruct(s, d) for s, d in outs],
        in_specs=specs or [vm] * len(args),
        out_specs=[vm] * len(outs),
        scratch_shapes=list(scratch),
        compiler_params=pltpu.CompilerParams(vmem_limit_bytes=vmem * MIB),
        cost_estimate=pl.CostEstimate(flops=flops, bytes_accessed=moved, transcendentals=exps),
        name=name,
    )(*args)


VM = pl.BlockSpec(memory_space=pltpu.VMEM)
SM = pl.BlockSpec(memory_space=pltpu.SMEM)


def slot_lines(experts, cap, valid_count, routes):
    rows = routes.shape[1]
    valid = iota((1, rows), 1) < valid_count
    ids = iota((experts, rows), 0)
    hot0 = ((ids == routes[0:1]) & valid).astype(F32)
    hot1 = ((ids == routes[1:2]) & valid).astype(F32)
    before = (iota((rows, rows), 0) < iota((rows, rows), 1)).astype(BF)
    rank = dot((hot0 + hot1).astype(BF), before)
    place = ids.astype(F32) * cap + rank
    bad = jnp.where(valid, 0.0, 1.0)
    slot0 = jnp.sum(hot0 * place, axis=0, keepdims=True) - bad
    slot1 = jnp.sum(hot1 * place, axis=0, keepdims=True) - bad
    return slot0, slot1


def route_kernel(experts, cap, nv_ref, routes_ref, grad_ref, packed_ref, slots_ref):
    rows = grad_ref.shape[0]
    slot0, slot1 = slot_lines(experts, cap, nv_ref[0], routes_ref[...])
    spots = iota((experts * cap, rows), 0)
    pick0 = spots == slot0.astype(jnp.int32)
    pick1 = spots == slot1.astype(jnp.int32)
    packed_ref[...] = dot((pick0 | pick1).astype(BF), grad_ref[...]).astype(BF)
    slots_ref[...] = jnp.concatenate([slot0, slot1, jnp.zeros((6, rows), F32)], axis=0)


def back_matrix(slots_ref, spots):
    rows = slots_ref.shape[1]
    where = iota((rows, spots), 1)
    slots = slots_ref[...].T.astype(jnp.int32)
    return ((where == slots[:, 0:1]) | (where == slots[:, 1:2])).astype(BF)


def bias_tiles(table_ref, head):
    dist = iota((8, TILE), 1)
    far = table_ref[NB - 1, head]
    curve = jnp.full((8, TILE), table_ref[0, head] - far, F32)
    for number, edge in enumerate(EDGES):
        curve = jnp.where(dist >= edge, table_ref[number + 1, head] - far, curve)
    spread = jnp.broadcast_to(curve[0:1], (TILE, TILE))
    ring = pltpu.roll(spread, 0, 1, stride=1, stride_axis=0)
    ahead = iota((TILE, TILE), 1) >= iota((TILE, TILE), 0)
    return jnp.where(ahead, ring, NEGATIVE), jnp.where(ahead, 0.0, ring)


def head_pieces(qkvt_ref, mask_rows, head, local_inner):
    start = pl.multiple_of(head * HD, HD)
    q = qkvt_ref[pl.ds(start, HD), :] * jnp.asarray(HD**-0.5, BF)
    k = qkvt_ref[pl.ds(local_inner + start, HD), :]
    v = qkvt_ref[pl.ds(2 * local_inner + start, HD), :]
    ones = jnp.ones((16, SEQ), BF)
    return jnp.concatenate([q, ones], 0), jnp.concatenate([k, mask_rows], 0), v, ones


def mask_block(length):
    keep = (iota((16, SEQ), 1) < length) | (iota((16, SEQ), 0) > 0)
    return jnp.where(keep, 0.0, NEGATIVE).astype(BF)


def score_pieces(k, q, block, near, below):
    cols = slice(block * TILE, (block + 1) * TILE)
    qb = q[:, cols]
    pieces = []
    if block >= 2:
        pieces.append((0, (block - 1) * TILE, dot(k[: (block - 1) * TILE], qb)))
    if block >= 1:
        lo = (block - 1) * TILE
        pieces.append((lo, block * TILE, dot(k[lo : lo + TILE], qb) + below))
    lo = block * TILE
    pieces.append((lo, lo + TILE, dot(k[lo : lo + TILE], qb) + near))
    return cols, pieces


def attn_fwd_kernel(first, heads, scal_ref, table_ref, *refs):
    if first:
        own_ref, other_ref, gain_ref, w_ref, ow_ref = refs[:5]
        normed_ref, qkvt_ref, mixt_ref, lse_ref, part_ref = refs[5:]
        half = own_ref.shape[0]
        core = scal_ref[0]
        for source, place in ((own_ref, core), (other_ref, 1 - core)):
            x = source[...].astype(F32)
            normed_ref[pl.ds(pl.multiple_of(place * half, half), half), :] = (
                x * rms(x) * gain_ref[...]
            ).astype(BF)
    else:
        normed_ref, w_ref, ow_ref, part_in = refs[:4]
        qkvt_ref, mixt_ref, lse_ref, keep_ref, send_ref, part_ref = refs[4:]
    local_inner = heads * HD
    qkvt_ref[...] = dot(w_ref[...], normed_ref[...], 1, 1).astype(BF)
    masks = mask_block(scal_ref[1])
    lse_ref[...] = jnp.zeros_like(lse_ref)

    for head in range(heads):
        near, below = bias_tiles(table_ref, head)
        q, kt, v, ones = head_pieces(qkvt_ref, masks, head, local_inner)
        k = kt.T
        vx = jnp.concatenate([v, ones], 0)
        for block in range(SEQ // TILE):
            cols, pieces = score_pieces(k, q, block, near, below)
            top = functools.reduce(
                jnp.maximum, [jnp.max(s, axis=0, keepdims=True) for _, _, s in pieces]
            )
            total = None
            for lo, hi, s in pieces:
                term = dot(vx[:, lo:hi], jnp.exp(s - top).astype(BF))
                total = term if total is None else total + term
            weight = total[HD : HD + 1]
            mixt_ref[head * HD : (head + 1) * HD, cols] = (total[:HD] / weight).astype(BF)
            lse_ref[head : head + 1, cols] = top + jnp.log(weight)
    part = dot(mixt_ref[...], ow_ref[...], 0, 0)
    if first:
        part_ref[...] = part
    else:
        part_ref[...] = part + part_in[...]
        half = keep_ref.shape[0]
        core = scal_ref[0]
        keep_ref[...] = part_ref[pl.ds(pl.multiple_of(core * half, half), half), :]
        send_ref[...] = part_ref[pl.ds(pl.multiple_of((1 - core) * half, half), half), :].astype(BF)


def attn_bwd_kernel(last, heads, scal_ref, table_ref, *refs):
    if last:
        (normed_ref, w_ref, ow_ref, qkvt_ref, mixt_ref, lse_ref, own_ref, other_ref, part_in) = refs[:9]
        gw_ref, gow_ref, gbias_ref, keep_ref, send_ref, ga_ref, got_ref, gt_ref, d0_ref, d1_ref, part_ref = refs[9:]
    else:
        (normed_ref, w_ref, ow_ref, qkvt_ref, mixt_ref, lse_ref, own_ref, other_ref) = refs[:8]
        gw_ref, gow_ref, gbias_ref, part_ref, ga_ref, got_ref, gt_ref, d0_ref, d1_ref = refs[8:]
    local_inner = heads * HD
    half = own_ref.shape[0]
    core = scal_ref[0]
    ga_ref[pl.ds(pl.multiple_of(core * half, half), half), :] = own_ref[...]
    ga_ref[pl.ds(pl.multiple_of((1 - core) * half, half), half), :] = other_ref[...]
    got_ref[...] = dot(ow_ref[...], ga_ref[...], 1, 1).astype(BF)
    gow_ref[...] = dot(mixt_ref[...], ga_ref[...]).astype(gow_ref.dtype)
    masks = mask_block(scal_ref[1])
    gbias_ref[...] = jnp.zeros_like(gbias_ref)
    ahead = iota((TILE, TILE), 1) >= iota((TILE, TILE), 0)
    spot = (iota((TILE, 128), 0) + 1) % TILE
    flip = (iota((TILE, TILE), 0) + iota((TILE, TILE), 1) == TILE - 1).astype(F32)
    bucket = jnp.zeros((TILE, 128), jnp.int32)
    for edge in EDGES:
        bucket = bucket + (spot >= edge).astype(jnp.int32)
    hot = (bucket == iota((TILE, 128), 1)).astype(F32)

    for head in range(heads):
        near, below = bias_tiles(table_ref, head)
        q, kt, vt, _ = head_pieces(qkvt_ref, masks, head, local_inner)
        k = kt.T
        v = vt.T
        rows = slice(head * HD, (head + 1) * HD)
        gt = got_ref[rows, :]
        delta = jnp.sum(gt.astype(F32) * mixt_ref[rows, :].astype(F32), axis=0, keepdims=True)
        gk = [None] * (SEQ // TILE)
        gv = [None] * (SEQ // TILE)
        far = jnp.zeros((8, TILE), F32)
        for block in range(SEQ // TILE):
            cols, pieces = score_pieces(k, q, block, near, below)
            gb = gt[:, cols]
            qb = q[:HD, cols]
            lse = lse_ref[head : head + 1, cols]
            db = delta[:, cols]
            gq = None
            for lo, hi, s in pieces:
                p = jnp.exp(s - lse)
                ds = p * (dot(v[lo:hi], gb) - db)
                pb = p.astype(BF)
                dsb = ds.astype(BF)
                term = dot(kt[:HD, lo:hi], dsb)
                gq = term if gq is None else gq + term
                tv = dot(pb, gb, 1, 1)
                tk = dot(dsb, qb, 1, 1)
                for tile in range(lo // TILE, hi // TILE):
                    part = slice(tile * TILE - lo, (tile + 1) * TILE - lo)
                    gv[tile] = tv[part] if gv[tile] is None else gv[tile] + tv[part]
                    gk[tile] = tk[part] if gk[tile] is None else gk[tile] + tk[part]
                if hi == (block + 1) * TILE:
                    d0_ref[...] = ds if block == 0 else d0_ref[...] + ds
                elif hi == block * TILE and lo == (block - 1) * TILE:
                    d1_ref[...] = ds if block == 1 else d1_ref[...] + ds
                else:
                    far = far + jnp.sum(ds.reshape((hi - lo) // 8, 8, TILE), axis=0)
            gt_ref[rows, cols] = (gq * HD**-0.5).astype(BF)
        for tile in range(SEQ // TILE):
            cols = slice(tile * TILE, (tile + 1) * TILE)
            gt_ref[local_inner + head * HD : local_inner + (head + 1) * HD, cols] = (
                gk[tile].T.astype(BF)
            )
            gt_ref[2 * local_inner + head * HD : 2 * local_inner + (head + 1) * HD, cols] = (
                gv[tile].T.astype(BF)
            )
        d1 = d1_ref[...]
        ring = jnp.where(ahead, d0_ref[...], d1)
        turned = pltpu.roll(
            dot(flip, ring, 1, 0, lax.Precision.HIGHEST), 0, 1, stride=1, stride_axis=0
        )
        far = far + jnp.sum(jnp.where(ahead, d1, 0.0).reshape(TILE // 8, 8, TILE), axis=0)
        line = jnp.sum(turned, axis=0, keepdims=True)
        sums = dot(
            jnp.broadcast_to(line, (8, TILE)), hot, 1, 0, lax.Precision.HIGHEST
        )
        sums = sums + jnp.where(iota((8, 128), 1) == NB - 1, jnp.sum(far), 0.0)
        gbias_ref[head : head + 1, :] = sums[0:1]
    gw_ref[...] = dot(gt_ref[...], normed_ref[...]).astype(gw_ref.dtype)
    part = dot(gt_ref[...], w_ref[...], 0, 0)
    if last:
        part_ref[...] = part + part_in[...]
        keep_ref[...] = part_ref[pl.ds(pl.multiple_of(core * half, half), half), :]
        send_ref[...] = part_ref[pl.ds(pl.multiple_of((1 - core) * half, half), half), :].astype(BF)
    else:
        part_ref[...] = part


def gates_of(experts, normed, router_t, routes):
    rows = normed.shape[0]
    logits = dot(router_t, normed, 1, 1)
    ids = iota((experts, rows), 0)
    signs = (ids == routes[0:1]).astype(F32) - (ids == routes[1:2]).astype(F32)
    gap = jnp.sum(logits * signs, axis=0, keepdims=True)
    return 1.0 / (1.0 + jnp.exp(-gap)), 1.0 / (1.0 + jnp.exp(gap))


def meta_lines(gate, code):
    rows = gate.shape[1]
    line = iota((8, rows), 0)
    high = gate.astype(BF).astype(F32)
    mid = (gate - high).astype(BF).astype(F32)
    low = gate - high - mid
    picked = jnp.where(line == 0, high, jnp.where(line == 1, mid, jnp.where(line == 2, low, 0.0)))
    return jnp.where(line == 3, code, picked).astype(BF)


def hidden_rows(x_ref, keep_ref, got_ref, gain_ref, hidden_ref):
    hidden = x_ref[...].astype(F32) + keep_ref[...] + got_ref[...].astype(F32)
    hidden_ref[...] = hidden
    return (hidden * rms(hidden) * gain_ref[...]).astype(BF)


def middle_kernel(
    experts, cap, x_ref, keep_ref, got_ref, gain_ref, router_ref, routes_ref, slots_ref, hidden_ref, packed_ref, meta_ref
):
    normed = hidden_rows(x_ref, keep_ref, got_ref, gain_ref, hidden_ref)
    slots = slots_ref[...].astype(jnp.int32)
    routes = routes_ref[...]
    where = iota((experts * cap, normed.shape[0]), 0)
    pick0 = where == slots[0:1]
    pick1 = where == slots[1:2]
    packed_ref[...] = dot((pick0 | pick1).astype(BF), normed).astype(BF)
    gate0, gate1 = gates_of(experts, normed, router_ref[...], routes)
    codes = (routes + 1).astype(F32)
    meta = dot(meta_lines(gate0, codes[1:2]), pick0.astype(BF), 1, 1) + dot(
        meta_lines(gate1, codes[0:1]), pick1.astype(BF), 1, 1
    )
    for number in range(experts):
        meta_ref[number] = meta[:, number * cap : (number + 1) * cap]


def middle_line_kernel(
    experts, x_ref, keep_ref, got_ref, gain_ref, router_ref, routes_ref, slots_ref, hidden_ref, normed_ref, info_ref
):
    normed = hidden_rows(x_ref, keep_ref, got_ref, gain_ref, hidden_ref)
    normed_ref[...] = normed
    routes = routes_ref[...]
    gate0, gate1 = gates_of(experts, normed, router_ref[...], routes)
    codes = (routes + 1).astype(F32)
    info_ref[...] = jnp.concatenate(
        [slots_ref[0:2], gate0, gate1, codes, jnp.zeros((2, normed.shape[0]), F32)], axis=0
    )


def gelu_pair(v):
    squared = v * v
    slope = GELU * (1.0 + 3 * CUBIC * squared)
    t = jnp.tanh(v * (GELU + GELU * CUBIC * squared))
    half = 0.5 + 0.5 * t
    return v * half, half + 0.5 * v * (1.0 - t * t) * slope


def flipped(me, k, count):
    total, bit = 0, 1
    while bit < count:
        total = total + lax.rem(me // bit + k // bit, 2) * bit
        bit *= 2
    return total


def weight_grads(xt_ref, geot_ref, act_ref, gi_ref, stage_ref, gw_ref, out_sem):
    tiles = D // TILE
    steps = 8 * tiles

    def columns(step):
        return pl.ds(pl.multiple_of(lax.rem(step, tiles) * TILE, TILE), TILE)

    def store(step, slot):
        half = lax.rem(step, 2 * tiles) // tiles
        return pltpu.make_async_copy(
            stage_ref.at[slot],
            gw_ref.at[step // (2 * tiles), pl.ds(pl.multiple_of(half * D, D), D), columns(step)],
            out_sem.at[slot],
        )

    def weights(step, carry):
        q = step // (2 * tiles)
        half = lax.rem(step, 2 * tiles) // tiles
        slot = lax.rem(step, 2)

        @pl.when(step >= 2)
        def _():
            store(step - 2, slot).wait()

        @pl.when(half == 0)
        def _():
            stage_ref[slot] = dot(xt_ref[...], gi_ref[q, :, columns(step)]).astype(BF)

        @pl.when(half == 1)
        def _():
            stage_ref[slot] = dot(geot_ref[...], act_ref[q, :, columns(step)]).astype(BF)

        store(step, slot).start()
        return carry

    lax.fori_loop(0, steps, weights, 0)
    for step in (steps - 2, steps - 1):
        store(step, step % 2).wait()


def expert_rows(x, geo, here, w_ref, xt_ref, geot_ref, act_ref, gi_ref, acc_ref):
    xt_ref[:, here] = x.T
    geot_ref[:, here] = geo.T
    worth = 0.0
    for q in range(4):
        inner = dot(x, w_ref[q, :D])
        grad_active = dot(geo, w_ref[q, D:], 1, 1)
        act, slope = gelu_pair(inner)
        gi = (slope * grad_active).astype(BF)
        act_ref[q, here] = act.astype(BF)
        gi_ref[q, here] = gi
        back = dot(gi, w_ref[q, :D], 1, 1)
        if q == 0:
            acc_ref[...] = back
        else:
            acc_ref[...] += back
        worth = worth + jnp.sum(act * grad_active, axis=1, keepdims=True)
    return worth


def expert_outs(start, size, column, act_ref, w_ref):
    here = pl.ds(pl.multiple_of(start, size), size)
    cols = pl.ds(pl.multiple_of(column * TILE, TILE), TILE)
    total = None
    for q in range(4):
        term = dot(act_ref[q, here], w_ref[q, D:, cols])
        total = term if total is None else total + term
    return cols, total


def expert_kernel(
    count, cap, packed_ref, send_meta_ref, grads_ref, router_ref, w0, w1, w2, w3,
    came_ref, result_ref, gw_ref, grouter_ref,
    w_ref, x_ref, xt_ref, geot_ref, act_ref, gi_ref, gsend_ref, meta_ref, acc_ref, stage_ref,
    x_send, x_recv, m_send, m_recv, r_send, r_recv, local_sem, w_sem, out_sem,
):
    me = lax.axis_index("expert")
    barrier = pltpu.get_barrier_semaphore()

    def peer(k):
        return flipped(me, k, count)

    source = peer

    def greet(k, carry):
        pl.semaphore_signal(
            barrier, inc=1, device_id={"expert": peer(k)}, device_id_type=pl.DeviceIdType.MESH
        )
        return carry

    lax.fori_loop(1, count, greet, 0)
    pl.semaphore_wait(barrier, count - 1)

    def rows_of(k):
        return pl.ds(pl.multiple_of(k * cap, cap), cap)

    def send_rows(k):
        return pltpu.make_async_remote_copy(
            src_ref=packed_ref.at[rows_of(peer(k))],
            dst_ref=x_ref.at[rows_of(k)],
            send_sem=x_send.at[k],
            recv_sem=x_recv.at[k],
            device_id={"expert": peer(k)},
            device_id_type=pl.DeviceIdType.MESH,
        )

    def send_meta(k):
        return pltpu.make_async_remote_copy(
            src_ref=send_meta_ref.at[peer(k)],
            dst_ref=meta_ref.at[k],
            send_sem=m_send.at[k],
            recv_sem=m_recv.at[k],
            device_id={"expert": peer(k)},
            device_id_type=pl.DeviceIdType.MESH,
        )

    def send_back(k):
        return pltpu.make_async_remote_copy(
            src_ref=gsend_ref.at[rows_of(k)],
            dst_ref=came_ref.at[rows_of(me)],
            send_sem=r_send.at[k],
            recv_sem=r_recv.at[k],
            device_id={"expert": source(k)},
            device_id_type=pl.DeviceIdType.MESH,
        )

    def start_sends(k, carry):
        send_meta(k).start()
        send_rows(k).start()
        return carry

    lax.fori_loop(count // 2, count, start_sends, 0)
    lax.fori_loop(1, count // 2, start_sends, 0)
    own_rows = pltpu.make_async_copy(packed_ref.at[rows_of(me)], x_ref.at[rows_of(0)], local_sem.at[0])
    own_rows.start()
    own_meta = pltpu.make_async_copy(send_meta_ref.at[me], meta_ref.at[0], local_sem.at[1])
    own_meta.start()
    loads = [
        pltpu.make_async_copy(w, w_ref.at[i], w_sem.at[i]) for i, w in enumerate((w0, w1, w2, w3))
    ]
    for load in loads:
        load.start()
    grouter_ref[...] = jnp.zeros_like(grouter_ref)
    experts = router_ref.shape[1]
    own_rows.wait()
    own_meta.wait()
    for load in loads:
        load.wait()
    group = max(1, CHUNK // cap)
    span = group * cap

    def chunk(j, carry):
        for i in range(group):
            k = j * group + i

            @pl.when(k > 0)
            def _():
                send_rows(k).wait_recv()
                send_meta(k).wait_recv()

        here = pl.ds(pl.multiple_of(j * span, span), span)
        meta = jnp.concatenate([meta_ref[j * group + i].T for i in range(group)], axis=0)
        gate = meta[:, 0:1] + meta[:, 1:2] + meta[:, 2:3]
        code = meta[:, 3:4].astype(jnp.int32)
        gy = jnp.concatenate([grads_ref[rows_of(source(j * group + i)), :] for i in range(group)], axis=0)
        geo = (gate * gy.astype(F32)).astype(BF)
        x = x_ref[here, :]
        worth = expert_rows(x, geo, here, w_ref, xt_ref, geot_ref, act_ref, gi_ref, acc_ref)
        ids = iota((span, experts), 1)
        signs = (ids == me).astype(F32) - (ids + 1 == code).astype(F32)
        share = jnp.where(code > 0, (1.0 - gate) * worth, 0.0) * signs
        high = share.astype(BF)
        low = (share - high.astype(F32)).astype(BF)
        gsend_ref[here, :] = (acc_ref[...] + dot(high, router_ref[...], 1, 1)).astype(BF)
        grouter_ref[...] += dot(high.T, x) + dot(low.T, x)
        for i in range(group):
            k = j * group + i

            @pl.when(k > 0)
            def _():
                send_back(k).start()

        return carry

    lax.fori_loop(0, count // group, chunk, 0)
    own_back = pltpu.make_async_copy(gsend_ref.at[rows_of(0)], came_ref.at[rows_of(me)], local_sem.at[0])
    own_back.start()

    def results(step, carry):
        j = step // (D // TILE)
        meta = jnp.concatenate([meta_ref[j * group + i].T for i in range(group)], axis=0)
        gate = meta[:, 0:1] + meta[:, 1:2] + meta[:, 2:3]
        cols, total = expert_outs(j * span, span, lax.rem(step, D // TILE), act_ref, w_ref)
        out = (gate * total).astype(BF)
        for i in range(group):
            result_ref[rows_of(source(j * group + i)), cols] = out[i * cap : (i + 1) * cap]
        return carry

    lax.fori_loop(0, count // group * (D // TILE), results, 0)
    weight_grads(xt_ref, geot_ref, act_ref, gi_ref, stage_ref, gw_ref, out_sem)
    own_back.wait()

    def finish(k, carry):
        send_rows(k).wait_send()
        send_meta(k).wait_send()
        send_back(k).wait()
        return carry

    lax.fori_loop(1, count, finish, 0)


def mesh_copy(src, dst, send_sem, recv_sem, target):
    return pltpu.make_async_remote_copy(
        src_ref=src,
        dst_ref=dst,
        send_sem=send_sem,
        recv_sem=recv_sem,
        device_id={"expert": target},
        device_id_type=pl.DeviceIdType.MESH,
    )


LINE = 4


def expert_line_kernel(
    cap, normed_ref, info_in, grads_ref, router_ref, w0, w1, w2, w3,
    came_ref, result_ref, gw_ref, grouter_ref,
    w_ref, block_ref, info_ref, x_ref, xs_ref, meta_ref, ms_ref, xt_ref, geot_ref, act_ref, gi_ref, acc_ref, stage_ref,
    b_send, b_recv, i_send, i_recv, x_send, x_recv, m_send, m_recv, r_send, r_recv, local_sem, w_sem, out_sem,
):
    count = 2 * LINE
    me = lax.axis_index("expert")
    place = me // 2
    side = me - 2 * place
    mate = me + 1 - 2 * side
    barrier = pltpu.get_barrier_semaphore()

    def greet(k, carry):
        pl.semaphore_signal(
            barrier,
            inc=1,
            device_id={"expert": lax.rem(me + k, count)},
            device_id_type=pl.DeviceIdType.MESH,
        )
        return carry

    lax.fori_loop(1, count, greet, 0)
    pl.semaphore_wait(barrier, count - 1)

    def along(block, step):
        return (
            mesh_copy(
                info_ref.at[block],
                info_ref.at[block],
                i_send.at[(step + 1) // 2, block],
                i_recv.at[block],
                me + 2 * step,
            ),
            mesh_copy(
                block_ref.at[block],
                block_ref.at[block],
                b_send.at[(step + 1) // 2, block],
                b_recv.at[block],
                me + 2 * step,
            ),
        )

    def across(block):
        return (
            mesh_copy(ms_ref.at[block], meta_ref.at[1, block], m_send.at[block], m_recv.at[block], mate),
            mesh_copy(xs_ref.at[block], x_ref.at[1, block], x_send.at[block], x_recv.at[block], mate),
        )

    def rows_of(number):
        return pl.ds(pl.multiple_of(number * cap, cap), cap)

    def origin(part, block):
        return 2 * block + side + part * (1 - 2 * side)

    def give_back(part, block):
        return mesh_copy(
            x_ref.at[part, block],
            came_ref.at[rows_of(me)],
            r_send.at[part, block],
            r_recv.at[me],
            origin(part, block),
        )

    def each(pair, act):
        for one in pair:
            act(one)

    own = (
        pltpu.make_async_copy(info_in, info_ref.at[place], local_sem.at[0]),
        pltpu.make_async_copy(normed_ref, block_ref.at[place], local_sem.at[1]),
    )
    each(own, lambda c: c.start())
    loads = [
        pltpu.make_async_copy(w, w_ref.at[i], w_sem.at[i]) for i, w in enumerate((w0, w1, w2, w3))
    ]
    each(loads, lambda c: c.start())
    each(own, lambda c: c.wait())

    @pl.when(place < LINE - 1)
    def _():
        each(along(place, 1), lambda c: c.start())

    @pl.when(place > 0)
    def _():
        each(along(place, -1), lambda c: c.start())

    experts = router_ref.shape[1]
    rows = normed_ref.shape[0]

    def select(block):
        info = info_ref[block]
        slots = info[0:2].astype(jnp.int32)
        lines0 = meta_lines(info[2:3], info[5:6])
        lines1 = meta_lines(info[3:4], info[4:5])
        for part, expert in ((1, mate), (0, me)):
            where = iota((cap, rows), 0) + expert * cap
            pick0 = where == slots[0:1]
            pick1 = where == slots[1:2]
            taken = dot((pick0 | pick1).astype(BF), block_ref[block]).astype(BF)
            meta = dot(lines0, pick0.astype(BF), 1, 1) + dot(lines1, pick1.astype(BF), 1, 1)
            if part:
                xs_ref[block] = taken
                ms_ref[block] = meta
                each(across(block), lambda c: c.start())
            else:
                x_ref[0, block] = taken
                meta_ref[0, block] = meta

    select(place)
    grouter_ref[...] = jnp.zeros_like(grouter_ref)
    each(loads, lambda c: c.wait())
    mirror = place // 2
    inward = place + mirror * (LINE - 1 - 2 * place)

    def block_at(i):
        step = i + inward * (1 - i // 2 - 2 * (i // 2 - i // (LINE - 1)))
        return step + mirror * (LINE - 1 - 2 * step)

    def chunk_at(c):
        part = lax.rem(c + 1, 2) - (7 - c) // 7 + c // 7
        return part, block_at((c + 1) // 2 - part * ((c + 1) // 2 - (c - 1) // 2))

    def accept(distance):
        for step in (-1, 1):
            block = place + step * distance
            inside = (block >= 0) & (block < LINE)

            @pl.when(inside)
            def _():
                each(along(block, -step), lambda c: c.wait_recv())
                ahead = place - step

                @pl.when((ahead >= 0) & (ahead < LINE))
                def _():
                    each(along(block, -step), lambda c: c.start())

        for step in (-1, 1):
            block = place + step * distance
            inside = (block >= 0) & (block < LINE)

            @pl.when(inside)
            def _():
                select(block)

    def chunk(c, carry):
        for distance in range(1, LINE):

            @pl.when(c == 2 * distance - 1)
            def _():
                accept(distance)

        part, block = chunk_at(c)

        @pl.when(part == 1)
        def _():
            each(across(block), lambda c: c.wait_recv())

        here = pl.ds(pl.multiple_of(c * cap, cap), cap)
        meta = meta_ref[part, block].T
        gate = meta[:, 0:1] + meta[:, 1:2] + meta[:, 2:3]
        code = meta[:, 3:4].astype(jnp.int32)
        geo = (gate * grads_ref[rows_of(origin(part, block)), :].astype(F32)).astype(BF)
        x = x_ref[part, block]
        worth = expert_rows(x, geo, here, w_ref, xt_ref, geot_ref, act_ref, gi_ref, acc_ref)
        ids = iota((cap, experts), 1)
        signs = (ids == me).astype(F32) - (ids + 1 == code).astype(F32)
        share = jnp.where(code > 0, (1.0 - gate) * worth, 0.0) * signs
        high = share.astype(BF)
        low = (share - high.astype(F32)).astype(BF)
        grouter_ref[...] += dot(high.T, x) + dot(low.T, x)
        x_ref[part, block] = (acc_ref[...] + dot(high, router_ref[...], 1, 1)).astype(BF)

        @pl.when(origin(part, block) != me)
        def _():
            give_back(part, block).start()

        return carry

    lax.fori_loop(0, count, chunk, 0)
    own_back = pltpu.make_async_copy(x_ref.at[0, place], came_ref.at[rows_of(me)], local_sem.at[0])
    own_back.start()

    def results(step, carry):
        first = step // (D // TILE) * LINE
        cols, total = expert_outs(first * cap, LINE * cap, lax.rem(step, D // TILE), act_ref, w_ref)
        for i in range(LINE):
            part, block = chunk_at(first + i)
            meta = meta_ref[part, block].T
            gate = meta[:, 0:1] + meta[:, 1:2] + meta[:, 2:3]
            result_ref[rows_of(origin(part, block)), cols] = (
                gate * total[i * cap : (i + 1) * cap]
            ).astype(BF)
        return carry

    lax.fori_loop(0, 2 * (D // TILE), results, 0)
    weight_grads(xt_ref, geot_ref, act_ref, gi_ref, stage_ref, gw_ref, out_sem)
    own_back.wait()

    for block in range(LINE):
        each(across(block), lambda c: c.wait_send())
        for step in (-1, 1):
            @pl.when((place + step >= 0) & (place + step < LINE) & ((place - block) * step >= 0))
            def _():
                each(along(block, step), lambda c: c.wait_send())

        for part in (0, 1):

            @pl.when(origin(part, block) != me)
            def _():
                give_back(part, block).wait_send()

    for number in range(count):

        @pl.when(number != me)
        def _():
            mesh_copy(
                x_ref.at[0, 0], came_ref.at[rows_of(number)], r_send.at[0, 0], r_recv.at[number], mate
            ).wait_recv()


def turn_kernel(nv_ref, came_ref, slots_ref, hidden_ref, gain_ref, grad_ref, gh_ref, ga_ref, gain_out):
    gn = dot(back_matrix(slots_ref, came_ref.shape[0]), came_ref[...])
    hidden = hidden_ref[...]
    scale = rms(hidden)
    unit = hidden * scale
    gain_out[...] = jnp.broadcast_to(jnp.sum(gn * unit, axis=0, keepdims=True), gain_out.shape)
    g = gn * gain_ref[...]
    valid = (iota((hidden.shape[0], 1), 0) < nv_ref[0]).astype(F32)
    gh = scale * (g - unit * jnp.mean(g * unit, axis=1, keepdims=True)) + valid * grad_ref[...].astype(F32)
    gh_ref[...] = gh
    ga_ref[...] = gh.astype(BF)


def output_kernel(nv_ref, came_ref, slots_ref, hidden_ref, out_ref):
    mix = dot(back_matrix(slots_ref, came_ref.shape[0]), came_ref[...])
    hidden = hidden_ref[...]
    valid = (iota((hidden.shape[0], 1), 0) < nv_ref[0]).astype(F32)
    out_ref[...] = (valid * (hidden + mix)).astype(BF)


def last_kernel(x_ref, keep_ref, got_ref, gain_ref, gh_ref, out_ref, gain_out):
    x = x_ref[...].astype(F32)
    scale = rms(x)
    unit = x * scale
    gn = keep_ref[...] + got_ref[...].astype(F32)
    gain_out[...] = jnp.broadcast_to(jnp.sum(gn * unit, axis=0, keepdims=True), gain_out.shape)
    g = gn * gain_ref[...]
    out_ref[...] = (
        gh_ref[...] + scale * (g - unit * jnp.mean(g * unit, axis=1, keepdims=True))
    ).astype(BF)


def moe(experts, cap, packed, meta, grads, router, quarters):
    spots = experts * cap
    anyspec = pl.BlockSpec(memory_space=pl.ANY)
    dma = pltpu.SemaphoreType.DMA
    return pl.pallas_call(
        functools.partial(expert_kernel, experts, cap),
        out_shape=[
            jax.ShapeDtypeStruct((spots, D), BF),
            jax.ShapeDtypeStruct((spots, D), BF),
            jax.ShapeDtypeStruct((4, 2 * D, D), BF),
            jax.ShapeDtypeStruct((experts, D), F32),
        ],
        in_specs=[anyspec, VM, VM, VM] + [anyspec] * 4,
        out_specs=[anyspec, VM, anyspec, VM],
        scratch_shapes=[
            pltpu.VMEM((4, 2 * D, D), BF),
            pltpu.VMEM((spots, D), BF),
            pltpu.VMEM((D, spots), BF),
            pltpu.VMEM((D, spots), BF),
            pltpu.VMEM((4, spots, D), BF),
            pltpu.VMEM((4, spots, D), BF),
            pltpu.VMEM((spots, D), BF),
            pltpu.VMEM((experts, 8, cap), F32),
            pltpu.VMEM((CHUNK, D), F32),
            pltpu.VMEM((2, D, TILE), BF),
            dma((experts,)),
            dma((experts,)),
            dma((experts,)),
            dma((experts,)),
            dma((experts,)),
            dma((experts,)),
            dma((2,)),
            dma((4,)),
            dma((2,)),
        ],
        compiler_params=pltpu.CompilerParams(
            collective_id=1, has_side_effects=True, vmem_limit_bytes=60 * MIB
        ),
        cost_estimate=pl.CostEstimate(flops=12 * spots * D * 4 * D, bytes_accessed=60 * MIB, transcendentals=0),
        name="experts",
    )(packed, meta, grads, router, *quarters)


def moe_line(experts, cap, normed, info, grads, router, quarters):
    rows = normed.shape[0]
    spots = experts * cap
    anyspec = pl.BlockSpec(memory_space=pl.ANY)
    dma = pltpu.SemaphoreType.DMA
    return pl.pallas_call(
        functools.partial(expert_line_kernel, cap),
        out_shape=[
            jax.ShapeDtypeStruct((spots, D), BF),
            jax.ShapeDtypeStruct((spots, D), BF),
            jax.ShapeDtypeStruct((4, 2 * D, D), BF),
            jax.ShapeDtypeStruct((experts, D), F32),
        ],
        in_specs=[VM, VM, VM, VM] + [anyspec] * 4,
        out_specs=[anyspec, VM, anyspec, VM],
        scratch_shapes=[
            pltpu.VMEM((4, 2 * D, D), BF),
            pltpu.VMEM((LINE, rows, D), BF),
            pltpu.VMEM((LINE, 8, rows), F32),
            pltpu.VMEM((2, LINE, cap, D), BF),
            pltpu.VMEM((LINE, cap, D), BF),
            pltpu.VMEM((2, LINE, 8, cap), F32),
            pltpu.VMEM((LINE, 8, cap), F32),
            pltpu.VMEM((D, spots), BF),
            pltpu.VMEM((D, spots), BF),
            pltpu.VMEM((4, spots, D), BF),
            pltpu.VMEM((4, spots, D), BF),
            pltpu.VMEM((cap, D), F32),
            pltpu.VMEM((2, D, TILE), BF),
            dma((2, LINE)),
            dma((LINE,)),
            dma((2, LINE)),
            dma((LINE,)),
            dma((LINE,)),
            dma((LINE,)),
            dma((LINE,)),
            dma((LINE,)),
            dma((2, LINE)),
            dma((experts,)),
            dma((2,)),
            dma((4,)),
            dma((2,)),
        ],
        compiler_params=pltpu.CompilerParams(
            collective_id=2, has_side_effects=True, vmem_limit_bytes=62 * MIB
        ),
        cost_estimate=pl.CostEstimate(flops=12 * spots * D * 4 * D, bytes_accessed=60 * MIB, transcendentals=0),
        name="experts_line",
    )(normed, info, grads, router, *quarters)


def shards(
    inputs,
    lengths,
    routes,
    attn_gain,
    qkv_weight,
    out_weight,
    rel_bias,
    moe_gain,
    router_weight,
    up_weight,
    down_weight,
    out_grad,
):
    rows = inputs.shape[0]
    rank = lax.axis_index("tensor")
    expert = lax.axis_index("expert")
    heads = rel_bias.shape[1]
    inner = heads * HD
    experts = router_weight.shape[1]
    cap = 4 * rows // experts
    spots = experts * cap
    core = rank % 2
    length = lengths[rank // 2]
    nvalid = jnp.clip(length - core * rows, 0, rows).astype(jnp.int32).reshape(1)
    scal = jnp.stack([core, length]).astype(jnp.int32)

    def swap(x, bit):
        return lax.ppermute(x, "tensor", [(i, i ^ bit) for i in range(4)])

    gain1 = attn_gain.reshape(1, D)
    gain2 = moe_gain.reshape(1, D)
    other = swap(inputs, 1)
    wt = jnp.transpose(qkv_weight.reshape(D, 3 * inner))
    pair_w = swap(jnp.concatenate([wt, out_weight], axis=0), 2)
    pair_table = swap(rel_bias, 2)

    routes_t = jnp.transpose(routes)
    packed_grad, slots = call(
        functools.partial(route_kernel, experts, cap),
        [((spots, D), BF), ((8, rows), F32)],
        (nvalid, routes_t, out_grad),
        [SM, VM, VM],
        flops=2 * spots * rows * D,
        moved=4 * MIB,
        name="route",
    )

    def exchange(x):
        return lax.all_to_all(
            x.reshape(experts, cap, x.shape[-1]), "expert", split_axis=0, concat_axis=0, tiled=True
        ).reshape(x.shape)

    grads_in = exchange(packed_grad)
    mine, pair_w = lax.optimization_barrier(
        (jnp.concatenate([up_weight[0], down_weight[0]], axis=0), pair_w)
    )
    far = swap(mine, 2)
    side = swap(mine, 1)

    attn_cost = dict(
        flops=2 * SEQ * D * 4 * inner + heads * SEQ * SEQ * 160, moved=6 * MIB, exps=heads * SEQ * SEQ
    )
    normed, qkvt0, mixt0, lse0, part0 = call(
        functools.partial(attn_fwd_kernel, True, heads),
        [((SEQ, D), BF), ((3 * inner, SEQ), BF), ((inner, SEQ), BF), ((8, SEQ), F32), ((SEQ, D), F32)],
        (scal, rel_bias, inputs, other, gain1, wt, out_weight),
        [SM, SM] + [VM] * 5,
        name="attend_own",
        **attn_cost,
    )
    wt1, ow1 = pair_w[: 3 * inner], pair_w[3 * inner :]
    qkvt1, mixt1, lse1, keep, send = call(
        functools.partial(attn_fwd_kernel, False, heads),
        [((3 * inner, SEQ), BF), ((inner, SEQ), BF), ((8, SEQ), F32), ((rows, D), F32), ((rows, D), BF)],
        (scal, pair_table, normed, wt1, ow1, part0),
        [SM, SM] + [VM] * 4,
        scratch=[pltpu.VMEM((SEQ, D), F32)],
        name="attend_pair",
        **attn_cost,
    )
    got = swap(send, 1)
    far, got = lax.optimization_barrier((far, got))
    quarters = [mine, side, far, swap(far, 1)]
    middle_args = (inputs, keep, got, gain2, jnp.transpose(router_weight), routes_t, slots)
    if experts == 2 * LINE and cap == TILE:
        hidden, normed_two, info = call(
            functools.partial(middle_line_kernel, experts),
            [((rows, D), F32), ((rows, D), BF), ((8, rows), F32)],
            middle_args,
            moved=6 * MIB,
            name="middle",
        )
        came, result, weight_parts, grad_router = moe_line(
            experts, cap, normed_two, info, grads_in, router_weight, quarters
        )
    else:
        hidden, packed_rows, meta = call(
            functools.partial(middle_kernel, experts, cap),
            [((rows, D), F32), ((spots, D), BF), ((experts, 8, cap), F32)],
            middle_args,
            flops=2 * spots * rows * D,
            moved=8 * MIB,
            name="middle",
        )
        came, result, weight_parts, grad_router = moe(
            experts, cap, packed_rows, meta, grads_in, router_weight, quarters
        )
    came_out = exchange(result)

    grads = weight_parts
    near = grads[0].astype(F32) + swap(grads[1], 1).astype(F32)
    away = grads[2].astype(F32) + swap(grads[3], 1).astype(F32)
    grad_weights = near + swap(away.astype(BF), 2).astype(F32)

    grad_hidden, grad_attended, moe_part = call(
        turn_kernel,
        [((rows, D), F32), ((rows, D), BF), ((8, D), F32)],
        (nvalid, came, slots, hidden, gain2, out_grad),
        [SM] + [VM] * 5,
        flops=2 * spots * rows * D,
        moved=8 * MIB,
        name="turn",
    )
    other_grad = swap(grad_attended, 1)
    bwd_cost = dict(
        flops=2 * SEQ * D * 10 * inner + heads * SEQ * SEQ * 400, moved=9 * MIB, exps=heads * SEQ * SEQ
    )
    work = [
        pltpu.VMEM((SEQ, D), BF),
        pltpu.VMEM((inner, SEQ), BF),
        pltpu.VMEM((3 * inner, SEQ), BF),
        pltpu.VMEM((TILE, TILE), F32),
        pltpu.VMEM((TILE, TILE), F32),
    ]
    gw1, gow1, gbias1, npart = call(
        functools.partial(attn_bwd_kernel, False, heads),
        [((3 * inner, D), BF), ((inner, D), BF), ((8, 128), F32), ((SEQ, D), F32)],
        (scal, pair_table, normed, wt1, ow1, qkvt1, mixt1, lse1, grad_attended, other_grad),
        [SM, SM] + [VM] * 8,
        scratch=work,
        name="attend_pair_back",
        **bwd_cost,
    )
    gpair = swap(jnp.concatenate([gw1, gow1], axis=0), 2)
    gw0, gow0, gbias0, keep_n, send_n = call(
        functools.partial(attn_bwd_kernel, True, heads),
        [((3 * inner, D), F32), ((inner, D), F32), ((8, 128), F32), ((rows, D), F32), ((rows, D), BF)],
        (scal, rel_bias, normed, wt, out_weight, qkvt0, mixt0, lse0, grad_attended, other_grad, npart),
        [SM, SM] + [VM] * 9,
        scratch=work + [pltpu.VMEM((SEQ, D), F32)],
        name="attend_own_back",
        **bwd_cost,
    )
    got_n = swap(send_n, 1)
    grad_inputs, attn_part = call(
        last_kernel,
        [((rows, D), BF), ((8, D), F32)],
        (inputs, keep_n, got_n, gain1, grad_hidden),
        moved=6 * MIB,
        name="last",
    )
    wide = (jnp.concatenate([gw0, gow0], axis=0) + gpair.astype(F32)).astype(BF)
    wide = lax.psum(wide, "expert").astype(F32)
    outputs = call(
        output_kernel,
        [((rows, D), BF)],
        (nvalid, came_out, slots, hidden),
        [SM] + [VM] * 3,
        flops=2 * spots * rows * D,
        moved=8 * MIB,
        name="outputs",
    )[0]

    own_bias = gbias0[:heads, :NB].reshape(1, -1)
    pair_bias = gbias1[:heads, :NB].reshape(1, -1)
    ranks = jnp.arange(4, dtype=jnp.int32)[:, None]
    bias_parts = jnp.where(ranks == rank, own_bias, 0.0) + jnp.where(ranks == (rank ^ 2), pair_bias, 0.0)
    small = jnp.concatenate(
        [attn_part[0], moe_part[0], jnp.transpose(grad_router).reshape(-1), bias_parts.reshape(-1)]
    )
    small = lax.psum(small, ("expert", "tensor"))
    bias_sum = lax.dynamic_slice(
        small[2 * D + experts * D :].reshape(4, heads * NB), (rank, 0), (1, heads * NB)
    )
    return (
        outputs,
        grad_inputs,
        small[:D],
        jnp.transpose(wide[: 3 * inner]).reshape(D, 3, inner),
        wide[3 * inner :],
        jnp.transpose(bias_sum.reshape(heads, NB)),
        small[D : 2 * D],
        small[2 * D : 2 * D + experts * D].reshape(D, experts),
        grad_weights[:D][None],
        jnp.transpose(grad_weights[D:])[None],
    )


def solution(mesh):
    return jax.shard_map(
        shards,
        mesh=mesh,
        in_specs=(
            P(("expert", "tensor"), None),
            P("expert"),
            P(("expert", "tensor"), None),
            P(),
            P(None, None, "tensor"),
            P("tensor", None),
            P(None, "tensor"),
            P(),
            P(),
            P("expert", None, "tensor"),
            P("expert", "tensor", None),
            P(("expert", "tensor"), None),
        ),
        out_specs=(
            P(("expert", "tensor"), None),
            P(("expert", "tensor"), None),
            P(),
            P(None, None, "tensor"),
            P("tensor", None),
            P(None, "tensor"),
            P(),
            P(),
            P("expert", None, "tensor"),
            P("expert", "tensor", None),
        ),
        check_vma=False,
    )
```

```python
import functools

import jax
import jax.numpy as jnp
from jax import lax
from jax.experimental import pallas as pl
from jax.experimental.pallas import tpu as pltpu
from jax.sharding import PartitionSpec as P

D = 768
HD = 64
NB = 32
MAXDIST = 128
SEQ = 1024
EPSILON = 1e-06
NEGATIVE = -1e30
TILE = 256
BF = jnp.bfloat16
F32 = jnp.float32
MIB = 2**20
CHUNK = 256
GELU = 0.7978845608028654
CUBIC = 0.044715


def bucket_edges():
    half_count = NB // 2
    short_edges = list(range(1, half_count))
    long_edges = [
        int(half_count * (MAXDIST / half_count) ** (step_index / half_count))
        for step_index in range(half_count)
    ]
    return short_edges + long_edges


EDGES = bucket_edges()


def dot(a, b, ca=1, cb=0, precision=None):
    return lax.dot_general(
        a, b, (((ca,), (cb,)), ((), ())), preferred_element_type=F32, precision=precision
    )


def iota(shape, dim):
    return lax.broadcasted_iota(jnp.int32, shape, dim)


def rms(v):
    return lax.rsqrt(jnp.mean(v * v, axis=-1, keepdims=True) + EPSILON)


def call(kernel, outs, args, specs=None, scratch=(), flops=0, moved=0, exps=0, vmem=56, name=None):
    vm = pl.BlockSpec(memory_space=pltpu.VMEM)
    return pl.pallas_call(
        kernel,
        out_shape=[jax.ShapeDtypeStruct(s, d) for s, d in outs],
        in_specs=specs or [vm] * len(args),
        out_specs=[vm] * len(outs),
        scratch_shapes=list(scratch),
        compiler_params=pltpu.CompilerParams(vmem_limit_bytes=vmem * MIB),
        cost_estimate=pl.CostEstimate(flops=flops, bytes_accessed=moved, transcendentals=exps),
        name=name,
    )(*args)


VM = pl.BlockSpec(memory_space=pltpu.VMEM)
SM = pl.BlockSpec(memory_space=pltpu.SMEM)


def slot_lines(experts, cap, valid_count, routes):
    rows = routes.shape[1]
    valid = iota((1, rows), 1) < valid_count
    ids = iota((experts, rows), 0)
    hot0 = ((ids == routes[0:1]) & valid).astype(F32)
    hot1 = ((ids == routes[1:2]) & valid).astype(F32)
    before = (iota((rows, rows), 0) < iota((rows, rows), 1)).astype(BF)
    rank = dot((hot0 + hot1).astype(BF), before)
    place = ids.astype(F32) * cap + rank
    bad = jnp.where(valid, 0.0, 1.0)
    slot0 = jnp.sum(hot0 * place, axis=0, keepdims=True) - bad
    slot1 = jnp.sum(hot1 * place, axis=0, keepdims=True) - bad
    return slot0, slot1


def route_kernel(experts, cap, nv_ref, routes_ref, grad_ref, packed_ref, slots_ref):
    rows = grad_ref.shape[0]
    slot0, slot1 = slot_lines(experts, cap, nv_ref[0], routes_ref[...])
    spots = iota((experts * cap, rows), 0)
    pick0 = spots == slot0.astype(jnp.int32)
    pick1 = spots == slot1.astype(jnp.int32)
    packed_ref[...] = dot((pick0 | pick1).astype(BF), grad_ref[...]).astype(BF)
    slots_ref[...] = jnp.concatenate([slot0, slot1, jnp.zeros((6, rows), F32)], axis=0)


def back_matrix(slots_ref, spots):
    rows = slots_ref.shape[1]
    where = iota((rows, spots), 1)
    slots = slots_ref[...].T.astype(jnp.int32)
    return ((where == slots[:, 0:1]) | (where == slots[:, 1:2])).astype(BF)


def bias_tiles(table_ref, head):
    dist = iota((8, TILE), 1)
    far = table_ref[NB - 1, head]
    curve = jnp.full((8, TILE), table_ref[0, head] - far, F32)
    for number, edge in enumerate(EDGES):
        curve = jnp.where(dist >= edge, table_ref[number + 1, head] - far, curve)
    spread = jnp.broadcast_to(curve[0:1], (TILE, TILE))
    ring = pltpu.roll(spread, 0, 1, stride=1, stride_axis=0)
    ahead = iota((TILE, TILE), 1) >= iota((TILE, TILE), 0)
    return jnp.where(ahead, ring, NEGATIVE), jnp.where(ahead, 0.0, ring)


def head_pieces(qkvt_ref, mask_rows, head, local_inner):
    start = pl.multiple_of(head * HD, HD)
    q = qkvt_ref[pl.ds(start, HD), :] * jnp.asarray(HD**-0.5, BF)
    k = qkvt_ref[pl.ds(local_inner + start, HD), :]
    v = qkvt_ref[pl.ds(2 * local_inner + start, HD), :]
    ones = jnp.ones((16, SEQ), BF)
    return jnp.concatenate([q, ones], 0), jnp.concatenate([k, mask_rows], 0), v, ones


def mask_block(length):
    keep = (iota((16, SEQ), 1) < length) | (iota((16, SEQ), 0) > 0)
    return jnp.where(keep, 0.0, NEGATIVE).astype(BF)


def score_pieces(k, q, block, near, below):
    cols = slice(block * TILE, (block + 1) * TILE)
    qb = q[:, cols]
    pieces = []
    if block >= 2:
        pieces.append((0, (block - 1) * TILE, dot(k[: (block - 1) * TILE], qb)))
    if block >= 1:
        lo = (block - 1) * TILE
        pieces.append((lo, block * TILE, dot(k[lo : lo + TILE], qb) + below))
    lo = block * TILE
    pieces.append((lo, lo + TILE, dot(k[lo : lo + TILE], qb) + near))
    return cols, pieces


def attn_fwd_kernel(first, heads, scal_ref, table_ref, *refs):
    if first:
        own_ref, other_ref, gain_ref, w_ref, ow_ref = refs[:5]
        normed_ref, qkvt_ref, mixt_ref, lse_ref, part_ref = refs[5:]
        half = own_ref.shape[0]
        core = scal_ref[0]
        for source, place in ((own_ref, core), (other_ref, 1 - core)):
            x = source[...].astype(F32)
            normed_ref[pl.ds(pl.multiple_of(place * half, half), half), :] = (
                x * rms(x) * gain_ref[...]
            ).astype(BF)
    else:
        normed_ref, w_ref, ow_ref, part_in = refs[:4]
        qkvt_ref, mixt_ref, lse_ref, keep_ref, send_ref, part_ref = refs[4:]
    local_inner = heads * HD
    qkvt_ref[...] = dot(w_ref[...], normed_ref[...], 1, 1).astype(BF)
    masks = mask_block(scal_ref[1])
    lse_ref[...] = jnp.zeros_like(lse_ref)

    for head in range(heads):
        near, below = bias_tiles(table_ref, head)
        q, kt, v, ones = head_pieces(qkvt_ref, masks, head, local_inner)
        k = kt.T
        vx = jnp.concatenate([v, ones], 0)
        for block in range(SEQ // TILE):
            cols, pieces = score_pieces(k, q, block, near, below)
            top = functools.reduce(
                jnp.maximum, [jnp.max(s, axis=0, keepdims=True) for _, _, s in pieces]
            )
            total = None
            for lo, hi, s in pieces:
                term = dot(vx[:, lo:hi], jnp.exp(s - top).astype(BF))
                total = term if total is None else total + term
            weight = total[HD : HD + 1]
            mixt_ref[head * HD : (head + 1) * HD, cols] = (total[:HD] / weight).astype(BF)
            lse_ref[head : head + 1, cols] = top + jnp.log(weight)
    part = dot(mixt_ref[...], ow_ref[...], 0, 0)
    if first:
        part_ref[...] = part
    else:
        part_ref[...] = part + part_in[...]
        half = keep_ref.shape[0]
        core = scal_ref[0]
        keep_ref[...] = part_ref[pl.ds(pl.multiple_of(core * half, half), half), :]
        send_ref[...] = part_ref[pl.ds(pl.multiple_of((1 - core) * half, half), half), :].astype(BF)


def attn_bwd_kernel(last, heads, scal_ref, table_ref, *refs):
    if last:
        (normed_ref, w_ref, ow_ref, qkvt_ref, mixt_ref, lse_ref, own_ref, other_ref, part_in) = refs[:9]
        gw_ref, gbias_ref, keep_ref, send_ref, ga_ref, got_ref, gt_ref, d0_ref, d1_ref, part_ref = refs[9:]
    else:
        (normed_ref, w_ref, ow_ref, qkvt_ref, mixt_ref, lse_ref, own_ref, other_ref) = refs[:8]
        gw_ref, gbias_ref, part_ref, ga_ref, got_ref, gt_ref, d0_ref, d1_ref = refs[8:]
    local_inner = heads * HD
    half = own_ref.shape[0]
    core = scal_ref[0]
    ga_ref[pl.ds(pl.multiple_of(core * half, half), half), :] = own_ref[...]
    ga_ref[pl.ds(pl.multiple_of((1 - core) * half, half), half), :] = other_ref[...]
    got_ref[...] = dot(ow_ref[...], ga_ref[...], 1, 1).astype(BF)
    gw_ref[3 * local_inner :] = dot(mixt_ref[...], ga_ref[...]).astype(gw_ref.dtype)
    masks = mask_block(scal_ref[1])
    gbias_ref[...] = jnp.zeros_like(gbias_ref)
    ahead = iota((TILE, TILE), 1) >= iota((TILE, TILE), 0)
    spot = (iota((TILE, 128), 0) + 1) % TILE
    flip = (iota((TILE, TILE), 0) + iota((TILE, TILE), 1) == TILE - 1).astype(F32)
    bucket = jnp.zeros((TILE, 128), jnp.int32)
    for edge in EDGES:
        bucket = bucket + (spot >= edge).astype(jnp.int32)
    hot = (bucket == iota((TILE, 128), 1)).astype(F32)

    for head in range(heads):
        near, below = bias_tiles(table_ref, head)
        q, kt, vt, _ = head_pieces(qkvt_ref, masks, head, local_inner)
        k = kt.T
        v = vt.T
        rows = slice(head * HD, (head + 1) * HD)
        gt = got_ref[rows, :]
        delta = jnp.sum(gt.astype(F32) * mixt_ref[rows, :].astype(F32), axis=0, keepdims=True)
        gk = [None] * (SEQ // TILE)
        gv = [None] * (SEQ // TILE)
        far = jnp.zeros((8, TILE), F32)
        for block in range(SEQ // TILE):
            cols, pieces = score_pieces(k, q, block, near, below)
            gb = gt[:, cols]
            qb = q[:HD, cols]
            lse = lse_ref[head : head + 1, cols]
            db = delta[:, cols]
            gq = None
            for lo, hi, s in pieces:
                p = jnp.exp(s - lse)
                ds = p * (dot(v[lo:hi], gb) - db)
                pb = p.astype(BF)
                dsb = ds.astype(BF)
                term = dot(kt[:HD, lo:hi], dsb)
                gq = term if gq is None else gq + term
                tv = dot(pb, gb, 1, 1)
                tk = dot(dsb, qb, 1, 1)
                for tile in range(lo // TILE, hi // TILE):
                    part = slice(tile * TILE - lo, (tile + 1) * TILE - lo)
                    gv[tile] = tv[part] if gv[tile] is None else gv[tile] + tv[part]
                    gk[tile] = tk[part] if gk[tile] is None else gk[tile] + tk[part]
                if hi == (block + 1) * TILE:
                    d0_ref[...] = ds if block == 0 else d0_ref[...] + ds
                elif hi == block * TILE and lo == (block - 1) * TILE:
                    d1_ref[...] = ds if block == 1 else d1_ref[...] + ds
                else:
                    far = far + jnp.sum(ds.reshape((hi - lo) // 8, 8, TILE), axis=0)
            gt_ref[rows, cols] = (gq * HD**-0.5).astype(BF)
        for tile in range(SEQ // TILE):
            cols = slice(tile * TILE, (tile + 1) * TILE)
            gt_ref[local_inner + head * HD : local_inner + (head + 1) * HD, cols] = (
                gk[tile].T.astype(BF)
            )
            gt_ref[2 * local_inner + head * HD : 2 * local_inner + (head + 1) * HD, cols] = (
                gv[tile].T.astype(BF)
            )
        d1 = d1_ref[...]
        ring = jnp.where(ahead, d0_ref[...], d1)
        turned = pltpu.roll(
            dot(flip, ring, 1, 0, lax.Precision.HIGHEST), 0, 1, stride=1, stride_axis=0
        )
        far = far + jnp.sum(jnp.where(ahead, d1, 0.0).reshape(TILE // 8, 8, TILE), axis=0)
        line = jnp.sum(turned, axis=0, keepdims=True)
        sums = dot(
            jnp.broadcast_to(line, (8, TILE)), hot, 1, 0, lax.Precision.HIGHEST
        )
        sums = sums + jnp.where(iota((8, 128), 1) == NB - 1, jnp.sum(far), 0.0)
        gbias_ref[head : head + 1, :] = sums[0:1]
    gw_ref[: 3 * local_inner] = dot(gt_ref[...], normed_ref[...]).astype(gw_ref.dtype)
    part = dot(gt_ref[...], w_ref[...], 0, 0)
    if last:
        part_ref[...] = part + part_in[...]
        keep_ref[...] = part_ref[pl.ds(pl.multiple_of(core * half, half), half), :]
        send_ref[...] = part_ref[pl.ds(pl.multiple_of((1 - core) * half, half), half), :].astype(BF)
    else:
        part_ref[...] = part


def gates_of(experts, normed, router_t, routes):
    rows = normed.shape[0]
    logits = dot(router_t, normed, 1, 1)
    ids = iota((experts, rows), 0)
    signs = (ids == routes[0:1]).astype(F32) - (ids == routes[1:2]).astype(F32)
    gap = jnp.sum(logits * signs, axis=0, keepdims=True)
    return 1.0 / (1.0 + jnp.exp(-gap)), 1.0 / (1.0 + jnp.exp(gap))


def meta_lines(gate, code):
    rows = gate.shape[1]
    line = iota((8, rows), 0)
    high = gate.astype(BF).astype(F32)
    mid = (gate - high).astype(BF).astype(F32)
    low = gate - high - mid
    picked = jnp.where(line == 0, high, jnp.where(line == 1, mid, jnp.where(line == 2, low, 0.0)))
    return jnp.where(line == 3, code, picked).astype(BF)


def hidden_rows(x_ref, keep_ref, got_ref, gain_ref, hidden_ref):
    hidden = x_ref[...].astype(F32) + keep_ref[...] + got_ref[...].astype(F32)
    hidden_ref[...] = hidden
    return (hidden * rms(hidden) * gain_ref[...]).astype(BF)


def middle_kernel(
    experts, cap, x_ref, keep_ref, got_ref, gain_ref, router_ref, routes_ref, slots_ref, hidden_ref, packed_ref, meta_ref
):
    normed = hidden_rows(x_ref, keep_ref, got_ref, gain_ref, hidden_ref)
    slots = slots_ref[...].astype(jnp.int32)
    routes = routes_ref[...]
    where = iota((experts * cap, normed.shape[0]), 0)
    pick0 = where == slots[0:1]
    pick1 = where == slots[1:2]
    packed_ref[...] = dot((pick0 | pick1).astype(BF), normed).astype(BF)
    gate0, gate1 = gates_of(experts, normed, router_ref[...], routes)
    codes = (routes + 1).astype(F32)
    meta = dot(meta_lines(gate0, codes[1:2]), pick0.astype(BF), 1, 1) + dot(
        meta_lines(gate1, codes[0:1]), pick1.astype(BF), 1, 1
    )
    for number in range(experts):
        meta_ref[number] = meta[:, number * cap : (number + 1) * cap]


def middle_line_kernel(
    experts, x_ref, keep_ref, got_ref, gain_ref, router_ref, routes_ref, slots_ref, hidden_ref, normed_ref, info_ref
):
    normed = hidden_rows(x_ref, keep_ref, got_ref, gain_ref, hidden_ref)
    normed_ref[...] = normed
    routes = routes_ref[...]
    gate0, gate1 = gates_of(experts, normed, router_ref[...], routes)
    codes = (routes + 1).astype(F32)
    info_ref[...] = jnp.concatenate(
        [slots_ref[0:2], gate0, gate1, codes, jnp.zeros((2, normed.shape[0]), F32)], axis=0
    )


def gelu_pair(v):
    squared = v * v
    slope = GELU * (1.0 + 3 * CUBIC * squared)
    t = jnp.tanh(v * (GELU + GELU * CUBIC * squared))
    half = 0.5 + 0.5 * t
    return v * half, half + 0.5 * v * (1.0 - t * t) * slope


def flipped(me, k, count):
    total, bit = 0, 1
    while bit < count:
        total = total + lax.rem(me // bit + k // bit, 2) * bit
        bit *= 2
    return total


def weight_grads(xt_ref, geot_ref, act_ref, gi_ref, stage_ref, stay_ref, away_ref, go_ref, out_sem):
    tiles = D // TILE
    steps = 8 * tiles

    def columns(step):
        return pl.ds(pl.multiple_of(lax.rem(step, tiles) * TILE, TILE), TILE)

    def store(step, slot, out_ref):
        half = lax.rem(step, 2 * tiles) // tiles
        return pltpu.make_async_copy(
            stage_ref.at[slot],
            out_ref.at[pl.ds(pl.multiple_of(half * D, D), D), columns(step)],
            out_sem.at[slot],
        )

    def weights(step, carry):
        q = step // (2 * tiles)
        half = lax.rem(step, 2 * tiles) // tiles
        slot = lax.rem(step, 2)

        @pl.when(step >= 2)
        def _():
            store(step - 2, slot, stay_ref).wait()

        @pl.when(half == 0)
        def _():
            stage_ref[slot] = dot(xt_ref[...], gi_ref[q, :, columns(step)]).astype(BF)

        @pl.when(half == 1)
        def _():
            stage_ref[slot] = dot(geot_ref[...], act_ref[q, :, columns(step)]).astype(BF)

        for number, out_ref in enumerate((stay_ref, away_ref, go_ref.at[0], go_ref.at[1])):

            @pl.when(q == number)
            def _():
                store(step, slot, out_ref).start()

        return carry

    lax.fori_loop(0, steps, weights, 0)
    for step in (steps - 2, steps - 1):
        store(step, step % 2, stay_ref).wait()


def expert_rows(x, geo, here, w_ref, xt_ref, geot_ref, act_ref, gi_ref, acc_ref):
    xt_ref[:, here] = x.T
    geot_ref[:, here] = geo.T
    worth = 0.0
    for q in range(4):
        inner = dot(x, w_ref[q, :D])
        grad_active = dot(geo, w_ref[q, D:], 1, 1)
        act, slope = gelu_pair(inner)
        gi = (slope * grad_active).astype(BF)
        act_ref[q, here] = act.astype(BF)
        gi_ref[q, here] = gi
        back = dot(gi, w_ref[q, :D], 1, 1)
        if q == 0:
            acc_ref[...] = back
        else:
            acc_ref[...] += back
        worth = worth + jnp.sum(act * grad_active, axis=1, keepdims=True)
    return worth


def expert_outs(start, size, column, act_ref, w_ref):
    here = pl.ds(pl.multiple_of(start, size), size)
    cols = pl.ds(pl.multiple_of(column * TILE, TILE), TILE)
    total = None
    for q in range(4):
        term = dot(act_ref[q, here], w_ref[q, D:, cols])
        total = term if total is None else total + term
    return cols, total


def expert_kernel(
    count, cap, packed_ref, send_meta_ref, grads_ref, router_ref, w0, w1, w2, w3,
    came_ref, result_ref, stay_ref, away_ref, go_ref, grouter_ref,
    w_ref, x_ref, xt_ref, geot_ref, act_ref, gi_ref, gsend_ref, meta_ref, acc_ref, stage_ref,
    x_send, x_recv, m_send, m_recv, r_send, r_recv, local_sem, w_sem, out_sem,
):
    me = lax.axis_index("expert")
    barrier = pltpu.get_barrier_semaphore()

    def peer(k):
        return flipped(me, k, count)

    source = peer

    def greet(k, carry):
        pl.semaphore_signal(
            barrier, inc=1, device_id={"expert": peer(k)}, device_id_type=pl.DeviceIdType.MESH
        )
        return carry

    lax.fori_loop(1, count, greet, 0)
    pl.semaphore_wait(barrier, count - 1)

    def rows_of(k):
        return pl.ds(pl.multiple_of(k * cap, cap), cap)

    def send_rows(k):
        return pltpu.make_async_remote_copy(
            src_ref=packed_ref.at[rows_of(peer(k))],
            dst_ref=x_ref.at[rows_of(k)],
            send_sem=x_send.at[k],
            recv_sem=x_recv.at[k],
            device_id={"expert": peer(k)},
            device_id_type=pl.DeviceIdType.MESH,
        )

    def send_meta(k):
        return pltpu.make_async_remote_copy(
            src_ref=send_meta_ref.at[peer(k)],
            dst_ref=meta_ref.at[k],
            send_sem=m_send.at[k],
            recv_sem=m_recv.at[k],
            device_id={"expert": peer(k)},
            device_id_type=pl.DeviceIdType.MESH,
        )

    def send_back(k):
        return pltpu.make_async_remote_copy(
            src_ref=gsend_ref.at[rows_of(k)],
            dst_ref=came_ref.at[rows_of(me)],
            send_sem=r_send.at[k],
            recv_sem=r_recv.at[k],
            device_id={"expert": source(k)},
            device_id_type=pl.DeviceIdType.MESH,
        )

    def start_sends(k, carry):
        send_meta(k).start()
        send_rows(k).start()
        return carry

    lax.fori_loop(count // 2, count, start_sends, 0)
    lax.fori_loop(1, count // 2, start_sends, 0)
    own_rows = pltpu.make_async_copy(packed_ref.at[rows_of(me)], x_ref.at[rows_of(0)], local_sem.at[0])
    own_rows.start()
    own_meta = pltpu.make_async_copy(send_meta_ref.at[me], meta_ref.at[0], local_sem.at[1])
    own_meta.start()
    loads = [
        pltpu.make_async_copy(w, w_ref.at[i], w_sem.at[i]) for i, w in enumerate((w0, w1, w2, w3))
    ]
    for load in loads:
        load.start()
    grouter_ref[...] = jnp.zeros_like(grouter_ref)
    experts = router_ref.shape[1]
    own_rows.wait()
    own_meta.wait()
    for load in loads:
        load.wait()
    group = max(1, CHUNK // cap)
    span = group * cap

    def chunk(j, carry):
        for i in range(group):
            k = j * group + i

            @pl.when(k > 0)
            def _():
                send_rows(k).wait_recv()
                send_meta(k).wait_recv()

        here = pl.ds(pl.multiple_of(j * span, span), span)
        meta = jnp.concatenate([meta_ref[j * group + i].T for i in range(group)], axis=0)
        gate = meta[:, 0:1] + meta[:, 1:2] + meta[:, 2:3]
        code = meta[:, 3:4].astype(jnp.int32)
        gy = jnp.concatenate([grads_ref[rows_of(source(j * group + i)), :] for i in range(group)], axis=0)
        geo = (gate * gy.astype(F32)).astype(BF)
        x = x_ref[here, :]
        worth = expert_rows(x, geo, here, w_ref, xt_ref, geot_ref, act_ref, gi_ref, acc_ref)
        ids = iota((span, experts), 1)
        signs = (ids == me).astype(F32) - (ids + 1 == code).astype(F32)
        share = jnp.where(code > 0, (1.0 - gate) * worth, 0.0) * signs
        high = share.astype(BF)
        low = (share - high.astype(F32)).astype(BF)
        gsend_ref[here, :] = (acc_ref[...] + dot(high, router_ref[...], 1, 1)).astype(BF)
        grouter_ref[...] += dot(high.T, x) + dot(low.T, x)
        for i in range(group):
            k = j * group + i

            @pl.when(k > 0)
            def _():
                send_back(k).start()

        return carry

    lax.fori_loop(0, count // group, chunk, 0)
    own_back = pltpu.make_async_copy(gsend_ref.at[rows_of(0)], came_ref.at[rows_of(me)], local_sem.at[0])
    own_back.start()

    def results(step, carry):
        j = step // (D // TILE)
        meta = jnp.concatenate([meta_ref[j * group + i].T for i in range(group)], axis=0)
        gate = meta[:, 0:1] + meta[:, 1:2] + meta[:, 2:3]
        cols, total = expert_outs(j * span, span, lax.rem(step, D // TILE), act_ref, w_ref)
        out = (gate * total).astype(BF)
        for i in range(group):
            result_ref[rows_of(source(j * group + i)), cols] = out[i * cap : (i + 1) * cap]
        return carry

    lax.fori_loop(0, count // group * (D // TILE), results, 0)
    weight_grads(xt_ref, geot_ref, act_ref, gi_ref, stage_ref, stay_ref, away_ref, go_ref, out_sem)
    own_back.wait()

    def finish(k, carry):
        send_rows(k).wait_send()
        send_meta(k).wait_send()
        send_back(k).wait()
        return carry

    lax.fori_loop(1, count, finish, 0)


def mesh_copy(src, dst, send_sem, recv_sem, target):
    return pltpu.make_async_remote_copy(
        src_ref=src,
        dst_ref=dst,
        send_sem=send_sem,
        recv_sem=recv_sem,
        device_id={"expert": target},
        device_id_type=pl.DeviceIdType.MESH,
    )


LINE = 4


def expert_line_kernel(
    cap, normed_ref, info_in, grads_ref, router_ref, up_ref, down_ref, far_up_ref, far_down_ref,
    came_ref, result_ref, stay_ref, away_ref, go_ref, grouter_ref,
    w_ref, block_ref, info_ref, x_ref, xs_ref, meta_ref, ms_ref, xt_ref, geot_ref, act_ref, gi_ref, acc_ref, stage_ref,
    b_send, b_recv, i_send, i_recv, x_send, x_recv, m_send, m_recv, r_send, r_recv, local_sem, w_sem, v_send, v_recv, out_sem,
):
    count = 2 * LINE
    me = lax.axis_index("expert")
    place = me // 2
    side = me - 2 * place
    mate = me + 1 - 2 * side
    barrier = pltpu.get_barrier_semaphore()

    def greet(k, carry):
        pl.semaphore_signal(
            barrier,
            inc=1,
            device_id={"expert": lax.rem(me + k, count)},
            device_id_type=pl.DeviceIdType.MESH,
        )
        return carry

    lax.fori_loop(1, count, greet, 0)
    core = flipped(lax.axis_index("tensor"), 1, 4)
    pl.semaphore_signal(
        barrier, inc=1, device_id={"tensor": core}, device_id_type=pl.DeviceIdType.MESH
    )
    pl.semaphore_wait(barrier, count)

    def along(block, step):
        return (
            mesh_copy(
                info_ref.at[block],
                info_ref.at[block],
                i_send.at[(step + 1) // 2, block],
                i_recv.at[block],
                me + 2 * step,
            ),
            mesh_copy(
                block_ref.at[block],
                block_ref.at[block],
                b_send.at[(step + 1) // 2, block],
                b_recv.at[block],
                me + 2 * step,
            ),
        )

    def across(block):
        return (
            mesh_copy(ms_ref.at[block], meta_ref.at[1, block], m_send.at[block], m_recv.at[block], mate),
            mesh_copy(xs_ref.at[block], x_ref.at[1, block], x_send.at[block], x_recv.at[block], mate),
        )

    def rows_of(number):
        return pl.ds(pl.multiple_of(number * cap, cap), cap)

    def origin(part, block):
        return 2 * block + side + part * (1 - 2 * side)

    def give_back(part, block):
        return mesh_copy(
            x_ref.at[part, block],
            came_ref.at[rows_of(me)],
            r_send.at[part, block],
            r_recv.at[me],
            origin(part, block),
        )

    def each(pair, act):
        for one in pair:
            act(one)

    own = (
        pltpu.make_async_copy(info_in, info_ref.at[place], local_sem.at[0]),
        pltpu.make_async_copy(normed_ref, block_ref.at[place], local_sem.at[1]),
    )
    each(own, lambda c: c.start())
    weights = (up_ref, down_ref, far_up_ref, far_down_ref)
    each(own, lambda c: c.wait())

    @pl.when(place < LINE - 1)
    def _():
        each(along(place, 1), lambda c: c.start())

    @pl.when(place > 0)
    def _():
        each(along(place, -1), lambda c: c.start())

    def load(i):
        return pltpu.make_async_copy(weights[i], w_ref.at[i // 2, pl.ds(i % 2 * D, D)], w_sem.at[i])

    def lend(i):
        return pltpu.make_async_remote_copy(
            src_ref=weights[i],
            dst_ref=w_ref.at[2 + i // 2, pl.ds(i % 2 * D, D)],
            send_sem=v_send.at[i],
            recv_sem=v_recv.at[i],
            device_id={"tensor": core},
            device_id_type=pl.DeviceIdType.MESH,
        )

    for i in range(4):
        load(i).start()
        lend(i).start()
    experts = router_ref.shape[1]
    rows = normed_ref.shape[0]

    def select(block):
        info = info_ref[block]
        slots = info[0:2].astype(jnp.int32)
        lines0 = meta_lines(info[2:3], info[5:6])
        lines1 = meta_lines(info[3:4], info[4:5])
        for part, expert in ((1, mate), (0, me)):
            where = iota((cap, rows), 0) + expert * cap
            pick0 = where == slots[0:1]
            pick1 = where == slots[1:2]
            taken = dot((pick0 | pick1).astype(BF), block_ref[block]).astype(BF)
            meta = dot(lines0, pick0.astype(BF), 1, 1) + dot(lines1, pick1.astype(BF), 1, 1)
            if part:
                xs_ref[block] = taken
                ms_ref[block] = meta
                each(across(block), lambda c: c.start())
            else:
                x_ref[0, block] = taken
                meta_ref[0, block] = meta

    select(place)
    grouter_ref[...] = jnp.zeros_like(grouter_ref)
    for i in range(4):
        load(i).wait()
        lend(i).wait_recv()
    mirror = place // 2
    inward = place + mirror * (LINE - 1 - 2 * place)

    def block_at(i):
        step = i + inward * (1 - i // 2 - 2 * (i // 2 - i // (LINE - 1)))
        return step + mirror * (LINE - 1 - 2 * step)

    def chunk_at(c):
        part = lax.rem(c + 1, 2) - (7 - c) // 7 + c // 7
        return part, block_at((c + 1) // 2 - part * ((c + 1) // 2 - (c - 1) // 2))

    def accept(distance):
        for step in (-1, 1):
            block = place + step * distance
            inside = (block >= 0) & (block < LINE)

            @pl.when(inside)
            def _():
                each(along(block, -step), lambda c: c.wait_recv())
                ahead = place - step

                @pl.when((ahead >= 0) & (ahead < LINE))
                def _():
                    each(along(block, -step), lambda c: c.start())

        for step in (-1, 1):
            block = place + step * distance
            inside = (block >= 0) & (block < LINE)

            @pl.when(inside)
            def _():
                select(block)

    def chunk(c, carry):
        for distance in range(1, LINE):

            @pl.when(c == 2 * distance - 1)
            def _():
                accept(distance)

        part, block = chunk_at(c)

        @pl.when(part == 1)
        def _():
            each(across(block), lambda c: c.wait_recv())

        here = pl.ds(pl.multiple_of(c * cap, cap), cap)
        meta = meta_ref[part, block].T
        gate = meta[:, 0:1] + meta[:, 1:2] + meta[:, 2:3]
        code = meta[:, 3:4].astype(jnp.int32)
        geo = (gate * grads_ref[rows_of(origin(part, block)), :].astype(F32)).astype(BF)
        x = x_ref[part, block]
        worth = expert_rows(x, geo, here, w_ref, xt_ref, geot_ref, act_ref, gi_ref, acc_ref)
        ids = iota((cap, experts), 1)
        signs = (ids == me).astype(F32) - (ids + 1 == code).astype(F32)
        share = jnp.where(code > 0, (1.0 - gate) * worth, 0.0) * signs
        high = share.astype(BF)
        low = (share - high.astype(F32)).astype(BF)
        grouter_ref[...] += dot(high.T, x) + dot(low.T, x)
        x_ref[part, block] = (acc_ref[...] + dot(high, router_ref[...], 1, 1)).astype(BF)

        @pl.when(origin(part, block) != me)
        def _():
            give_back(part, block).start()

        return carry

    lax.fori_loop(0, count, chunk, 0)
    own_back = pltpu.make_async_copy(x_ref.at[0, place], came_ref.at[rows_of(me)], local_sem.at[0])
    own_back.start()

    def results(step, carry):
        first = step // (D // TILE) * LINE
        cols, total = expert_outs(first * cap, LINE * cap, lax.rem(step, D // TILE), act_ref, w_ref)
        for i in range(LINE):
            part, block = chunk_at(first + i)
            meta = meta_ref[part, block].T
            gate = meta[:, 0:1] + meta[:, 1:2] + meta[:, 2:3]
            result_ref[rows_of(origin(part, block)), cols] = (
                gate * total[i * cap : (i + 1) * cap]
            ).astype(BF)
        return carry

    lax.fori_loop(0, 2 * (D // TILE), results, 0)
    weight_grads(xt_ref, geot_ref, act_ref, gi_ref, stage_ref, stay_ref, away_ref, go_ref, out_sem)
    own_back.wait()
    for i in range(4):
        lend(i).wait_send()
    for block in range(LINE):
        each(across(block), lambda c: c.wait_send())
        for step in (-1, 1):
            @pl.when((place + step >= 0) & (place + step < LINE) & ((place - block) * step >= 0))
            def _():
                each(along(block, step), lambda c: c.wait_send())

        for part in (0, 1):

            @pl.when(origin(part, block) != me)
            def _():
                give_back(part, block).wait_send()

    for number in range(count):

        @pl.when(number != me)
        def _():
            mesh_copy(
                x_ref.at[0, 0], came_ref.at[rows_of(number)], r_send.at[0, 0], r_recv.at[number], mate
            ).wait_recv()


def turn_kernel(nv_ref, came_ref, slots_ref, hidden_ref, gain_ref, grad_ref, gh_ref, ga_ref, gain_out):
    gn = dot(back_matrix(slots_ref, came_ref.shape[0]), came_ref[...])
    hidden = hidden_ref[...]
    scale = rms(hidden)
    unit = hidden * scale
    gain_out[...] = jnp.broadcast_to(jnp.sum(gn * unit, axis=0, keepdims=True), gain_out.shape)
    g = gn * gain_ref[...]
    valid = (iota((hidden.shape[0], 1), 0) < nv_ref[0]).astype(F32)
    gh = scale * (g - unit * jnp.mean(g * unit, axis=1, keepdims=True)) + valid * grad_ref[...].astype(F32)
    gh_ref[...] = gh
    ga_ref[...] = gh.astype(BF)


def output_kernel(nv_ref, came_ref, slots_ref, hidden_ref, out_ref):
    mix = dot(back_matrix(slots_ref, came_ref.shape[0]), came_ref[...])
    hidden = hidden_ref[...]
    valid = (iota((hidden.shape[0], 1), 0) < nv_ref[0]).astype(F32)
    out_ref[...] = (valid * (hidden + mix)).astype(BF)


def last_kernel(x_ref, keep_ref, got_ref, gain_ref, gh_ref, out_ref, gain_out):
    x = x_ref[...].astype(F32)
    scale = rms(x)
    unit = x * scale
    gn = keep_ref[...] + got_ref[...].astype(F32)
    gain_out[...] = jnp.broadcast_to(jnp.sum(gn * unit, axis=0, keepdims=True), gain_out.shape)
    g = gn * gain_ref[...]
    out_ref[...] = (
        gh_ref[...] + scale * (g - unit * jnp.mean(g * unit, axis=1, keepdims=True))
    ).astype(BF)


def moe(experts, cap, packed, meta, grads, router, quarters):
    spots = experts * cap
    anyspec = pl.BlockSpec(memory_space=pl.ANY)
    dma = pltpu.SemaphoreType.DMA
    return pl.pallas_call(
        functools.partial(expert_kernel, experts, cap),
        out_shape=[
            jax.ShapeDtypeStruct((spots, D), BF),
            jax.ShapeDtypeStruct((spots, D), BF),
            jax.ShapeDtypeStruct((2 * D, D), BF),
            jax.ShapeDtypeStruct((2 * D, D), BF),
            jax.ShapeDtypeStruct((2, 2 * D, D), BF),
            jax.ShapeDtypeStruct((experts, D), F32),
        ],
        in_specs=[anyspec, VM, VM, VM] + [anyspec] * 4,
        out_specs=[anyspec, VM, anyspec, anyspec, anyspec, VM],
        scratch_shapes=[
            pltpu.VMEM((4, 2 * D, D), BF),
            pltpu.VMEM((spots, D), BF),
            pltpu.VMEM((D, spots), BF),
            pltpu.VMEM((D, spots), BF),
            pltpu.VMEM((4, spots, D), BF),
            pltpu.VMEM((4, spots, D), BF),
            pltpu.VMEM((spots, D), BF),
            pltpu.VMEM((experts, 8, cap), F32),
            pltpu.VMEM((CHUNK, D), F32),
            pltpu.VMEM((2, D, TILE), BF),
            dma((experts,)),
            dma((experts,)),
            dma((experts,)),
            dma((experts,)),
            dma((experts,)),
            dma((experts,)),
            dma((2,)),
            dma((4,)),
            dma((2,)),
        ],
        compiler_params=pltpu.CompilerParams(
            collective_id=1, has_side_effects=True, vmem_limit_bytes=60 * MIB
        ),
        cost_estimate=pl.CostEstimate(flops=12 * spots * D * 4 * D, bytes_accessed=60 * MIB, transcendentals=0),
        name="experts",
    )(packed, meta, grads, router, *quarters)


def moe_line(experts, cap, normed, info, grads, router, weights):
    rows = normed.shape[0]
    spots = experts * cap
    anyspec = pl.BlockSpec(memory_space=pl.ANY)
    dma = pltpu.SemaphoreType.DMA
    return pl.pallas_call(
        functools.partial(expert_line_kernel, cap),
        out_shape=[
            jax.ShapeDtypeStruct((spots, D), BF),
            jax.ShapeDtypeStruct((spots, D), BF),
            jax.ShapeDtypeStruct((2 * D, D), BF),
            jax.ShapeDtypeStruct((2 * D, D), BF),
            jax.ShapeDtypeStruct((2, 2 * D, D), BF),
            jax.ShapeDtypeStruct((experts, D), F32),
        ],
        in_specs=[VM, VM, VM, VM] + [anyspec] * 4,
        out_specs=[anyspec, VM, anyspec, anyspec, anyspec, VM],
        scratch_shapes=[
            pltpu.VMEM((4, 2 * D, D), BF),
            pltpu.VMEM((LINE, rows, D), BF),
            pltpu.VMEM((LINE, 8, rows), F32),
            pltpu.VMEM((2, LINE, cap, D), BF),
            pltpu.VMEM((LINE, cap, D), BF),
            pltpu.VMEM((2, LINE, 8, cap), F32),
            pltpu.VMEM((LINE, 8, cap), F32),
            pltpu.VMEM((D, spots), BF),
            pltpu.VMEM((D, spots), BF),
            pltpu.VMEM((4, spots, D), BF),
            pltpu.VMEM((4, spots, D), BF),
            pltpu.VMEM((cap, D), F32),
            pltpu.VMEM((2, D, TILE), BF),
            dma((2, LINE)),
            dma((LINE,)),
            dma((2, LINE)),
            dma((LINE,)),
            dma((LINE,)),
            dma((LINE,)),
            dma((LINE,)),
            dma((LINE,)),
            dma((2, LINE)),
            dma((experts,)),
            dma((2,)),
            dma((4,)),
            dma((4,)),
            dma((4,)),
            dma((2,)),
        ],
        compiler_params=pltpu.CompilerParams(
            collective_id=2, has_side_effects=True, vmem_limit_bytes=62 * MIB
        ),
        cost_estimate=pl.CostEstimate(flops=12 * spots * D * 4 * D, bytes_accessed=60 * MIB, transcendentals=0),
        name="experts_line",
    )(normed, info, grads, router, *weights)


def tail_kernel(
    gw_ref, pair_ref, keep_ref, send_ref, x_in, gain_ref, gh_ref, moe_ref, router_ref, bias0_ref, bias1_ref,
    gwt_out, gow_out, gin_out, small_out,
    part_ref, cross_ref, line_ref, from_ref, all_ref, got_ref, lines_ref, few_ref, ranks_ref,
    a_send, a_recv, b_send, b_recv, c_send, c_recv, d_send, d_recv, s_send, s_recv, f_send, f_recv, t_send, t_recv, g_send, g_recv,
):
    count = 2 * LINE
    me = lax.axis_index("expert")
    rank = lax.axis_index("tensor")
    place = me // 2
    side = me - 2 * place
    mate = me + 1 - 2 * side
    size = part_ref.shape[0] // count
    barrier = pltpu.get_barrier_semaphore()
    for k in range(1, count):
        pl.semaphore_signal(
            barrier, inc=1, device_id={"expert": flipped(me, k, count)}, device_id_type=pl.DeviceIdType.MESH
        )
    for k in range(1, 4):
        pl.semaphore_signal(
            barrier, inc=1, device_id={"tensor": flipped(rank, k, 4)}, device_id_type=pl.DeviceIdType.MESH
        )
    pl.semaphore_wait(barrier, count + 2)

    def tensor_copy(src, dst, send_sem, recv_sem, target):
        return pltpu.make_async_remote_copy(
            src_ref=src,
            dst_ref=dst,
            send_sem=send_sem,
            recv_sem=recv_sem,
            device_id={"tensor": target},
            device_id_type=pl.DeviceIdType.MESH,
        )

    def slab(which, number):
        return pl.ds(pl.multiple_of((which * LINE + number) * size, size), size)

    swap = tensor_copy(send_ref, got_ref, s_send, s_recv, flipped(rank, 1, 4))
    swap.start()
    part_ref[...] = (gw_ref[...] + pair_ref[...].astype(F32)).astype(BF)
    rows = gwt_out.shape[1]

    def cross(number):
        return mesh_copy(
            part_ref.at[slab(1 - side, number)], cross_ref.at[number], a_send.at[number], a_recv.at[number], mate
        )

    def along(number):
        return mesh_copy(
            line_ref.at[number], from_ref.at[place], b_send.at[number], b_recv.at[place], 2 * number + side
        )

    def spread(number):
        return mesh_copy(
            all_ref.at[slab(side, place)],
            all_ref.at[slab(side, place)],
            c_send.at[number],
            c_recv.at[place],
            2 * number + side,
        )

    def over(number):
        return mesh_copy(
            all_ref.at[slab(side, number)], all_ref.at[slab(side, number)], d_send.at[number], d_recv.at[number], mate
        )

    for number in range(LINE):
        cross(number).start()

    swap.wait()
    x = x_in[...].astype(F32)
    scale = rms(x)
    unit = x * scale
    gn = keep_ref[...] + got_ref[...].astype(F32)
    attn = jnp.sum(gn * unit, axis=0, keepdims=True)
    g = gn * gain_ref[...]
    gin_out[...] = (gh_ref[...] + scale * (g - unit * jnp.mean(g * unit, axis=1, keepdims=True))).astype(BF)

    heads = gow_out.shape[0] // HD
    blank = jnp.zeros((1, 128), F32)

    def flat(bias_ref):
        line = [bias_ref[h : h + 1, :NB] for h in range(heads)]
        return jnp.concatenate(line + [jnp.zeros((1, 128 - heads * NB), F32)], axis=1)

    own_bias, pair_bias = flat(bias0_ref), flat(bias1_ref)
    other = flipped(rank, 2, 4)
    for j in range(D // 128):
        lines_ref[j] = router_ref[:, j * 128 : (j + 1) * 128]
    for j, row in ((6, attn), (7, moe_ref[0:1])):
        places = [2 * (j - 6), 2 * (j - 6) + 1]
        bias = [
            jnp.where(rank == p, own_bias, blank) + jnp.where(other == p, pair_bias, blank) for p in places
        ]
        lines_ref[j] = jnp.concatenate([row[:, i * 128 : (i + 1) * 128] for i in range(6)] + bias, axis=0)

    def small(k):
        return mesh_copy(
            lines_ref.at[flipped(me, k, count)], few_ref.at[k], f_send.at[k], f_recv.at[k], flipped(me, k, count)
        )

    def rank_copy(k):
        return tensor_copy(
            ranks_ref.at[rank], ranks_ref.at[rank], t_send.at[k], t_recv.at[k], flipped(rank, k, 4)
        )

    def rank_from(k):
        return tensor_copy(
            ranks_ref.at[rank], ranks_ref.at[flipped(rank, k, 4)], t_send.at[k], t_recv.at[k], flipped(rank, k, 4)
        )

    def small_spread(k):
        return mesh_copy(
            small_out.at[me], small_out.at[me], g_send.at[k], g_recv.at[k], flipped(me, k, count)
        )

    def small_from(k):
        return mesh_copy(
            small_out.at[me], small_out.at[flipped(me, k, count)], g_send.at[k], g_recv.at[k], flipped(me, k, count)
        )

    for k in range(1, count):
        small(k).start()

    for number in range(LINE):

        @pl.when(number != place)
        def _():
            cross(number).wait_recv()
            line_ref[number] = (
                part_ref[slab(side, number)].astype(F32) + cross_ref[number].astype(F32)
            ).astype(BF)
            along(number).start()

    total = lines_ref[me]
    for k in range(1, count):
        small(k).wait_recv()
        total = total + few_ref[k]
    ranks_ref[rank] = total
    for k in range(1, 4):
        rank_copy(k).start()

    for number in range(LINE):

        @pl.when(number == place)
        def _():
            cross(number).wait_recv()

    whole = part_ref[slab(side, place)].astype(F32) + cross_ref[place].astype(F32)
    from_ref[place] = whole.astype(BF)
    for k in range(1, LINE):
        number = lax.rem(place + k, LINE)
        mesh_copy(
            line_ref.at[number], from_ref.at[number], b_send.at[number], b_recv.at[number], mate
        ).wait_recv()
        whole = whole + from_ref[number].astype(F32)
    all_ref[slab(side, place)] = whole.astype(BF)
    over(place).start()
    for number in range(LINE):

        @pl.when(number != place)
        def _():
            spread(number).start()

    for k in range(1, 4):
        rank_from(k).wait_recv()
    small_out[me] = ranks_ref[0] + ranks_ref[1] + ranks_ref[2] + ranks_ref[3]
    for k in range(1, count):
        small_spread(k).start()

    for k in range(1, LINE):
        number = lax.rem(place + k, LINE)
        mesh_copy(
            all_ref.at[slab(side, number)], all_ref.at[slab(side, number)], c_send.at[number], c_recv.at[number], mate
        ).wait_recv()
        over(number).start()
    for k in range(1, count):
        small_from(k).wait_recv()
    for number in range(LINE):
        mesh_copy(
            all_ref.at[slab(1 - side, number)],
            all_ref.at[slab(1 - side, number)],
            d_send.at[number],
            d_recv.at[number],
            mate,
        ).wait_recv()
    gwt_out[...] = all_ref[:rows].astype(F32).T
    gow_out[...] = all_ref[rows:].astype(F32)
    for number in range(LINE):
        cross(number).wait_send()
        over(number).wait_send()

        @pl.when(number != place)
        def _():
            along(number).wait_send()
            spread(number).wait_send()

    for k in range(1, count):
        small(k).wait_send()
        small_spread(k).wait_send()
    for k in range(1, 4):
        rank_copy(k).wait_send()


def tail(args, rows, local):
    dma = pltpu.SemaphoreType.DMA
    count = 2 * LINE
    part = (3 * local + local) // count
    sems = [dma((LINE,))] * 8 + [dma, dma] + [dma((count,))] * 2 + [dma((4,))] * 2 + [dma((count,))] * 2
    return pl.pallas_call(
        tail_kernel,
        out_shape=[
            jax.ShapeDtypeStruct((D, 3 * local), F32),
            jax.ShapeDtypeStruct((local, D), F32),
            jax.ShapeDtypeStruct((rows, D), BF),
            jax.ShapeDtypeStruct((count, 8, 128), F32),
        ],
        in_specs=[VM] * 11,
        out_specs=[VM] * 4,
        scratch_shapes=[
            pltpu.VMEM((4 * local, D), BF),
            pltpu.VMEM((LINE, part, D), BF),
            pltpu.VMEM((LINE, part, D), BF),
            pltpu.VMEM((LINE, part, D), BF),
            pltpu.VMEM((4 * local, D), BF),
            pltpu.VMEM((rows, D), BF),
            pltpu.VMEM((count, 8, 128), F32),
            pltpu.VMEM((count, 8, 128), F32),
            pltpu.VMEM((4, 8, 128), F32),
        ]
        + sems,
        compiler_params=pltpu.CompilerParams(
            collective_id=3, has_side_effects=True, vmem_limit_bytes=48 * MIB
        ),
        cost_estimate=pl.CostEstimate(flops=0, bytes_accessed=100 * MIB, transcendentals=0),
        name="tail",
    )(*args)


def shards(
    inputs,
    lengths,
    routes,
    attn_gain,
    qkv_weight,
    out_weight,
    rel_bias,
    moe_gain,
    router_weight,
    up_weight,
    down_weight,
    out_grad,
):
    rows = inputs.shape[0]
    rank = lax.axis_index("tensor")
    expert = lax.axis_index("expert")
    heads = rel_bias.shape[1]
    inner = heads * HD
    experts = router_weight.shape[1]
    cap = 4 * rows // experts
    spots = experts * cap
    core = rank % 2
    length = lengths[rank // 2]
    nvalid = jnp.clip(length - core * rows, 0, rows).astype(jnp.int32).reshape(1)
    scal = jnp.stack([core, length]).astype(jnp.int32)

    def swap(x, bit):
        return lax.ppermute(x, "tensor", [(i, i ^ bit) for i in range(4)])

    gain1 = attn_gain.reshape(1, D)
    gain2 = moe_gain.reshape(1, D)
    other = swap(inputs, 1)
    wt = jnp.transpose(qkv_weight.reshape(D, 3 * inner))
    pair_w = swap(jnp.concatenate([wt, out_weight], axis=0), 2)
    pair_table = swap(rel_bias, 2)

    routes_t = jnp.transpose(routes)
    packed_grad, slots = call(
        functools.partial(route_kernel, experts, cap),
        [((spots, D), BF), ((8, rows), F32)],
        (nvalid, routes_t, out_grad),
        [SM, VM, VM],
        flops=2 * spots * rows * D,
        moved=4 * MIB,
        name="route",
    )

    def exchange(x):
        return lax.all_to_all(
            x.reshape(experts, cap, x.shape[-1]), "expert", split_axis=0, concat_axis=0, tiled=True
        ).reshape(x.shape)

    grads_in = exchange(packed_grad)
    up, down = up_weight[0], down_weight[0]
    up, down, pair_w, pair_table = lax.optimization_barrier((up, down, pair_w, pair_table))
    far_up, far_down = swap(up, 2), swap(down, 2)

    attn_cost = dict(
        flops=2 * SEQ * D * 4 * inner + heads * SEQ * SEQ * 160, moved=6 * MIB, exps=heads * SEQ * SEQ
    )
    normed, qkvt0, mixt0, lse0, part0 = call(
        functools.partial(attn_fwd_kernel, True, heads),
        [((SEQ, D), BF), ((3 * inner, SEQ), BF), ((inner, SEQ), BF), ((8, SEQ), F32), ((SEQ, D), F32)],
        (scal, rel_bias, inputs, other, gain1, wt, out_weight),
        [SM, SM] + [VM] * 5,
        name="attend_own",
        **attn_cost,
    )
    wt1, ow1 = pair_w[: 3 * inner], pair_w[3 * inner :]
    qkvt1, mixt1, lse1, keep, send = call(
        functools.partial(attn_fwd_kernel, False, heads),
        [((3 * inner, SEQ), BF), ((inner, SEQ), BF), ((8, SEQ), F32), ((rows, D), F32), ((rows, D), BF)],
        (scal, pair_table, normed, wt1, ow1, part0),
        [SM, SM] + [VM] * 4,
        scratch=[pltpu.VMEM((SEQ, D), F32)],
        name="attend_pair",
        **attn_cost,
    )
    got = swap(send, 1)
    middle_args = (inputs, keep, got, gain2, jnp.transpose(router_weight), routes_t, slots)
    line = experts == 2 * LINE and cap == TILE
    if line:
        hidden, normed_two, info = call(
            functools.partial(middle_line_kernel, experts),
            [((rows, D), F32), ((rows, D), BF), ((8, rows), F32)],
            middle_args,
            moved=6 * MIB,
            name="middle",
        )
        far_up, far_down, info = lax.optimization_barrier((far_up, far_down, info))
        came, result, stay, away, go, grad_router = moe_line(
            experts, cap, normed_two, info, grads_in, router_weight, (up, down, far_up, far_down)
        )
    else:
        mine = jnp.concatenate([up, down], axis=0)
        far = jnp.concatenate([far_up, far_down], axis=0)
        quarters = [mine, far, swap(mine, 1), swap(far, 1)]
        hidden, packed_rows, meta = call(
            functools.partial(middle_kernel, experts, cap),
            [((rows, D), F32), ((spots, D), BF), ((experts, 8, cap), F32)],
            middle_args,
            flops=2 * spots * rows * D,
            moved=8 * MIB,
            name="middle",
        )
        came, result, stay, away, go, grad_router = moe(
            experts, cap, packed_rows, meta, grads_in, router_weight, quarters
        )
    came_out = exchange(result)
    came_go = swap(go, 1)
    grad_hidden, grad_attended, moe_part = call(
        turn_kernel,
        [((rows, D), F32), ((rows, D), BF), ((8, D), F32)],
        (nvalid, came, slots, hidden, gain2, out_grad),
        [SM] + [VM] * 5,
        flops=2 * spots * rows * D,
        moved=8 * MIB,
        name="turn",
    )
    other_grad = swap(grad_attended, 1)
    away = (away.astype(F32) + came_go[1].astype(F32)).astype(BF)
    bwd_cost = dict(
        flops=2 * SEQ * D * 10 * inner + heads * SEQ * SEQ * 400, moved=9 * MIB, exps=heads * SEQ * SEQ
    )
    work = [
        pltpu.VMEM((SEQ, D), BF),
        pltpu.VMEM((inner, SEQ), BF),
        pltpu.VMEM((3 * inner, SEQ), BF),
        pltpu.VMEM((TILE, TILE), F32),
        pltpu.VMEM((TILE, TILE), F32),
    ]
    gpart, gbias1, npart = call(
        functools.partial(attn_bwd_kernel, False, heads),
        [((4 * inner, D), BF), ((8, 128), F32), ((SEQ, D), F32)],
        (scal, pair_table, normed, wt1, ow1, qkvt1, mixt1, lse1, grad_attended, other_grad),
        [SM, SM] + [VM] * 8,
        scratch=work,
        name="attend_pair_back",
        **bwd_cost,
    )
    gpair = swap(gpart, 2)
    gown, gbias0, keep_n, send_n = call(
        functools.partial(attn_bwd_kernel, True, heads),
        [((4 * inner, D), F32), ((8, 128), F32), ((rows, D), F32), ((rows, D), BF)],
        (scal, rel_bias, normed, wt, out_weight, qkvt0, mixt0, lse0, grad_attended, other_grad, npart),
        [SM, SM] + [VM] * 9,
        scratch=work + [pltpu.VMEM((SEQ, D), F32)],
        name="attend_own_back",
        **bwd_cost,
    )
    away, gpair, gown = lax.optimization_barrier((away, gpair, gown))
    came_away = swap(away, 2)
    if line:
        gwt, gow, grad_inputs, small = tail(
            (
                gown, gpair, keep_n, send_n, inputs, gain1, grad_hidden, moe_part, grad_router, gbias0, gbias1,
            ),
            rows,
            inner,
        )
    else:
        got_n = swap(send_n, 1)
        grad_inputs, attn_part = call(
            last_kernel,
            [((rows, D), BF), ((8, D), F32)],
            (inputs, keep_n, got_n, gain1, grad_hidden),
            moved=6 * MIB,
            name="last",
        )
        wide = (gown + gpair.astype(F32)).astype(BF)
        wide = lax.psum(wide, "expert").astype(F32)
    outputs = call(
        output_kernel,
        [((rows, D), BF)],
        (nvalid, came_out, slots, hidden),
        [SM] + [VM] * 3,
        flops=2 * spots * rows * D,
        moved=8 * MIB,
        name="outputs",
    )[0]

    if line:
        attn_sum = small[6, :6].reshape(D)
        moe_sum = small[7, :6].reshape(D)
        router_sum = jnp.transpose(small[:6], (0, 2, 1)).reshape(D, experts)
        bias_sum = lax.dynamic_slice(small[6:, 6:].reshape(4, 128), (rank, 0), (1, heads * NB))
    else:
        gwt, gow = jnp.transpose(wide[: 3 * inner]), wide[3 * inner :]
        own_bias = gbias0[:heads, :NB].reshape(1, -1)
        pair_bias = gbias1[:heads, :NB].reshape(1, -1)
        ranks = jnp.arange(4, dtype=jnp.int32)[:, None]
        bias_parts = jnp.where(ranks == rank, own_bias, 0.0) + jnp.where(
            ranks == (rank ^ 2), pair_bias, 0.0
        )
        small = jnp.concatenate(
            [attn_part[0], moe_part[0], jnp.transpose(grad_router).reshape(-1), bias_parts.reshape(-1)]
        )
        small = lax.psum(small, ("expert", "tensor"))
        attn_sum, moe_sum = small[:D], small[D : 2 * D]
        router_sum = small[2 * D : 2 * D + experts * D].reshape(D, experts)
        bias_sum = lax.dynamic_slice(
            small[2 * D + experts * D :].reshape(4, heads * NB), (rank, 0), (1, heads * NB)
        )
    grad_weights = stay.astype(F32) + came_go[0].astype(F32) + came_away.astype(F32)
    return (
        outputs,
        grad_inputs,
        attn_sum,
        gwt.reshape(D, 3, inner),
        gow,
        jnp.transpose(bias_sum.reshape(heads, NB)),
        moe_sum,
        router_sum,
        grad_weights[:D][None],
        jnp.transpose(grad_weights[D:])[None],
    )


def solution(mesh):
    return jax.shard_map(
        shards,
        mesh=mesh,
        in_specs=(
            P(("expert", "tensor"), None),
            P("expert"),
            P(("expert", "tensor"), None),
            P(),
            P(None, None, "tensor"),
            P("tensor", None),
            P(None, "tensor"),
            P(),
            P(),
            P("expert", None, "tensor"),
            P("expert", "tensor", None),
            P(("expert", "tensor"), None),
        ),
        out_specs=(
            P(("expert", "tensor"), None),
            P(("expert", "tensor"), None),
            P(),
            P(None, None, "tensor"),
            P("tensor", None),
            P(None, "tensor"),
            P(),
            P(),
            P("expert", None, "tensor"),
            P("expert", "tensor", None),
        ),
        check_vma=False,
    )
```

```python
import functools

import jax
import jax.numpy as jnp
from jax import lax
from jax.experimental import pallas as pl
from jax.experimental.pallas import tpu as pltpu
from jax.sharding import PartitionSpec as P

D = 768
HD = 64
NB = 32
MAXDIST = 128
SEQ = 1024
EPSILON = 1e-06
NEGATIVE = -1e30
TILE = 256
BF = jnp.bfloat16
F32 = jnp.float32
MIB = 2**20
CHUNK = 256
GELU = 0.7978845608028654
CUBIC = 0.044715


def bucket_edges():
    half_count = NB // 2
    short_edges = list(range(1, half_count))
    long_edges = [
        int(half_count * (MAXDIST / half_count) ** (step_index / half_count))
        for step_index in range(half_count)
    ]
    return short_edges + long_edges


EDGES = bucket_edges()


def dot(a, b, ca=1, cb=0, precision=None):
    return lax.dot_general(
        a, b, (((ca,), (cb,)), ((), ())), preferred_element_type=F32, precision=precision
    )


def iota(shape, dim):
    return lax.broadcasted_iota(jnp.int32, shape, dim)


def rms(v):
    return lax.rsqrt(jnp.mean(v * v, axis=-1, keepdims=True) + EPSILON)


def call(kernel, outs, args, specs=None, scratch=(), flops=0, moved=0, exps=0, vmem=56, name=None):
    vm = pl.BlockSpec(memory_space=pltpu.VMEM)
    return pl.pallas_call(
        kernel,
        out_shape=[jax.ShapeDtypeStruct(s, d) for s, d in outs],
        in_specs=specs or [vm] * len(args),
        out_specs=[vm] * len(outs),
        scratch_shapes=list(scratch),
        compiler_params=pltpu.CompilerParams(vmem_limit_bytes=vmem * MIB),
        cost_estimate=pl.CostEstimate(flops=flops, bytes_accessed=moved, transcendentals=exps),
        name=name,
    )(*args)


VM = pl.BlockSpec(memory_space=pltpu.VMEM)
SM = pl.BlockSpec(memory_space=pltpu.SMEM)


def slot_lines(experts, cap, valid_count, routes):
    rows = routes.shape[1]
    valid = iota((1, rows), 1) < valid_count
    ids = iota((experts, rows), 0)
    hot0 = ((ids == routes[0:1]) & valid).astype(F32)
    hot1 = ((ids == routes[1:2]) & valid).astype(F32)
    before = (iota((rows, rows), 0) < iota((rows, rows), 1)).astype(BF)
    rank = dot((hot0 + hot1).astype(BF), before)
    place = ids.astype(F32) * cap + rank
    bad = jnp.where(valid, 0.0, 1.0)
    slot0 = jnp.sum(hot0 * place, axis=0, keepdims=True) - bad
    slot1 = jnp.sum(hot1 * place, axis=0, keepdims=True) - bad
    return slot0, slot1


def route_kernel(experts, cap, nv_ref, routes_ref, grad_ref, packed_ref, slots_ref):
    rows = grad_ref.shape[0]
    slot0, slot1 = slot_lines(experts, cap, nv_ref[0], routes_ref[...])
    spots = iota((experts * cap, rows), 0)
    pick0 = spots == slot0.astype(jnp.int32)
    pick1 = spots == slot1.astype(jnp.int32)
    packed_ref[...] = dot((pick0 | pick1).astype(BF), grad_ref[...]).astype(BF)
    slots_ref[...] = jnp.concatenate([slot0, slot1, jnp.zeros((6, rows), F32)], axis=0)


def back_matrix(slots_ref, spots):
    rows = slots_ref.shape[1]
    where = iota((rows, spots), 1)
    slots = slots_ref[...].T.astype(jnp.int32)
    return ((where == slots[:, 0:1]) | (where == slots[:, 1:2])).astype(BF)


def bias_tiles(table_ref, head):
    dist = iota((8, TILE), 1)
    far = table_ref[NB - 1, head]
    curve = jnp.full((8, TILE), table_ref[0, head] - far, F32)
    for number, edge in enumerate(EDGES):
        curve = jnp.where(dist >= edge, table_ref[number + 1, head] - far, curve)
    spread = jnp.broadcast_to(curve[0:1], (TILE, TILE))
    ring = pltpu.roll(spread, 0, 1, stride=1, stride_axis=0)
    ahead = iota((TILE, TILE), 1) >= iota((TILE, TILE), 0)
    return jnp.where(ahead, ring, NEGATIVE), jnp.where(ahead, 0.0, ring)


def head_pieces(qkvt_ref, mask_rows, head, local_inner):
    start = pl.multiple_of(head * HD, HD)
    q = qkvt_ref[pl.ds(start, HD), :] * jnp.asarray(HD**-0.5, BF)
    k = qkvt_ref[pl.ds(local_inner + start, HD), :]
    v = qkvt_ref[pl.ds(2 * local_inner + start, HD), :]
    ones = jnp.ones((16, SEQ), BF)
    return jnp.concatenate([q, ones], 0), jnp.concatenate([k, mask_rows], 0), v, ones


def mask_block(length):
    keep = (iota((16, SEQ), 1) < length) | (iota((16, SEQ), 0) > 0)
    return jnp.where(keep, 0.0, NEGATIVE).astype(BF)


def score_pieces(k, q, block, near, below):
    cols = slice(block * TILE, (block + 1) * TILE)
    qb = q[:, cols]
    pieces = []
    if block >= 2:
        pieces.append((0, (block - 1) * TILE, dot(k[: (block - 1) * TILE], qb)))
    if block >= 1:
        lo = (block - 1) * TILE
        pieces.append((lo, block * TILE, dot(k[lo : lo + TILE], qb) + below))
    lo = block * TILE
    pieces.append((lo, lo + TILE, dot(k[lo : lo + TILE], qb) + near))
    return cols, pieces


def attn_fwd_kernel(first, heads, scal_ref, table_ref, *refs):
    if first:
        own_ref, other_ref, gain_ref, w_ref, ow_ref = refs[:5]
        normed_ref, qkvt_ref, mixt_ref, lse_ref, part_ref = refs[5:]
        half = own_ref.shape[0]
        core = lax.rem(lax.axis_index("tensor"), 2)
        for source, place in ((own_ref, core), (other_ref, 1 - core)):
            x = source[...].astype(F32)
            normed_ref[pl.ds(pl.multiple_of(place * half, half), half), :] = (
                x * rms(x) * gain_ref[...]
            ).astype(BF)
    else:
        normed_ref, w_ref, ow_ref, part_in = refs[:4]
        qkvt_ref, mixt_ref, lse_ref, keep_ref, send_ref, part_ref = refs[4:]
    local_inner = heads * HD
    qkvt_ref[...] = dot(w_ref[...], normed_ref[...], 1, 1).astype(BF)
    masks = mask_block(scal_ref[1])
    lse_ref[...] = jnp.zeros_like(lse_ref)

    for head in range(heads):
        near, below = bias_tiles(table_ref, head)
        q, kt, v, ones = head_pieces(qkvt_ref, masks, head, local_inner)
        k = kt.T
        vx = jnp.concatenate([v, ones], 0)
        for block in range(SEQ // TILE):
            cols, pieces = score_pieces(k, q, block, near, below)
            top = functools.reduce(
                jnp.maximum, [jnp.max(s, axis=0, keepdims=True) for _, _, s in pieces]
            )
            total = None
            for lo, hi, s in pieces:
                term = dot(vx[:, lo:hi], jnp.exp(s - top).astype(BF))
                total = term if total is None else total + term
            weight = total[HD : HD + 1]
            mixt_ref[head * HD : (head + 1) * HD, cols] = (total[:HD] / weight).astype(BF)
            lse_ref[head : head + 1, cols] = top + jnp.log(weight)
    part = dot(mixt_ref[...], ow_ref[...], 0, 0)
    if first:
        part_ref[...] = part
    else:
        part_ref[...] = part + part_in[...]
        half = keep_ref.shape[0]
        core = lax.rem(lax.axis_index("tensor"), 2)
        keep_ref[...] = part_ref[pl.ds(pl.multiple_of(core * half, half), half), :]
        send_ref[...] = part_ref[pl.ds(pl.multiple_of((1 - core) * half, half), half), :].astype(BF)


def attn_bwd_kernel(last, heads, scal_ref, table_ref, *refs):
    if last:
        (normed_ref, w_ref, ow_ref, qkvt_ref, mixt_ref, lse_ref, own_ref, other_ref, part_in) = refs[:9]
        gw_ref, gbias_ref, keep_ref, send_ref, ga_ref, got_ref, gt_ref, d0_ref, d1_ref, part_ref = refs[9:]
    else:
        (normed_ref, w_ref, ow_ref, qkvt_ref, mixt_ref, lse_ref, own_ref, other_ref) = refs[:8]
        gw_ref, gbias_ref, part_ref, ga_ref, got_ref, gt_ref, d0_ref, d1_ref = refs[8:]
    local_inner = heads * HD
    half = own_ref.shape[0]
    core = lax.rem(lax.axis_index("tensor"), 2)
    ga_ref[pl.ds(pl.multiple_of(core * half, half), half), :] = own_ref[...]
    ga_ref[pl.ds(pl.multiple_of((1 - core) * half, half), half), :] = other_ref[...]
    got_ref[...] = dot(ow_ref[...], ga_ref[...], 1, 1).astype(BF)
    gw_ref[3 * local_inner :] = dot(mixt_ref[...], ga_ref[...]).astype(gw_ref.dtype)
    masks = mask_block(scal_ref[1])
    gbias_ref[...] = jnp.zeros_like(gbias_ref)
    ahead = iota((TILE, TILE), 1) >= iota((TILE, TILE), 0)
    spot = (iota((TILE, 128), 0) + 1) % TILE
    flip = (iota((TILE, TILE), 0) + iota((TILE, TILE), 1) == TILE - 1).astype(F32)
    bucket = jnp.zeros((TILE, 128), jnp.int32)
    for edge in EDGES:
        bucket = bucket + (spot >= edge).astype(jnp.int32)
    hot = (bucket == iota((TILE, 128), 1)).astype(F32)

    for head in range(heads):
        near, below = bias_tiles(table_ref, head)
        q, kt, vt, _ = head_pieces(qkvt_ref, masks, head, local_inner)
        k = kt.T
        v = vt.T
        rows = slice(head * HD, (head + 1) * HD)
        gt = got_ref[rows, :]
        delta = jnp.sum(gt.astype(F32) * mixt_ref[rows, :].astype(F32), axis=0, keepdims=True)
        gk = [None] * (SEQ // TILE)
        gv = [None] * (SEQ // TILE)
        far = jnp.zeros((8, TILE), F32)
        for block in range(SEQ // TILE):
            cols, pieces = score_pieces(k, q, block, near, below)
            gb = gt[:, cols]
            qb = q[:HD, cols]
            lse = lse_ref[head : head + 1, cols]
            db = delta[:, cols]
            gq = None
            for lo, hi, s in pieces:
                p = jnp.exp(s - lse)
                ds = p * (dot(v[lo:hi], gb) - db)
                pb = p.astype(BF)
                dsb = ds.astype(BF)
                term = dot(kt[:HD, lo:hi], dsb)
                gq = term if gq is None else gq + term
                tv = dot(pb, gb, 1, 1)
                tk = dot(dsb, qb, 1, 1)
                for tile in range(lo // TILE, hi // TILE):
                    part = slice(tile * TILE - lo, (tile + 1) * TILE - lo)
                    gv[tile] = tv[part] if gv[tile] is None else gv[tile] + tv[part]
                    gk[tile] = tk[part] if gk[tile] is None else gk[tile] + tk[part]
                if hi == (block + 1) * TILE:
                    d0_ref[...] = ds if block == 0 else d0_ref[...] + ds
                elif hi == block * TILE and lo == (block - 1) * TILE:
                    d1_ref[...] = ds if block == 1 else d1_ref[...] + ds
                else:
                    far = far + jnp.sum(ds.reshape((hi - lo) // 8, 8, TILE), axis=0)
            gt_ref[rows, cols] = (gq * HD**-0.5).astype(BF)
        for tile in range(SEQ // TILE):
            cols = slice(tile * TILE, (tile + 1) * TILE)
            gt_ref[local_inner + head * HD : local_inner + (head + 1) * HD, cols] = (
                gk[tile].T.astype(BF)
            )
            gt_ref[2 * local_inner + head * HD : 2 * local_inner + (head + 1) * HD, cols] = (
                gv[tile].T.astype(BF)
            )
        d1 = d1_ref[...]
        ring = jnp.where(ahead, d0_ref[...], d1)
        turned = pltpu.roll(
            dot(flip, ring, 1, 0, lax.Precision.HIGHEST), 0, 1, stride=1, stride_axis=0
        )
        far = far + jnp.sum(jnp.where(ahead, d1, 0.0).reshape(TILE // 8, 8, TILE), axis=0)
        line = jnp.sum(turned, axis=0, keepdims=True)
        sums = dot(
            jnp.broadcast_to(line, (8, TILE)), hot, 1, 0, lax.Precision.HIGHEST
        )
        sums = sums + jnp.where(iota((8, 128), 1) == NB - 1, jnp.sum(far), 0.0)
        gbias_ref[head : head + 1, :] = sums[0:1]
    gw_ref[: 3 * local_inner] = dot(gt_ref[...], normed_ref[...]).astype(gw_ref.dtype)
    part = dot(gt_ref[...], w_ref[...], 0, 0)
    if last:
        part_ref[...] = part + part_in[...]
        keep_ref[...] = part_ref[pl.ds(pl.multiple_of(core * half, half), half), :]
        send_ref[...] = part_ref[pl.ds(pl.multiple_of((1 - core) * half, half), half), :].astype(BF)
    else:
        part_ref[...] = part


def gates_of(experts, normed, router_t, routes):
    rows = normed.shape[0]
    logits = dot(router_t, normed, 1, 1)
    ids = iota((experts, rows), 0)
    signs = (ids == routes[0:1]).astype(F32) - (ids == routes[1:2]).astype(F32)
    gap = jnp.sum(logits * signs, axis=0, keepdims=True)
    return 1.0 / (1.0 + jnp.exp(-gap)), 1.0 / (1.0 + jnp.exp(gap))


def meta_lines(gate, code):
    rows = gate.shape[1]
    line = iota((8, rows), 0)
    high = gate.astype(BF).astype(F32)
    mid = (gate - high).astype(BF).astype(F32)
    low = gate - high - mid
    picked = jnp.where(line == 0, high, jnp.where(line == 1, mid, jnp.where(line == 2, low, 0.0)))
    return jnp.where(line == 3, code, picked).astype(BF)


def hidden_rows(x_ref, keep_ref, got_ref, gain_ref, hidden_ref):
    hidden = x_ref[...].astype(F32) + keep_ref[...] + got_ref[...].astype(F32)
    hidden_ref[...] = hidden
    return (hidden * rms(hidden) * gain_ref[...]).astype(BF)


def middle_kernel(
    experts, cap, x_ref, keep_ref, got_ref, gain_ref, router_ref, routes_ref, slots_ref, hidden_ref, packed_ref, meta_ref
):
    normed = hidden_rows(x_ref, keep_ref, got_ref, gain_ref, hidden_ref)
    slots = slots_ref[...].astype(jnp.int32)
    routes = routes_ref[...]
    where = iota((experts * cap, normed.shape[0]), 0)
    pick0 = where == slots[0:1]
    pick1 = where == slots[1:2]
    packed_ref[...] = dot((pick0 | pick1).astype(BF), normed).astype(BF)
    gate0, gate1 = gates_of(experts, normed, router_ref[...], routes)
    codes = (routes + 1).astype(F32)
    meta = dot(meta_lines(gate0, codes[1:2]), pick0.astype(BF), 1, 1) + dot(
        meta_lines(gate1, codes[0:1]), pick1.astype(BF), 1, 1
    )
    for number in range(experts):
        meta_ref[number] = meta[:, number * cap : (number + 1) * cap]


def middle_line_kernel(
    experts, x_ref, keep_ref, got_ref, gain_ref, router_ref, routes_ref, slots_ref, hidden_ref, normed_ref, info_ref
):
    normed = hidden_rows(x_ref, keep_ref, got_ref, gain_ref, hidden_ref)
    normed_ref[...] = normed
    routes = routes_ref[...]
    gate0, gate1 = gates_of(experts, normed, router_ref[...], routes)
    codes = (routes + 1).astype(F32)
    info_ref[...] = jnp.concatenate(
        [slots_ref[0:2], gate0, gate1, codes, jnp.zeros((2, normed.shape[0]), F32)], axis=0
    )


def gelu_pair(v):
    squared = v * v
    slope = GELU * (1.0 + 3 * CUBIC * squared)
    t = jnp.tanh(v * (GELU + GELU * CUBIC * squared))
    half = 0.5 + 0.5 * t
    return v * half, half + 0.5 * v * (1.0 - t * t) * slope


def flipped(me, k, count):
    total, bit = 0, 1
    while bit < count:
        total = total + lax.rem(me // bit + k // bit, 2) * bit
        bit *= 2
    return total


def weight_grads(xt_ref, geot_ref, act_ref, gi_ref, stage_ref, stay_ref, away_ref, go_ref, out_sem):
    tiles = D // TILE
    steps = 8 * tiles

    def columns(step):
        return pl.ds(pl.multiple_of(lax.rem(step, tiles) * TILE, TILE), TILE)

    def store(step, slot, out_ref):
        half = lax.rem(step, 2 * tiles) // tiles
        return pltpu.make_async_copy(
            stage_ref.at[slot],
            out_ref.at[pl.ds(pl.multiple_of(half * D, D), D), columns(step)],
            out_sem.at[slot],
        )

    def weights(step, carry):
        q = step // (2 * tiles)
        half = lax.rem(step, 2 * tiles) // tiles
        slot = lax.rem(step, 2)

        @pl.when(step >= 2)
        def _():
            store(step - 2, slot, stay_ref).wait()

        @pl.when(half == 0)
        def _():
            stage_ref[slot] = dot(xt_ref[...], gi_ref[q, :, columns(step)]).astype(BF)

        @pl.when(half == 1)
        def _():
            stage_ref[slot] = dot(geot_ref[...], act_ref[q, :, columns(step)]).astype(BF)

        for number, out_ref in enumerate((stay_ref, away_ref, go_ref.at[0], go_ref.at[1])):

            @pl.when(q == number)
            def _():
                store(step, slot, out_ref).start()

        return carry

    lax.fori_loop(0, steps, weights, 0)
    for step in (steps - 2, steps - 1):
        store(step, step % 2, stay_ref).wait()


def expert_rows(x, geo, here, w_ref, xt_ref, geot_ref, act_ref, gi_ref, acc_ref):
    xt_ref[:, here] = x.T
    geot_ref[:, here] = geo.T
    worth = 0.0
    for q in range(4):
        inner = dot(x, w_ref[q, :D])
        grad_active = dot(geo, w_ref[q, D:], 1, 1)
        act, slope = gelu_pair(inner)
        gi = (slope * grad_active).astype(BF)
        act_ref[q, here] = act.astype(BF)
        gi_ref[q, here] = gi
        back = dot(gi, w_ref[q, :D], 1, 1)
        if q == 0:
            acc_ref[...] = back
        else:
            acc_ref[...] += back
        worth = worth + jnp.sum(act * grad_active, axis=1, keepdims=True)
    return worth


def expert_outs(start, size, column, act_ref, w_ref):
    here = pl.ds(pl.multiple_of(start, size), size)
    cols = pl.ds(pl.multiple_of(column * TILE, TILE), TILE)
    total = None
    for q in range(4):
        term = dot(act_ref[q, here], w_ref[q, D:, cols])
        total = term if total is None else total + term
    return cols, total


def expert_kernel(
    count, cap, packed_ref, send_meta_ref, grads_ref, router_ref, w0, w1, w2, w3,
    came_ref, result_ref, stay_ref, away_ref, go_ref, grouter_ref,
    w_ref, x_ref, xt_ref, geot_ref, act_ref, gi_ref, gsend_ref, meta_ref, acc_ref, stage_ref,
    x_send, x_recv, m_send, m_recv, r_send, r_recv, local_sem, w_sem, out_sem,
):
    me = lax.axis_index("expert")
    barrier = pltpu.get_barrier_semaphore()

    def peer(k):
        return flipped(me, k, count)

    source = peer

    def greet(k, carry):
        pl.semaphore_signal(
            barrier, inc=1, device_id={"expert": peer(k)}, device_id_type=pl.DeviceIdType.MESH
        )
        return carry

    lax.fori_loop(1, count, greet, 0)
    pl.semaphore_wait(barrier, count - 1)

    def rows_of(k):
        return pl.ds(pl.multiple_of(k * cap, cap), cap)

    def send_rows(k):
        return pltpu.make_async_remote_copy(
            src_ref=packed_ref.at[rows_of(peer(k))],
            dst_ref=x_ref.at[rows_of(k)],
            send_sem=x_send.at[k],
            recv_sem=x_recv.at[k],
            device_id={"expert": peer(k)},
            device_id_type=pl.DeviceIdType.MESH,
        )

    def send_meta(k):
        return pltpu.make_async_remote_copy(
            src_ref=send_meta_ref.at[peer(k)],
            dst_ref=meta_ref.at[k],
            send_sem=m_send.at[k],
            recv_sem=m_recv.at[k],
            device_id={"expert": peer(k)},
            device_id_type=pl.DeviceIdType.MESH,
        )

    def send_back(k):
        return pltpu.make_async_remote_copy(
            src_ref=gsend_ref.at[rows_of(k)],
            dst_ref=came_ref.at[rows_of(me)],
            send_sem=r_send.at[k],
            recv_sem=r_recv.at[k],
            device_id={"expert": source(k)},
            device_id_type=pl.DeviceIdType.MESH,
        )

    def start_sends(k, carry):
        send_meta(k).start()
        send_rows(k).start()
        return carry

    lax.fori_loop(count // 2, count, start_sends, 0)
    lax.fori_loop(1, count // 2, start_sends, 0)
    own_rows = pltpu.make_async_copy(packed_ref.at[rows_of(me)], x_ref.at[rows_of(0)], local_sem.at[0])
    own_rows.start()
    own_meta = pltpu.make_async_copy(send_meta_ref.at[me], meta_ref.at[0], local_sem.at[1])
    own_meta.start()
    loads = [
        pltpu.make_async_copy(w, w_ref.at[i], w_sem.at[i]) for i, w in enumerate((w0, w1, w2, w3))
    ]
    for load in loads:
        load.start()
    grouter_ref[...] = jnp.zeros_like(grouter_ref)
    experts = router_ref.shape[1]
    own_rows.wait()
    own_meta.wait()
    for load in loads:
        load.wait()
    group = max(1, CHUNK // cap)
    span = group * cap

    def chunk(j, carry):
        for i in range(group):
            k = j * group + i

            @pl.when(k > 0)
            def _():
                send_rows(k).wait_recv()
                send_meta(k).wait_recv()

        here = pl.ds(pl.multiple_of(j * span, span), span)
        meta = jnp.concatenate([meta_ref[j * group + i].T for i in range(group)], axis=0)
        gate = meta[:, 0:1] + meta[:, 1:2] + meta[:, 2:3]
        code = meta[:, 3:4].astype(jnp.int32)
        gy = jnp.concatenate([grads_ref[rows_of(source(j * group + i)), :] for i in range(group)], axis=0)
        geo = (gate * gy.astype(F32)).astype(BF)
        x = x_ref[here, :]
        worth = expert_rows(x, geo, here, w_ref, xt_ref, geot_ref, act_ref, gi_ref, acc_ref)
        ids = iota((span, experts), 1)
        signs = (ids == me).astype(F32) - (ids + 1 == code).astype(F32)
        share = jnp.where(code > 0, (1.0 - gate) * worth, 0.0) * signs
        high = share.astype(BF)
        low = (share - high.astype(F32)).astype(BF)
        gsend_ref[here, :] = (acc_ref[...] + dot(high, router_ref[...], 1, 1)).astype(BF)
        grouter_ref[...] += dot(high.T, x) + dot(low.T, x)
        for i in range(group):
            k = j * group + i

            @pl.when(k > 0)
            def _():
                send_back(k).start()

        return carry

    lax.fori_loop(0, count // group, chunk, 0)
    own_back = pltpu.make_async_copy(gsend_ref.at[rows_of(0)], came_ref.at[rows_of(me)], local_sem.at[0])
    own_back.start()

    def results(step, carry):
        j = step // (D // TILE)
        meta = jnp.concatenate([meta_ref[j * group + i].T for i in range(group)], axis=0)
        gate = meta[:, 0:1] + meta[:, 1:2] + meta[:, 2:3]
        cols, total = expert_outs(j * span, span, lax.rem(step, D // TILE), act_ref, w_ref)
        out = (gate * total).astype(BF)
        for i in range(group):
            result_ref[rows_of(source(j * group + i)), cols] = out[i * cap : (i + 1) * cap]
        return carry

    lax.fori_loop(0, count // group * (D // TILE), results, 0)
    weight_grads(xt_ref, geot_ref, act_ref, gi_ref, stage_ref, stay_ref, away_ref, go_ref, out_sem)
    own_back.wait()

    def finish(k, carry):
        send_rows(k).wait_send()
        send_meta(k).wait_send()
        send_back(k).wait()
        return carry

    lax.fori_loop(1, count, finish, 0)


def mesh_copy(src, dst, send_sem, recv_sem, target):
    return pltpu.make_async_remote_copy(
        src_ref=src,
        dst_ref=dst,
        send_sem=send_sem,
        recv_sem=recv_sem,
        device_id={"expert": target},
        device_id_type=pl.DeviceIdType.MESH,
    )


LINE = 4


def expert_line_kernel(
    cap, normed_ref, info_in, grads_ref, router_ref, up_ref, down_ref, far_up_ref, far_down_ref,
    came_ref, result_ref, stay_ref, away_ref, go_ref, grouter_ref,
    w_ref, block_ref, info_ref, x_ref, xs_ref, meta_ref, ms_ref, xt_ref, geot_ref, act_ref, gi_ref, acc_ref, stage_ref,
    b_send, b_recv, i_send, i_recv, x_send, x_recv, m_send, m_recv, r_send, r_recv, local_sem, w_sem, v_send, v_recv, out_sem,
):
    count = 2 * LINE
    me = lax.axis_index("expert")
    place = me // 2
    side = me - 2 * place
    mate = me + 1 - 2 * side
    barrier = pltpu.get_barrier_semaphore()

    def greet(k, carry):
        pl.semaphore_signal(
            barrier,
            inc=1,
            device_id={"expert": lax.rem(me + k, count)},
            device_id_type=pl.DeviceIdType.MESH,
        )
        return carry

    lax.fori_loop(1, count, greet, 0)
    core = flipped(lax.axis_index("tensor"), 1, 4)
    pl.semaphore_signal(
        barrier, inc=1, device_id={"tensor": core}, device_id_type=pl.DeviceIdType.MESH
    )
    pl.semaphore_wait(barrier, count)

    def along(block, step):
        return (
            mesh_copy(
                info_ref.at[block],
                info_ref.at[block],
                i_send.at[(step + 1) // 2, block],
                i_recv.at[block],
                me + 2 * step,
            ),
            mesh_copy(
                block_ref.at[block],
                block_ref.at[block],
                b_send.at[(step + 1) // 2, block],
                b_recv.at[block],
                me + 2 * step,
            ),
        )

    def across(block):
        return (
            mesh_copy(ms_ref.at[block], meta_ref.at[1, block], m_send.at[block], m_recv.at[block], mate),
            mesh_copy(xs_ref.at[block], x_ref.at[1, block], x_send.at[block], x_recv.at[block], mate),
        )

    def rows_of(number):
        return pl.ds(pl.multiple_of(number * cap, cap), cap)

    def origin(part, block):
        return 2 * block + side + part * (1 - 2 * side)

    def give_back(part, block):
        return mesh_copy(
            x_ref.at[part, block],
            came_ref.at[rows_of(me)],
            r_send.at[part, block],
            r_recv.at[me],
            origin(part, block),
        )

    def each(pair, act):
        for one in pair:
            act(one)

    own = (
        pltpu.make_async_copy(info_in, info_ref.at[place], local_sem.at[0]),
        pltpu.make_async_copy(normed_ref, block_ref.at[place], local_sem.at[1]),
    )
    each(own, lambda c: c.start())
    weights = (up_ref, down_ref, far_up_ref, far_down_ref)
    each(own, lambda c: c.wait())

    @pl.when(place < LINE - 1)
    def _():
        each(along(place, 1), lambda c: c.start())

    @pl.when(place > 0)
    def _():
        each(along(place, -1), lambda c: c.start())

    def load(i):
        return pltpu.make_async_copy(weights[i], w_ref.at[i // 2, pl.ds(i % 2 * D, D)], w_sem.at[i])

    def lend(i):
        return pltpu.make_async_remote_copy(
            src_ref=weights[i],
            dst_ref=w_ref.at[2 + i // 2, pl.ds(i % 2 * D, D)],
            send_sem=v_send.at[i],
            recv_sem=v_recv.at[i],
            device_id={"tensor": core},
            device_id_type=pl.DeviceIdType.MESH,
        )

    for i in range(4):
        load(i).start()
        lend(i).start()
    experts = router_ref.shape[1]
    rows = normed_ref.shape[0]

    def select(block):
        info = info_ref[block]
        slots = info[0:2].astype(jnp.int32)
        lines0 = meta_lines(info[2:3], info[5:6])
        lines1 = meta_lines(info[3:4], info[4:5])
        for part, expert in ((1, mate), (0, me)):
            where = iota((cap, rows), 0) + expert * cap
            pick0 = where == slots[0:1]
            pick1 = where == slots[1:2]
            taken = dot((pick0 | pick1).astype(BF), block_ref[block]).astype(BF)
            meta = dot(lines0, pick0.astype(BF), 1, 1) + dot(lines1, pick1.astype(BF), 1, 1)
            if part:
                xs_ref[block] = taken
                ms_ref[block] = meta
                each(across(block), lambda c: c.start())
            else:
                x_ref[0, block] = taken
                meta_ref[0, block] = meta

    select(place)
    grouter_ref[...] = jnp.zeros_like(grouter_ref)
    for i in range(4):
        load(i).wait()
        lend(i).wait_recv()
    mirror = place // 2
    inward = place + mirror * (LINE - 1 - 2 * place)

    def block_at(i):
        step = i + inward * (1 - i // 2 - 2 * (i // 2 - i // (LINE - 1)))
        return step + mirror * (LINE - 1 - 2 * step)

    def chunk_at(c):
        part = lax.rem(c + 1, 2) - (7 - c) // 7 + c // 7
        return part, block_at((c + 1) // 2 - part * ((c + 1) // 2 - (c - 1) // 2))

    def accept(distance):
        for step in (-1, 1):
            block = place + step * distance
            inside = (block >= 0) & (block < LINE)

            @pl.when(inside)
            def _():
                each(along(block, -step), lambda c: c.wait_recv())
                ahead = place - step

                @pl.when((ahead >= 0) & (ahead < LINE))
                def _():
                    each(along(block, -step), lambda c: c.start())

        for step in (-1, 1):
            block = place + step * distance
            inside = (block >= 0) & (block < LINE)

            @pl.when(inside)
            def _():
                select(block)

    def chunk(c, carry):
        for distance in range(1, LINE):

            @pl.when(c == 2 * distance - 1)
            def _():
                accept(distance)

        part, block = chunk_at(c)

        @pl.when(part == 1)
        def _():
            each(across(block), lambda c: c.wait_recv())

        here = pl.ds(pl.multiple_of(c * cap, cap), cap)
        meta = meta_ref[part, block].T
        gate = meta[:, 0:1] + meta[:, 1:2] + meta[:, 2:3]
        code = meta[:, 3:4].astype(jnp.int32)
        geo = (gate * grads_ref[rows_of(origin(part, block)), :].astype(F32)).astype(BF)
        x = x_ref[part, block]
        worth = expert_rows(x, geo, here, w_ref, xt_ref, geot_ref, act_ref, gi_ref, acc_ref)
        ids = iota((cap, experts), 1)
        signs = (ids == me).astype(F32) - (ids + 1 == code).astype(F32)
        share = jnp.where(code > 0, (1.0 - gate) * worth, 0.0) * signs
        high = share.astype(BF)
        low = (share - high.astype(F32)).astype(BF)
        grouter_ref[...] += dot(high.T, x) + dot(low.T, x)
        x_ref[part, block] = (acc_ref[...] + dot(high, router_ref[...], 1, 1)).astype(BF)

        @pl.when(origin(part, block) != me)
        def _():
            give_back(part, block).start()

        return carry

    lax.fori_loop(0, count, chunk, 0)
    own_back = pltpu.make_async_copy(x_ref.at[0, place], came_ref.at[rows_of(me)], local_sem.at[0])
    own_back.start()

    def results(step, carry):
        first = step // (D // TILE) * LINE
        cols, total = expert_outs(first * cap, LINE * cap, lax.rem(step, D // TILE), act_ref, w_ref)
        for i in range(LINE):
            part, block = chunk_at(first + i)
            meta = meta_ref[part, block].T
            gate = meta[:, 0:1] + meta[:, 1:2] + meta[:, 2:3]
            result_ref[rows_of(origin(part, block)), cols] = (
                gate * total[i * cap : (i + 1) * cap]
            ).astype(BF)
        return carry

    lax.fori_loop(0, 2 * (D // TILE), results, 0)
    weight_grads(xt_ref, geot_ref, act_ref, gi_ref, stage_ref, stay_ref, away_ref, go_ref, out_sem)
    own_back.wait()
    for i in range(4):
        lend(i).wait_send()
    for block in range(LINE):
        each(across(block), lambda c: c.wait_send())
        for step in (-1, 1):
            @pl.when((place + step >= 0) & (place + step < LINE) & ((place - block) * step >= 0))
            def _():
                each(along(block, step), lambda c: c.wait_send())

        for part in (0, 1):

            @pl.when(origin(part, block) != me)
            def _():
                give_back(part, block).wait_send()

    for number in range(count):

        @pl.when(number != me)
        def _():
            mesh_copy(
                x_ref.at[0, 0], came_ref.at[rows_of(number)], r_send.at[0, 0], r_recv.at[number], mate
            ).wait_recv()


def turn_kernel(nv_ref, came_ref, slots_ref, hidden_ref, gain_ref, grad_ref, gh_ref, ga_ref, gain_out):
    gn = dot(back_matrix(slots_ref, came_ref.shape[0]), came_ref[...])
    hidden = hidden_ref[...]
    scale = rms(hidden)
    unit = hidden * scale
    gain_out[...] = jnp.broadcast_to(jnp.sum(gn * unit, axis=0, keepdims=True), gain_out.shape)
    g = gn * gain_ref[...]
    valid = (iota((hidden.shape[0], 1), 0) < nv_ref[0]).astype(F32)
    gh = scale * (g - unit * jnp.mean(g * unit, axis=1, keepdims=True)) + valid * grad_ref[...].astype(F32)
    gh_ref[...] = gh
    ga_ref[...] = gh.astype(BF)


def output_kernel(nv_ref, came_ref, slots_ref, hidden_ref, out_ref):
    mix = dot(back_matrix(slots_ref, came_ref.shape[0]), came_ref[...])
    hidden = hidden_ref[...]
    valid = (iota((hidden.shape[0], 1), 0) < nv_ref[0]).astype(F32)
    out_ref[...] = (valid * (hidden + mix)).astype(BF)


def last_kernel(x_ref, keep_ref, got_ref, gain_ref, gh_ref, out_ref, gain_out):
    x = x_ref[...].astype(F32)
    scale = rms(x)
    unit = x * scale
    gn = keep_ref[...] + got_ref[...].astype(F32)
    gain_out[...] = jnp.broadcast_to(jnp.sum(gn * unit, axis=0, keepdims=True), gain_out.shape)
    g = gn * gain_ref[...]
    out_ref[...] = (
        gh_ref[...] + scale * (g - unit * jnp.mean(g * unit, axis=1, keepdims=True))
    ).astype(BF)


def moe(experts, cap, packed, meta, grads, router, quarters):
    spots = experts * cap
    anyspec = pl.BlockSpec(memory_space=pl.ANY)
    dma = pltpu.SemaphoreType.DMA
    return pl.pallas_call(
        functools.partial(expert_kernel, experts, cap),
        out_shape=[
            jax.ShapeDtypeStruct((spots, D), BF),
            jax.ShapeDtypeStruct((spots, D), BF),
            jax.ShapeDtypeStruct((2 * D, D), BF),
            jax.ShapeDtypeStruct((2 * D, D), BF),
            jax.ShapeDtypeStruct((2, 2 * D, D), BF),
            jax.ShapeDtypeStruct((experts, D), F32),
        ],
        in_specs=[anyspec, VM, VM, VM] + [anyspec] * 4,
        out_specs=[anyspec, VM, anyspec, anyspec, anyspec, VM],
        scratch_shapes=[
            pltpu.VMEM((4, 2 * D, D), BF),
            pltpu.VMEM((spots, D), BF),
            pltpu.VMEM((D, spots), BF),
            pltpu.VMEM((D, spots), BF),
            pltpu.VMEM((4, spots, D), BF),
            pltpu.VMEM((4, spots, D), BF),
            pltpu.VMEM((spots, D), BF),
            pltpu.VMEM((experts, 8, cap), F32),
            pltpu.VMEM((CHUNK, D), F32),
            pltpu.VMEM((2, D, TILE), BF),
            dma((experts,)),
            dma((experts,)),
            dma((experts,)),
            dma((experts,)),
            dma((experts,)),
            dma((experts,)),
            dma((2,)),
            dma((4,)),
            dma((2,)),
        ],
        compiler_params=pltpu.CompilerParams(
            collective_id=1, has_side_effects=True, vmem_limit_bytes=60 * MIB
        ),
        cost_estimate=pl.CostEstimate(flops=12 * spots * D * 4 * D, bytes_accessed=60 * MIB, transcendentals=0),
        name="experts",
    )(packed, meta, grads, router, *quarters)


def moe_line(experts, cap, normed, info, grads, router, weights):
    rows = normed.shape[0]
    spots = experts * cap
    anyspec = pl.BlockSpec(memory_space=pl.ANY)
    dma = pltpu.SemaphoreType.DMA
    return pl.pallas_call(
        functools.partial(expert_line_kernel, cap),
        out_shape=[
            jax.ShapeDtypeStruct((spots, D), BF),
            jax.ShapeDtypeStruct((spots, D), BF),
            jax.ShapeDtypeStruct((2 * D, D), BF),
            jax.ShapeDtypeStruct((2 * D, D), BF),
            jax.ShapeDtypeStruct((2, 2 * D, D), BF),
            jax.ShapeDtypeStruct((experts, D), F32),
        ],
        in_specs=[VM, VM, VM, VM] + [anyspec] * 4,
        out_specs=[anyspec, VM, anyspec, anyspec, anyspec, VM],
        scratch_shapes=[
            pltpu.VMEM((4, 2 * D, D), BF),
            pltpu.VMEM((LINE, rows, D), BF),
            pltpu.VMEM((LINE, 8, rows), F32),
            pltpu.VMEM((2, LINE, cap, D), BF),
            pltpu.VMEM((LINE, cap, D), BF),
            pltpu.VMEM((2, LINE, 8, cap), F32),
            pltpu.VMEM((LINE, 8, cap), F32),
            pltpu.VMEM((D, spots), BF),
            pltpu.VMEM((D, spots), BF),
            pltpu.VMEM((4, spots, D), BF),
            pltpu.VMEM((4, spots, D), BF),
            pltpu.VMEM((cap, D), F32),
            pltpu.VMEM((2, D, TILE), BF),
            dma((2, LINE)),
            dma((LINE,)),
            dma((2, LINE)),
            dma((LINE,)),
            dma((LINE,)),
            dma((LINE,)),
            dma((LINE,)),
            dma((LINE,)),
            dma((2, LINE)),
            dma((experts,)),
            dma((2,)),
            dma((4,)),
            dma((4,)),
            dma((4,)),
            dma((2,)),
        ],
        compiler_params=pltpu.CompilerParams(
            collective_id=2, has_side_effects=True, vmem_limit_bytes=62 * MIB
        ),
        cost_estimate=pl.CostEstimate(flops=12 * spots * D * 4 * D, bytes_accessed=60 * MIB, transcendentals=0),
        name="experts_line",
    )(normed, info, grads, router, *weights)


def tensor_copy(src, dst, send_sem, recv_sem, target):
    return pltpu.make_async_remote_copy(
        src_ref=src,
        dst_ref=dst,
        send_sem=send_sem,
        recv_sem=recv_sem,
        device_id={"tensor": target},
        device_id_type=pl.DeviceIdType.MESH,
    )


def sums(
    pair_done, beside, gw_ref, pair_ref, keep_ref, send_ref, x_in, gain_ref, gh_ref, moe_ref, router_ref, bias0_ref, bias1_ref,
    gwt_out, gow_out, gin_out, small_out,
    part_ref, cross_ref, line_ref, from_ref, all_ref, got_ref, lines_ref, few_ref, ranks_ref,
    a_send, a_recv, b_send, b_recv, c_send, c_recv, d_send, d_recv, s_send, s_recv, f_send, f_recv, t_send, t_recv, g_send, g_recv,
):
    count = 2 * LINE
    me = lax.axis_index("expert")
    rank = lax.axis_index("tensor")
    place = me // 2
    side = me - 2 * place
    mate = me + 1 - 2 * side
    size = part_ref.shape[0] // count
    def slab(which, number):
        return pl.ds(pl.multiple_of((which * LINE + number) * size, size), size)

    swap = tensor_copy(send_ref, got_ref, s_send, s_recv, flipped(rank, 1, 4))
    swap.start()
    pair_done()
    part_ref[...] = (gw_ref[...] + pair_ref[...].astype(F32)).astype(BF)
    rows = gwt_out.shape[1]

    def cross(number):
        return mesh_copy(
            part_ref.at[slab(1 - side, number)], cross_ref.at[number], a_send.at[number], a_recv.at[number], mate
        )

    def along(number):
        return mesh_copy(
            line_ref.at[number], from_ref.at[place], b_send.at[number], b_recv.at[place], 2 * number + side
        )

    def spread(number):
        return mesh_copy(
            all_ref.at[slab(side, place)],
            all_ref.at[slab(side, place)],
            c_send.at[number],
            c_recv.at[place],
            2 * number + side,
        )

    def over(number):
        return mesh_copy(
            all_ref.at[slab(side, number)], all_ref.at[slab(side, number)], d_send.at[number], d_recv.at[number], mate
        )

    for number in range(LINE):
        cross(number).start()

    swap.wait()
    x = x_in[...].astype(F32)
    scale = rms(x)
    unit = x * scale
    gn = keep_ref[...] + got_ref[...].astype(F32)
    attn = jnp.sum(gn * unit, axis=0, keepdims=True)
    g = gn * gain_ref[...]
    gin_out[...] = (gh_ref[...] + scale * (g - unit * jnp.mean(g * unit, axis=1, keepdims=True))).astype(BF)

    heads = gow_out.shape[0] // HD
    blank = jnp.zeros((1, 128), F32)

    def flat(bias_ref):
        line = [bias_ref[h : h + 1, :NB] for h in range(heads)]
        return jnp.concatenate(line + [jnp.zeros((1, 128 - heads * NB), F32)], axis=1)

    own_bias, pair_bias = flat(bias0_ref), flat(bias1_ref)
    other = flipped(rank, 2, 4)
    for j in range(D // 128):
        lines_ref[j] = router_ref[:, j * 128 : (j + 1) * 128]
    for j, row in ((6, attn), (7, moe_ref[0:1])):
        places = [2 * (j - 6), 2 * (j - 6) + 1]
        bias = [
            jnp.where(rank == p, own_bias, blank) + jnp.where(other == p, pair_bias, blank) for p in places
        ]
        lines_ref[j] = jnp.concatenate([row[:, i * 128 : (i + 1) * 128] for i in range(6)] + bias, axis=0)

    def small(k):
        return mesh_copy(
            lines_ref.at[flipped(me, k, count)], few_ref.at[k], f_send.at[k], f_recv.at[k], flipped(me, k, count)
        )

    def rank_copy(k):
        return tensor_copy(
            ranks_ref.at[rank], ranks_ref.at[rank], t_send.at[k], t_recv.at[k], flipped(rank, k, 4)
        )

    def rank_from(k):
        return tensor_copy(
            ranks_ref.at[rank], ranks_ref.at[flipped(rank, k, 4)], t_send.at[k], t_recv.at[k], flipped(rank, k, 4)
        )

    def small_spread(k):
        return mesh_copy(
            small_out.at[me], small_out.at[me], g_send.at[k], g_recv.at[k], flipped(me, k, count)
        )

    def small_from(k):
        return mesh_copy(
            small_out.at[me], small_out.at[flipped(me, k, count)], g_send.at[k], g_recv.at[k], flipped(me, k, count)
        )

    for k in range(1, count):
        small(k).start()

    for number in range(LINE):

        @pl.when(number != place)
        def _():
            cross(number).wait_recv()
            line_ref[number] = (
                part_ref[slab(side, number)].astype(F32) + cross_ref[number].astype(F32)
            ).astype(BF)
            along(number).start()

    total = lines_ref[me]
    for k in range(1, count):
        small(k).wait_recv()
        total = total + few_ref[k]
    ranks_ref[rank] = total
    for k in range(1, 4):
        rank_copy(k).start()

    for number in range(LINE):

        @pl.when(number == place)
        def _():
            cross(number).wait_recv()

    beside()
    whole = part_ref[slab(side, place)].astype(F32) + cross_ref[place].astype(F32)
    from_ref[place] = whole.astype(BF)
    for k in range(1, LINE):
        number = lax.rem(place + k, LINE)
        mesh_copy(
            line_ref.at[number], from_ref.at[number], b_send.at[number], b_recv.at[number], mate
        ).wait_recv()
        whole = whole + from_ref[number].astype(F32)
    all_ref[slab(side, place)] = whole.astype(BF)
    over(place).start()
    for number in range(LINE):

        @pl.when(number != place)
        def _():
            spread(number).start()

    for k in range(1, 4):
        rank_from(k).wait_recv()
    small_out[me] = ranks_ref[0] + ranks_ref[1] + ranks_ref[2] + ranks_ref[3]
    for k in range(1, count):
        small_spread(k).start()

    for k in range(1, LINE):
        number = lax.rem(place + k, LINE)
        mesh_copy(
            all_ref.at[slab(side, number)], all_ref.at[slab(side, number)], c_send.at[number], c_recv.at[number], mate
        ).wait_recv()
        over(number).start()
    for k in range(1, count):
        small_from(k).wait_recv()
    for number in range(LINE):
        mesh_copy(
            all_ref.at[slab(1 - side, number)],
            all_ref.at[slab(1 - side, number)],
            d_send.at[number],
            d_recv.at[number],
            mate,
        ).wait_recv()
    gwt_out[...] = all_ref[:rows].astype(F32).T
    gow_out[...] = all_ref[rows:].astype(F32)
    for number in range(LINE):
        cross(number).wait_send()
        over(number).wait_send()

        @pl.when(number != place)
        def _():
            along(number).wait_send()
            spread(number).wait_send()

    for k in range(1, count):
        small(k).wait_send()
        small_spread(k).wait_send()
    for k in range(1, 4):
        rank_copy(k).wait_send()


PARTS = 6


def finish_kernel(
    heads, cap, nv_ref, scal_ref, table0_ref, table1_ref,
    came_ref, slots_ref, hidden_ref, gain2_ref, grad_ref, gain1_ref, router_ref,
    result_in, go_in, away_in, x_in, normed_in, wt_in, ow_in, pw_in, qkvt0_in, mixt0_in, lse0_in, qkvt1_in, mixt1_in, lse1_in,
    out_ref, gin_out, gwt_out, gow_out, small_out, came_go_ref, came_away_ref,
    outs_ref, gorecv_ref, away_ref, x_ref, normed_ref, wt_ref, ow_ref, pw_ref, qkvt0_ref, mixt0_ref, lse0_ref, qkvt1_ref, mixt1_ref, lse1_ref,
    gh_ref, ga_ref, other_ref, moe_ref, gpart_ref, gpair_ref, gown_ref, bias0_ref, bias1_ref, keep_ref, send_ref,
    all_ga_ref, got_ref, gt_ref, d0_ref, d1_ref, npart_ref,
    o_send, o_recv, v_send, v_recv, y_send, y_recv, w_send, w_recv, e_send, e_recv, load_sem, *tail_refs,
):
    count = 2 * LINE
    me = lax.axis_index("expert")
    rank = lax.axis_index("tensor")
    core = flipped(rank, 1, 4)
    away_rank = flipped(rank, 2, 4)
    barrier = pltpu.get_barrier_semaphore()
    for k in range(1, count):
        pl.semaphore_signal(
            barrier, inc=1, device_id={"expert": flipped(me, k, count)}, device_id_type=pl.DeviceIdType.MESH
        )
    for k in range(1, 4):
        pl.semaphore_signal(
            barrier, inc=1, device_id={"tensor": flipped(rank, k, 4)}, device_id_type=pl.DeviceIdType.MESH
        )
    pl.semaphore_wait(barrier, count + 2)

    def rows_of(number):
        return pl.ds(pl.multiple_of(number * cap, cap), cap)

    def result(k):
        return mesh_copy(
            result_in.at[rows_of(flipped(me, k, count))],
            outs_ref.at[rows_of(me)],
            o_send.at[k],
            o_recv.at[k],
            flipped(me, k, count),
        )

    order = list(range(LINE, count)) + list(range(1, LINE))
    for k in order:
        result(k).start()
    own_result = pltpu.make_async_copy(result_in.at[rows_of(me)], outs_ref.at[rows_of(me)], load_sem.at[0])
    own_result.start()
    away_load = pltpu.make_async_copy(away_in, away_ref, load_sem.at[1])
    away_load.start()
    go_away = tensor_copy(go_in.at[1], gorecv_ref, v_send.at[0], v_recv.at[0], core)
    go_away.start()
    go_stay = tensor_copy(go_in.at[0], came_go_ref, v_send.at[1], v_recv.at[1], core)
    places = (
        (normed_in, normed_ref),
        (pw_in, pw_ref),
        (qkvt1_in, qkvt1_ref),
        (mixt1_in, mixt1_ref),
        (lse1_in, lse1_ref),
        (wt_in, wt_ref),
        (ow_in, ow_ref),
        (qkvt0_in, qkvt0_ref),
        (mixt0_in, mixt0_ref),
        (lse0_in, lse0_ref),
        (x_in, x_ref),
    )
    loads = [pltpu.make_async_copy(a, b, load_sem.at[i + 2]) for i, (a, b) in enumerate(places)]
    for load in loads:
        load.start()

    turn_kernel(nv_ref, came_ref, slots_ref, hidden_ref, gain2_ref, grad_ref, gh_ref, ga_ref, moe_ref)
    ga_swap = tensor_copy(ga_ref, other_ref, w_send, w_recv, core)
    ga_swap.start()
    away_load.wait()
    go_away.wait_recv()
    size = away_ref.shape[0] // PARTS

    def lines(i):
        return pl.ds(i * size, size)

    def away(i):
        return tensor_copy(
            away_ref.at[lines(i)], came_away_ref.at[lines(i)], y_send.at[i], y_recv.at[i], away_rank
        )

    for i in range(PARTS):
        away_ref[lines(i)] = (
            away_ref[lines(i)].astype(F32) + gorecv_ref[lines(i)].astype(F32)
        ).astype(BF)
        if i < 2:
            away(i).start()
    ga_swap.wait()
    go_stay.start()
    for load in loads:
        load.wait()
    inner = heads * HD
    attn_bwd_kernel(
        False, heads, scal_ref, table1_ref,
        normed_ref, pw_ref.at[: 3 * inner], pw_ref.at[3 * inner :], qkvt1_ref, mixt1_ref, lse1_ref, ga_ref, other_ref,
        gpart_ref, bias1_ref, npart_ref, all_ga_ref, got_ref, gt_ref, d0_ref, d1_ref,
    )
    pair = tensor_copy(gpart_ref, gpair_ref, e_send, e_recv, away_rank)
    pair.start()
    attn_bwd_kernel(
        True, heads, scal_ref, table0_ref,
        normed_ref, wt_ref, ow_ref, qkvt0_ref, mixt0_ref, lse0_ref, ga_ref, other_ref, npart_ref,
        gown_ref, bias0_ref, keep_ref, send_ref, all_ga_ref, got_ref, gt_ref, d0_ref, d1_ref, npart_ref,
    )

    def pair_done():
        pair.wait_recv()
        for i in range(2, PARTS):
            away(i).start()

    def beside():
        own_result.wait()
        for k in order:
            result(k).wait_recv()
        output_kernel(nv_ref, outs_ref, slots_ref, hidden_ref, out_ref)

    sums(
        pair_done, beside, gown_ref, gpair_ref, keep_ref, send_ref, x_ref, gain1_ref, gh_ref, moe_ref, router_ref,
        bias0_ref, bias1_ref, gwt_out, gow_out, gin_out, small_out, *tail_refs,
    )
    for k in order:
        result(k).wait_send()
    pair.wait_send()
    go_away.wait_send()
    go_stay.wait()
    for i in range(PARTS):
        away(i).wait()


def finish(heads, cap, scalars, arrays, others):
    dma = pltpu.SemaphoreType.DMA
    count = 2 * LINE
    spots = count * cap
    rows = arrays[2].shape[0]
    local = heads * HD
    part = 4 * local // count
    anyspec = pl.BlockSpec(memory_space=pl.ANY)
    half = (rows, D)
    tail_sems = [dma((LINE,))] * 8 + [dma, dma] + [dma((count,))] * 2 + [dma((4,))] * 2 + [dma((count,))] * 2
    shapes = [
        ((spots, D), BF), ((2 * D, D), BF), ((2 * D, D), BF), (half, BF), ((SEQ, D), BF), ((3 * local, D), BF),
        ((local, D), BF), ((4 * local, D), BF), ((3 * local, SEQ), BF), ((local, SEQ), BF), ((8, SEQ), F32),
        ((3 * local, SEQ), BF), ((local, SEQ), BF), ((8, SEQ), F32),
        (half, F32), (half, BF), (half, BF), ((8, D), F32), ((4 * local, D), BF), ((4 * local, D), BF),
        ((4 * local, D), F32), ((8, 128), F32), ((8, 128), F32), (half, F32), (half, BF),
        ((SEQ, D), BF), ((local, SEQ), BF), ((3 * local, SEQ), BF), ((TILE, TILE), F32), ((TILE, TILE), F32), ((SEQ, D), F32),
    ]
    tail_shapes = [
        ((4 * local, D), BF), ((LINE, part, D), BF), ((LINE, part, D), BF), ((LINE, part, D), BF), ((4 * local, D), BF),
        (half, BF), ((count, 8, 128), F32), ((count, 8, 128), F32), ((4, 8, 128), F32),
    ]
    return pl.pallas_call(
        functools.partial(finish_kernel, heads, cap),
        out_shape=[
            jax.ShapeDtypeStruct(half, BF),
            jax.ShapeDtypeStruct(half, BF),
            jax.ShapeDtypeStruct((D, 3 * local), F32),
            jax.ShapeDtypeStruct((local, D), F32),
            jax.ShapeDtypeStruct((count, 8, 128), F32),
            jax.ShapeDtypeStruct((2 * D, D), BF),
            jax.ShapeDtypeStruct((2 * D, D), BF),
        ],
        in_specs=[SM] * len(scalars) + [VM] * len(arrays) + [anyspec] * len(others),
        out_specs=[VM] * 5 + [anyspec] * 2,
        scratch_shapes=[pltpu.VMEM(*v) for v in shapes]
        + [dma((count,)), dma((count,)), dma((2,)), dma((2,)), dma((PARTS,)), dma((PARTS,)), dma, dma, dma, dma, dma((16,))]
        + [pltpu.VMEM(*v) for v in tail_shapes]
        + tail_sems,
        compiler_params=pltpu.CompilerParams(
            collective_id=3, has_side_effects=True, vmem_limit_bytes=62 * MIB
        ),
        cost_estimate=pl.CostEstimate(flops=0, bytes_accessed=200 * MIB, transcendentals=0),
        name="finish",
    )(*scalars, *arrays, *others)


def shards(
    inputs,
    lengths,
    routes,
    attn_gain,
    qkv_weight,
    out_weight,
    rel_bias,
    moe_gain,
    router_weight,
    up_weight,
    down_weight,
    out_grad,
):
    rows = inputs.shape[0]
    rank = lax.axis_index("tensor")
    expert = lax.axis_index("expert")
    heads = rel_bias.shape[1]
    inner = heads * HD
    experts = router_weight.shape[1]
    cap = 4 * rows // experts
    spots = experts * cap
    core = rank % 2
    length = lengths[rank // 2]
    nvalid = jnp.clip(length - core * rows, 0, rows).astype(jnp.int32).reshape(1)
    scal = jnp.stack([core, length]).astype(jnp.int32)

    def swap(x, bit):
        return lax.ppermute(x, "tensor", [(i, i ^ bit) for i in range(4)])

    gain1 = attn_gain.reshape(1, D)
    gain2 = moe_gain.reshape(1, D)
    other = swap(inputs, 1)
    wt = jnp.transpose(qkv_weight.reshape(D, 3 * inner))
    pair_w = swap(jnp.concatenate([wt, out_weight], axis=0), 2)
    pair_table = swap(rel_bias, 2)

    routes_t = jnp.transpose(routes)
    packed_grad, slots = call(
        functools.partial(route_kernel, experts, cap),
        [((spots, D), BF), ((8, rows), F32)],
        (nvalid, routes_t, out_grad),
        [SM, VM, VM],
        flops=2 * spots * rows * D,
        moved=4 * MIB,
        name="route",
    )

    def exchange(x):
        return lax.all_to_all(
            x.reshape(experts, cap, x.shape[-1]), "expert", split_axis=0, concat_axis=0, tiled=True
        ).reshape(x.shape)

    grads_in = exchange(packed_grad)
    up, down = up_weight[0], down_weight[0]
    up, down, pair_w, pair_table = lax.optimization_barrier((up, down, pair_w, pair_table))
    far_up, far_down = swap(up, 2), swap(down, 2)

    attn_cost = dict(
        flops=2 * SEQ * D * 4 * inner + heads * SEQ * SEQ * 160, moved=6 * MIB, exps=heads * SEQ * SEQ
    )
    normed, qkvt0, mixt0, lse0, part0 = call(
        functools.partial(attn_fwd_kernel, True, heads),
        [((SEQ, D), BF), ((3 * inner, SEQ), BF), ((inner, SEQ), BF), ((8, SEQ), F32), ((SEQ, D), F32)],
        (scal, rel_bias, inputs, other, gain1, wt, out_weight),
        [SM, SM] + [VM] * 5,
        name="attend_own",
        **attn_cost,
    )
    wt1, ow1 = pair_w[: 3 * inner], pair_w[3 * inner :]
    qkvt1, mixt1, lse1, keep, send = call(
        functools.partial(attn_fwd_kernel, False, heads),
        [((3 * inner, SEQ), BF), ((inner, SEQ), BF), ((8, SEQ), F32), ((rows, D), F32), ((rows, D), BF)],
        (scal, pair_table, normed, wt1, ow1, part0),
        [SM, SM] + [VM] * 4,
        scratch=[pltpu.VMEM((SEQ, D), F32)],
        name="attend_pair",
        **attn_cost,
    )
    got = swap(send, 1)
    middle_args = (inputs, keep, got, gain2, jnp.transpose(router_weight), routes_t, slots)
    line = experts == 2 * LINE and cap == TILE
    if line:
        hidden, normed_two, info = call(
            functools.partial(middle_line_kernel, experts),
            [((rows, D), F32), ((rows, D), BF), ((8, rows), F32)],
            middle_args,
            moved=6 * MIB,
            name="middle",
        )
        far_up, far_down, info = lax.optimization_barrier((far_up, far_down, info))
        came, result, stay, away, go, grad_router = moe_line(
            experts, cap, normed_two, info, grads_in, router_weight, (up, down, far_up, far_down)
        )
    else:
        mine = jnp.concatenate([up, down], axis=0)
        far = jnp.concatenate([far_up, far_down], axis=0)
        quarters = [mine, far, swap(mine, 1), swap(far, 1)]
        hidden, packed_rows, meta = call(
            functools.partial(middle_kernel, experts, cap),
            [((rows, D), F32), ((spots, D), BF), ((experts, 8, cap), F32)],
            middle_args,
            flops=2 * spots * rows * D,
            moved=8 * MIB,
            name="middle",
        )
        came, result, stay, away, go, grad_router = moe(
            experts, cap, packed_rows, meta, grads_in, router_weight, quarters
        )
    if line:
        outputs, grad_inputs, gwt, gow, small, go_stay, came_away = finish(
            heads,
            cap,
            (nvalid, scal, rel_bias, pair_table),
            (came, slots, hidden, gain2, out_grad, gain1, grad_router),
            (result, go, away, inputs, normed, wt, out_weight, pair_w, qkvt0, mixt0, lse0, qkvt1, mixt1, lse1),
        )
    else:
        came_out = exchange(result)
        came_go = swap(go, 1)
        grad_hidden, grad_attended, moe_part = call(
            turn_kernel,
            [((rows, D), F32), ((rows, D), BF), ((8, D), F32)],
            (nvalid, came, slots, hidden, gain2, out_grad),
            [SM] + [VM] * 5,
            flops=2 * spots * rows * D,
            moved=8 * MIB,
            name="turn",
        )
        other_grad = swap(grad_attended, 1)
        away = (away.astype(F32) + came_go[1].astype(F32)).astype(BF)
        bwd_cost = dict(
            flops=2 * SEQ * D * 10 * inner + heads * SEQ * SEQ * 400, moved=9 * MIB, exps=heads * SEQ * SEQ
        )
        work = [
            pltpu.VMEM((SEQ, D), BF),
            pltpu.VMEM((inner, SEQ), BF),
            pltpu.VMEM((3 * inner, SEQ), BF),
            pltpu.VMEM((TILE, TILE), F32),
            pltpu.VMEM((TILE, TILE), F32),
        ]
        gpart, gbias1, npart = call(
            functools.partial(attn_bwd_kernel, False, heads),
            [((4 * inner, D), BF), ((8, 128), F32), ((SEQ, D), F32)],
            (scal, pair_table, normed, wt1, ow1, qkvt1, mixt1, lse1, grad_attended, other_grad),
            [SM, SM] + [VM] * 8,
            scratch=work,
            name="attend_pair_back",
            **bwd_cost,
        )
        gpair = swap(gpart, 2)
        gown, gbias0, keep_n, send_n = call(
            functools.partial(attn_bwd_kernel, True, heads),
            [((4 * inner, D), F32), ((8, 128), F32), ((rows, D), F32), ((rows, D), BF)],
            (scal, rel_bias, normed, wt, out_weight, qkvt0, mixt0, lse0, grad_attended, other_grad, npart),
            [SM, SM] + [VM] * 9,
            scratch=work + [pltpu.VMEM((SEQ, D), F32)],
            name="attend_own_back",
            **bwd_cost,
        )
        away, gpair, gown = lax.optimization_barrier((away, gpair, gown))
        came_away = swap(away, 2)
        got_n = swap(send_n, 1)
        grad_inputs, attn_part = call(
            last_kernel,
            [((rows, D), BF), ((8, D), F32)],
            (inputs, keep_n, got_n, gain1, grad_hidden),
            moved=6 * MIB,
            name="last",
        )
        wide = (gown + gpair.astype(F32)).astype(BF)
        wide = lax.psum(wide, "expert").astype(F32)
        outputs = call(
            output_kernel,
            [((rows, D), BF)],
            (nvalid, came_out, slots, hidden),
            [SM] + [VM] * 3,
            flops=2 * spots * rows * D,
            moved=8 * MIB,
            name="outputs",
        )[0]
        go_stay = came_go[0]

    if line:
        attn_sum = small[6, :6].reshape(D)
        moe_sum = small[7, :6].reshape(D)
        router_sum = jnp.transpose(small[:6], (0, 2, 1)).reshape(D, experts)
        bias_sum = lax.dynamic_slice(small[6:, 6:].reshape(4, 128), (rank, 0), (1, heads * NB))
    else:
        gwt, gow = jnp.transpose(wide[: 3 * inner]), wide[3 * inner :]
        own_bias = gbias0[:heads, :NB].reshape(1, -1)
        pair_bias = gbias1[:heads, :NB].reshape(1, -1)
        ranks = jnp.arange(4, dtype=jnp.int32)[:, None]
        bias_parts = jnp.where(ranks == rank, own_bias, 0.0) + jnp.where(
            ranks == (rank ^ 2), pair_bias, 0.0
        )
        small = jnp.concatenate(
            [attn_part[0], moe_part[0], jnp.transpose(grad_router).reshape(-1), bias_parts.reshape(-1)]
        )
        small = lax.psum(small, ("expert", "tensor"))
        attn_sum, moe_sum = small[:D], small[D : 2 * D]
        router_sum = small[2 * D : 2 * D + experts * D].reshape(D, experts)
        bias_sum = lax.dynamic_slice(
            small[2 * D + experts * D :].reshape(4, heads * NB), (rank, 0), (1, heads * NB)
        )
    grad_weights = stay.astype(F32) + go_stay.astype(F32) + came_away.astype(F32)
    return (
        outputs,
        grad_inputs,
        attn_sum,
        gwt.reshape(D, 3, inner),
        gow,
        jnp.transpose(bias_sum.reshape(heads, NB)),
        moe_sum,
        router_sum,
        grad_weights[:D][None],
        jnp.transpose(grad_weights[D:])[None],
    )


def solution(mesh):
    return jax.shard_map(
        shards,
        mesh=mesh,
        in_specs=(
            P(("expert", "tensor"), None),
            P("expert"),
            P(("expert", "tensor"), None),
            P(),
            P(None, None, "tensor"),
            P("tensor", None),
            P(None, "tensor"),
            P(),
            P(),
            P("expert", None, "tensor"),
            P("expert", "tensor", None),
            P(("expert", "tensor"), None),
        ),
        out_specs=(
            P(("expert", "tensor"), None),
            P(("expert", "tensor"), None),
            P(),
            P(None, None, "tensor"),
            P("tensor", None),
            P(None, "tensor"),
            P(),
            P(),
            P("expert", None, "tensor"),
            P("expert", "tensor", None),
        ),
        check_vma=False,
    )
```

```python
import functools

import jax
import jax.numpy as jnp
from jax import lax
from jax.experimental import pallas as pl
from jax.experimental.pallas import tpu as pltpu
from jax.sharding import PartitionSpec as P

D = 768
HD = 64
NB = 32
MAXDIST = 128
SEQ = 1024
EPSILON = 1e-06
NEGATIVE = -1e30
TILE = 256
BF = jnp.bfloat16
F32 = jnp.float32
MIB = 2**20
CHUNK = 256
GELU = 0.7978845608028654
CUBIC = 0.044715


def bucket_edges():
    half_count = NB // 2
    short_edges = list(range(1, half_count))
    long_edges = [
        int(half_count * (MAXDIST / half_count) ** (step_index / half_count))
        for step_index in range(half_count)
    ]
    return short_edges + long_edges


EDGES = bucket_edges()


def dot(a, b, ca=1, cb=0, precision=None):
    return lax.dot_general(
        a, b, (((ca,), (cb,)), ((), ())), preferred_element_type=F32, precision=precision
    )


def iota(shape, dim):
    return lax.broadcasted_iota(jnp.int32, shape, dim)


def rms(v):
    return lax.rsqrt(jnp.mean(v * v, axis=-1, keepdims=True) + EPSILON)


def call(kernel, outs, args, specs=None, scratch=(), flops=0, moved=0, exps=0, vmem=56, name=None):
    vm = pl.BlockSpec(memory_space=pltpu.VMEM)
    return pl.pallas_call(
        kernel,
        out_shape=[jax.ShapeDtypeStruct(s, d) for s, d in outs],
        in_specs=specs or [vm] * len(args),
        out_specs=[vm] * len(outs),
        scratch_shapes=list(scratch),
        compiler_params=pltpu.CompilerParams(vmem_limit_bytes=vmem * MIB),
        cost_estimate=pl.CostEstimate(flops=flops, bytes_accessed=moved, transcendentals=exps),
        name=name,
    )(*args)


def own_length(lengths_ref):
    return lengths_ref[lax.axis_index("tensor") // 2]


def own_valid(lengths_ref, rows):
    half = lax.rem(lax.axis_index("tensor"), 2)
    return jnp.clip(own_length(lengths_ref) - half * rows, 0, rows)


VM = pl.BlockSpec(memory_space=pltpu.VMEM)
SM = pl.BlockSpec(memory_space=pltpu.SMEM)


def slot_lines(experts, cap, valid_count, routes):
    rows = routes.shape[1]
    valid = iota((1, rows), 1) < valid_count
    ids = iota((experts, rows), 0)
    hot0 = ((ids == routes[0:1]) & valid).astype(F32)
    hot1 = ((ids == routes[1:2]) & valid).astype(F32)
    before = (iota((rows, rows), 0) < iota((rows, rows), 1)).astype(BF)
    rank = dot((hot0 + hot1).astype(BF), before)
    place = ids.astype(F32) * cap + rank
    bad = jnp.where(valid, 0.0, 1.0)
    slot0 = jnp.sum(hot0 * place, axis=0, keepdims=True) - bad
    slot1 = jnp.sum(hot1 * place, axis=0, keepdims=True) - bad
    return slot0, slot1


def route_kernel(experts, cap, lengths_ref, routes_ref, grad_ref, packed_ref, slots_ref):
    rows = grad_ref.shape[0]
    slot0, slot1 = slot_lines(experts, cap, own_valid(lengths_ref, routes_ref.shape[1]), routes_ref[...])
    spots = iota((experts * cap, rows), 0)
    pick0 = spots == slot0.astype(jnp.int32)
    pick1 = spots == slot1.astype(jnp.int32)
    packed_ref[...] = dot((pick0 | pick1).astype(BF), grad_ref[...]).astype(BF)
    slots_ref[...] = jnp.concatenate([slot0, slot1, jnp.zeros((6, rows), F32)], axis=0)


def slots_kernel(experts, cap, lengths_ref, routes_ref, slots_ref):
    rows = routes_ref.shape[1]
    slot0, slot1 = slot_lines(experts, cap, own_valid(lengths_ref, routes_ref.shape[1]), routes_ref[...])
    slots_ref[...] = jnp.concatenate([slot0, slot1, jnp.zeros((6, rows), F32)], axis=0)


def back_matrix(slots_ref, spots):
    rows = slots_ref.shape[1]
    where = iota((rows, spots), 1)
    slots = slots_ref[...].T.astype(jnp.int32)
    return ((where == slots[:, 0:1]) | (where == slots[:, 1:2])).astype(BF)


def bias_tiles(table_ref, head):
    dist = iota((8, TILE), 1)
    line = table_ref[head : head + 1, :]
    line = line - line[:, NB - 1 :]
    curve = jnp.broadcast_to(line[:, 0:1], (8, TILE))
    for number, edge in enumerate(EDGES):
        curve = jnp.where(dist >= edge, line[:, number + 1 : number + 2], curve)
    spread = jnp.broadcast_to(curve[0:1], (TILE, TILE))
    ring = pltpu.roll(spread, 0, 1, stride=1, stride_axis=0)
    ahead = iota((TILE, TILE), 1) >= iota((TILE, TILE), 0)
    return jnp.where(ahead, ring, NEGATIVE), jnp.where(ahead, 0.0, ring)


def head_pieces(qkvt_ref, mask_rows, head, local_inner):
    start = pl.multiple_of(head * HD, HD)
    q = qkvt_ref[pl.ds(start, HD), :] * jnp.asarray(HD**-0.5, BF)
    k = qkvt_ref[pl.ds(local_inner + start, HD), :]
    v = qkvt_ref[pl.ds(2 * local_inner + start, HD), :]
    ones = jnp.ones((16, SEQ), BF)
    return jnp.concatenate([q, ones], 0), jnp.concatenate([k, mask_rows], 0), v, ones


def mask_block(length):
    keep = (iota((16, SEQ), 1) < length) | (iota((16, SEQ), 0) > 0)
    return jnp.where(keep, 0.0, NEGATIVE).astype(BF)


def score_pieces(k, q, block, near, below):
    cols = slice(block * TILE, (block + 1) * TILE)
    qb = q[:, cols]
    pieces = []
    if block >= 2:
        pieces.append((0, (block - 1) * TILE, dot(k[: (block - 1) * TILE], qb)))
    if block >= 1:
        lo = (block - 1) * TILE
        pieces.append((lo, block * TILE, dot(k[lo : lo + TILE], qb) + below))
    lo = block * TILE
    pieces.append((lo, lo + TILE, dot(k[lo : lo + TILE], qb) + near))
    return cols, pieces


def attn_fwd_kernel(first, heads, lengths_ref, table_ref, *refs):
    if first:
        own_ref, other_ref, gain_ref, w_ref, ow_ref = refs[:5]
        normed_ref, qkvt_ref, mixt_ref, lse_ref, part_ref = refs[5:]
        half = own_ref.shape[0]
        core = lax.rem(lax.axis_index("tensor"), 2)
        for source, place in ((own_ref, core), (other_ref, 1 - core)):
            x = source[...].astype(F32)
            normed_ref[pl.ds(pl.multiple_of(place * half, half), half), :] = (
                x * rms(x) * gain_ref[...]
            ).astype(BF)
    else:
        normed_ref, w_ref, ow_ref, part_in = refs[:4]
        qkvt_ref, mixt_ref, lse_ref, keep_ref, send_ref, part_ref = refs[4:]
    local_inner = heads * HD
    qkvt_ref[...] = dot(w_ref[...], normed_ref[...], 1, 1).astype(BF)
    masks = mask_block(own_length(lengths_ref))
    lse_ref[...] = jnp.zeros_like(lse_ref)

    for head in range(heads):
        near, below = bias_tiles(table_ref, head)
        q, kt, v, ones = head_pieces(qkvt_ref, masks, head, local_inner)
        k = kt.T
        vx = jnp.concatenate([v, ones], 0)
        for block in range(SEQ // TILE):
            cols, pieces = score_pieces(k, q, block, near, below)
            top = functools.reduce(
                jnp.maximum, [jnp.max(s, axis=0, keepdims=True) for _, _, s in pieces]
            )
            total = None
            for lo, hi, s in pieces:
                term = dot(vx[:, lo:hi], jnp.exp(s - top).astype(BF))
                total = term if total is None else total + term
            weight = total[HD : HD + 1]
            mixt_ref[head * HD : (head + 1) * HD, cols] = (total[:HD] / weight).astype(BF)
            lse_ref[head : head + 1, cols] = top + jnp.log(weight)
    part = dot(mixt_ref[...], ow_ref[...], 0, 0)
    if first:
        part_ref[...] = part
    else:
        part_ref[...] = part + part_in[...]
        half = keep_ref.shape[0]
        core = lax.rem(lax.axis_index("tensor"), 2)
        keep_ref[...] = part_ref[pl.ds(pl.multiple_of(core * half, half), half), :]
        send_ref[...] = part_ref[pl.ds(pl.multiple_of((1 - core) * half, half), half), :].astype(BF)


def attn_bwd_kernel(last, heads, lengths_ref, table_ref, *refs):
    if last:
        (normed_ref, w_ref, ow_ref, qkvt_ref, mixt_ref, lse_ref, own_ref, other_ref, part_in) = refs[:9]
        gw_ref, gbias_ref, keep_ref, send_ref, ga_ref, got_ref, gt_ref, d0_ref, d1_ref, part_ref = refs[9:]
    else:
        (normed_ref, w_ref, ow_ref, qkvt_ref, mixt_ref, lse_ref, own_ref, other_ref) = refs[:8]
        gw_ref, gbias_ref, part_ref, ga_ref, got_ref, gt_ref, d0_ref, d1_ref = refs[8:]
    local_inner = heads * HD
    half = own_ref.shape[0]
    core = lax.rem(lax.axis_index("tensor"), 2)
    ga_ref[pl.ds(pl.multiple_of(core * half, half), half), :] = own_ref[...]
    ga_ref[pl.ds(pl.multiple_of((1 - core) * half, half), half), :] = other_ref[...]
    got_ref[...] = dot(ow_ref[...], ga_ref[...], 1, 1).astype(BF)
    gw_ref[3 * local_inner :] = dot(mixt_ref[...], ga_ref[...]).astype(gw_ref.dtype)
    masks = mask_block(own_length(lengths_ref))
    gbias_ref[...] = jnp.zeros_like(gbias_ref)
    ahead = iota((TILE, TILE), 1) >= iota((TILE, TILE), 0)
    spot = (iota((TILE, 128), 0) + 1) % TILE
    flip = (iota((TILE, TILE), 0) + iota((TILE, TILE), 1) == TILE - 1).astype(F32)
    bucket = jnp.zeros((TILE, 128), jnp.int32)
    for edge in EDGES:
        bucket = bucket + (spot >= edge).astype(jnp.int32)
    hot = (bucket == iota((TILE, 128), 1)).astype(F32)

    for head in range(heads):
        near, below = bias_tiles(table_ref, head)
        q, kt, vt, _ = head_pieces(qkvt_ref, masks, head, local_inner)
        k = kt.T
        v = vt.T
        rows = slice(head * HD, (head + 1) * HD)
        gt = got_ref[rows, :]
        delta = jnp.sum(gt.astype(F32) * mixt_ref[rows, :].astype(F32), axis=0, keepdims=True)
        gk = [None] * (SEQ // TILE)
        gv = [None] * (SEQ // TILE)
        far = jnp.zeros((8, TILE), F32)
        for block in range(SEQ // TILE):
            cols, pieces = score_pieces(k, q, block, near, below)
            gb = gt[:, cols]
            qb = q[:HD, cols]
            lse = lse_ref[head : head + 1, cols]
            db = delta[:, cols]
            gq = None
            for lo, hi, s in pieces:
                p = jnp.exp(s - lse)
                ds = p * (dot(v[lo:hi], gb) - db)
                pb = p.astype(BF)
                dsb = ds.astype(BF)
                term = dot(kt[:HD, lo:hi], dsb)
                gq = term if gq is None else gq + term
                tv = dot(pb, gb, 1, 1)
                tk = dot(dsb, qb, 1, 1)
                for tile in range(lo // TILE, hi // TILE):
                    part = slice(tile * TILE - lo, (tile + 1) * TILE - lo)
                    gv[tile] = tv[part] if gv[tile] is None else gv[tile] + tv[part]
                    gk[tile] = tk[part] if gk[tile] is None else gk[tile] + tk[part]
                if hi == (block + 1) * TILE:
                    d0_ref[...] = ds if block == 0 else d0_ref[...] + ds
                elif hi == block * TILE and lo == (block - 1) * TILE:
                    d1_ref[...] = ds if block == 1 else d1_ref[...] + ds
                else:
                    far = far + jnp.sum(ds.reshape((hi - lo) // 8, 8, TILE), axis=0)
            gt_ref[rows, cols] = (gq * HD**-0.5).astype(BF)
        for tile in range(SEQ // TILE):
            cols = slice(tile * TILE, (tile + 1) * TILE)
            gt_ref[local_inner + head * HD : local_inner + (head + 1) * HD, cols] = (
                gk[tile].T.astype(BF)
            )
            gt_ref[2 * local_inner + head * HD : 2 * local_inner + (head + 1) * HD, cols] = (
                gv[tile].T.astype(BF)
            )
        d1 = d1_ref[...]
        ring = jnp.where(ahead, d0_ref[...], d1)
        turned = pltpu.roll(
            dot(flip, ring, 1, 0, lax.Precision.HIGHEST), 0, 1, stride=1, stride_axis=0
        )
        far = far + jnp.sum(jnp.where(ahead, d1, 0.0).reshape(TILE // 8, 8, TILE), axis=0)
        line = jnp.sum(turned, axis=0, keepdims=True)
        sums = dot(
            jnp.broadcast_to(line, (8, TILE)), hot, 1, 0, lax.Precision.HIGHEST
        )
        sums = sums + jnp.where(iota((8, 128), 1) == NB - 1, jnp.sum(far), 0.0)
        gbias_ref[head : head + 1, :] = sums[0:1]
    gw_ref[: 3 * local_inner] = dot(gt_ref[...], normed_ref[...]).astype(gw_ref.dtype)
    part = dot(gt_ref[...], w_ref[...], 0, 0)
    if last:
        part_ref[...] = part + part_in[...]
        keep_ref[...] = part_ref[pl.ds(pl.multiple_of(core * half, half), half), :]
        send_ref[...] = part_ref[pl.ds(pl.multiple_of((1 - core) * half, half), half), :].astype(BF)
    else:
        part_ref[...] = part


def gates_of(experts, normed, router_t, routes):
    rows = normed.shape[0]
    logits = dot(router_t, normed, 1, 1)
    ids = iota((experts, rows), 0)
    signs = (ids == routes[0:1]).astype(F32) - (ids == routes[1:2]).astype(F32)
    gap = jnp.sum(logits * signs, axis=0, keepdims=True)
    return 1.0 / (1.0 + jnp.exp(-gap)), 1.0 / (1.0 + jnp.exp(gap))


def meta_lines(gate, code):
    rows = gate.shape[1]
    line = iota((8, rows), 0)
    high = gate.astype(BF).astype(F32)
    mid = (gate - high).astype(BF).astype(F32)
    low = gate - high - mid
    picked = jnp.where(line == 0, high, jnp.where(line == 1, mid, jnp.where(line == 2, low, 0.0)))
    return jnp.where(line == 3, code, picked).astype(BF)


def hidden_rows(x_ref, keep_ref, got_ref, gain_ref, hidden_ref):
    hidden = x_ref[...].astype(F32) + keep_ref[...] + got_ref[...].astype(F32)
    hidden_ref[...] = hidden
    return (hidden * rms(hidden) * gain_ref[...]).astype(BF)


def middle_kernel(
    experts, cap, x_ref, keep_ref, got_ref, gain_ref, router_ref, routes_ref, slots_ref, hidden_ref, packed_ref, meta_ref
):
    normed = hidden_rows(x_ref, keep_ref, got_ref, gain_ref, hidden_ref)
    slots = slots_ref[...].astype(jnp.int32)
    routes = routes_ref[...]
    where = iota((experts * cap, normed.shape[0]), 0)
    pick0 = where == slots[0:1]
    pick1 = where == slots[1:2]
    packed_ref[...] = dot((pick0 | pick1).astype(BF), normed).astype(BF)
    gate0, gate1 = gates_of(experts, normed, router_ref[...], routes)
    codes = (routes + 1).astype(F32)
    meta = dot(meta_lines(gate0, codes[1:2]), pick0.astype(BF), 1, 1) + dot(
        meta_lines(gate1, codes[0:1]), pick1.astype(BF), 1, 1
    )
    for number in range(experts):
        meta_ref[number] = meta[:, number * cap : (number + 1) * cap]


def middle_line_kernel(
    experts, x_ref, keep_ref, got_ref, gain_ref, router_ref, routes_ref, slots_ref, hidden_ref, normed_ref, info_ref
):
    normed = hidden_rows(x_ref, keep_ref, got_ref, gain_ref, hidden_ref)
    normed_ref[...] = normed
    routes = routes_ref[...]
    gate0, gate1 = gates_of(experts, normed, router_ref[...], routes)
    codes = (routes + 1).astype(F32)
    info_ref[...] = jnp.concatenate(
        [slots_ref[0:2], gate0, gate1, codes, jnp.zeros((2, normed.shape[0]), F32)], axis=0
    )


def gelu_pair(v):
    squared = v * v
    slope = GELU * (1.0 + 3 * CUBIC * squared)
    t = jnp.tanh(v * (GELU + GELU * CUBIC * squared))
    half = 0.5 + 0.5 * t
    return v * half, half + 0.5 * v * (1.0 - t * t) * slope


def flipped(me, k, count):
    total, bit = 0, 1
    while bit < count:
        total = total + lax.rem(me // bit + k // bit, 2) * bit
        bit *= 2
    return total


def weight_grads(xt_ref, geot_ref, act_ref, gi_ref, stage_ref, stay_ref, away_ref, go_ref, out_sem):
    tiles = D // TILE
    steps = 8 * tiles

    def columns(step):
        return pl.ds(pl.multiple_of(lax.rem(step, tiles) * TILE, TILE), TILE)

    def store(step, slot, out_ref):
        half = lax.rem(step, 2 * tiles) // tiles
        return pltpu.make_async_copy(
            stage_ref.at[slot],
            out_ref.at[pl.ds(pl.multiple_of(half * D, D), D), columns(step)],
            out_sem.at[slot],
        )

    def weights(step, carry):
        q = step // (2 * tiles)
        half = lax.rem(step, 2 * tiles) // tiles
        slot = lax.rem(step, 2)

        @pl.when(step >= 2)
        def _():
            store(step - 2, slot, stay_ref).wait()

        @pl.when(half == 0)
        def _():
            stage_ref[slot] = dot(xt_ref[...], gi_ref[q, :, columns(step)]).astype(BF)

        @pl.when(half == 1)
        def _():
            stage_ref[slot] = dot(geot_ref[...], act_ref[q, :, columns(step)]).astype(BF)

        for number, out_ref in enumerate((stay_ref, away_ref, go_ref.at[0], go_ref.at[1])):

            @pl.when(q == number)
            def _():
                store(step, slot, out_ref).start()

        return carry

    lax.fori_loop(0, steps, weights, 0)
    for step in (steps - 2, steps - 1):
        store(step, step % 2, stay_ref).wait()


def expert_rows(x, geo, here, w_ref, xt_ref, geot_ref, act_ref, gi_ref, acc_ref):
    xt_ref[:, here] = x.T
    geot_ref[:, here] = geo.T
    worth = 0.0
    for q in range(4):
        inner = dot(x, w_ref[q, :D])
        grad_active = dot(geo, w_ref[q, D:], 1, 1)
        act, slope = gelu_pair(inner)
        gi = (slope * grad_active).astype(BF)
        act_ref[q, here] = act.astype(BF)
        gi_ref[q, here] = gi
        back = dot(gi, w_ref[q, :D], 1, 1)
        if q == 0:
            acc_ref[...] = back
        else:
            acc_ref[...] += back
        worth = worth + jnp.sum(act * grad_active, axis=1, keepdims=True)
    return worth


def expert_outs(start, size, column, act_ref, w_ref):
    here = pl.ds(pl.multiple_of(start, size), size)
    cols = pl.ds(pl.multiple_of(column * TILE, TILE), TILE)
    total = None
    for q in range(4):
        term = dot(act_ref[q, here], w_ref[q, D:, cols])
        total = term if total is None else total + term
    return cols, total


def expert_kernel(
    count, cap, packed_ref, send_meta_ref, grads_ref, router_ref, w0, w1, w2, w3,
    came_ref, result_ref, stay_ref, away_ref, go_ref, grouter_ref,
    w_ref, x_ref, xt_ref, geot_ref, act_ref, gi_ref, gsend_ref, meta_ref, acc_ref, stage_ref,
    x_send, x_recv, m_send, m_recv, r_send, r_recv, local_sem, w_sem, out_sem,
):
    me = lax.axis_index("expert")
    barrier = pltpu.get_barrier_semaphore()

    def peer(k):
        return flipped(me, k, count)

    source = peer

    def greet(k, carry):
        pl.semaphore_signal(
            barrier, inc=1, device_id={"expert": peer(k)}, device_id_type=pl.DeviceIdType.MESH
        )
        return carry

    lax.fori_loop(1, count, greet, 0)
    pl.semaphore_wait(barrier, count - 1)

    def rows_of(k):
        return pl.ds(pl.multiple_of(k * cap, cap), cap)

    def send_rows(k):
        return pltpu.make_async_remote_copy(
            src_ref=packed_ref.at[rows_of(peer(k))],
            dst_ref=x_ref.at[rows_of(k)],
            send_sem=x_send.at[k],
            recv_sem=x_recv.at[k],
            device_id={"expert": peer(k)},
            device_id_type=pl.DeviceIdType.MESH,
        )

    def send_meta(k):
        return pltpu.make_async_remote_copy(
            src_ref=send_meta_ref.at[peer(k)],
            dst_ref=meta_ref.at[k],
            send_sem=m_send.at[k],
            recv_sem=m_recv.at[k],
            device_id={"expert": peer(k)},
            device_id_type=pl.DeviceIdType.MESH,
        )

    def send_back(k):
        return pltpu.make_async_remote_copy(
            src_ref=gsend_ref.at[rows_of(k)],
            dst_ref=came_ref.at[rows_of(me)],
            send_sem=r_send.at[k],
            recv_sem=r_recv.at[k],
            device_id={"expert": source(k)},
            device_id_type=pl.DeviceIdType.MESH,
        )

    def start_sends(k, carry):
        send_meta(k).start()
        send_rows(k).start()
        return carry

    lax.fori_loop(count // 2, count, start_sends, 0)
    lax.fori_loop(1, count // 2, start_sends, 0)
    own_rows = pltpu.make_async_copy(packed_ref.at[rows_of(me)], x_ref.at[rows_of(0)], local_sem.at[0])
    own_rows.start()
    own_meta = pltpu.make_async_copy(send_meta_ref.at[me], meta_ref.at[0], local_sem.at[1])
    own_meta.start()
    loads = [
        pltpu.make_async_copy(w, w_ref.at[i], w_sem.at[i]) for i, w in enumerate((w0, w1, w2, w3))
    ]
    for load in loads:
        load.start()
    grouter_ref[...] = jnp.zeros_like(grouter_ref)
    experts = router_ref.shape[1]
    own_rows.wait()
    own_meta.wait()
    for load in loads:
        load.wait()
    group = max(1, CHUNK // cap)
    span = group * cap

    def chunk(j, carry):
        for i in range(group):
            k = j * group + i

            @pl.when(k > 0)
            def _():
                send_rows(k).wait_recv()
                send_meta(k).wait_recv()

        here = pl.ds(pl.multiple_of(j * span, span), span)
        meta = jnp.concatenate([meta_ref[j * group + i].T for i in range(group)], axis=0)
        gate = meta[:, 0:1] + meta[:, 1:2] + meta[:, 2:3]
        code = meta[:, 3:4].astype(jnp.int32)
        gy = jnp.concatenate([grads_ref[rows_of(source(j * group + i)), :] for i in range(group)], axis=0)
        geo = (gate * gy.astype(F32)).astype(BF)
        x = x_ref[here, :]
        worth = expert_rows(x, geo, here, w_ref, xt_ref, geot_ref, act_ref, gi_ref, acc_ref)
        ids = iota((span, experts), 1)
        signs = (ids == me).astype(F32) - (ids + 1 == code).astype(F32)
        share = jnp.where(code > 0, (1.0 - gate) * worth, 0.0) * signs
        high = share.astype(BF)
        low = (share - high.astype(F32)).astype(BF)
        gsend_ref[here, :] = (acc_ref[...] + dot(high, router_ref[...], 1, 1)).astype(BF)
        grouter_ref[...] += dot(high.T, x) + dot(low.T, x)
        for i in range(group):
            k = j * group + i

            @pl.when(k > 0)
            def _():
                send_back(k).start()

        return carry

    lax.fori_loop(0, count // group, chunk, 0)
    own_back = pltpu.make_async_copy(gsend_ref.at[rows_of(0)], came_ref.at[rows_of(me)], local_sem.at[0])
    own_back.start()

    def results(step, carry):
        j = step // (D // TILE)
        meta = jnp.concatenate([meta_ref[j * group + i].T for i in range(group)], axis=0)
        gate = meta[:, 0:1] + meta[:, 1:2] + meta[:, 2:3]
        cols, total = expert_outs(j * span, span, lax.rem(step, D // TILE), act_ref, w_ref)
        out = (gate * total).astype(BF)
        for i in range(group):
            result_ref[rows_of(source(j * group + i)), cols] = out[i * cap : (i + 1) * cap]
        return carry

    lax.fori_loop(0, count // group * (D // TILE), results, 0)
    weight_grads(xt_ref, geot_ref, act_ref, gi_ref, stage_ref, stay_ref, away_ref, go_ref, out_sem)
    own_back.wait()

    def finish(k, carry):
        send_rows(k).wait_send()
        send_meta(k).wait_send()
        send_back(k).wait()
        return carry

    lax.fori_loop(1, count, finish, 0)


def mesh_copy(src, dst, send_sem, recv_sem, target):
    return pltpu.make_async_remote_copy(
        src_ref=src,
        dst_ref=dst,
        send_sem=send_sem,
        recv_sem=recv_sem,
        device_id={"expert": target},
        device_id_type=pl.DeviceIdType.MESH,
    )


LINE = 4


def expert_line_kernel(
    cap, normed_ref, info_in, router_ref, grads_in, near_ref, near_info_ref, up_ref, down_ref, far_up_ref, far_half_ref,
    came_ref, result_ref, stay_ref, away_ref, go_ref, grouter_ref,
    grads_ref, w_ref, block_ref, info_ref, x_ref, xs_ref, meta_ref, ms_ref, xt_ref, geot_ref, act_ref, gi_ref, acc_ref, stage_ref,
    b_send, b_recv, i_send, i_recv, x_send, x_recv, m_send, m_recv, r_send, r_recv, local_sem, w_sem, v_send, v_recv, y_send, y_recv, grads_sem, near_sem, out_sem,
):
    count = 2 * LINE
    me = lax.axis_index("expert")
    place = me // 2
    side = me - 2 * place
    mate = me + 1 - 2 * side
    barrier = pltpu.get_barrier_semaphore()

    def greet(k, carry):
        pl.semaphore_signal(
            barrier,
            inc=1,
            device_id={"expert": lax.rem(me + k, count)},
            device_id_type=pl.DeviceIdType.MESH,
        )
        return carry

    lax.fori_loop(1, count, greet, 0)
    core = flipped(lax.axis_index("tensor"), 1, 4)
    pl.semaphore_signal(
        barrier, inc=1, device_id={"tensor": core}, device_id_type=pl.DeviceIdType.MESH
    )
    away = flipped(lax.axis_index("tensor"), 2, 4)
    pl.semaphore_signal(
        barrier, inc=1, device_id={"tensor": away}, device_id_type=pl.DeviceIdType.MESH
    )
    pl.semaphore_wait(barrier, count + 1)

    def along(block, step):
        return (
            mesh_copy(
                info_ref.at[block],
                info_ref.at[block],
                i_send.at[(step + 1) // 2, block],
                i_recv.at[block],
                me + 2 * step,
            ),
            mesh_copy(
                block_ref.at[block],
                block_ref.at[block],
                b_send.at[(step + 1) // 2, block],
                b_recv.at[block],
                me + 2 * step,
            ),
        )

    def across(block):
        return (
            mesh_copy(ms_ref.at[block], meta_ref.at[1, block], m_send.at[block], m_recv.at[block], mate),
            mesh_copy(xs_ref.at[block], x_ref.at[1, block], x_send.at[block], x_recv.at[block], mate),
        )

    def rows_of(number):
        return pl.ds(pl.multiple_of(number * cap, cap), cap)

    def origin(part, block):
        return 2 * block + side + part * (1 - 2 * side)

    def give_back(part, block):
        return mesh_copy(
            x_ref.at[part, block],
            came_ref.at[rows_of(me)],
            r_send.at[part, block],
            r_recv.at[me],
            origin(part, block),
        )

    def each(pair, act):
        for one in pair:
            act(one)

    own = (
        pltpu.make_async_copy(info_in, info_ref.at[place], local_sem.at[0]),
        pltpu.make_async_copy(normed_ref, block_ref.at[place], local_sem.at[1]),
    )
    each(own, lambda c: c.start())
    rest = D // 2
    far_down = tensor_copy(down_ref.at[rest:], w_ref.at[1, D + rest :], y_send, y_recv, away)
    far_down.start()
    grads_load = pltpu.make_async_copy(grads_in, grads_ref, grads_sem)
    grads_load.start()
    near = [
        (
            pltpu.make_async_copy(near_info_ref.at[i], info_ref.at[place + 2 * i - 1], near_sem.at[i]),
            pltpu.make_async_copy(near_ref.at[i], block_ref.at[place + 2 * i - 1], near_sem.at[i + 2]),
        )
        for i in range(2)
    ]
    inside = [place > 0, place < LINE - 1]
    for i in range(2):

        @pl.when(inside[i])
        def _():
            each(near[i], lambda c: c.start())

    weights = (
        (up_ref, 0, 0, D), (down_ref, 0, D, D), (far_up_ref, 1, 0, D), (far_half_ref, 1, D, rest),
        (w_ref.at[1, D + rest :], 1, D + rest, rest),
    )

    def load(i):
        source, q, start, size = weights[i]
        return pltpu.make_async_copy(source, w_ref.at[q, start : start + size], w_sem.at[i])

    def lend(i):
        source, q, start, size = weights[i]
        return tensor_copy(source, w_ref.at[2 + q, start : start + size], v_send.at[i], v_recv.at[i], core)

    for i in range(2):

        @pl.when(inside[i])
        def _():
            each(near[i], lambda c: c.wait())

            @pl.when(inside[1 - i])
            def _():
                each(along(place + 2 * i - 1, 1 - 2 * i), lambda c: c.start())

    for i in range(4):
        load(i).start()
        lend(i).start()
    each(own, lambda c: c.wait())
    experts = router_ref.shape[0]
    rows = normed_ref.shape[0]

    def select(block):
        info = info_ref[block]
        slots = info[0:2].astype(jnp.int32)
        lines0 = meta_lines(info[2:3], info[5:6])
        lines1 = meta_lines(info[3:4], info[4:5])
        for part, expert in ((1, mate), (0, me)):
            where = iota((cap, rows), 0) + expert * cap
            pick0 = where == slots[0:1]
            pick1 = where == slots[1:2]
            taken = dot((pick0 | pick1).astype(BF), block_ref[block]).astype(BF)
            meta = dot(lines0, pick0.astype(BF), 1, 1) + dot(lines1, pick1.astype(BF), 1, 1)
            if part:
                xs_ref[block] = taken
                ms_ref[block] = meta
                each(across(block), lambda c: c.start())
            else:
                x_ref[0, block] = taken
                meta_ref[0, block] = meta

    select(place)
    grouter_ref[...] = jnp.zeros_like(grouter_ref)
    mirror = place // 2
    inward = place + mirror * (LINE - 1 - 2 * place)

    def block_at(i):
        step = i + inward * (1 - i // 2 - 2 * (i // 2 - i // (LINE - 1)))
        return step + mirror * (LINE - 1 - 2 * step)

    def chunk_at(c):
        part = lax.rem(c + 1, 2) - (7 - c) // 7 + c // 7
        return part, block_at((c + 1) // 2 - part * ((c + 1) // 2 - (c - 1) // 2))

    for i in range(2):

        @pl.when(inside[i])
        def _():
            select(place + 2 * i - 1)

    grads_load.wait()
    for i in range(4):
        load(i).wait()
        lend(i).wait_recv()
    far_down.wait_recv()
    lend(4).start()
    lend(4).wait_recv()

    def chunk(c, carry):
        for distance in range(2, LINE):

            @pl.when(c == 4 * distance - 7)
            def _():
                line_accept(place, distance, along, select)

        part, block = chunk_at(c)

        @pl.when(part == 1)
        def _():
            each(across(block), lambda c: c.wait_recv())

        here = pl.ds(pl.multiple_of(c * cap, cap), cap)
        meta = meta_ref[part, block].T
        gate = meta[:, 0:1] + meta[:, 1:2] + meta[:, 2:3]
        code = meta[:, 3:4].astype(jnp.int32)
        geo = (gate * grads_ref[part, block].astype(F32)).astype(BF)
        x = x_ref[part, block]
        worth = expert_rows(x, geo, here, w_ref, xt_ref, geot_ref, act_ref, gi_ref, acc_ref)
        ids = iota((cap, experts), 1)
        signs = (ids == me).astype(F32) - (ids + 1 == code).astype(F32)
        share = jnp.where(code > 0, (1.0 - gate) * worth, 0.0) * signs
        high = share.astype(BF)
        low = (share - high.astype(F32)).astype(BF)
        grouter_ref[...] += dot(high.T, x) + dot(low.T, x)
        x_ref[part, block] = (acc_ref[...] + dot(high, router_ref[...])).astype(BF)

        @pl.when(origin(part, block) != me)
        def _():
            give_back(part, block).start()

        return carry

    lax.fori_loop(0, count, chunk, 0)
    own_back = pltpu.make_async_copy(x_ref.at[0, place], came_ref.at[rows_of(me)], local_sem.at[0])
    own_back.start()

    def results(step, carry):
        first = step // (D // TILE) * LINE
        cols, total = expert_outs(first * cap, LINE * cap, lax.rem(step, D // TILE), act_ref, w_ref)
        for i in range(LINE):
            part, block = chunk_at(first + i)
            meta = meta_ref[part, block].T
            gate = meta[:, 0:1] + meta[:, 1:2] + meta[:, 2:3]
            result_ref[rows_of(origin(part, block)), cols] = (
                gate * total[i * cap : (i + 1) * cap]
            ).astype(BF)
        return carry

    lax.fori_loop(0, 2 * (D // TILE), results, 0)
    weight_grads(xt_ref, geot_ref, act_ref, gi_ref, stage_ref, stay_ref, away_ref, go_ref, out_sem)
    own_back.wait()
    for i in range(5):
        lend(i).wait_send()
    far_down.wait_send()
    line_sent(place, along, 1)
    for block in range(LINE):
        each(across(block), lambda c: c.wait_send())
        for part in (0, 1):

            @pl.when(origin(part, block) != me)
            def _():
                give_back(part, block).wait_send()

    for number in range(count):

        @pl.when(number != me)
        def _():
            mesh_copy(
                x_ref.at[0, 0], came_ref.at[rows_of(number)], r_send.at[0, 0], r_recv.at[number], mate
            ).wait_recv()


def turn_kernel(lengths_ref, came_ref, slots_ref, hidden_ref, gain_ref, grad_ref, gh_ref, ga_ref, gain_out):
    gn = dot(back_matrix(slots_ref, came_ref.shape[0]), came_ref[...])
    hidden = hidden_ref[...]
    scale = rms(hidden)
    unit = hidden * scale
    gain_out[...] = jnp.broadcast_to(jnp.sum(gn * unit, axis=0, keepdims=True), gain_out.shape)
    g = gn * gain_ref[...]
    valid = (iota((hidden.shape[0], 1), 0) < own_valid(lengths_ref, hidden.shape[0])).astype(F32)
    gh = scale * (g - unit * jnp.mean(g * unit, axis=1, keepdims=True)) + valid * grad_ref[...].astype(F32)
    gh_ref[...] = gh
    ga_ref[...] = gh.astype(BF)


def output_kernel(lengths_ref, came_ref, slots_ref, hidden_ref, out_ref):
    mix = dot(back_matrix(slots_ref, came_ref.shape[0]), came_ref[...])
    hidden = hidden_ref[...]
    valid = (iota((hidden.shape[0], 1), 0) < own_valid(lengths_ref, hidden.shape[0])).astype(F32)
    out_ref[...] = (valid * (hidden + mix)).astype(BF)


def last_kernel(x_ref, keep_ref, got_ref, gain_ref, gh_ref, out_ref, gain_out):
    x = x_ref[...].astype(F32)
    scale = rms(x)
    unit = x * scale
    gn = keep_ref[...] + got_ref[...].astype(F32)
    gain_out[...] = jnp.broadcast_to(jnp.sum(gn * unit, axis=0, keepdims=True), gain_out.shape)
    g = gn * gain_ref[...]
    out_ref[...] = (
        gh_ref[...] + scale * (g - unit * jnp.mean(g * unit, axis=1, keepdims=True))
    ).astype(BF)


def moe(experts, cap, packed, meta, grads, router, quarters):
    spots = experts * cap
    anyspec = pl.BlockSpec(memory_space=pl.ANY)
    dma = pltpu.SemaphoreType.DMA
    return pl.pallas_call(
        functools.partial(expert_kernel, experts, cap),
        out_shape=[
            jax.ShapeDtypeStruct((spots, D), BF),
            jax.ShapeDtypeStruct((spots, D), BF),
            jax.ShapeDtypeStruct((2 * D, D), BF),
            jax.ShapeDtypeStruct((2 * D, D), BF),
            jax.ShapeDtypeStruct((2, 2 * D, D), BF),
            jax.ShapeDtypeStruct((experts, D), F32),
        ],
        in_specs=[anyspec, VM, VM, VM] + [anyspec] * 4,
        out_specs=[anyspec, VM, anyspec, anyspec, anyspec, VM],
        scratch_shapes=[
            pltpu.VMEM((4, 2 * D, D), BF),
            pltpu.VMEM((spots, D), BF),
            pltpu.VMEM((D, spots), BF),
            pltpu.VMEM((D, spots), BF),
            pltpu.VMEM((4, spots, D), BF),
            pltpu.VMEM((4, spots, D), BF),
            pltpu.VMEM((spots, D), BF),
            pltpu.VMEM((experts, 8, cap), F32),
            pltpu.VMEM((CHUNK, D), F32),
            pltpu.VMEM((2, D, TILE), BF),
            dma((experts,)),
            dma((experts,)),
            dma((experts,)),
            dma((experts,)),
            dma((experts,)),
            dma((experts,)),
            dma((2,)),
            dma((4,)),
            dma((2,)),
        ],
        compiler_params=pltpu.CompilerParams(
            collective_id=1, has_side_effects=True, vmem_limit_bytes=60 * MIB
        ),
        cost_estimate=pl.CostEstimate(flops=12 * spots * D * 4 * D, bytes_accessed=60 * MIB, transcendentals=0),
        name="experts",
    )(packed, meta, grads, router, *quarters)


def moe_line(experts, cap, normed, info, router, others):
    rows = normed.shape[0]
    spots = experts * cap
    anyspec = pl.BlockSpec(memory_space=pl.ANY)
    dma = pltpu.SemaphoreType.DMA
    return pl.pallas_call(
        functools.partial(expert_line_kernel, cap),
        out_shape=[
            jax.ShapeDtypeStruct((spots, D), BF),
            jax.ShapeDtypeStruct((spots, D), BF),
            jax.ShapeDtypeStruct((2 * D, D), BF),
            jax.ShapeDtypeStruct((2 * D, D), BF),
            jax.ShapeDtypeStruct((2, 2 * D, D), BF),
            jax.ShapeDtypeStruct((experts, D), F32),
        ],
        in_specs=[VM, VM, VM] + [anyspec] * 7,
        out_specs=[anyspec, VM, anyspec, anyspec, anyspec, VM],
        scratch_shapes=[
            pltpu.VMEM((2, LINE, cap, D), BF),
            pltpu.VMEM((4, 2 * D, D), BF),
            pltpu.VMEM((LINE, rows, D), BF),
            pltpu.VMEM((LINE, 8, rows), F32),
            pltpu.VMEM((2, LINE, cap, D), BF),
            pltpu.VMEM((LINE, cap, D), BF),
            pltpu.VMEM((2, LINE, 8, cap), F32),
            pltpu.VMEM((LINE, 8, cap), F32),
            pltpu.VMEM((D, spots), BF),
            pltpu.VMEM((D, spots), BF),
            pltpu.VMEM((4, spots, D), BF),
            pltpu.VMEM((4, spots, D), BF),
            pltpu.VMEM((cap, D), F32),
            pltpu.VMEM((2, D, TILE), BF),
            dma((2, LINE)),
            dma((LINE,)),
            dma((2, LINE)),
            dma((LINE,)),
            dma((LINE,)),
            dma((LINE,)),
            dma((LINE,)),
            dma((LINE,)),
            dma((2, LINE)),
            dma((experts,)),
            dma((2,)),
            dma((4,)),
            dma((5,)),
            dma((5,)),
            dma,
            dma,
            dma,
            dma((4,)),
            dma((2,)),
        ],
        compiler_params=pltpu.CompilerParams(
            collective_id=2, has_side_effects=True, vmem_limit_bytes=62 * MIB
        ),
        cost_estimate=pl.CostEstimate(flops=12 * spots * D * 4 * D, bytes_accessed=60 * MIB, transcendentals=0),
        name="experts_line",
    )(normed, info, router, *others)


def tensor_copy(src, dst, send_sem, recv_sem, target):
    return pltpu.make_async_remote_copy(
        src_ref=src,
        dst_ref=dst,
        send_sem=send_sem,
        recv_sem=recv_sem,
        device_id={"tensor": target},
        device_id_type=pl.DeviceIdType.MESH,
    )


def sums(
    pair_done, beside, gw_ref, pair_ref, keep_ref, send_ref, x_in, gain_ref, gh_ref, moe_ref, router_ref, bias0_ref, bias1_ref,
    gwt_out, gow_out, gin_out, attn_out, moe_out, router_out, bias_out,
    small_out, part_ref, cross_ref, line_ref, from_ref, all_ref, got_ref, lines_ref, few_ref, ranks_ref,
    a_send, a_recv, b_send, b_recv, c_send, c_recv, d_send, d_recv, s_send, s_recv, f_send, f_recv, t_send, t_recv, g_send, g_recv,
):
    count = 2 * LINE
    me = lax.axis_index("expert")
    rank = lax.axis_index("tensor")
    place = me // 2
    side = me - 2 * place
    mate = me + 1 - 2 * side
    size = part_ref.shape[0] // count
    def slab(which, number):
        return pl.ds(pl.multiple_of((which * LINE + number) * size, size), size)

    swap = tensor_copy(send_ref, got_ref, s_send, s_recv, flipped(rank, 1, 4))
    swap.start()
    pair_done()
    part_ref[...] = (gw_ref[...] + pair_ref[...].astype(F32)).astype(BF)
    rows = gwt_out.shape[0]

    def cross(number):
        return mesh_copy(
            part_ref.at[slab(1 - side, number)], cross_ref.at[number], a_send.at[number], a_recv.at[number], mate
        )

    def along(number):
        return mesh_copy(
            line_ref.at[number], from_ref.at[place], b_send.at[number], b_recv.at[place], 2 * number + side
        )

    def spread(number):
        return mesh_copy(
            all_ref.at[slab(side, place)],
            all_ref.at[slab(side, place)],
            c_send.at[number],
            c_recv.at[place],
            2 * number + side,
        )

    def over(number):
        return mesh_copy(
            all_ref.at[slab(side, number)], all_ref.at[slab(side, number)], d_send.at[number], d_recv.at[number], mate
        )

    for number in range(LINE):
        cross(number).start()

    swap.wait()
    x = x_in[...].astype(F32)
    scale = rms(x)
    unit = x * scale
    gn = keep_ref[...] + got_ref[...].astype(F32)
    attn = jnp.sum(gn * unit, axis=0, keepdims=True)
    g = gn * gain_ref[...]
    gin_out[...] = (gh_ref[...] + scale * (g - unit * jnp.mean(g * unit, axis=1, keepdims=True))).astype(BF)

    heads = gow_out.shape[0] // HD
    blank = jnp.zeros((1, 128), F32)

    def flat(bias_ref):
        line = [bias_ref[h : h + 1, :NB] for h in range(heads)]
        return jnp.concatenate(line + [jnp.zeros((1, 128 - heads * NB), F32)], axis=1)

    own_bias, pair_bias = flat(bias0_ref), flat(bias1_ref)
    other = flipped(rank, 2, 4)
    for j in range(D // 128):
        lines_ref[j] = router_ref[:, j * 128 : (j + 1) * 128]
    for j, row in ((6, attn), (7, moe_ref[0:1])):
        places = [2 * (j - 6), 2 * (j - 6) + 1]
        bias = [
            jnp.where(rank == p, own_bias, blank) + jnp.where(other == p, pair_bias, blank) for p in places
        ]
        lines_ref[j] = jnp.concatenate([row[:, i * 128 : (i + 1) * 128] for i in range(6)] + bias, axis=0)

    def small(k):
        return mesh_copy(
            lines_ref.at[flipped(me, k, count)], few_ref.at[k], f_send.at[k], f_recv.at[k], flipped(me, k, count)
        )

    def rank_copy(k):
        return tensor_copy(
            ranks_ref.at[rank], ranks_ref.at[rank], t_send.at[k], t_recv.at[k], flipped(rank, k, 4)
        )

    def rank_from(k):
        return tensor_copy(
            ranks_ref.at[rank], ranks_ref.at[flipped(rank, k, 4)], t_send.at[k], t_recv.at[k], flipped(rank, k, 4)
        )

    def small_spread(k):
        return mesh_copy(
            small_out.at[me], small_out.at[me], g_send.at[k], g_recv.at[k], flipped(me, k, count)
        )

    def small_from(k):
        return mesh_copy(
            small_out.at[me], small_out.at[flipped(me, k, count)], g_send.at[k], g_recv.at[k], flipped(me, k, count)
        )

    for k in range(1, count):
        small(k).start()

    for number in range(LINE):

        @pl.when(number != place)
        def _():
            cross(number).wait_recv()
            line_ref[number] = (
                part_ref[slab(side, number)].astype(F32) + cross_ref[number].astype(F32)
            ).astype(BF)
            along(number).start()

    total = lines_ref[me]
    for k in range(1, count):
        small(k).wait_recv()
        total = total + few_ref[k]
    ranks_ref[rank] = total
    for k in range(1, 4):
        rank_copy(k).start()

    for number in range(LINE):

        @pl.when(number == place)
        def _():
            cross(number).wait_recv()

    beside()
    whole = part_ref[slab(side, place)].astype(F32) + cross_ref[place].astype(F32)
    from_ref[place] = whole.astype(BF)
    for k in range(1, LINE):
        number = lax.rem(place + k, LINE)
        mesh_copy(
            line_ref.at[number], from_ref.at[number], b_send.at[number], b_recv.at[number], mate
        ).wait_recv()
        whole = whole + from_ref[number].astype(F32)
    all_ref[slab(side, place)] = whole.astype(BF)
    over(place).start()
    for number in range(LINE):

        @pl.when(number != place)
        def _():
            spread(number).start()

    for k in range(1, 4):
        rank_from(k).wait_recv()
    small_out[me] = ranks_ref[0] + ranks_ref[1] + ranks_ref[2] + ranks_ref[3]
    for k in range(1, count):
        small_spread(k).start()

    for k in range(1, LINE):
        number = lax.rem(place + k, LINE)
        mesh_copy(
            all_ref.at[slab(side, number)], all_ref.at[slab(side, number)], c_send.at[number], c_recv.at[number], mate
        ).wait_recv()
        over(number).start()
    for k in range(1, count):
        small_from(k).wait_recv()
    for number in range(LINE):
        mesh_copy(
            all_ref.at[slab(1 - side, number)],
            all_ref.at[slab(1 - side, number)],
            d_send.at[number],
            d_recv.at[number],
            mate,
        ).wait_recv()
    attn_out[...] = jnp.concatenate([small_out[6, i : i + 1] for i in range(6)], axis=1)
    moe_out[...] = jnp.concatenate([small_out[7, i : i + 1] for i in range(6)], axis=1)
    router_out[...] = jnp.concatenate([small_out[j] for j in range(D // 128)], axis=1)
    bias = functools.reduce(
        jnp.add,
        [jnp.where(rank == p, small_out[6 + p // 2, 6 + p % 2 : 7 + p % 2], blank) for p in range(4)],
    )
    bias_out[...] = jnp.concatenate([bias[:, h * NB : (h + 1) * NB] for h in range(heads)], axis=0)
    gwt_out[...] = all_ref[:rows].astype(F32)
    gow_out[...] = all_ref[rows:].astype(F32)
    for number in range(LINE):
        cross(number).wait_send()
        over(number).wait_send()

        @pl.when(number != place)
        def _():
            along(number).wait_send()
            spread(number).wait_send()

    for k in range(1, count):
        small(k).wait_send()
        small_spread(k).wait_send()
    for k in range(1, 4):
        rank_copy(k).wait_send()


PARTS = 6


def finish_kernel(
    heads, cap, lengths_ref,
    table0_ref, table1_ref, came_ref, slots_ref, hidden_ref, gain2_ref, grad_ref, gain1_ref, router_ref,
    result_in, go_in, away_in, x_in, normed_in, wt_in, ow_in, pw_in, qkvt0_in, mixt0_in, lse0_in, qkvt1_in, mixt1_in, lse1_in,
    out_ref, gin_out, gwt_out, gow_out, attn_out, moe_out, router_out, bias_out, came_go_ref, came_away_ref,
    outs_ref, gorecv_ref, away_ref, x_ref, normed_ref, wt_ref, ow_ref, pw_ref, qkvt0_ref, mixt0_ref, lse0_ref, qkvt1_ref, mixt1_ref, lse1_ref,
    gh_ref, ga_ref, other_ref, moe_ref, gpart_ref, gpair_ref, gown_ref, bias0_ref, bias1_ref, keep_ref, send_ref,
    all_ga_ref, got_ref, gt_ref, d0_ref, d1_ref, npart_ref,
    o_send, o_recv, v_send, v_recv, y_send, y_recv, w_send, w_recv, e_send, e_recv, load_sem, *tail_refs,
):
    count = 2 * LINE
    me = lax.axis_index("expert")
    rank = lax.axis_index("tensor")
    core = flipped(rank, 1, 4)
    away_rank = flipped(rank, 2, 4)
    barrier = pltpu.get_barrier_semaphore()
    for k in range(1, count):
        pl.semaphore_signal(
            barrier, inc=1, device_id={"expert": flipped(me, k, count)}, device_id_type=pl.DeviceIdType.MESH
        )
    for k in range(1, 4):
        pl.semaphore_signal(
            barrier, inc=1, device_id={"tensor": flipped(rank, k, 4)}, device_id_type=pl.DeviceIdType.MESH
        )
    pl.semaphore_wait(barrier, count + 2)

    def rows_of(number):
        return pl.ds(pl.multiple_of(number * cap, cap), cap)

    def result(k):
        return mesh_copy(
            result_in.at[rows_of(flipped(me, k, count))],
            outs_ref.at[rows_of(me)],
            o_send.at[k],
            o_recv.at[k],
            flipped(me, k, count),
        )

    order = list(range(LINE, count)) + list(range(1, LINE))
    for k in order:
        result(k).start()
    own_result = pltpu.make_async_copy(result_in.at[rows_of(me)], outs_ref.at[rows_of(me)], load_sem.at[0])
    own_result.start()
    away_load = pltpu.make_async_copy(away_in, away_ref, load_sem.at[1])
    away_load.start()
    go_away = tensor_copy(go_in.at[1], gorecv_ref, v_send.at[0], v_recv.at[0], core)
    go_away.start()
    go_stay = tensor_copy(go_in.at[0], came_go_ref, v_send.at[1], v_recv.at[1], core)
    places = (
        (normed_in, normed_ref),
        (pw_in, pw_ref),
        (qkvt1_in, qkvt1_ref),
        (mixt1_in, mixt1_ref),
        (lse1_in, lse1_ref),
        (wt_in, wt_ref),
        (ow_in, ow_ref),
        (qkvt0_in, qkvt0_ref),
        (mixt0_in, mixt0_ref),
        (lse0_in, lse0_ref),
        (x_in, x_ref),
    )
    loads = [pltpu.make_async_copy(a, b, load_sem.at[i + 2]) for i, (a, b) in enumerate(places)]
    for load in loads:
        load.start()

    turn_kernel(lengths_ref, came_ref, slots_ref, hidden_ref, gain2_ref, grad_ref, gh_ref, ga_ref, moe_ref)
    ga_swap = tensor_copy(ga_ref, other_ref, w_send, w_recv, core)
    ga_swap.start()
    away_load.wait()
    go_away.wait_recv()
    size = away_ref.shape[0] // PARTS

    def lines(i):
        return pl.ds(i * size, size)

    def away(i):
        return tensor_copy(
            away_ref.at[lines(i)], came_away_ref.at[lines(i)], y_send.at[i], y_recv.at[i], away_rank
        )

    for i in range(PARTS):
        away_ref[lines(i)] = (
            away_ref[lines(i)].astype(F32) + gorecv_ref[lines(i)].astype(F32)
        ).astype(BF)
        if i < 2:
            away(i).start()
    ga_swap.wait()
    go_stay.start()
    for load in loads:
        load.wait()
    inner = heads * HD
    attn_bwd_kernel(
        False, heads, lengths_ref, table1_ref,
        normed_ref, pw_ref.at[: 3 * inner], pw_ref.at[3 * inner :], qkvt1_ref, mixt1_ref, lse1_ref, ga_ref, other_ref,
        gpart_ref, bias1_ref, npart_ref, all_ga_ref, got_ref, gt_ref, d0_ref, d1_ref,
    )
    pair = tensor_copy(gpart_ref, gpair_ref, e_send, e_recv, away_rank)
    pair.start()
    attn_bwd_kernel(
        True, heads, lengths_ref, table0_ref,
        normed_ref, wt_ref, ow_ref, qkvt0_ref, mixt0_ref, lse0_ref, ga_ref, other_ref, npart_ref,
        gown_ref, bias0_ref, keep_ref, send_ref, all_ga_ref, got_ref, gt_ref, d0_ref, d1_ref, npart_ref,
    )

    def pair_done():
        pair.wait_recv()
        for i in range(2, PARTS):
            away(i).start()

    def beside():
        own_result.wait()
        for k in order:
            result(k).wait_recv()
        output_kernel(lengths_ref, outs_ref, slots_ref, hidden_ref, out_ref)

    sums(
        pair_done, beside, gown_ref, gpair_ref, keep_ref, send_ref, x_ref, gain1_ref, gh_ref, moe_ref, router_ref,
        bias0_ref, bias1_ref, gwt_out, gow_out, gin_out, attn_out, moe_out, router_out, bias_out, *tail_refs,
    )
    for k in order:
        result(k).wait_send()
    pair.wait_send()
    go_away.wait_send()
    go_stay.wait()
    for i in range(PARTS):
        away(i).wait()


def finish(heads, cap, scalars, arrays, others):
    dma = pltpu.SemaphoreType.DMA
    count = 2 * LINE
    spots = count * cap
    rows = arrays[4].shape[0]
    local = heads * HD
    part = 4 * local // count
    anyspec = pl.BlockSpec(memory_space=pl.ANY)
    half = (rows, D)
    tail_sems = [dma((LINE,))] * 8 + [dma, dma] + [dma((count,))] * 2 + [dma((4,))] * 2 + [dma((count,))] * 2
    shapes = [
        ((spots, D), BF), ((2 * D, D), BF), ((2 * D, D), BF), (half, BF), ((SEQ, D), BF), ((3 * local, D), BF),
        ((local, D), BF), ((4 * local, D), BF), ((3 * local, SEQ), BF), ((local, SEQ), BF), ((8, SEQ), F32),
        ((3 * local, SEQ), BF), ((local, SEQ), BF), ((8, SEQ), F32),
        (half, F32), (half, BF), (half, BF), ((8, D), F32), ((4 * local, D), BF), ((4 * local, D), BF),
        ((4 * local, D), F32), ((8, 128), F32), ((8, 128), F32), (half, F32), (half, BF),
        ((SEQ, D), BF), ((local, SEQ), BF), ((3 * local, SEQ), BF), ((TILE, TILE), F32), ((TILE, TILE), F32), ((SEQ, D), F32),
    ]
    tail_shapes = [
        ((count, 8, 128), F32),
        ((4 * local, D), BF), ((LINE, part, D), BF), ((LINE, part, D), BF), ((LINE, part, D), BF), ((4 * local, D), BF),
        (half, BF), ((count, 8, 128), F32), ((count, 8, 128), F32), ((4, 8, 128), F32),
    ]
    return pl.pallas_call(
        functools.partial(finish_kernel, heads, cap),
        out_shape=[
            jax.ShapeDtypeStruct(half, BF),
            jax.ShapeDtypeStruct(half, BF),
            jax.ShapeDtypeStruct((3 * local, D), F32),
            jax.ShapeDtypeStruct((local, D), F32),
            jax.ShapeDtypeStruct((1, D), F32),
            jax.ShapeDtypeStruct((1, D), F32),
            jax.ShapeDtypeStruct((count, D), F32),
            jax.ShapeDtypeStruct((heads, NB), F32),
            jax.ShapeDtypeStruct((2 * D, D), BF),
            jax.ShapeDtypeStruct((2 * D, D), BF),
        ],
        in_specs=[SM] * len(scalars) + [VM] * len(arrays) + [anyspec] * len(others),
        out_specs=[VM] * 8 + [anyspec] * 2,
        scratch_shapes=[pltpu.VMEM(*v) for v in shapes]
        + [dma((count,)), dma((count,)), dma((2,)), dma((2,)), dma((PARTS,)), dma((PARTS,)), dma, dma, dma, dma, dma((16,))]
        + [pltpu.VMEM(*v) for v in tail_shapes]
        + tail_sems,
        compiler_params=pltpu.CompilerParams(
            collective_id=3, has_side_effects=True, vmem_limit_bytes=62 * MIB
        ),
        cost_estimate=pl.CostEstimate(flops=0, bytes_accessed=200 * MIB, transcendentals=0),
        name="finish",
    )(*scalars, *arrays, *others)


def line_accept(place, distance, copies, take):
    for step in (-1, 1):
        block = place + step * distance

        @pl.when((block >= 0) & (block < LINE))
        def _():
            for one in copies(block, -step):
                one.wait_recv()
            ahead = place - step

            @pl.when((ahead >= 0) & (ahead < LINE))
            def _():
                for one in copies(block, -step):
                    one.start()

    for step in (-1, 1):
        block = place + step * distance

        @pl.when((block >= 0) & (block < LINE))
        def _():
            take(block)


def line_sent(place, copies, least):
    for block in range(LINE):
        for step in (-1, 1):

            @pl.when((place + step >= 0) & (place + step < LINE) & ((place - block) * step >= least))
            def _():
                for one in copies(block, step):
                    one.wait_send()


def begin_kernel(
    heads, cap, lengths_ref,
    table_ref, x_ref, gain1_ref, wt_ref, ow_ref, routes_ref, grad_ref, router_ref, gain2_ref, up_ref, down_ref,
    normed_out, qkvt0_out, mixt0_out, lse0_out, qkvt1_out, mixt1_out, lse1_out, hidden_ref, normed2_ref, info_ref, slots_ref,
    pw_ref, table1_ref, gy_ref, far_up_ref, far_half_ref, near_ref, near_info_ref,
    other_ref, got_ref, part_ref, keep_ref, send_ref, block_ref, places_ref, gsend_ref, gkeep_ref,
    normed_ref, qkvt0_ref, mixt0_ref, lse0_ref, qkvt1_ref, mixt1_ref, lse1_ref,
    b_send, b_recv, i_send, i_recv, x_send, x_recv, v_send, v_recv, y_send, y_recv, n_send, n_recv, keep_sem, store_sem,
):
    count = 2 * LINE
    me = lax.axis_index("expert")
    rank = lax.axis_index("tensor")
    place = me // 2
    side = me - 2 * place
    mate = me + 1 - 2 * side
    core = flipped(rank, 1, 4)
    away = flipped(rank, 2, 4)
    inner = heads * HD
    barrier = pltpu.get_barrier_semaphore()
    for k in range(1, count):
        pl.semaphore_signal(
            barrier, inc=1, device_id={"expert": flipped(me, k, count)}, device_id_type=pl.DeviceIdType.MESH
        )
    for target in (core, away):
        pl.semaphore_signal(
            barrier, inc=1, device_id={"tensor": target}, device_id_type=pl.DeviceIdType.MESH
        )
    pl.semaphore_wait(barrier, count + 1)

    swap = tensor_copy(x_ref, other_ref, v_send.at[0], v_recv.at[0], core)
    swap.start()
    pair = (
        tensor_copy(ow_ref, pw_ref.at[3 * inner :], y_send.at[0], y_recv.at[0], away),
        tensor_copy(wt_ref, pw_ref.at[: 3 * inner], y_send.at[1], y_recv.at[1], away),
        tensor_copy(table_ref, table1_ref, y_send.at[2], y_recv.at[2], away),
    )
    for one in pair:
        one.start()
    far = (
        tensor_copy(up_ref, far_up_ref, y_send.at[3], y_recv.at[3], away),
        tensor_copy(down_ref.at[: D // 2], far_half_ref, y_send.at[4], y_recv.at[4], away),
    )

    def along(block, step):
        return (
            mesh_copy(
                places_ref.at[block], places_ref.at[block], i_send.at[(step + 1) // 2, block], i_recv.at[block], me + 2 * step
            ),
            mesh_copy(
                block_ref.at[block], block_ref.at[block], b_send.at[(step + 1) // 2, block], b_recv.at[block], me + 2 * step
            ),
        )

    def across(block):
        return mesh_copy(gsend_ref.at[block], gy_ref.at[1, block], x_send.at[block], x_recv.at[block], mate)

    def keep(block):
        return pltpu.make_async_copy(gkeep_ref.at[block], gy_ref.at[0, block], keep_sem.at[block])

    rows = grad_ref.shape[0]

    def take(block):
        slots = places_ref[block, 0:2].astype(jnp.int32)
        for part, expert in ((1, mate), (0, me)):
            where = iota((cap, rows), 0) + expert * cap
            picks = ((where == slots[0:1]) | (where == slots[1:2])).astype(BF)
            taken = dot(picks, block_ref[block]).astype(BF)
            if part:
                gsend_ref[block] = taken
                across(block).start()
            else:
                gkeep_ref[block] = taken
                keep(block).start()

    block_ref[place] = grad_ref[...]
    slots_kernel(count, cap, lengths_ref, routes_ref, slots_ref)
    places_ref[place] = slots_ref[...]
    for step in (-1, 1):

        @pl.when((place + step >= 0) & (place + step < LINE))
        def _():
            for one in along(place, step):
                one.start()

    take(place)
    swap.wait()
    attn_fwd_kernel(
        True, heads, lengths_ref, table_ref, x_ref, other_ref, gain1_ref, wt_ref, ow_ref,
        normed_ref, qkvt0_ref, mixt0_ref, lse0_ref, part_ref,
    )
    first = (
        (normed_ref, normed_out), (qkvt0_ref, qkvt0_out), (mixt0_ref, mixt0_out), (lse0_ref, lse0_out),
    )
    second = ((qkvt1_ref, qkvt1_out), (mixt1_ref, mixt1_out), (lse1_ref, lse1_out))
    stores = [pltpu.make_async_copy(a, b, store_sem.at[i]) for i, (a, b) in enumerate(first + second)]
    for store in stores[:4]:
        store.start()
    line_accept(place, 1, along, take)
    for one in pair:
        one.wait_recv()
    for one in far:
        one.start()
    attn_fwd_kernel(
        False, heads, lengths_ref, table1_ref, normed_ref, pw_ref.at[: 3 * inner], pw_ref.at[3 * inner :], part_ref,
        qkvt1_ref, mixt1_ref, lse1_ref, keep_ref, send_ref, part_ref,
    )
    back = tensor_copy(send_ref, got_ref, v_send.at[1], v_recv.at[1], core)
    back.start()
    for store in stores[4:]:
        store.start()
    line_accept(place, 2, along, take)
    back.wait()
    middle_line_kernel(
        count, x_ref, keep_ref, got_ref, gain2_ref, router_ref, routes_ref, slots_ref, hidden_ref, normed2_ref, info_ref
    )
    inside = [place > 0, place < LINE - 1]

    def neighbour(i):
        target = me + 2 * (1 - 2 * i)
        return (
            mesh_copy(info_ref, near_info_ref.at[i], n_send.at[i], n_recv.at[i], target),
            mesh_copy(normed2_ref, near_ref.at[i], n_send.at[i + 2], n_recv.at[i + 2], target),
        )

    for i in range(2):

        @pl.when(inside[1 - i])
        def _():
            for one in neighbour(i):
                one.start()

    line_accept(place, 3, along, take)
    for block in range(LINE):
        keep(block).wait()
        across(block).wait()
    line_sent(place, along, 0)
    for store in stores:
        store.wait()
    for one in pair:
        one.wait_send()
    for one in far:
        one.wait()
    for i in range(2):

        @pl.when(inside[i])
        def _():
            for one in neighbour(1 - i):
                one.wait_send()
            for one in neighbour(i):
                one.wait_recv()


def begin(heads, cap, scalars, arrays, others):
    dma = pltpu.SemaphoreType.DMA
    rows = arrays[1].shape[0]
    local = heads * HD
    anyspec = pl.BlockSpec(memory_space=pl.ANY)
    half = (rows, D)
    kept = [
        ((SEQ, D), BF), ((3 * local, SEQ), BF), ((local, SEQ), BF), ((8, SEQ), F32),
        ((3 * local, SEQ), BF), ((local, SEQ), BF), ((8, SEQ), F32),
    ]
    outs = kept + [
        (half, F32), (half, BF), ((8, rows), F32), ((8, rows), F32), ((4 * local, D), BF), ((heads, NB), F32),
        ((2, LINE, cap, D), BF), ((D, D), BF), ((D // 2, D), BF), ((2, rows, D), BF), ((2, 8, rows), F32),
    ]
    shapes = [
        (half, BF), (half, BF), ((SEQ, D), F32), (half, F32), (half, BF), ((LINE, rows, D), BF), ((LINE, 8, rows), F32),
        ((LINE, cap, D), BF), ((LINE, cap, D), BF),
    ] + kept
    return pl.pallas_call(
        functools.partial(begin_kernel, heads, cap),
        out_shape=[jax.ShapeDtypeStruct(*v) for v in outs],
        in_specs=[SM] * len(scalars) + [VM] * len(arrays) + [anyspec] * len(others),
        out_specs=[anyspec] * 7 + [VM] * 6 + [anyspec] * 5,
        scratch_shapes=[pltpu.VMEM(*v) for v in shapes]
        + [dma((2, LINE)), dma((LINE,)), dma((2, LINE)), dma((LINE,)), dma((LINE,)), dma((LINE,))]
        + [dma((2,)), dma((2,)), dma((5,)), dma((5,)), dma((4,)), dma((4,)), dma((LINE,)), dma((7,))],
        compiler_params=pltpu.CompilerParams(
            collective_id=4, has_side_effects=True, vmem_limit_bytes=56 * MIB
        ),
        cost_estimate=pl.CostEstimate(flops=0, bytes_accessed=200 * MIB, transcendentals=0),
        name="begin",
    )(*scalars, *arrays, *others)


def shards(
    inputs,
    lengths,
    routes,
    attn_gain,
    qkv_weight,
    out_weight,
    rel_bias,
    moe_gain,
    router_weight,
    up_weight,
    down_weight,
    out_grad,
):
    rows = inputs.shape[0]
    rank = lax.axis_index("tensor")
    expert = lax.axis_index("expert")
    heads = rel_bias.shape[1]
    inner = heads * HD
    experts = router_weight.shape[1]
    cap = 4 * rows // experts
    spots = experts * cap
    table = jnp.transpose(rel_bias)

    def swap(x, bit):
        return lax.ppermute(x, "tensor", [(i, i ^ bit) for i in range(4)])

    gain1 = attn_gain.reshape(1, D)
    gain2 = moe_gain.reshape(1, D)
    wt = jnp.transpose(qkv_weight.reshape(D, 3 * inner))
    routes_t = jnp.transpose(routes)
    up, down = up_weight[0], down_weight[0]
    line = experts == 2 * LINE and cap == TILE
    if line:
        router_t = jnp.transpose(router_weight)
        (
            normed, qkvt0, mixt0, lse0, qkvt1, mixt1, lse1, hidden, normed_two, info, slots, pair_w, pair_table, grads_in, far_up, far_half, near, near_info,
        ) = begin(
            heads,
            cap,
            (lengths,),
            (table, inputs, gain1, wt, out_weight, routes_t, out_grad, router_t, gain2),
            (up, down),
        )
        came, result, stay, away, go, grad_router = moe_line(
            experts, cap, normed_two, info, router_t, (grads_in, near, near_info, up, down, far_up, far_half)
        )
    else:
        other = swap(inputs, 1)
        pair_w = swap(jnp.concatenate([wt, out_weight], axis=0), 2)
        pair_table = swap(table, 2)

        packed_grad, slots = call(
            functools.partial(route_kernel, experts, cap),
            [((spots, D), BF), ((8, rows), F32)],
            (lengths, routes_t, out_grad),
            [SM, VM, VM],
            flops=2 * spots * rows * D,
            moved=4 * MIB,
            name="route",
        )

        def exchange(x):
            return lax.all_to_all(
                x.reshape(experts, cap, x.shape[-1]), "expert", split_axis=0, concat_axis=0, tiled=True
            ).reshape(x.shape)

        grads_in = exchange(packed_grad)
        up, down, pair_w, pair_table = lax.optimization_barrier((up, down, pair_w, pair_table))
        far_up, far_down = swap(up, 2), swap(down, 2)

        attn_cost = dict(
            flops=2 * SEQ * D * 4 * inner + heads * SEQ * SEQ * 160, moved=6 * MIB, exps=heads * SEQ * SEQ
        )
        normed, qkvt0, mixt0, lse0, part0 = call(
            functools.partial(attn_fwd_kernel, True, heads),
            [((SEQ, D), BF), ((3 * inner, SEQ), BF), ((inner, SEQ), BF), ((8, SEQ), F32), ((SEQ, D), F32)],
            (lengths, table, inputs, other, gain1, wt, out_weight),
            [SM] + [VM] * 1 + [VM] * 5,
            name="attend_own",
            **attn_cost,
        )
        wt1, ow1 = pair_w[: 3 * inner], pair_w[3 * inner :]
        qkvt1, mixt1, lse1, keep, send = call(
            functools.partial(attn_fwd_kernel, False, heads),
            [((3 * inner, SEQ), BF), ((inner, SEQ), BF), ((8, SEQ), F32), ((rows, D), F32), ((rows, D), BF)],
            (lengths, pair_table, normed, wt1, ow1, part0),
            [SM] + [VM] * 1 + [VM] * 4,
            scratch=[pltpu.VMEM((SEQ, D), F32)],
            name="attend_pair",
            **attn_cost,
        )
        got = swap(send, 1)
        middle_args = (inputs, keep, got, gain2, jnp.transpose(router_weight), routes_t, slots)
        mine = jnp.concatenate([up, down], axis=0)
        far = jnp.concatenate([far_up, far_down], axis=0)
        quarters = [mine, far, swap(mine, 1), swap(far, 1)]
        hidden, packed_rows, meta = call(
            functools.partial(middle_kernel, experts, cap),
            [((rows, D), F32), ((spots, D), BF), ((experts, 8, cap), F32)],
            middle_args,
            flops=2 * spots * rows * D,
            moved=8 * MIB,
            name="middle",
        )
        came, result, stay, away, go, grad_router = moe(
            experts, cap, packed_rows, meta, grads_in, router_weight, quarters
        )
    if line:
        outputs, grad_inputs, gwt, gow, attn_sum, moe_sum, router_sum, bias_sum, go_stay, came_away = finish(
            heads,
            cap,
            (lengths,),
            (table, pair_table, came, slots, hidden, gain2, out_grad, gain1, grad_router),
            (result, go, away, inputs, normed, wt, out_weight, pair_w, qkvt0, mixt0, lse0, qkvt1, mixt1, lse1),
        )
    else:
        came_out = exchange(result)
        came_go = swap(go, 1)
        grad_hidden, grad_attended, moe_part = call(
            turn_kernel,
            [((rows, D), F32), ((rows, D), BF), ((8, D), F32)],
            (lengths, came, slots, hidden, gain2, out_grad),
            [SM] + [VM] * 5,
            flops=2 * spots * rows * D,
            moved=8 * MIB,
            name="turn",
        )
        other_grad = swap(grad_attended, 1)
        away = (away.astype(F32) + came_go[1].astype(F32)).astype(BF)
        bwd_cost = dict(
            flops=2 * SEQ * D * 10 * inner + heads * SEQ * SEQ * 400, moved=9 * MIB, exps=heads * SEQ * SEQ
        )
        work = [
            pltpu.VMEM((SEQ, D), BF),
            pltpu.VMEM((inner, SEQ), BF),
            pltpu.VMEM((3 * inner, SEQ), BF),
            pltpu.VMEM((TILE, TILE), F32),
            pltpu.VMEM((TILE, TILE), F32),
        ]
        gpart, gbias1, npart = call(
            functools.partial(attn_bwd_kernel, False, heads),
            [((4 * inner, D), BF), ((8, 128), F32), ((SEQ, D), F32)],
            (lengths, pair_table, normed, wt1, ow1, qkvt1, mixt1, lse1, grad_attended, other_grad),
            [SM] + [VM] * 1 + [VM] * 8,
            scratch=work,
            name="attend_pair_back",
            **bwd_cost,
        )
        gpair = swap(gpart, 2)
        gown, gbias0, keep_n, send_n = call(
            functools.partial(attn_bwd_kernel, True, heads),
            [((4 * inner, D), F32), ((8, 128), F32), ((rows, D), F32), ((rows, D), BF)],
            (lengths, table, normed, wt, out_weight, qkvt0, mixt0, lse0, grad_attended, other_grad, npart),
            [SM] + [VM] * 1 + [VM] * 9,
            scratch=work + [pltpu.VMEM((SEQ, D), F32)],
            name="attend_own_back",
            **bwd_cost,
        )
        away, gpair, gown = lax.optimization_barrier((away, gpair, gown))
        came_away = swap(away, 2)
        got_n = swap(send_n, 1)
        grad_inputs, attn_part = call(
            last_kernel,
            [((rows, D), BF), ((8, D), F32)],
            (inputs, keep_n, got_n, gain1, grad_hidden),
            moved=6 * MIB,
            name="last",
        )
        wide = (gown + gpair.astype(F32)).astype(BF)
        wide = lax.psum(wide, "expert").astype(F32)
        outputs = call(
            output_kernel,
            [((rows, D), BF)],
            (lengths, came_out, slots, hidden),
            [SM] + [VM] * 3,
            flops=2 * spots * rows * D,
            moved=8 * MIB,
            name="outputs",
        )[0]
        go_stay = came_go[0]

    if line:
        attn_sum, moe_sum = attn_sum.reshape(D), moe_sum.reshape(D)
        router_sum = jnp.transpose(router_sum)
    else:
        gwt, gow = wide[: 3 * inner], wide[3 * inner :]
        own_bias = gbias0[:heads, :NB].reshape(1, -1)
        pair_bias = gbias1[:heads, :NB].reshape(1, -1)
        ranks = jnp.arange(4, dtype=jnp.int32)[:, None]
        bias_parts = jnp.where(ranks == rank, own_bias, 0.0) + jnp.where(
            ranks == (rank ^ 2), pair_bias, 0.0
        )
        small = jnp.concatenate(
            [attn_part[0], moe_part[0], jnp.transpose(grad_router).reshape(-1), bias_parts.reshape(-1)]
        )
        small = lax.psum(small, ("expert", "tensor"))
        attn_sum, moe_sum = small[:D], small[D : 2 * D]
        router_sum = small[2 * D : 2 * D + experts * D].reshape(D, experts)
        bias_sum = lax.dynamic_slice(
            small[2 * D + experts * D :].reshape(4, heads * NB), (rank, 0), (1, heads * NB)
        )
    grad_weights = stay.astype(F32) + go_stay.astype(F32) + came_away.astype(F32)
    return (
        outputs,
        grad_inputs,
        attn_sum,
        jnp.transpose(gwt).reshape(D, 3, inner),
        gow,
        jnp.transpose(bias_sum.reshape(heads, NB)),
        moe_sum,
        router_sum,
        grad_weights[:D][None],
        jnp.transpose(grad_weights[D:])[None],
    )


def solution(mesh):
    return jax.shard_map(
        shards,
        mesh=mesh,
        in_specs=(
            P(("expert", "tensor"), None),
            P("expert"),
            P(("expert", "tensor"), None),
            P(),
            P(None, None, "tensor"),
            P("tensor", None),
            P(None, "tensor"),
            P(),
            P(),
            P("expert", None, "tensor"),
            P("expert", "tensor", None),
            P(("expert", "tensor"), None),
        ),
        out_specs=(
            P(("expert", "tensor"), None),
            P(("expert", "tensor"), None),
            P(),
            P(None, None, "tensor"),
            P("tensor", None),
            P(None, "tensor"),
            P(),
            P(),
            P("expert", None, "tensor"),
            P("expert", "tensor", None),
        ),
        check_vma=False,
    )
```

```python
import functools

import jax
import jax.numpy as jnp
from jax import lax
from jax.experimental import pallas as pl
from jax.experimental.pallas import tpu as pltpu
from jax.sharding import PartitionSpec as P

D = 768
HD = 64
NB = 32
MAXDIST = 128
SEQ = 1024
EPSILON = 1e-06
NEGATIVE = -1e30
TILE = 256
BF = jnp.bfloat16
F32 = jnp.float32
MIB = 2**20
CHUNK = 256
GELU = 0.7978845608028654
CUBIC = 0.044715


def bucket_edges():
    half_count = NB // 2
    short_edges = list(range(1, half_count))
    long_edges = [
        int(half_count * (MAXDIST / half_count) ** (step_index / half_count))
        for step_index in range(half_count)
    ]
    return short_edges + long_edges


EDGES = bucket_edges()


def dot(a, b, ca=1, cb=0, precision=None):
    return lax.dot_general(
        a, b, (((ca,), (cb,)), ((), ())), preferred_element_type=F32, precision=precision
    )


def iota(shape, dim):
    return lax.broadcasted_iota(jnp.int32, shape, dim)


def rms(v):
    return lax.rsqrt(jnp.mean(v * v, axis=-1, keepdims=True) + EPSILON)


def call(kernel, outs, args, specs=None, scratch=(), flops=0, moved=0, exps=0, vmem=56, name=None):
    vm = pl.BlockSpec(memory_space=pltpu.VMEM)
    return pl.pallas_call(
        kernel,
        out_shape=[jax.ShapeDtypeStruct(s, d) for s, d in outs],
        in_specs=specs or [vm] * len(args),
        out_specs=[vm] * len(outs),
        scratch_shapes=list(scratch),
        compiler_params=pltpu.CompilerParams(vmem_limit_bytes=vmem * MIB),
        cost_estimate=pl.CostEstimate(flops=flops, bytes_accessed=moved, transcendentals=exps),
        name=name,
    )(*args)


def own_length(lengths_ref):
    return lengths_ref[lax.axis_index("tensor") // 2]


def own_valid(lengths_ref, rows):
    half = lax.rem(lax.axis_index("tensor"), 2)
    return jnp.clip(own_length(lengths_ref) - half * rows, 0, rows)


def as_row(ref):
    return ref[...].reshape(1, D)


VM = pl.BlockSpec(memory_space=pltpu.VMEM)
SM = pl.BlockSpec(memory_space=pltpu.SMEM)


def slot_lines(experts, cap, valid_count, routes):
    rows = routes.shape[1]
    valid = iota((1, rows), 1) < valid_count
    ids = iota((experts, rows), 0)
    hot0 = ((ids == routes[0:1]) & valid).astype(F32)
    hot1 = ((ids == routes[1:2]) & valid).astype(F32)
    before = (iota((rows, rows), 0) < iota((rows, rows), 1)).astype(BF)
    rank = dot((hot0 + hot1).astype(BF), before)
    place = ids.astype(F32) * cap + rank
    bad = jnp.where(valid, 0.0, 1.0)
    slot0 = jnp.sum(hot0 * place, axis=0, keepdims=True) - bad
    slot1 = jnp.sum(hot1 * place, axis=0, keepdims=True) - bad
    return slot0, slot1


def route_kernel(experts, cap, lengths_ref, routes_ref, grad_ref, packed_ref, slots_ref):
    rows = grad_ref.shape[0]
    slot0, slot1 = slot_lines(experts, cap, own_valid(lengths_ref, routes_ref.shape[1]), routes_ref[...])
    spots = iota((experts * cap, rows), 0)
    pick0 = spots == slot0.astype(jnp.int32)
    pick1 = spots == slot1.astype(jnp.int32)
    packed_ref[...] = dot((pick0 | pick1).astype(BF), grad_ref[...]).astype(BF)
    slots_ref[...] = jnp.concatenate([slot0, slot1, jnp.zeros((6, rows), F32)], axis=0)


def slots_kernel(experts, cap, lengths_ref, routes_ref, slots_ref):
    rows = routes_ref.shape[1]
    slot0, slot1 = slot_lines(experts, cap, own_valid(lengths_ref, routes_ref.shape[1]), routes_ref[...])
    slots_ref[...] = jnp.concatenate([slot0, slot1, jnp.zeros((6, rows), F32)], axis=0)


def back_matrix(slots_ref, spots):
    rows = slots_ref.shape[1]
    where = iota((rows, spots), 1)
    slots = slots_ref[...].T.astype(jnp.int32)
    return ((where == slots[:, 0:1]) | (where == slots[:, 1:2])).astype(BF)


def bias_tiles(table_ref, head):
    dist = iota((8, TILE), 1)
    line = table_ref[head : head + 1, :]
    line = line - line[:, NB - 1 :]
    curve = jnp.broadcast_to(line[:, 0:1], (8, TILE))
    for number, edge in enumerate(EDGES):
        curve = jnp.where(dist >= edge, line[:, number + 1 : number + 2], curve)
    spread = jnp.broadcast_to(curve[0:1], (TILE, TILE))
    ring = pltpu.roll(spread, 0, 1, stride=1, stride_axis=0)
    ahead = iota((TILE, TILE), 1) >= iota((TILE, TILE), 0)
    return jnp.where(ahead, ring, NEGATIVE), jnp.where(ahead, 0.0, ring)


def head_pieces(qkvt_ref, mask_rows, head, local_inner):
    start = pl.multiple_of(head * HD, HD)
    q = qkvt_ref[pl.ds(start, HD), :] * jnp.asarray(HD**-0.5, BF)
    k = qkvt_ref[pl.ds(local_inner + start, HD), :]
    v = qkvt_ref[pl.ds(2 * local_inner + start, HD), :]
    ones = jnp.ones((16, SEQ), BF)
    return jnp.concatenate([q, ones], 0), jnp.concatenate([k, mask_rows], 0), v, ones


def mask_block(length):
    keep = (iota((16, SEQ), 1) < length) | (iota((16, SEQ), 0) > 0)
    return jnp.where(keep, 0.0, NEGATIVE).astype(BF)


def score_pieces(k, q, block, near, below):
    cols = slice(block * TILE, (block + 1) * TILE)
    qb = q[:, cols]
    pieces = []
    if block >= 2:
        pieces.append((0, (block - 1) * TILE, dot(k[: (block - 1) * TILE], qb)))
    if block >= 1:
        lo = (block - 1) * TILE
        pieces.append((lo, block * TILE, dot(k[lo : lo + TILE], qb) + below))
    lo = block * TILE
    pieces.append((lo, lo + TILE, dot(k[lo : lo + TILE], qb) + near))
    return cols, pieces


def attn_fwd_kernel(first, heads, lengths_ref, table_ref, *refs):
    if first:
        own_ref, other_ref, gain_ref, w_ref, ow_ref = refs[:5]
        normed_ref, qkvt_ref, mixt_ref, lse_ref, part_ref = refs[5:]
        half = own_ref.shape[0]
        core = lax.rem(lax.axis_index("tensor"), 2)
        for source, place in ((own_ref, core), (other_ref, 1 - core)):
            x = source[...].astype(F32)
            normed_ref[pl.ds(pl.multiple_of(place * half, half), half), :] = (
                x * rms(x) * as_row(gain_ref)
            ).astype(BF)
    else:
        normed_ref, w_ref, ow_ref, part_in = refs[:4]
        qkvt_ref, mixt_ref, lse_ref, keep_ref, send_ref, part_ref = refs[4:]
    local_inner = heads * HD
    qkvt_ref[...] = dot(w_ref[...], normed_ref[...], 1, 1).astype(BF)
    masks = mask_block(own_length(lengths_ref))
    lse_ref[...] = jnp.zeros_like(lse_ref)

    for head in range(heads):
        near, below = bias_tiles(table_ref, head)
        q, kt, v, ones = head_pieces(qkvt_ref, masks, head, local_inner)
        k = kt.T
        vx = jnp.concatenate([v, ones], 0)
        for block in range(SEQ // TILE):
            cols, pieces = score_pieces(k, q, block, near, below)
            top = functools.reduce(
                jnp.maximum, [jnp.max(s, axis=0, keepdims=True) for _, _, s in pieces]
            )
            total = None
            for lo, hi, s in pieces:
                term = dot(vx[:, lo:hi], jnp.exp(s - top).astype(BF))
                total = term if total is None else total + term
            weight = total[HD : HD + 1]
            mixt_ref[head * HD : (head + 1) * HD, cols] = (total[:HD] / weight).astype(BF)
            lse_ref[head : head + 1, cols] = top + jnp.log(weight)
    part = dot(mixt_ref[...], ow_ref[...], 0, 0)
    if first:
        part_ref[...] = part
    else:
        part_ref[...] = part + part_in[...]
        half = keep_ref.shape[0]
        core = lax.rem(lax.axis_index("tensor"), 2)
        keep_ref[...] = part_ref[pl.ds(pl.multiple_of(core * half, half), half), :]
        send_ref[...] = part_ref[pl.ds(pl.multiple_of((1 - core) * half, half), half), :].astype(BF)


def attn_bwd_kernel(early, last, heads, lengths_ref, table_ref, *refs):
    if last:
        (normed_ref, w_ref, ow_ref, qkvt_ref, mixt_ref, lse_ref, own_ref, other_ref, part_in) = refs[:9]
        gw_ref, gbias_ref, keep_ref, send_ref, ga_ref, got_ref, gt_ref, d0_ref, d1_ref, part_ref = refs[9:]
    else:
        (normed_ref, w_ref, ow_ref, qkvt_ref, mixt_ref, lse_ref, own_ref, other_ref) = refs[:8]
        gw_ref, gbias_ref, part_ref, ga_ref, got_ref, gt_ref, d0_ref, d1_ref = refs[8:]
    local_inner = heads * HD
    half = own_ref.shape[0]
    core = lax.rem(lax.axis_index("tensor"), 2)
    ga_ref[pl.ds(pl.multiple_of(core * half, half), half), :] = own_ref[...]
    ga_ref[pl.ds(pl.multiple_of((1 - core) * half, half), half), :] = other_ref[...]
    got_ref[...] = dot(ow_ref[...], ga_ref[...], 1, 1).astype(BF)
    gw_ref[3 * local_inner :] = dot(mixt_ref[...], ga_ref[...]).astype(gw_ref.dtype)
    if early is not None:
        early()
    masks = mask_block(own_length(lengths_ref))
    gbias_ref[...] = jnp.zeros_like(gbias_ref)
    ahead = iota((TILE, TILE), 1) >= iota((TILE, TILE), 0)
    spot = (iota((TILE, 128), 0) + 1) % TILE
    flip = (iota((TILE, TILE), 0) + iota((TILE, TILE), 1) == TILE - 1).astype(F32)
    bucket = jnp.zeros((TILE, 128), jnp.int32)
    for edge in EDGES:
        bucket = bucket + (spot >= edge).astype(jnp.int32)
    hot = (bucket == iota((TILE, 128), 1)).astype(F32)

    for head in range(heads):
        near, below = bias_tiles(table_ref, head)
        q, kt, vt, _ = head_pieces(qkvt_ref, masks, head, local_inner)
        k = kt.T
        v = vt.T
        rows = slice(head * HD, (head + 1) * HD)
        gt = got_ref[rows, :]
        delta = jnp.sum(gt.astype(F32) * mixt_ref[rows, :].astype(F32), axis=0, keepdims=True)
        gk = [None] * (SEQ // TILE)
        gv = [None] * (SEQ // TILE)
        far = jnp.zeros((8, TILE), F32)
        for block in range(SEQ // TILE):
            cols, pieces = score_pieces(k, q, block, near, below)
            gb = gt[:, cols]
            qb = q[:HD, cols]
            lse = lse_ref[head : head + 1, cols]
            db = delta[:, cols]
            gq = None
            for lo, hi, s in pieces:
                p = jnp.exp(s - lse)
                ds = p * (dot(v[lo:hi], gb) - db)
                pb = p.astype(BF)
                dsb = ds.astype(BF)
                term = dot(kt[:HD, lo:hi], dsb)
                gq = term if gq is None else gq + term
                tv = dot(pb, gb, 1, 1)
                tk = dot(dsb, qb, 1, 1)
                for tile in range(lo // TILE, hi // TILE):
                    part = slice(tile * TILE - lo, (tile + 1) * TILE - lo)
                    gv[tile] = tv[part] if gv[tile] is None else gv[tile] + tv[part]
                    gk[tile] = tk[part] if gk[tile] is None else gk[tile] + tk[part]
                if hi == (block + 1) * TILE:
                    d0_ref[...] = ds if block == 0 else d0_ref[...] + ds
                elif hi == block * TILE and lo == (block - 1) * TILE:
                    d1_ref[...] = ds if block == 1 else d1_ref[...] + ds
                else:
                    far = far + jnp.sum(ds.reshape((hi - lo) // 8, 8, TILE), axis=0)
            gt_ref[rows, cols] = (gq * HD**-0.5).astype(BF)
        for tile in range(SEQ // TILE):
            cols = slice(tile * TILE, (tile + 1) * TILE)
            gt_ref[local_inner + head * HD : local_inner + (head + 1) * HD, cols] = (
                gk[tile].T.astype(BF)
            )
            gt_ref[2 * local_inner + head * HD : 2 * local_inner + (head + 1) * HD, cols] = (
                gv[tile].T.astype(BF)
            )
        d1 = d1_ref[...]
        ring = jnp.where(ahead, d0_ref[...], d1)
        turned = pltpu.roll(
            dot(flip, ring, 1, 0, lax.Precision.HIGHEST), 0, 1, stride=1, stride_axis=0
        )
        far = far + jnp.sum(jnp.where(ahead, d1, 0.0).reshape(TILE // 8, 8, TILE), axis=0)
        line = jnp.sum(turned, axis=0, keepdims=True)
        sums = dot(
            jnp.broadcast_to(line, (8, TILE)), hot, 1, 0, lax.Precision.HIGHEST
        )
        sums = sums + jnp.where(iota((8, 128), 1) == NB - 1, jnp.sum(far), 0.0)
        gbias_ref[head : head + 1, :] = sums[0:1]
    gw_ref[: 3 * local_inner] = dot(gt_ref[...], normed_ref[...]).astype(gw_ref.dtype)
    part = dot(gt_ref[...], w_ref[...], 0, 0)
    if last:
        part_ref[...] = part + part_in[...]
        keep_ref[...] = part_ref[pl.ds(pl.multiple_of(core * half, half), half), :]
        send_ref[...] = part_ref[pl.ds(pl.multiple_of((1 - core) * half, half), half), :].astype(BF)
    else:
        part_ref[...] = part


def gates_of(experts, normed, router_t, routes):
    rows = normed.shape[0]
    logits = dot(router_t, normed, 1, 1)
    ids = iota((experts, rows), 0)
    signs = (ids == routes[0:1]).astype(F32) - (ids == routes[1:2]).astype(F32)
    gap = jnp.sum(logits * signs, axis=0, keepdims=True)
    return 1.0 / (1.0 + jnp.exp(-gap)), 1.0 / (1.0 + jnp.exp(gap))


def meta_lines(gate, code):
    rows = gate.shape[1]
    line = iota((8, rows), 0)
    high = gate.astype(BF).astype(F32)
    mid = (gate - high).astype(BF).astype(F32)
    low = gate - high - mid
    picked = jnp.where(line == 0, high, jnp.where(line == 1, mid, jnp.where(line == 2, low, 0.0)))
    return jnp.where(line == 3, code, picked).astype(BF)


def hidden_rows(x_ref, keep_ref, got_ref, gain_ref, hidden_ref):
    hidden = x_ref[...].astype(F32) + keep_ref[...] + got_ref[...].astype(F32)
    hidden_ref[...] = hidden
    return (hidden * rms(hidden) * as_row(gain_ref)).astype(BF)


def middle_kernel(
    experts, cap, x_ref, keep_ref, got_ref, gain_ref, router_ref, routes_ref, slots_ref, hidden_ref, packed_ref, meta_ref
):
    normed = hidden_rows(x_ref, keep_ref, got_ref, gain_ref, hidden_ref)
    slots = slots_ref[...].astype(jnp.int32)
    routes = routes_ref[...]
    where = iota((experts * cap, normed.shape[0]), 0)
    pick0 = where == slots[0:1]
    pick1 = where == slots[1:2]
    packed_ref[...] = dot((pick0 | pick1).astype(BF), normed).astype(BF)
    gate0, gate1 = gates_of(experts, normed, router_ref[...], routes)
    codes = (routes + 1).astype(F32)
    meta = dot(meta_lines(gate0, codes[1:2]), pick0.astype(BF), 1, 1) + dot(
        meta_lines(gate1, codes[0:1]), pick1.astype(BF), 1, 1
    )
    for number in range(experts):
        meta_ref[number] = meta[:, number * cap : (number + 1) * cap]


def middle_line_kernel(
    experts, x_ref, keep_ref, got_ref, gain_ref, router_ref, routes_ref, slots_ref, hidden_ref, normed_ref, info_ref
):
    normed = hidden_rows(x_ref, keep_ref, got_ref, gain_ref, hidden_ref)
    normed_ref[...] = normed
    routes = routes_ref[...]
    gate0, gate1 = gates_of(experts, normed, router_ref[...], routes)
    codes = (routes + 1).astype(F32)
    info_ref[...] = jnp.concatenate(
        [slots_ref[0:2], gate0, gate1, codes, jnp.zeros((2, normed.shape[0]), F32)], axis=0
    )


def gelu_pair(v):
    squared = v * v
    slope = GELU * (1.0 + 3 * CUBIC * squared)
    t = jnp.tanh(v * (GELU + GELU * CUBIC * squared))
    half = 0.5 + 0.5 * t
    return v * half, half + 0.5 * v * (1.0 - t * t) * slope


def flipped(me, k, count):
    total, bit = 0, 1
    while bit < count:
        total = total + lax.rem(me // bit + k // bit, 2) * bit
        bit *= 2
    return total


def weight_grads(xt_ref, geot_ref, act_ref, gi_ref, stage_ref, stay_ref, away_ref, go_ref, out_sem):
    tiles = D // TILE
    steps = 8 * tiles

    def columns(step):
        return pl.ds(pl.multiple_of(lax.rem(step, tiles) * TILE, TILE), TILE)

    def store(step, slot, out_ref):
        half = lax.rem(step, 2 * tiles) // tiles
        return pltpu.make_async_copy(
            stage_ref.at[slot],
            out_ref.at[pl.ds(pl.multiple_of(half * D, D), D), columns(step)],
            out_sem.at[slot],
        )

    def weights(step, carry):
        q = step // (2 * tiles)
        half = lax.rem(step, 2 * tiles) // tiles
        slot = lax.rem(step, 2)

        @pl.when(step >= 2)
        def _():
            store(step - 2, slot, stay_ref).wait()

        @pl.when(half == 0)
        def _():
            stage_ref[slot] = dot(xt_ref[...], gi_ref[q, :, columns(step)]).astype(BF)

        @pl.when(half == 1)
        def _():
            stage_ref[slot] = dot(geot_ref[...], act_ref[q, :, columns(step)]).astype(BF)

        for number, out_ref in enumerate((stay_ref, away_ref, go_ref.at[0], go_ref.at[1])):

            @pl.when(q == number)
            def _():
                store(step, slot, out_ref).start()

        return carry

    lax.fori_loop(0, steps, weights, 0)
    for step in (steps - 2, steps - 1):
        store(step, step % 2, stay_ref).wait()


def expert_rows(ready, x, geo, here, w_ref, xt_ref, geot_ref, act_ref, gi_ref, acc_ref):
    xt_ref[:, here] = x.T
    geot_ref[:, here] = geo.T
    worth = 0.0
    for q in (0, 2, 1, 3):
        if q == 1:
            ready()
        inner = dot(x, w_ref[q, :D])
        grad_active = dot(geo, w_ref[q, D:], 1, 1)
        act, slope = gelu_pair(inner)
        gi = (slope * grad_active).astype(BF)
        act_ref[q, here] = act.astype(BF)
        gi_ref[q, here] = gi
        back = dot(gi, w_ref[q, :D], 1, 1)
        if q == 0:
            acc_ref[...] = back
        else:
            acc_ref[...] += back
        worth = worth + jnp.sum(act * grad_active, axis=1, keepdims=True)
    return worth


def expert_outs(start, size, column, act_ref, w_ref):
    here = pl.ds(pl.multiple_of(start, size), size)
    cols = pl.ds(pl.multiple_of(column * TILE, TILE), TILE)
    total = None
    for q in range(4):
        term = dot(act_ref[q, here], w_ref[q, D:, cols])
        total = term if total is None else total + term
    return cols, total


def expert_kernel(
    count, cap, packed_ref, send_meta_ref, grads_ref, router_ref, w0, w1, w2, w3,
    came_ref, result_ref, stay_ref, away_ref, go_ref, grouter_ref,
    w_ref, x_ref, xt_ref, geot_ref, act_ref, gi_ref, gsend_ref, meta_ref, acc_ref, stage_ref,
    x_send, x_recv, m_send, m_recv, r_send, r_recv, local_sem, w_sem, out_sem,
):
    me = lax.axis_index("expert")
    barrier = pltpu.get_barrier_semaphore()

    def peer(k):
        return flipped(me, k, count)

    source = peer

    def greet(k, carry):
        pl.semaphore_signal(
            barrier, inc=1, device_id={"expert": peer(k)}, device_id_type=pl.DeviceIdType.MESH
        )
        return carry

    lax.fori_loop(1, count, greet, 0)
    pl.semaphore_wait(barrier, count - 1)

    def rows_of(k):
        return pl.ds(pl.multiple_of(k * cap, cap), cap)

    def send_rows(k):
        return pltpu.make_async_remote_copy(
            src_ref=packed_ref.at[rows_of(peer(k))],
            dst_ref=x_ref.at[rows_of(k)],
            send_sem=x_send.at[k],
            recv_sem=x_recv.at[k],
            device_id={"expert": peer(k)},
            device_id_type=pl.DeviceIdType.MESH,
        )

    def send_meta(k):
        return pltpu.make_async_remote_copy(
            src_ref=send_meta_ref.at[peer(k)],
            dst_ref=meta_ref.at[k],
            send_sem=m_send.at[k],
            recv_sem=m_recv.at[k],
            device_id={"expert": peer(k)},
            device_id_type=pl.DeviceIdType.MESH,
        )

    def send_back(k):
        return pltpu.make_async_remote_copy(
            src_ref=gsend_ref.at[rows_of(k)],
            dst_ref=came_ref.at[rows_of(me)],
            send_sem=r_send.at[k],
            recv_sem=r_recv.at[k],
            device_id={"expert": source(k)},
            device_id_type=pl.DeviceIdType.MESH,
        )

    def start_sends(k, carry):
        send_meta(k).start()
        send_rows(k).start()
        return carry

    lax.fori_loop(count // 2, count, start_sends, 0)
    lax.fori_loop(1, count // 2, start_sends, 0)
    own_rows = pltpu.make_async_copy(packed_ref.at[rows_of(me)], x_ref.at[rows_of(0)], local_sem.at[0])
    own_rows.start()
    own_meta = pltpu.make_async_copy(send_meta_ref.at[me], meta_ref.at[0], local_sem.at[1])
    own_meta.start()
    loads = [
        pltpu.make_async_copy(w, w_ref.at[i], w_sem.at[i]) for i, w in enumerate((w0, w1, w2, w3))
    ]
    for load in loads:
        load.start()
    grouter_ref[...] = jnp.zeros_like(grouter_ref)
    experts = router_ref.shape[1]
    own_rows.wait()
    own_meta.wait()
    for load in loads:
        load.wait()
    group = max(1, CHUNK // cap)
    span = group * cap

    def chunk(j, carry):
        for i in range(group):
            k = j * group + i

            @pl.when(k > 0)
            def _():
                send_rows(k).wait_recv()
                send_meta(k).wait_recv()

        here = pl.ds(pl.multiple_of(j * span, span), span)
        meta = jnp.concatenate([meta_ref[j * group + i].T for i in range(group)], axis=0)
        gate = meta[:, 0:1] + meta[:, 1:2] + meta[:, 2:3]
        code = meta[:, 3:4].astype(jnp.int32)
        gy = jnp.concatenate([grads_ref[rows_of(source(j * group + i)), :] for i in range(group)], axis=0)
        geo = (gate * gy.astype(F32)).astype(BF)
        x = x_ref[here, :]
        worth = expert_rows(lambda: None, x, geo, here, w_ref, xt_ref, geot_ref, act_ref, gi_ref, acc_ref)
        ids = iota((span, experts), 1)
        signs = (ids == me).astype(F32) - (ids + 1 == code).astype(F32)
        share = jnp.where(code > 0, (1.0 - gate) * worth, 0.0) * signs
        high = share.astype(BF)
        low = (share - high.astype(F32)).astype(BF)
        gsend_ref[here, :] = (acc_ref[...] + dot(high, router_ref[...], 1, 1)).astype(BF)
        grouter_ref[...] += dot(high.T, x) + dot(low.T, x)
        for i in range(group):
            k = j * group + i

            @pl.when(k > 0)
            def _():
                send_back(k).start()

        return carry

    lax.fori_loop(0, count // group, chunk, 0)
    own_back = pltpu.make_async_copy(gsend_ref.at[rows_of(0)], came_ref.at[rows_of(me)], local_sem.at[0])
    own_back.start()

    def results(step, carry):
        j = step // (D // TILE)
        meta = jnp.concatenate([meta_ref[j * group + i].T for i in range(group)], axis=0)
        gate = meta[:, 0:1] + meta[:, 1:2] + meta[:, 2:3]
        cols, total = expert_outs(j * span, span, lax.rem(step, D // TILE), act_ref, w_ref)
        out = (gate * total).astype(BF)
        for i in range(group):
            result_ref[rows_of(source(j * group + i)), cols] = out[i * cap : (i + 1) * cap]
        return carry

    lax.fori_loop(0, count // group * (D // TILE), results, 0)
    weight_grads(xt_ref, geot_ref, act_ref, gi_ref, stage_ref, stay_ref, away_ref, go_ref, out_sem)
    own_back.wait()

    def finish(k, carry):
        send_rows(k).wait_send()
        send_meta(k).wait_send()
        send_back(k).wait()
        return carry

    lax.fori_loop(1, count, finish, 0)


def mesh_copy(src, dst, send_sem, recv_sem, target):
    return pltpu.make_async_remote_copy(
        src_ref=src,
        dst_ref=dst,
        send_sem=send_sem,
        recv_sem=recv_sem,
        device_id={"expert": target},
        device_id_type=pl.DeviceIdType.MESH,
    )


LINE = 4


def expert_line_kernel(
    cap, normed_ref, info_in, router_ref, grads_in, near_ref, near_info_ref, up_ref, down_ref, far_up_ref, far_half_ref,
    came_ref, result_ref, stay_ref, away_ref, go_ref, grouter_ref,
    grads_ref, w_ref, block_ref, info_ref, x_ref, xs_ref, meta_ref, ms_ref, xt_ref, geot_ref, act_ref, gi_ref, acc_ref, stage_ref,
    b_send, b_recv, i_send, i_recv, x_send, x_recv, m_send, m_recv, r_send, r_recv, local_sem, w_sem, v_send, v_recv, y_send, y_recv, grads_sem, near_sem, out_sem,
):
    count = 2 * LINE
    me = lax.axis_index("expert")
    place = me // 2
    side = me - 2 * place
    mate = me + 1 - 2 * side
    barrier = pltpu.get_barrier_semaphore()

    def greet(k, carry):
        pl.semaphore_signal(
            barrier,
            inc=1,
            device_id={"expert": lax.rem(me + k, count)},
            device_id_type=pl.DeviceIdType.MESH,
        )
        return carry

    lax.fori_loop(1, count, greet, 0)
    core = flipped(lax.axis_index("tensor"), 1, 4)
    pl.semaphore_signal(
        barrier, inc=1, device_id={"tensor": core}, device_id_type=pl.DeviceIdType.MESH
    )
    away = flipped(lax.axis_index("tensor"), 2, 4)
    pl.semaphore_signal(
        barrier, inc=1, device_id={"tensor": away}, device_id_type=pl.DeviceIdType.MESH
    )
    pl.semaphore_wait(barrier, count + 1)

    def along(block, step):
        return (
            mesh_copy(
                info_ref.at[block],
                info_ref.at[block],
                i_send.at[(step + 1) // 2, block],
                i_recv.at[block],
                me + 2 * step,
            ),
            mesh_copy(
                block_ref.at[block],
                block_ref.at[block],
                b_send.at[(step + 1) // 2, block],
                b_recv.at[block],
                me + 2 * step,
            ),
        )

    def across(block):
        return (
            mesh_copy(ms_ref.at[block], meta_ref.at[1, block], m_send.at[block], m_recv.at[block], mate),
            mesh_copy(xs_ref.at[block], x_ref.at[1, block], x_send.at[block], x_recv.at[block], mate),
        )

    def rows_of(number):
        return pl.ds(pl.multiple_of(number * cap, cap), cap)

    def origin(part, block):
        return 2 * block + side + part * (1 - 2 * side)

    def give_back(part, block):
        return mesh_copy(
            x_ref.at[part, block],
            came_ref.at[rows_of(me)],
            r_send.at[part, block],
            r_recv.at[me],
            origin(part, block),
        )

    def each(pair, act):
        for one in pair:
            act(one)

    own = (
        pltpu.make_async_copy(info_in, info_ref.at[place], local_sem.at[0]),
        pltpu.make_async_copy(normed_ref, block_ref.at[place], local_sem.at[1]),
    )
    each(own, lambda c: c.start())
    rest = D // 4 * 3
    far_down = tensor_copy(down_ref.at[rest:], w_ref.at[1, D + rest :], y_send, y_recv, away)
    far_down.start()
    grads_load = pltpu.make_async_copy(grads_in, grads_ref, grads_sem)
    grads_load.start()
    near = [
        (
            pltpu.make_async_copy(near_info_ref.at[i], info_ref.at[place + 2 * i - 1], near_sem.at[i]),
            pltpu.make_async_copy(near_ref.at[i], block_ref.at[place + 2 * i - 1], near_sem.at[i + 2]),
        )
        for i in range(2)
    ]
    inside = [place > 0, place < LINE - 1]
    for i in range(2):

        @pl.when(inside[i])
        def _():
            each(near[i], lambda c: c.start())

    weights = (
        (up_ref, 0, 0, D), (down_ref, 0, D, D), (far_up_ref, 1, 0, D), (far_half_ref, 1, D, rest),
        (w_ref.at[1, D + rest :], 1, D + rest, D - rest),
    )

    def load(i):
        source, q, start, size = weights[i]
        return pltpu.make_async_copy(source, w_ref.at[q, start : start + size], w_sem.at[i])

    def lend(i):
        source, q, start, size = weights[i]
        return tensor_copy(source, w_ref.at[2 + q, start : start + size], v_send.at[i], v_recv.at[i], core)

    for i in range(2):

        @pl.when(inside[i])
        def _():
            each(near[i], lambda c: c.wait())

            @pl.when(inside[1 - i])
            def _():
                each(along(place + 2 * i - 1, 1 - 2 * i), lambda c: c.start())

    for i in range(4):
        load(i).start()
        lend(i).start()
    each(own, lambda c: c.wait())
    experts = router_ref.shape[0]
    rows = normed_ref.shape[0]

    def select(block):
        info = info_ref[block]
        slots = info[0:2].astype(jnp.int32)
        lines0 = meta_lines(info[2:3], info[5:6])
        lines1 = meta_lines(info[3:4], info[4:5])
        for part, expert in ((1, mate), (0, me)):
            where = iota((cap, rows), 0) + expert * cap
            pick0 = where == slots[0:1]
            pick1 = where == slots[1:2]
            taken = dot((pick0 | pick1).astype(BF), block_ref[block]).astype(BF)
            meta = dot(lines0, pick0.astype(BF), 1, 1) + dot(lines1, pick1.astype(BF), 1, 1)
            if part:
                xs_ref[block] = taken
                ms_ref[block] = meta
                each(across(block), lambda c: c.start())
            else:
                x_ref[0, block] = taken
                meta_ref[0, block] = meta

    select(place)
    grouter_ref[...] = jnp.zeros_like(grouter_ref)
    mirror = place // 2
    inward = place + mirror * (LINE - 1 - 2 * place)

    def block_at(i):
        step = i + inward * (1 - i // 2 - 2 * (i // 2 - i // (LINE - 1)))
        return step + mirror * (LINE - 1 - 2 * step)

    outer = sum(d * 8**i for i, d in enumerate((0, 1, 4, 2, 5, 3, 6, 7)))
    inner = sum(d * 8**i for i, d in enumerate((0, 1, 4, 2, 5, 3, 6, 7)))
    chunks = outer + inward * (inner - outer)

    def chunk_at(power):
        digit = lax.rem(chunks // power, 8)
        return digit // 4, block_at(lax.rem(digit, 4))

    for i in range(2):

        @pl.when(inside[i])
        def _():
            select(place + 2 * i - 1)

    grads_load.wait()
    for i in range(2):
        load(i).wait()
        lend(i).wait_recv()

    def far_ready(c):
        @pl.when(c == 0)
        def _():
            far_down.wait_recv()
            lend(4).start()
            for i in (2, 3):
                load(i).wait()
                lend(i).wait_recv()
            lend(4).wait_recv()


    def chunk(c, power):
        for distance in range(2, LINE):

            @pl.when(c == 4 * distance - 7)
            def _():
                line_accept(place, distance, along, select)

        part, block = chunk_at(power)

        @pl.when(part == 1)
        def _():
            each(across(block), lambda c: c.wait_recv())

        here = pl.ds(pl.multiple_of(c * cap, cap), cap)
        meta = meta_ref[part, block].T
        gate = meta[:, 0:1] + meta[:, 1:2] + meta[:, 2:3]
        code = meta[:, 3:4].astype(jnp.int32)
        geo = (gate * grads_ref[part, block].astype(F32)).astype(BF)
        x = x_ref[part, block]
        worth = expert_rows(lambda: far_ready(c), x, geo, here, w_ref, xt_ref, geot_ref, act_ref, gi_ref, acc_ref)
        ids = iota((cap, experts), 1)
        signs = (ids == me).astype(F32) - (ids + 1 == code).astype(F32)
        share = jnp.where(code > 0, (1.0 - gate) * worth, 0.0) * signs
        high = share.astype(BF)
        low = (share - high.astype(F32)).astype(BF)
        grouter_ref[...] += dot(high.T, x) + dot(low.T, x)
        x_ref[part, block] = (acc_ref[...] + dot(high, router_ref[...])).astype(BF)

        @pl.when(origin(part, block) != me)
        def _():
            give_back(part, block).start()

        return power * 8

    lax.fori_loop(0, count, chunk, jnp.int32(1))
    own_back = pltpu.make_async_copy(x_ref.at[0, place], came_ref.at[rows_of(me)], local_sem.at[0])
    own_back.start()

    def results(step, carry):
        first = step // (D // TILE) * LINE
        cols, total = expert_outs(first * cap, LINE * cap, lax.rem(step, D // TILE), act_ref, w_ref)
        for i in range(LINE):
            part, block = chunk_at((1 + first // LINE * (8**LINE - 1)) * 8**i)
            meta = meta_ref[part, block].T
            gate = meta[:, 0:1] + meta[:, 1:2] + meta[:, 2:3]
            result_ref[rows_of(origin(part, block)), cols] = (
                gate * total[i * cap : (i + 1) * cap]
            ).astype(BF)
        return carry

    lax.fori_loop(0, 2 * (D // TILE), results, 0)
    weight_grads(xt_ref, geot_ref, act_ref, gi_ref, stage_ref, stay_ref, away_ref, go_ref, out_sem)
    own_back.wait()
    for i in range(5):
        lend(i).wait_send()
    far_down.wait_send()
    line_sent(place, along, 1)
    for block in range(LINE):
        each(across(block), lambda c: c.wait_send())
        for part in (0, 1):

            @pl.when(origin(part, block) != me)
            def _():
                give_back(part, block).wait_send()

    for number in range(count):

        @pl.when(number != me)
        def _():
            mesh_copy(
                x_ref.at[0, 0], came_ref.at[rows_of(number)], r_send.at[0, 0], r_recv.at[number], mate
            ).wait_recv()


def turn_kernel(lengths_ref, came_ref, slots_ref, hidden_ref, gain_ref, grad_ref, gh_ref, ga_ref, gain_out):
    gn = dot(back_matrix(slots_ref, came_ref.shape[0]), came_ref[...])
    hidden = hidden_ref[...]
    scale = rms(hidden)
    unit = hidden * scale
    gain_out[...] = jnp.broadcast_to(jnp.sum(gn * unit, axis=0, keepdims=True), gain_out.shape)
    g = gn * as_row(gain_ref)
    valid = (iota((hidden.shape[0], 1), 0) < own_valid(lengths_ref, hidden.shape[0])).astype(F32)
    gh = scale * (g - unit * jnp.mean(g * unit, axis=1, keepdims=True)) + valid * grad_ref[...].astype(F32)
    gh_ref[...] = gh
    ga_ref[...] = gh.astype(BF)


def output_kernel(lengths_ref, came_ref, slots_ref, hidden_ref, out_ref):
    mix = dot(back_matrix(slots_ref, came_ref.shape[0]), came_ref[...])
    hidden = hidden_ref[...]
    valid = (iota((hidden.shape[0], 1), 0) < own_valid(lengths_ref, hidden.shape[0])).astype(F32)
    out_ref[...] = (valid * (hidden + mix)).astype(BF)


def last_kernel(x_ref, keep_ref, got_ref, gain_ref, gh_ref, out_ref, gain_out):
    x = x_ref[...].astype(F32)
    scale = rms(x)
    unit = x * scale
    gn = keep_ref[...] + got_ref[...].astype(F32)
    gain_out[...] = jnp.broadcast_to(jnp.sum(gn * unit, axis=0, keepdims=True), gain_out.shape)
    g = gn * as_row(gain_ref)
    out_ref[...] = (
        gh_ref[...] + scale * (g - unit * jnp.mean(g * unit, axis=1, keepdims=True))
    ).astype(BF)


def moe(experts, cap, packed, meta, grads, router, quarters):
    spots = experts * cap
    anyspec = pl.BlockSpec(memory_space=pl.ANY)
    dma = pltpu.SemaphoreType.DMA
    return pl.pallas_call(
        functools.partial(expert_kernel, experts, cap),
        out_shape=[
            jax.ShapeDtypeStruct((spots, D), BF),
            jax.ShapeDtypeStruct((spots, D), BF),
            jax.ShapeDtypeStruct((2 * D, D), BF),
            jax.ShapeDtypeStruct((2 * D, D), BF),
            jax.ShapeDtypeStruct((2, 2 * D, D), BF),
            jax.ShapeDtypeStruct((experts, D), F32),
        ],
        in_specs=[anyspec, VM, VM, VM] + [anyspec] * 4,
        out_specs=[anyspec, VM, anyspec, anyspec, anyspec, VM],
        scratch_shapes=[
            pltpu.VMEM((4, 2 * D, D), BF),
            pltpu.VMEM((spots, D), BF),
            pltpu.VMEM((D, spots), BF),
            pltpu.VMEM((D, spots), BF),
            pltpu.VMEM((4, spots, D), BF),
            pltpu.VMEM((4, spots, D), BF),
            pltpu.VMEM((spots, D), BF),
            pltpu.VMEM((experts, 8, cap), F32),
            pltpu.VMEM((CHUNK, D), F32),
            pltpu.VMEM((2, D, TILE), BF),
            dma((experts,)),
            dma((experts,)),
            dma((experts,)),
            dma((experts,)),
            dma((experts,)),
            dma((experts,)),
            dma((2,)),
            dma((4,)),
            dma((2,)),
        ],
        compiler_params=pltpu.CompilerParams(
            collective_id=1, has_side_effects=True, vmem_limit_bytes=60 * MIB
        ),
        cost_estimate=pl.CostEstimate(flops=12 * spots * D * 4 * D, bytes_accessed=60 * MIB, transcendentals=0),
        name="experts",
    )(packed, meta, grads, router, *quarters)


def moe_line(experts, cap, normed, info, router, others):
    rows = normed.shape[0]
    spots = experts * cap
    anyspec = pl.BlockSpec(memory_space=pl.ANY)
    dma = pltpu.SemaphoreType.DMA
    return pl.pallas_call(
        functools.partial(expert_line_kernel, cap),
        out_shape=[
            jax.ShapeDtypeStruct((spots, D), BF),
            jax.ShapeDtypeStruct((spots, D), BF),
            jax.ShapeDtypeStruct((2 * D, D), BF),
            jax.ShapeDtypeStruct((2 * D, D), BF),
            jax.ShapeDtypeStruct((2, 2 * D, D), BF),
            jax.ShapeDtypeStruct((experts, D), F32),
        ],
        in_specs=[VM, VM, VM] + [anyspec] * 7,
        out_specs=[anyspec, VM, anyspec, anyspec, anyspec, VM],
        scratch_shapes=[
            pltpu.VMEM((2, LINE, cap, D), BF),
            pltpu.VMEM((4, 2 * D, D), BF),
            pltpu.VMEM((LINE, rows, D), BF),
            pltpu.VMEM((LINE, 8, rows), F32),
            pltpu.VMEM((2, LINE, cap, D), BF),
            pltpu.VMEM((LINE, cap, D), BF),
            pltpu.VMEM((2, LINE, 8, cap), F32),
            pltpu.VMEM((LINE, 8, cap), F32),
            pltpu.VMEM((D, spots), BF),
            pltpu.VMEM((D, spots), BF),
            pltpu.VMEM((4, spots, D), BF),
            pltpu.VMEM((4, spots, D), BF),
            pltpu.VMEM((cap, D), F32),
            pltpu.VMEM((2, D, TILE), BF),
            dma((2, LINE)),
            dma((LINE,)),
            dma((2, LINE)),
            dma((LINE,)),
            dma((LINE,)),
            dma((LINE,)),
            dma((LINE,)),
            dma((LINE,)),
            dma((2, LINE)),
            dma((experts,)),
            dma((2,)),
            dma((4,)),
            dma((5,)),
            dma((5,)),
            dma,
            dma,
            dma,
            dma((4,)),
            dma((2,)),
        ],
        compiler_params=pltpu.CompilerParams(
            collective_id=2, has_side_effects=True, vmem_limit_bytes=62 * MIB
        ),
        cost_estimate=pl.CostEstimate(flops=12 * spots * D * 4 * D, bytes_accessed=60 * MIB, transcendentals=0),
        name="experts_line",
    )(normed, info, router, *others)


def tensor_copy(src, dst, send_sem, recv_sem, target):
    return pltpu.make_async_remote_copy(
        src_ref=src,
        dst_ref=dst,
        send_sem=send_sem,
        recv_sem=recv_sem,
        device_id={"tensor": target},
        device_id_type=pl.DeviceIdType.MESH,
    )


def sums(
    pair_done, beside, gw_ref, pair_ref, keep_ref, send_ref, x_in, gain_ref, gh_ref, moe_ref, router_ref, bias0_ref, bias1_ref,
    gwt_out, gow_out, gin_out, attn_out, moe_out, router_out, bias_out,
    small_out, part_ref, cross_ref, line_ref, from_ref, all_ref, got_ref, lines_ref, few_ref, ranks_ref,
    a_send, a_recv, b_send, b_recv, c_send, c_recv, d_send, d_recv, s_send, s_recv, f_send, f_recv, t_send, t_recv, g_send, g_recv,
):
    count = 2 * LINE
    me = lax.axis_index("expert")
    rank = lax.axis_index("tensor")
    place = me // 2
    side = me - 2 * place
    mate = me + 1 - 2 * side
    size = part_ref.shape[0] // count
    def slab(which, number):
        return pl.ds(pl.multiple_of((which * LINE + number) * size, size), size)

    swap = tensor_copy(send_ref, got_ref, s_send, s_recv, flipped(rank, 1, 4))
    swap.start()
    pair_done()
    part_ref[...] = (gw_ref[...] + pair_ref[...].astype(F32)).astype(BF)
    rows = gwt_out.shape[0]

    def cross(number):
        return mesh_copy(
            part_ref.at[slab(1 - side, number)], cross_ref.at[number], a_send.at[number], a_recv.at[number], mate
        )

    def along(number):
        return mesh_copy(
            line_ref.at[number], from_ref.at[place], b_send.at[number], b_recv.at[place], 2 * number + side
        )

    def spread(number):
        return mesh_copy(
            all_ref.at[slab(side, place)],
            all_ref.at[slab(side, place)],
            c_send.at[number],
            c_recv.at[place],
            2 * number + side,
        )

    def over(number):
        return mesh_copy(
            all_ref.at[slab(side, number)], all_ref.at[slab(side, number)], d_send.at[number], d_recv.at[number], mate
        )

    for number in range(LINE):
        cross(number).start()

    swap.wait()
    x = x_in[...].astype(F32)
    scale = rms(x)
    unit = x * scale
    gn = keep_ref[...] + got_ref[...].astype(F32)
    attn = jnp.sum(gn * unit, axis=0, keepdims=True)
    g = gn * as_row(gain_ref)
    gin_out[...] = (gh_ref[...] + scale * (g - unit * jnp.mean(g * unit, axis=1, keepdims=True))).astype(BF)

    heads = gow_out.shape[0] // HD
    blank = jnp.zeros((1, 128), F32)

    def flat(bias_ref):
        line = [bias_ref[h : h + 1, :NB] for h in range(heads)]
        return jnp.concatenate(line + [jnp.zeros((1, 128 - heads * NB), F32)], axis=1)

    own_bias, pair_bias = flat(bias0_ref), flat(bias1_ref)
    other = flipped(rank, 2, 4)
    for j in range(D // 128):
        lines_ref[j] = router_ref[:, j * 128 : (j + 1) * 128]
    for j, row in ((6, attn), (7, moe_ref[0:1])):
        places = [2 * (j - 6), 2 * (j - 6) + 1]
        bias = [
            jnp.where(rank == p, own_bias, blank) + jnp.where(other == p, pair_bias, blank) for p in places
        ]
        lines_ref[j] = jnp.concatenate([row[:, i * 128 : (i + 1) * 128] for i in range(6)] + bias, axis=0)

    def small(k):
        return mesh_copy(
            lines_ref.at[flipped(me, k, count)], few_ref.at[k], f_send.at[k], f_recv.at[k], flipped(me, k, count)
        )

    def rank_copy(k):
        return tensor_copy(
            ranks_ref.at[rank], ranks_ref.at[rank], t_send.at[k], t_recv.at[k], flipped(rank, k, 4)
        )

    def rank_from(k):
        return tensor_copy(
            ranks_ref.at[rank], ranks_ref.at[flipped(rank, k, 4)], t_send.at[k], t_recv.at[k], flipped(rank, k, 4)
        )

    def small_spread(k):
        return mesh_copy(
            small_out.at[me], small_out.at[me], g_send.at[k], g_recv.at[k], flipped(me, k, count)
        )

    def small_from(k):
        return mesh_copy(
            small_out.at[me], small_out.at[flipped(me, k, count)], g_send.at[k], g_recv.at[k], flipped(me, k, count)
        )

    for k in range(1, count):
        small(k).start()

    for number in range(LINE):

        @pl.when(number != place)
        def _():
            cross(number).wait_recv()
            line_ref[number] = (
                part_ref[slab(side, number)].astype(F32) + cross_ref[number].astype(F32)
            ).astype(BF)
            along(number).start()

    total = lines_ref[me]
    for k in range(1, count):
        small(k).wait_recv()
        total = total + few_ref[k]
    ranks_ref[rank] = total
    for k in range(1, 4):
        rank_copy(k).start()

    for number in range(LINE):

        @pl.when(number == place)
        def _():
            cross(number).wait_recv()

    beside()
    whole = part_ref[slab(side, place)].astype(F32) + cross_ref[place].astype(F32)
    from_ref[place] = whole.astype(BF)
    for k in range(1, LINE):
        number = lax.rem(place + k, LINE)
        mesh_copy(
            line_ref.at[number], from_ref.at[number], b_send.at[number], b_recv.at[number], mate
        ).wait_recv()
        whole = whole + from_ref[number].astype(F32)
    all_ref[slab(side, place)] = whole.astype(BF)
    over(place).start()
    for number in range(LINE):

        @pl.when(number != place)
        def _():
            spread(number).start()

    for k in range(1, 4):
        rank_from(k).wait_recv()
    small_out[me] = ranks_ref[0] + ranks_ref[1] + ranks_ref[2] + ranks_ref[3]
    for k in range(1, count):
        small_spread(k).start()

    for k in range(1, LINE):
        number = lax.rem(place + k, LINE)
        mesh_copy(
            all_ref.at[slab(side, number)], all_ref.at[slab(side, number)], c_send.at[number], c_recv.at[number], mate
        ).wait_recv()
        over(number).start()
    for k in range(1, count):
        small_from(k).wait_recv()
    for number in range(LINE):
        mesh_copy(
            all_ref.at[slab(1 - side, number)],
            all_ref.at[slab(1 - side, number)],
            d_send.at[number],
            d_recv.at[number],
            mate,
        ).wait_recv()
    attn_out[...] = jnp.concatenate([small_out[6, i : i + 1] for i in range(6)], axis=1).reshape(D)
    moe_out[...] = jnp.concatenate([small_out[7, i : i + 1] for i in range(6)], axis=1).reshape(D)
    router_out[...] = jnp.concatenate([small_out[j] for j in range(D // 128)], axis=1)
    bias = functools.reduce(
        jnp.add,
        [jnp.where(rank == p, small_out[6 + p // 2, 6 + p % 2 : 7 + p % 2], blank) for p in range(4)],
    )
    bias_out[...] = jnp.concatenate([bias[:, h * NB : (h + 1) * NB] for h in range(heads)], axis=0)
    gwt_out[...] = all_ref[:rows].astype(F32)
    gow_out[...] = all_ref[rows:].astype(F32)
    for number in range(LINE):
        cross(number).wait_send()
        over(number).wait_send()

        @pl.when(number != place)
        def _():
            along(number).wait_send()
            spread(number).wait_send()

    for k in range(1, count):
        small(k).wait_send()
        small_spread(k).wait_send()
    for k in range(1, 4):
        rank_copy(k).wait_send()


PARTS = 6


def finish_kernel(
    heads, cap, lengths_ref,
    table0_ref, table1_ref, slots_ref, gain2_ref, gain1_ref, router_ref,
    came_in, hidden_in, grad_in, result_in, go_in, away_in, x_in, normed_in, wt_in, ow_in, pw_in, qkvt0_in, mixt0_in, lse0_in, qkvt1_in, mixt1_in, lse1_in,
    out_ref, gin_out, gwt_out, gow_out, attn_out, moe_out, router_out, bias_out, came_go_ref, came_away_ref,
    came_ref, hidden_ref, grad_ref, outs_ref, gorecv_ref, away_ref, x_ref, normed_ref, wt_ref, ow_ref, pw_ref, qkvt0_ref, mixt0_ref, lse0_ref, qkvt1_ref, mixt1_ref, lse1_ref,
    gh_ref, ga_ref, other_ref, moe_ref, gpart_ref, gpair_ref, gown_ref, bias0_ref, bias1_ref, keep_ref, send_ref,
    all_ga_ref, got_ref, gt_ref, d0_ref, d1_ref, npart_ref,
    o_send, o_recv, v_send, v_recv, y_send, y_recv, w_send, w_recv, e_send, e_recv, load_sem, *tail_refs,
):
    count = 2 * LINE
    me = lax.axis_index("expert")
    rank = lax.axis_index("tensor")
    core = flipped(rank, 1, 4)
    away_rank = flipped(rank, 2, 4)
    places = (
        (came_in, came_ref),
        (hidden_in, hidden_ref),
        (grad_in, grad_ref),
        (normed_in, normed_ref),
        (pw_in, pw_ref),
        (qkvt1_in, qkvt1_ref),
        (mixt1_in, mixt1_ref),
        (lse1_in, lse1_ref),
        (wt_in, wt_ref),
        (ow_in, ow_ref),
        (qkvt0_in, qkvt0_ref),
        (mixt0_in, mixt0_ref),
        (lse0_in, lse0_ref),
        (x_in, x_ref),
    )
    loads = [pltpu.make_async_copy(a, b, load_sem.at[i + 2]) for i, (a, b) in enumerate(places)]
    for load in loads:
        load.start()
    barrier = pltpu.get_barrier_semaphore()
    for k in range(1, count):
        pl.semaphore_signal(
            barrier, inc=1, device_id={"expert": flipped(me, k, count)}, device_id_type=pl.DeviceIdType.MESH
        )
    for k in range(1, 4):
        pl.semaphore_signal(
            barrier, inc=1, device_id={"tensor": flipped(rank, k, 4)}, device_id_type=pl.DeviceIdType.MESH
        )
    pl.semaphore_wait(barrier, count + 2)

    def rows_of(number):
        return pl.ds(pl.multiple_of(number * cap, cap), cap)

    def result(k):
        return mesh_copy(
            result_in.at[rows_of(flipped(me, k, count))],
            outs_ref.at[rows_of(me)],
            o_send.at[k],
            o_recv.at[k],
            flipped(me, k, count),
        )

    order = list(range(LINE, count)) + list(range(1, LINE))
    for k in order:
        result(k).start()
    own_result = pltpu.make_async_copy(result_in.at[rows_of(me)], outs_ref.at[rows_of(me)], load_sem.at[0])
    own_result.start()
    away_load = pltpu.make_async_copy(away_in, away_ref, load_sem.at[1])
    away_load.start()
    go_away = tensor_copy(go_in.at[1], gorecv_ref, v_send.at[0], v_recv.at[0], core)
    go_away.start()
    go_stay = tensor_copy(go_in.at[0], came_go_ref, v_send.at[1], v_recv.at[1], core)
    for load in loads[:3]:
        load.wait()
    turn_kernel(lengths_ref, came_ref, slots_ref, hidden_ref, gain2_ref, grad_ref, gh_ref, ga_ref, moe_ref)
    ga_swap = tensor_copy(ga_ref, other_ref, w_send, w_recv, core)
    ga_swap.start()
    away_load.wait()
    go_away.wait_recv()
    size = away_ref.shape[0] // PARTS

    def lines(i):
        return pl.ds(i * size, size)

    def away(i):
        return tensor_copy(
            away_ref.at[lines(i)], came_away_ref.at[lines(i)], y_send.at[i], y_recv.at[i], away_rank
        )

    for i in range(PARTS):
        away_ref[lines(i)] = (
            away_ref[lines(i)].astype(F32) + gorecv_ref[lines(i)].astype(F32)
        ).astype(BF)
        if i < 1:
            away(i).start()
    ga_swap.wait()
    go_stay.start()
    for load in loads[3:]:
        load.wait()
    inner = heads * HD
    split = ((slice(3 * inner, 4 * inner), 0), (slice(0, 3 * inner), 1))
    pair = [
        tensor_copy(gpart_ref.at[lines_of], gpair_ref.at[lines_of], e_send.at[i], e_recv.at[i], away_rank)
        for lines_of, i in split
    ]
    attn_bwd_kernel(
        pair[0].start, False, heads, lengths_ref, table1_ref,
        normed_ref, pw_ref.at[: 3 * inner], pw_ref.at[3 * inner :], qkvt1_ref, mixt1_ref, lse1_ref, ga_ref, other_ref,
        gpart_ref, bias1_ref, npart_ref, all_ga_ref, got_ref, gt_ref, d0_ref, d1_ref,
    )
    pair[1].start()
    attn_bwd_kernel(
        None, True, heads, lengths_ref, table0_ref,
        normed_ref, wt_ref, ow_ref, qkvt0_ref, mixt0_ref, lse0_ref, ga_ref, other_ref, npart_ref,
        gown_ref, bias0_ref, keep_ref, send_ref, all_ga_ref, got_ref, gt_ref, d0_ref, d1_ref, npart_ref,
    )

    def pair_done():
        for one in pair:
            one.wait_recv()
        for i in range(1, PARTS):
            away(i).start()

    def beside():
        own_result.wait()
        for k in order:
            result(k).wait_recv()
        output_kernel(lengths_ref, outs_ref, slots_ref, hidden_ref, out_ref)

    sums(
        pair_done, beside, gown_ref, gpair_ref, keep_ref, send_ref, x_ref, gain1_ref, gh_ref, moe_ref, router_ref,
        bias0_ref, bias1_ref, gwt_out, gow_out, gin_out, attn_out, moe_out, router_out, bias_out, *tail_refs,
    )
    for k in order:
        result(k).wait_send()
    for one in pair:
        one.wait_send()
    go_away.wait_send()
    go_stay.wait()
    for i in range(PARTS):
        away(i).wait()


def finish(heads, cap, scalars, arrays, others):
    dma = pltpu.SemaphoreType.DMA
    count = 2 * LINE
    spots = count * cap
    rows = others[1].shape[0]
    local = heads * HD
    part = 4 * local // count
    anyspec = pl.BlockSpec(memory_space=pl.ANY)
    half = (rows, D)
    tail_sems = [dma((LINE,))] * 8 + [dma, dma] + [dma((count,))] * 2 + [dma((4,))] * 2 + [dma((count,))] * 2
    shapes = [
        ((spots, D), BF), (half, F32), (half, BF),
        ((spots, D), BF), ((2 * D, D), BF), ((2 * D, D), BF), (half, BF), ((SEQ, D), BF), ((3 * local, D), BF),
        ((local, D), BF), ((4 * local, D), BF), ((3 * local, SEQ), BF), ((local, SEQ), BF), ((8, SEQ), F32),
        ((3 * local, SEQ), BF), ((local, SEQ), BF), ((8, SEQ), F32),
        (half, F32), (half, BF), (half, BF), ((8, D), F32), ((4 * local, D), BF), ((4 * local, D), BF),
        ((4 * local, D), F32), ((8, 128), F32), ((8, 128), F32), (half, F32), (half, BF),
        ((SEQ, D), BF), ((local, SEQ), BF), ((3 * local, SEQ), BF), ((TILE, TILE), F32), ((TILE, TILE), F32), ((SEQ, D), F32),
    ]
    tail_shapes = [
        ((count, 8, 128), F32),
        ((4 * local, D), BF), ((LINE, part, D), BF), ((LINE, part, D), BF), ((LINE, part, D), BF), ((4 * local, D), BF),
        (half, BF), ((count, 8, 128), F32), ((count, 8, 128), F32), ((4, 8, 128), F32),
    ]
    return pl.pallas_call(
        functools.partial(finish_kernel, heads, cap),
        out_shape=[
            jax.ShapeDtypeStruct(half, BF),
            jax.ShapeDtypeStruct(half, BF),
            jax.ShapeDtypeStruct((3 * local, D), F32),
            jax.ShapeDtypeStruct((local, D), F32),
            jax.ShapeDtypeStruct((D,), F32),
            jax.ShapeDtypeStruct((D,), F32),
            jax.ShapeDtypeStruct((count, D), F32),
            jax.ShapeDtypeStruct((heads, NB), F32),
            jax.ShapeDtypeStruct((2 * D, D), BF),
            jax.ShapeDtypeStruct((2 * D, D), BF),
        ],
        in_specs=[SM] * len(scalars) + [VM] * len(arrays) + [anyspec] * len(others),
        out_specs=[VM] * 8 + [anyspec] * 2,
        scratch_shapes=[pltpu.VMEM(*v) for v in shapes]
        + [dma((count,)), dma((count,)), dma((2,)), dma((2,)), dma((PARTS,)), dma((PARTS,)), dma, dma, dma((2,)), dma((2,)), dma((16,))]
        + [pltpu.VMEM(*v) for v in tail_shapes]
        + tail_sems,
        compiler_params=pltpu.CompilerParams(
            collective_id=3, has_side_effects=True, vmem_limit_bytes=62 * MIB
        ),
        cost_estimate=pl.CostEstimate(flops=0, bytes_accessed=200 * MIB, transcendentals=0),
        name="finish",
    )(*scalars, *arrays, *others)


def line_accept(place, distance, copies, take):
    for step in (-1, 1):
        block = place + step * distance

        @pl.when((block >= 0) & (block < LINE))
        def _():
            for one in copies(block, -step):
                one.wait_recv()
            ahead = place - step

            @pl.when((ahead >= 0) & (ahead < LINE))
            def _():
                for one in copies(block, -step):
                    one.start()

    for step in (-1, 1):
        block = place + step * distance

        @pl.when((block >= 0) & (block < LINE))
        def _():
            take(block)


def line_sent(place, copies, least):
    for block in range(LINE):
        for step in (-1, 1):

            @pl.when((place + step >= 0) & (place + step < LINE) & ((place - block) * step >= least))
            def _():
                for one in copies(block, step):
                    one.wait_send()


def begin_kernel(
    heads, cap, lengths_ref,
    table_ref, x_ref, gain1_ref, wt_ref, ow_ref, routes_ref, grad_ref, router_ref, gain2_ref, up_ref, down_ref,
    normed_out, qkvt0_out, mixt0_out, lse0_out, qkvt1_out, mixt1_out, lse1_out, hidden_ref, normed2_ref, info_ref, slots_ref,
    pw_ref, table1_ref, gy_ref, far_up_ref, far_half_ref, near_ref, near_info_ref,
    other_ref, got_ref, part_ref, keep_ref, send_ref, block_ref, places_ref, gsend_ref, gkeep_ref,
    normed_ref, qkvt0_ref, mixt0_ref, lse0_ref, qkvt1_ref, mixt1_ref, lse1_ref,
    b_send, b_recv, i_send, i_recv, x_send, x_recv, v_send, v_recv, y_send, y_recv, n_send, n_recv, keep_sem, store_sem,
):
    count = 2 * LINE
    me = lax.axis_index("expert")
    rank = lax.axis_index("tensor")
    place = me // 2
    side = me - 2 * place
    mate = me + 1 - 2 * side
    core = flipped(rank, 1, 4)
    away = flipped(rank, 2, 4)
    inner = heads * HD
    barrier = pltpu.get_barrier_semaphore()
    for k in range(1, count):
        pl.semaphore_signal(
            barrier, inc=1, device_id={"expert": flipped(me, k, count)}, device_id_type=pl.DeviceIdType.MESH
        )
    for target in (core, away):
        pl.semaphore_signal(
            barrier, inc=1, device_id={"tensor": target}, device_id_type=pl.DeviceIdType.MESH
        )
    pl.semaphore_wait(barrier, count + 1)

    swap = tensor_copy(x_ref, other_ref, v_send.at[0], v_recv.at[0], core)
    swap.start()
    pair = (
        tensor_copy(ow_ref, pw_ref.at[3 * inner :], y_send.at[0], y_recv.at[0], away),
        tensor_copy(wt_ref, pw_ref.at[: 3 * inner], y_send.at[1], y_recv.at[1], away),
        tensor_copy(table_ref, table1_ref, y_send.at[2], y_recv.at[2], away),
    )
    for one in pair:
        one.start()
    far = (
        tensor_copy(up_ref, far_up_ref, y_send.at[3], y_recv.at[3], away),
        tensor_copy(down_ref.at[: D // 4 * 3], far_half_ref, y_send.at[4], y_recv.at[4], away),
    )

    def along(block, step):
        return (
            mesh_copy(
                places_ref.at[block], places_ref.at[block], i_send.at[(step + 1) // 2, block], i_recv.at[block], me + 2 * step
            ),
            mesh_copy(
                block_ref.at[block], block_ref.at[block], b_send.at[(step + 1) // 2, block], b_recv.at[block], me + 2 * step
            ),
        )

    def across(block):
        return mesh_copy(gsend_ref.at[block], gy_ref.at[1, block], x_send.at[block], x_recv.at[block], mate)

    def keep(block):
        return pltpu.make_async_copy(gkeep_ref.at[block], gy_ref.at[0, block], keep_sem.at[block])

    rows = grad_ref.shape[0]

    def take(block):
        slots = places_ref[block, 0:2].astype(jnp.int32)
        for part, expert in ((1, mate), (0, me)):
            where = iota((cap, rows), 0) + expert * cap
            picks = ((where == slots[0:1]) | (where == slots[1:2])).astype(BF)
            taken = dot(picks, block_ref[block]).astype(BF)
            if part:
                gsend_ref[block] = taken
                across(block).start()
            else:
                gkeep_ref[block] = taken
                keep(block).start()

    block_ref[place] = grad_ref[...]
    slots_kernel(count, cap, lengths_ref, routes_ref, slots_ref)
    places_ref[place] = slots_ref[...]
    for step in (-1, 1):

        @pl.when((place + step >= 0) & (place + step < LINE))
        def _():
            for one in along(place, step):
                one.start()

    take(place)
    swap.wait()
    attn_fwd_kernel(
        True, heads, lengths_ref, table_ref, x_ref, other_ref, gain1_ref, wt_ref, ow_ref,
        normed_ref, qkvt0_ref, mixt0_ref, lse0_ref, part_ref,
    )
    first = (
        (normed_ref, normed_out), (qkvt0_ref, qkvt0_out), (mixt0_ref, mixt0_out), (lse0_ref, lse0_out),
    )
    second = ((qkvt1_ref, qkvt1_out), (mixt1_ref, mixt1_out), (lse1_ref, lse1_out))
    stores = [pltpu.make_async_copy(a, b, store_sem.at[i]) for i, (a, b) in enumerate(first + second)]
    for store in stores[:4]:
        store.start()
    line_accept(place, 1, along, take)
    for one in pair:
        one.wait_recv()
    for one in far:
        one.start()
    attn_fwd_kernel(
        False, heads, lengths_ref, table1_ref, normed_ref, pw_ref.at[: 3 * inner], pw_ref.at[3 * inner :], part_ref,
        qkvt1_ref, mixt1_ref, lse1_ref, keep_ref, send_ref, part_ref,
    )
    back = tensor_copy(send_ref, got_ref, v_send.at[1], v_recv.at[1], core)
    back.start()
    for store in stores[4:]:
        store.start()
    line_accept(place, 2, along, take)
    back.wait()
    middle_line_kernel(
        count, x_ref, keep_ref, got_ref, gain2_ref, router_ref, routes_ref, slots_ref, hidden_ref, normed2_ref, info_ref
    )
    inside = [place > 0, place < LINE - 1]

    def neighbour(i):
        target = me + 2 * (1 - 2 * i)
        return (
            mesh_copy(info_ref, near_info_ref.at[i], n_send.at[i], n_recv.at[i], target),
            mesh_copy(normed2_ref, near_ref.at[i], n_send.at[i + 2], n_recv.at[i + 2], target),
        )

    for i in range(2):

        @pl.when(inside[1 - i])
        def _():
            for one in neighbour(i):
                one.start()

    line_accept(place, 3, along, take)
    for block in range(LINE):
        keep(block).wait()
        across(block).wait()
    line_sent(place, along, 0)
    for store in stores:
        store.wait()
    for one in pair:
        one.wait_send()
    for one in far:
        one.wait()
    for i in range(2):

        @pl.when(inside[i])
        def _():
            for one in neighbour(1 - i):
                one.wait_send()
            for one in neighbour(i):
                one.wait_recv()


def begin(heads, cap, scalars, arrays, others):
    dma = pltpu.SemaphoreType.DMA
    rows = arrays[1].shape[0]
    local = heads * HD
    anyspec = pl.BlockSpec(memory_space=pl.ANY)
    half = (rows, D)
    kept = [
        ((SEQ, D), BF), ((3 * local, SEQ), BF), ((local, SEQ), BF), ((8, SEQ), F32),
        ((3 * local, SEQ), BF), ((local, SEQ), BF), ((8, SEQ), F32),
    ]
    outs = kept + [
        (half, F32), (half, BF), ((8, rows), F32), ((8, rows), F32), ((4 * local, D), BF), ((heads, NB), F32),
        ((2, LINE, cap, D), BF), ((D, D), BF), ((D // 4 * 3, D), BF), ((2, rows, D), BF), ((2, 8, rows), F32),
    ]
    shapes = [
        (half, BF), (half, BF), ((SEQ, D), F32), (half, F32), (half, BF), ((LINE, rows, D), BF), ((LINE, 8, rows), F32),
        ((LINE, cap, D), BF), ((LINE, cap, D), BF),
    ] + kept
    return pl.pallas_call(
        functools.partial(begin_kernel, heads, cap),
        out_shape=[jax.ShapeDtypeStruct(*v) for v in outs],
        in_specs=[SM] * len(scalars) + [VM] * len(arrays) + [anyspec] * len(others),
        out_specs=[anyspec] * 7 + [VM] * 6 + [anyspec] * 5,
        scratch_shapes=[pltpu.VMEM(*v) for v in shapes]
        + [dma((2, LINE)), dma((LINE,)), dma((2, LINE)), dma((LINE,)), dma((LINE,)), dma((LINE,))]
        + [dma((2,)), dma((2,)), dma((5,)), dma((5,)), dma((4,)), dma((4,)), dma((LINE,)), dma((7,))],
        compiler_params=pltpu.CompilerParams(
            collective_id=4, has_side_effects=True, vmem_limit_bytes=56 * MIB
        ),
        cost_estimate=pl.CostEstimate(flops=0, bytes_accessed=200 * MIB, transcendentals=0),
        name="begin",
    )(*scalars, *arrays, *others)


def shards(
    inputs,
    lengths,
    routes,
    attn_gain,
    qkv_weight,
    out_weight,
    rel_bias,
    moe_gain,
    router_weight,
    up_weight,
    down_weight,
    out_grad,
):
    rows = inputs.shape[0]
    rank = lax.axis_index("tensor")
    expert = lax.axis_index("expert")
    heads = rel_bias.shape[1]
    inner = heads * HD
    experts = router_weight.shape[1]
    cap = 4 * rows // experts
    spots = experts * cap
    table = jnp.transpose(rel_bias)

    def swap(x, bit):
        return lax.ppermute(x, "tensor", [(i, i ^ bit) for i in range(4)])

    gain1, gain2 = attn_gain, moe_gain
    wt = jnp.transpose(qkv_weight.reshape(D, 3 * inner))
    routes_t = jnp.transpose(routes)
    up, down = up_weight[0], down_weight[0]
    line = experts == 2 * LINE and cap == TILE
    if line:
        router_t = jnp.transpose(router_weight)
        (
            normed, qkvt0, mixt0, lse0, qkvt1, mixt1, lse1, hidden, normed_two, info, slots, pair_w, pair_table, grads_in, far_up, far_half, near, near_info,
        ) = begin(
            heads,
            cap,
            (lengths,),
            (table, inputs, gain1, wt, out_weight, routes_t, out_grad, router_t, gain2),
            (up, down),
        )
        came, result, stay, away, go, grad_router = moe_line(
            experts, cap, normed_two, info, router_t, (grads_in, near, near_info, up, down, far_up, far_half)
        )
    else:
        other = swap(inputs, 1)
        pair_w = swap(jnp.concatenate([wt, out_weight], axis=0), 2)
        pair_table = swap(table, 2)

        packed_grad, slots = call(
            functools.partial(route_kernel, experts, cap),
            [((spots, D), BF), ((8, rows), F32)],
            (lengths, routes_t, out_grad),
            [SM, VM, VM],
            flops=2 * spots * rows * D,
            moved=4 * MIB,
            name="route",
        )

        def exchange(x):
            return lax.all_to_all(
                x.reshape(experts, cap, x.shape[-1]), "expert", split_axis=0, concat_axis=0, tiled=True
            ).reshape(x.shape)

        grads_in = exchange(packed_grad)
        up, down, pair_w, pair_table = lax.optimization_barrier((up, down, pair_w, pair_table))
        far_up, far_down = swap(up, 2), swap(down, 2)

        attn_cost = dict(
            flops=2 * SEQ * D * 4 * inner + heads * SEQ * SEQ * 160, moved=6 * MIB, exps=heads * SEQ * SEQ
        )
        normed, qkvt0, mixt0, lse0, part0 = call(
            functools.partial(attn_fwd_kernel, True, heads),
            [((SEQ, D), BF), ((3 * inner, SEQ), BF), ((inner, SEQ), BF), ((8, SEQ), F32), ((SEQ, D), F32)],
            (lengths, table, inputs, other, gain1, wt, out_weight),
            [SM] + [VM] * 1 + [VM] * 5,
            name="attend_own",
            **attn_cost,
        )
        wt1, ow1 = pair_w[: 3 * inner], pair_w[3 * inner :]
        qkvt1, mixt1, lse1, keep, send = call(
            functools.partial(attn_fwd_kernel, False, heads),
            [((3 * inner, SEQ), BF), ((inner, SEQ), BF), ((8, SEQ), F32), ((rows, D), F32), ((rows, D), BF)],
            (lengths, pair_table, normed, wt1, ow1, part0),
            [SM] + [VM] * 1 + [VM] * 4,
            scratch=[pltpu.VMEM((SEQ, D), F32)],
            name="attend_pair",
            **attn_cost,
        )
        got = swap(send, 1)
        middle_args = (inputs, keep, got, gain2, jnp.transpose(router_weight), routes_t, slots)
        mine = jnp.concatenate([up, down], axis=0)
        far = jnp.concatenate([far_up, far_down], axis=0)
        quarters = [mine, far, swap(mine, 1), swap(far, 1)]
        hidden, packed_rows, meta = call(
            functools.partial(middle_kernel, experts, cap),
            [((rows, D), F32), ((spots, D), BF), ((experts, 8, cap), F32)],
            middle_args,
            flops=2 * spots * rows * D,
            moved=8 * MIB,
            name="middle",
        )
        came, result, stay, away, go, grad_router = moe(
            experts, cap, packed_rows, meta, grads_in, router_weight, quarters
        )
    if line:
        outputs, grad_inputs, gwt, gow, attn_sum, moe_sum, router_sum, bias_sum, go_stay, came_away = finish(
            heads,
            cap,
            (lengths,),
            (table, pair_table, slots, gain2, gain1, grad_router),
            (came, hidden, out_grad, result, go, away, inputs, normed, wt, out_weight, pair_w, qkvt0, mixt0, lse0, qkvt1, mixt1, lse1),
        )
    else:
        came_out = exchange(result)
        came_go = swap(go, 1)
        grad_hidden, grad_attended, moe_part = call(
            turn_kernel,
            [((rows, D), F32), ((rows, D), BF), ((8, D), F32)],
            (lengths, came, slots, hidden, gain2, out_grad),
            [SM] + [VM] * 5,
            flops=2 * spots * rows * D,
            moved=8 * MIB,
            name="turn",
        )
        other_grad = swap(grad_attended, 1)
        away = (away.astype(F32) + came_go[1].astype(F32)).astype(BF)
        bwd_cost = dict(
            flops=2 * SEQ * D * 10 * inner + heads * SEQ * SEQ * 400, moved=9 * MIB, exps=heads * SEQ * SEQ
        )
        work = [
            pltpu.VMEM((SEQ, D), BF),
            pltpu.VMEM((inner, SEQ), BF),
            pltpu.VMEM((3 * inner, SEQ), BF),
            pltpu.VMEM((TILE, TILE), F32),
            pltpu.VMEM((TILE, TILE), F32),
        ]
        gpart, gbias1, npart = call(
            functools.partial(attn_bwd_kernel, None, False, heads),
            [((4 * inner, D), BF), ((8, 128), F32), ((SEQ, D), F32)],
            (lengths, pair_table, normed, wt1, ow1, qkvt1, mixt1, lse1, grad_attended, other_grad),
            [SM] + [VM] * 1 + [VM] * 8,
            scratch=work,
            name="attend_pair_back",
            **bwd_cost,
        )
        gpair = swap(gpart, 2)
        gown, gbias0, keep_n, send_n = call(
            functools.partial(attn_bwd_kernel, None, True, heads),
            [((4 * inner, D), F32), ((8, 128), F32), ((rows, D), F32), ((rows, D), BF)],
            (lengths, table, normed, wt, out_weight, qkvt0, mixt0, lse0, grad_attended, other_grad, npart),
            [SM] + [VM] * 1 + [VM] * 9,
            scratch=work + [pltpu.VMEM((SEQ, D), F32)],
            name="attend_own_back",
            **bwd_cost,
        )
        away, gpair, gown = lax.optimization_barrier((away, gpair, gown))
        came_away = swap(away, 2)
        got_n = swap(send_n, 1)
        grad_inputs, attn_part = call(
            last_kernel,
            [((rows, D), BF), ((8, D), F32)],
            (inputs, keep_n, got_n, gain1, grad_hidden),
            moved=6 * MIB,
            name="last",
        )
        wide = (gown + gpair.astype(F32)).astype(BF)
        wide = lax.psum(wide, "expert").astype(F32)
        outputs = call(
            output_kernel,
            [((rows, D), BF)],
            (lengths, came_out, slots, hidden),
            [SM] + [VM] * 3,
            flops=2 * spots * rows * D,
            moved=8 * MIB,
            name="outputs",
        )[0]
        go_stay = came_go[0]

    if line:
        router_sum = jnp.transpose(router_sum)
    else:
        gwt, gow = wide[: 3 * inner], wide[3 * inner :]
        own_bias = gbias0[:heads, :NB].reshape(1, -1)
        pair_bias = gbias1[:heads, :NB].reshape(1, -1)
        ranks = jnp.arange(4, dtype=jnp.int32)[:, None]
        bias_parts = jnp.where(ranks == rank, own_bias, 0.0) + jnp.where(
            ranks == (rank ^ 2), pair_bias, 0.0
        )
        small = jnp.concatenate(
            [attn_part[0], moe_part[0], jnp.transpose(grad_router).reshape(-1), bias_parts.reshape(-1)]
        )
        small = lax.psum(small, ("expert", "tensor"))
        attn_sum, moe_sum = small[:D], small[D : 2 * D]
        router_sum = small[2 * D : 2 * D + experts * D].reshape(D, experts)
        bias_sum = lax.dynamic_slice(
            small[2 * D + experts * D :].reshape(4, heads * NB), (rank, 0), (1, heads * NB)
        )
    grad_up, grad_down = (
        stay[rows_of].astype(F32) + go_stay[rows_of].astype(F32) + came_away[rows_of].astype(F32)
        for rows_of in (slice(0, D), slice(D, 2 * D))
    )
    return (
        outputs,
        grad_inputs,
        attn_sum,
        jnp.transpose(gwt).reshape(D, 3, inner),
        gow,
        jnp.transpose(bias_sum.reshape(heads, NB)),
        moe_sum,
        router_sum,
        grad_up[None],
        jnp.transpose(grad_down)[None],
    )


def solution(mesh):
    return jax.shard_map(
        shards,
        mesh=mesh,
        in_specs=(
            P(("expert", "tensor"), None),
            P("expert"),
            P(("expert", "tensor"), None),
            P(),
            P(None, None, "tensor"),
            P("tensor", None),
            P(None, "tensor"),
            P(),
            P(),
            P("expert", None, "tensor"),
            P("expert", "tensor", None),
            P(("expert", "tensor"), None),
        ),
        out_specs=(
            P(("expert", "tensor"), None),
            P(("expert", "tensor"), None),
            P(),
            P(None, None, "tensor"),
            P("tensor", None),
            P(None, "tensor"),
            P(),
            P(),
            P("expert", None, "tensor"),
            P("expert", "tensor", None),
        ),
        check_vma=False,
    )
```

```python
import functools

import jax
import jax.numpy as jnp
from jax import lax
from jax.experimental import pallas as pl
from jax.experimental.pallas import tpu as pltpu
from jax.sharding import PartitionSpec as P

D = 768
HD = 64
NB = 32
MAXDIST = 128
SEQ = 1024
EPSILON = 1e-06
NEGATIVE = -1e30
TILE = 256
BF = jnp.bfloat16
F32 = jnp.float32
MIB = 2**20
CHUNK = 256
GELU = 0.7978845608028654
CUBIC = 0.044715


def bucket_edges():
    half_count = NB // 2
    short_edges = list(range(1, half_count))
    long_edges = [
        int(half_count * (MAXDIST / half_count) ** (step_index / half_count))
        for step_index in range(half_count)
    ]
    return short_edges + long_edges


EDGES = bucket_edges()


def dot(a, b, ca=1, cb=0, precision=None):
    return lax.dot_general(
        a, b, (((ca,), (cb,)), ((), ())), preferred_element_type=F32, precision=precision
    )


def iota(shape, dim):
    return lax.broadcasted_iota(jnp.int32, shape, dim)


def rms(v):
    return lax.rsqrt(jnp.mean(v * v, axis=-1, keepdims=True) + EPSILON)


def call(kernel, outs, args, specs=None, scratch=(), flops=0, moved=0, exps=0, vmem=56, name=None):
    vm = pl.BlockSpec(memory_space=pltpu.VMEM)
    return pl.pallas_call(
        kernel,
        out_shape=[jax.ShapeDtypeStruct(s, d) for s, d in outs],
        in_specs=specs or [vm] * len(args),
        out_specs=[vm] * len(outs),
        scratch_shapes=list(scratch),
        compiler_params=pltpu.CompilerParams(vmem_limit_bytes=vmem * MIB),
        cost_estimate=pl.CostEstimate(flops=flops, bytes_accessed=moved, transcendentals=exps),
        name=name,
    )(*args)


def own_length(lengths_ref):
    return lengths_ref[lax.axis_index("tensor") // 2]


def own_valid(lengths_ref, rows):
    half = lax.rem(lax.axis_index("tensor"), 2)
    return jnp.clip(own_length(lengths_ref) - half * rows, 0, rows)


def as_row(ref):
    return ref[...].reshape(1, D)


VM = pl.BlockSpec(memory_space=pltpu.VMEM)
SM = pl.BlockSpec(memory_space=pltpu.SMEM)


def slot_lines(experts, cap, valid_count, routes):
    rows = routes.shape[1]
    valid = iota((1, rows), 1) < valid_count
    ids = iota((experts, rows), 0)
    hot0 = ((ids == routes[0:1]) & valid).astype(F32)
    hot1 = ((ids == routes[1:2]) & valid).astype(F32)
    before = (iota((rows, rows), 0) < iota((rows, rows), 1)).astype(BF)
    rank = dot((hot0 + hot1).astype(BF), before)
    place = ids.astype(F32) * cap + rank
    bad = jnp.where(valid, 0.0, 1.0)
    slot0 = jnp.sum(hot0 * place, axis=0, keepdims=True) - bad
    slot1 = jnp.sum(hot1 * place, axis=0, keepdims=True) - bad
    return slot0, slot1


def route_kernel(experts, cap, lengths_ref, routes_ref, grad_ref, packed_ref, slots_ref):
    rows = grad_ref.shape[0]
    slot0, slot1 = slot_lines(experts, cap, own_valid(lengths_ref, routes_ref.shape[1]), routes_ref[...])
    spots = iota((experts * cap, rows), 0)
    pick0 = spots == slot0.astype(jnp.int32)
    pick1 = spots == slot1.astype(jnp.int32)
    packed_ref[...] = dot((pick0 | pick1).astype(BF), grad_ref[...]).astype(BF)
    slots_ref[...] = jnp.concatenate([slot0, slot1, jnp.zeros((6, rows), F32)], axis=0)


def slots_kernel(experts, cap, lengths_ref, routes_ref, slots_ref):
    rows = routes_ref.shape[1]
    slot0, slot1 = slot_lines(experts, cap, own_valid(lengths_ref, routes_ref.shape[1]), routes_ref[...])
    slots_ref[...] = jnp.concatenate([slot0, slot1, jnp.zeros((6, rows), F32)], axis=0)


def back_matrix(slots_ref, spots):
    rows = slots_ref.shape[1]
    where = iota((rows, spots), 1)
    slots = slots_ref[...].T.astype(jnp.int32)
    return ((where == slots[:, 0:1]) | (where == slots[:, 1:2])).astype(BF)


def bias_tiles(table_ref, head):
    dist = iota((8, TILE), 1)
    line = table_ref[head : head + 1, :]
    line = line - line[:, NB - 1 :]
    curve = jnp.broadcast_to(line[:, 0:1], (8, TILE))
    for number, edge in enumerate(EDGES):
        curve = jnp.where(dist >= edge, line[:, number + 1 : number + 2], curve)
    spread = jnp.broadcast_to(curve[0:1], (TILE, TILE))
    ring = pltpu.roll(spread, 0, 1, stride=1, stride_axis=0)
    ahead = iota((TILE, TILE), 1) >= iota((TILE, TILE), 0)
    return jnp.where(ahead, ring, NEGATIVE), jnp.where(ahead, 0.0, ring)


def head_pieces(qkvt_ref, mask_rows, head, local_inner):
    start = pl.multiple_of(head * HD, HD)
    q = qkvt_ref[pl.ds(start, HD), :] * jnp.asarray(HD**-0.5, BF)
    k = qkvt_ref[pl.ds(local_inner + start, HD), :]
    v = qkvt_ref[pl.ds(2 * local_inner + start, HD), :]
    ones = jnp.ones((16, SEQ), BF)
    return jnp.concatenate([q, ones], 0), jnp.concatenate([k, mask_rows], 0), v, ones


def mask_block(length):
    keep = (iota((16, SEQ), 1) < length) | (iota((16, SEQ), 0) > 0)
    return jnp.where(keep, 0.0, NEGATIVE).astype(BF)


def score_pieces(k, q, block, near, below):
    cols = slice(block * TILE, (block + 1) * TILE)
    qb = q[:, cols]
    pieces = []
    if block >= 2:
        pieces.append((0, (block - 1) * TILE, dot(k[: (block - 1) * TILE], qb)))
    if block >= 1:
        lo = (block - 1) * TILE
        pieces.append((lo, block * TILE, dot(k[lo : lo + TILE], qb) + below))
    lo = block * TILE
    pieces.append((lo, lo + TILE, dot(k[lo : lo + TILE], qb) + near))
    return cols, pieces


def attn_fwd_kernel(first, heads, lengths_ref, table_ref, *refs):
    if first:
        own_ref, other_ref, gain_ref, w_ref, ow_ref = refs[:5]
        normed_ref, qkvt_ref, mixt_ref, lse_ref, part_ref = refs[5:]
        half = own_ref.shape[0]
        core = lax.rem(lax.axis_index("tensor"), 2)
        for source, place in ((own_ref, core), (other_ref, 1 - core)):
            x = source[...].astype(F32)
            normed_ref[pl.ds(pl.multiple_of(place * half, half), half), :] = (
                x * rms(x) * as_row(gain_ref)
            ).astype(BF)
    else:
        normed_ref, w_ref, ow_ref, part_in = refs[:4]
        qkvt_ref, mixt_ref, lse_ref, keep_ref, send_ref, part_ref = refs[4:]
    local_inner = heads * HD
    qkvt_ref[...] = dot(w_ref[...], normed_ref[...], 1, 1).astype(BF)
    masks = mask_block(own_length(lengths_ref))
    lse_ref[...] = jnp.zeros_like(lse_ref)

    for head in range(heads):
        near, below = bias_tiles(table_ref, head)
        q, kt, v, ones = head_pieces(qkvt_ref, masks, head, local_inner)
        k = kt.T
        vx = jnp.concatenate([v, ones], 0)
        for block in range(SEQ // TILE):
            cols, pieces = score_pieces(k, q, block, near, below)
            top = functools.reduce(
                jnp.maximum, [jnp.max(s, axis=0, keepdims=True) for _, _, s in pieces]
            )
            total = None
            for lo, hi, s in pieces:
                term = dot(vx[:, lo:hi], jnp.exp(s - top).astype(BF))
                total = term if total is None else total + term
            weight = total[HD : HD + 1]
            mixt_ref[head * HD : (head + 1) * HD, cols] = (total[:HD] / weight).astype(BF)
            lse_ref[head : head + 1, cols] = top + jnp.log(weight)
    part = dot(mixt_ref[...], ow_ref[...], 0, 0)
    if first:
        part_ref[...] = part
    else:
        part_ref[...] = part + part_in[...]
        half = keep_ref.shape[0]
        core = lax.rem(lax.axis_index("tensor"), 2)
        keep_ref[...] = part_ref[pl.ds(pl.multiple_of(core * half, half), half), :]
        send_ref[...] = part_ref[pl.ds(pl.multiple_of((1 - core) * half, half), half), :].astype(BF)


def attn_bwd_kernel(early, last, heads, lengths_ref, table_ref, *refs):
    if last:
        (normed_ref, w_ref, ow_ref, qkvt_ref, mixt_ref, lse_ref, own_ref, other_ref, part_in) = refs[:9]
        gw_ref, gbias_ref, keep_ref, send_ref, ga_ref, got_ref, gt_ref, d0_ref, d1_ref, part_ref = refs[9:]
    else:
        (normed_ref, w_ref, ow_ref, qkvt_ref, mixt_ref, lse_ref, own_ref, other_ref) = refs[:8]
        gw_ref, gbias_ref, part_ref, ga_ref, got_ref, gt_ref, d0_ref, d1_ref = refs[8:]
    local_inner = heads * HD
    half = own_ref.shape[0]
    core = lax.rem(lax.axis_index("tensor"), 2)
    ga_ref[pl.ds(pl.multiple_of(core * half, half), half), :] = own_ref[...]
    ga_ref[pl.ds(pl.multiple_of((1 - core) * half, half), half), :] = other_ref[...]
    got_ref[...] = dot(ow_ref[...], ga_ref[...], 1, 1).astype(BF)
    gw_ref[3 * local_inner :] = dot(mixt_ref[...], ga_ref[...]).astype(gw_ref.dtype)
    if early is not None:
        early()
    masks = mask_block(own_length(lengths_ref))
    gbias_ref[...] = jnp.zeros_like(gbias_ref)
    ahead = iota((TILE, TILE), 1) >= iota((TILE, TILE), 0)
    spot = (iota((TILE, 128), 0) + 1) % TILE
    flip = (iota((TILE, TILE), 0) + iota((TILE, TILE), 1) == TILE - 1).astype(F32)
    bucket = jnp.zeros((TILE, 128), jnp.int32)
    for edge in EDGES:
        bucket = bucket + (spot >= edge).astype(jnp.int32)
    hot = (bucket == iota((TILE, 128), 1)).astype(F32)

    for head in range(heads):
        near, below = bias_tiles(table_ref, head)
        q, kt, vt, _ = head_pieces(qkvt_ref, masks, head, local_inner)
        k = kt.T
        v = vt.T
        rows = slice(head * HD, (head + 1) * HD)
        gt = got_ref[rows, :]
        delta = jnp.sum(gt.astype(F32) * mixt_ref[rows, :].astype(F32), axis=0, keepdims=True)
        gk = [None] * (SEQ // TILE)
        gv = [None] * (SEQ // TILE)
        far = jnp.zeros((8, TILE), F32)
        for block in range(SEQ // TILE):
            cols, pieces = score_pieces(k, q, block, near, below)
            gb = gt[:, cols]
            qb = q[:HD, cols]
            lse = lse_ref[head : head + 1, cols]
            db = delta[:, cols]
            gq = None
            for lo, hi, s in pieces:
                p = jnp.exp(s - lse)
                ds = p * (dot(v[lo:hi], gb) - db)
                pb = p.astype(BF)
                dsb = ds.astype(BF)
                term = dot(kt[:HD, lo:hi], dsb)
                gq = term if gq is None else gq + term
                tv = dot(pb, gb, 1, 1)
                tk = dot(dsb, qb, 1, 1)
                for tile in range(lo // TILE, hi // TILE):
                    part = slice(tile * TILE - lo, (tile + 1) * TILE - lo)
                    gv[tile] = tv[part] if gv[tile] is None else gv[tile] + tv[part]
                    gk[tile] = tk[part] if gk[tile] is None else gk[tile] + tk[part]
                if hi == (block + 1) * TILE:
                    d0_ref[...] = ds if block == 0 else d0_ref[...] + ds
                elif hi == block * TILE and lo == (block - 1) * TILE:
                    d1_ref[...] = ds if block == 1 else d1_ref[...] + ds
                else:
                    far = far + jnp.sum(ds.reshape((hi - lo) // 8, 8, TILE), axis=0)
            gt_ref[rows, cols] = (gq * HD**-0.5).astype(BF)
        for tile in range(SEQ // TILE):
            cols = slice(tile * TILE, (tile + 1) * TILE)
            gt_ref[local_inner + head * HD : local_inner + (head + 1) * HD, cols] = (
                gk[tile].T.astype(BF)
            )
            gt_ref[2 * local_inner + head * HD : 2 * local_inner + (head + 1) * HD, cols] = (
                gv[tile].T.astype(BF)
            )
        d1 = d1_ref[...]
        ring = jnp.where(ahead, d0_ref[...], d1)
        turned = pltpu.roll(
            dot(flip, ring, 1, 0, lax.Precision.HIGHEST), 0, 1, stride=1, stride_axis=0
        )
        far = far + jnp.sum(jnp.where(ahead, d1, 0.0).reshape(TILE // 8, 8, TILE), axis=0)
        line = jnp.sum(turned, axis=0, keepdims=True)
        sums = dot(
            jnp.broadcast_to(line, (8, TILE)), hot, 1, 0, lax.Precision.HIGHEST
        )
        sums = sums + jnp.where(iota((8, 128), 1) == NB - 1, jnp.sum(far), 0.0)
        gbias_ref[head : head + 1, :] = sums[0:1]
    gw_ref[: 3 * local_inner] = dot(gt_ref[...], normed_ref[...]).astype(gw_ref.dtype)
    part = dot(gt_ref[...], w_ref[...], 0, 0)
    if last:
        part_ref[...] = part + part_in[...]
        keep_ref[...] = part_ref[pl.ds(pl.multiple_of(core * half, half), half), :]
        send_ref[...] = part_ref[pl.ds(pl.multiple_of((1 - core) * half, half), half), :].astype(BF)
    else:
        part_ref[...] = part


def gates_of(experts, normed, router_t, routes):
    rows = normed.shape[0]
    logits = dot(router_t, normed, 1, 1)
    ids = iota((experts, rows), 0)
    signs = (ids == routes[0:1]).astype(F32) - (ids == routes[1:2]).astype(F32)
    gap = jnp.sum(logits * signs, axis=0, keepdims=True)
    return 1.0 / (1.0 + jnp.exp(-gap)), 1.0 / (1.0 + jnp.exp(gap))


def meta_lines(gate, code):
    rows = gate.shape[1]
    line = iota((8, rows), 0)
    high = gate.astype(BF).astype(F32)
    mid = (gate - high).astype(BF).astype(F32)
    low = gate - high - mid
    picked = jnp.where(line == 0, high, jnp.where(line == 1, mid, jnp.where(line == 2, low, 0.0)))
    return jnp.where(line == 3, code, picked).astype(BF)


def hidden_rows(x_ref, keep_ref, got_ref, gain_ref, hidden_ref):
    hidden = x_ref[...].astype(F32) + keep_ref[...] + got_ref[...].astype(F32)
    hidden_ref[...] = hidden
    return (hidden * rms(hidden) * as_row(gain_ref)).astype(BF)


def middle_kernel(
    experts, cap, x_ref, keep_ref, got_ref, gain_ref, router_ref, routes_ref, slots_ref, hidden_ref, packed_ref, meta_ref
):
    normed = hidden_rows(x_ref, keep_ref, got_ref, gain_ref, hidden_ref)
    slots = slots_ref[...].astype(jnp.int32)
    routes = routes_ref[...]
    where = iota((experts * cap, normed.shape[0]), 0)
    pick0 = where == slots[0:1]
    pick1 = where == slots[1:2]
    packed_ref[...] = dot((pick0 | pick1).astype(BF), normed).astype(BF)
    gate0, gate1 = gates_of(experts, normed, router_ref[...], routes)
    codes = (routes + 1).astype(F32)
    meta = dot(meta_lines(gate0, codes[1:2]), pick0.astype(BF), 1, 1) + dot(
        meta_lines(gate1, codes[0:1]), pick1.astype(BF), 1, 1
    )
    for number in range(experts):
        meta_ref[number] = meta[:, number * cap : (number + 1) * cap]


def middle_line_kernel(
    experts, x_ref, keep_ref, got_ref, gain_ref, router_ref, routes_ref, slots_ref, hidden_ref, normed_ref, info_ref
):
    normed = hidden_rows(x_ref, keep_ref, got_ref, gain_ref, hidden_ref)
    normed_ref[...] = normed
    routes = routes_ref[...]
    gate0, gate1 = gates_of(experts, normed, router_ref[...], routes)
    codes = (routes + 1).astype(F32)
    info_ref[...] = jnp.concatenate(
        [slots_ref[0:2], gate0, gate1, codes, jnp.zeros((2, normed.shape[0]), F32)], axis=0
    )


def gelu_pair(v):
    squared = v * v
    slope = GELU * (1.0 + 3 * CUBIC * squared)
    t = jnp.tanh(v * (GELU + GELU * CUBIC * squared))
    half = 0.5 + 0.5 * t
    return v * half, half + 0.5 * v * (1.0 - t * t) * slope


def flipped(me, k, count):
    total, bit = 0, 1
    while bit < count:
        total = total + lax.rem(me // bit + k // bit, 2) * bit
        bit *= 2
    return total


def weight_grads(xt_ref, geot_ref, act_ref, gi_ref, stage_ref, turned_ref, stay_ref, away_ref, go_ref, out_sem):
    tiles = D // TILE
    steps = 8 * tiles

    def columns(step):
        return pl.ds(pl.multiple_of(lax.rem(step, tiles) * TILE, TILE), TILE)

    def store(step, slot, out_ref, half):
        if half:
            there = pl.ds(pl.multiple_of(D + lax.rem(step, tiles) * TILE, TILE), TILE)
            return pltpu.make_async_copy(turned_ref.at[slot], out_ref.at[there], out_sem.at[slot])
        return pltpu.make_async_copy(stage_ref.at[slot], out_ref.at[:D, columns(step)], out_sem.at[slot])

    def weights(step, carry):
        q = step // (2 * tiles)
        half = lax.rem(step, 2 * tiles) // tiles
        slot = lax.rem(step, 2)

        outs = (stay_ref, away_ref, go_ref.at[0], go_ref.at[1])

        @pl.when(step >= 2)
        def _():
            store(step - 2, slot, stay_ref, 0).wait()

        @pl.when(half == 0)
        def _():
            stage_ref[slot] = dot(xt_ref[...], gi_ref[q, :, columns(step)]).astype(BF)

        @pl.when(half == 1)
        def _():
            turned_ref[slot] = dot(geot_ref[...], act_ref[q, :, columns(step)]).astype(BF).T

        for number, out_ref in enumerate(outs):
            for kind in range(2):

                @pl.when((q == number) & (half == kind))
                def _():
                    store(step, slot, out_ref, kind).start()

        return carry

    lax.fori_loop(0, steps, weights, 0)
    for step in (steps - 2, steps - 1):
        store(step, step % 2, stay_ref, 1).wait()


def expert_rows(ready, x, geo, here, w_ref, xt_ref, geot_ref, act_ref, gi_ref, acc_ref):
    xt_ref[:, here] = x.T
    geot_ref[:, here] = geo.T
    worth = 0.0
    for q in (0, 2, 1, 3):
        if q == 1:
            ready()
        inner = dot(x, w_ref[q, :D])
        grad_active = dot(geo, w_ref[q, D:], 1, 1)
        act, slope = gelu_pair(inner)
        gi = (slope * grad_active).astype(BF)
        act_ref[q, here] = act.astype(BF)
        gi_ref[q, here] = gi
        back = dot(gi, w_ref[q, :D], 1, 1)
        if q == 0:
            acc_ref[...] = back
        else:
            acc_ref[...] += back
        worth = worth + jnp.sum(act * grad_active, axis=1, keepdims=True)
    return worth


def expert_outs(start, size, column, act_ref, w_ref):
    here = pl.ds(pl.multiple_of(start, size), size)
    cols = pl.ds(pl.multiple_of(column * TILE, TILE), TILE)
    total = None
    for q in range(4):
        term = dot(act_ref[q, here], w_ref[q, D:, cols])
        total = term if total is None else total + term
    return cols, total


def expert_kernel(
    count, cap, packed_ref, send_meta_ref, grads_ref, router_ref, w0, w1, w2, w3,
    came_ref, result_ref, stay_ref, away_ref, go_ref, grouter_ref,
    w_ref, x_ref, xt_ref, geot_ref, act_ref, gi_ref, gsend_ref, meta_ref, acc_ref, stage_ref, turned_ref,
    x_send, x_recv, m_send, m_recv, r_send, r_recv, local_sem, w_sem, out_sem,
):
    me = lax.axis_index("expert")
    barrier = pltpu.get_barrier_semaphore()

    def peer(k):
        return flipped(me, k, count)

    source = peer

    def greet(k, carry):
        pl.semaphore_signal(
            barrier, inc=1, device_id={"expert": peer(k)}, device_id_type=pl.DeviceIdType.MESH
        )
        return carry

    lax.fori_loop(1, count, greet, 0)
    pl.semaphore_wait(barrier, count - 1)

    def rows_of(k):
        return pl.ds(pl.multiple_of(k * cap, cap), cap)

    def send_rows(k):
        return pltpu.make_async_remote_copy(
            src_ref=packed_ref.at[rows_of(peer(k))],
            dst_ref=x_ref.at[rows_of(k)],
            send_sem=x_send.at[k],
            recv_sem=x_recv.at[k],
            device_id={"expert": peer(k)},
            device_id_type=pl.DeviceIdType.MESH,
        )

    def send_meta(k):
        return pltpu.make_async_remote_copy(
            src_ref=send_meta_ref.at[peer(k)],
            dst_ref=meta_ref.at[k],
            send_sem=m_send.at[k],
            recv_sem=m_recv.at[k],
            device_id={"expert": peer(k)},
            device_id_type=pl.DeviceIdType.MESH,
        )

    def send_back(k):
        return pltpu.make_async_remote_copy(
            src_ref=gsend_ref.at[rows_of(k)],
            dst_ref=came_ref.at[rows_of(me)],
            send_sem=r_send.at[k],
            recv_sem=r_recv.at[k],
            device_id={"expert": source(k)},
            device_id_type=pl.DeviceIdType.MESH,
        )

    def start_sends(k, carry):
        send_meta(k).start()
        send_rows(k).start()
        return carry

    lax.fori_loop(count // 2, count, start_sends, 0)
    lax.fori_loop(1, count // 2, start_sends, 0)
    own_rows = pltpu.make_async_copy(packed_ref.at[rows_of(me)], x_ref.at[rows_of(0)], local_sem.at[0])
    own_rows.start()
    own_meta = pltpu.make_async_copy(send_meta_ref.at[me], meta_ref.at[0], local_sem.at[1])
    own_meta.start()
    loads = [
        pltpu.make_async_copy(w, w_ref.at[i], w_sem.at[i]) for i, w in enumerate((w0, w1, w2, w3))
    ]
    for load in loads:
        load.start()
    grouter_ref[...] = jnp.zeros_like(grouter_ref)
    experts = router_ref.shape[1]
    own_rows.wait()
    own_meta.wait()
    for load in loads:
        load.wait()
    group = max(1, CHUNK // cap)
    span = group * cap

    def chunk(j, carry):
        for i in range(group):
            k = j * group + i

            @pl.when(k > 0)
            def _():
                send_rows(k).wait_recv()
                send_meta(k).wait_recv()

        here = pl.ds(pl.multiple_of(j * span, span), span)
        meta = jnp.concatenate([meta_ref[j * group + i].T for i in range(group)], axis=0)
        gate = meta[:, 0:1] + meta[:, 1:2] + meta[:, 2:3]
        code = meta[:, 3:4].astype(jnp.int32)
        gy = jnp.concatenate([grads_ref[rows_of(source(j * group + i)), :] for i in range(group)], axis=0)
        geo = (gate * gy.astype(F32)).astype(BF)
        x = x_ref[here, :]
        worth = expert_rows(lambda: None, x, geo, here, w_ref, xt_ref, geot_ref, act_ref, gi_ref, acc_ref)
        ids = iota((span, experts), 1)
        signs = (ids == me).astype(F32) - (ids + 1 == code).astype(F32)
        share = jnp.where(code > 0, (1.0 - gate) * worth, 0.0) * signs
        high = share.astype(BF)
        low = (share - high.astype(F32)).astype(BF)
        gsend_ref[here, :] = (acc_ref[...] + dot(high, router_ref[...], 1, 1)).astype(BF)
        grouter_ref[...] += dot(high.T, x) + dot(low.T, x)
        for i in range(group):
            k = j * group + i

            @pl.when(k > 0)
            def _():
                send_back(k).start()

        return carry

    lax.fori_loop(0, count // group, chunk, 0)
    own_back = pltpu.make_async_copy(gsend_ref.at[rows_of(0)], came_ref.at[rows_of(me)], local_sem.at[0])
    own_back.start()

    def results(step, carry):
        j = step // (D // TILE)
        meta = jnp.concatenate([meta_ref[j * group + i].T for i in range(group)], axis=0)
        gate = meta[:, 0:1] + meta[:, 1:2] + meta[:, 2:3]
        cols, total = expert_outs(j * span, span, lax.rem(step, D // TILE), act_ref, w_ref)
        out = (gate * total).astype(BF)
        for i in range(group):
            result_ref[rows_of(source(j * group + i)), cols] = out[i * cap : (i + 1) * cap]
        return carry

    lax.fori_loop(0, count // group * (D // TILE), results, 0)
    weight_grads(xt_ref, geot_ref, act_ref, gi_ref, stage_ref, turned_ref, stay_ref, away_ref, go_ref, out_sem)
    own_back.wait()

    def finish(k, carry):
        send_rows(k).wait_send()
        send_meta(k).wait_send()
        send_back(k).wait()
        return carry

    lax.fori_loop(1, count, finish, 0)


def mesh_copy(src, dst, send_sem, recv_sem, target):
    return pltpu.make_async_remote_copy(
        src_ref=src,
        dst_ref=dst,
        send_sem=send_sem,
        recv_sem=recv_sem,
        device_id={"expert": target},
        device_id_type=pl.DeviceIdType.MESH,
    )


LINE = 4


def expert_line_kernel(
    cap, normed_ref, info_in, router_ref, grads_in, near_ref, near_info_ref, up_ref, down_ref, far_up_ref, far_half_ref,
    came_ref, result_out, stay_ref, away_ref, go_ref, grouter_ref,
    result_ref, grads_ref, w_ref, block_ref, info_ref, x_ref, xs_ref, meta_ref, ms_ref, xt_ref, geot_ref, act_ref, gi_ref, acc_ref, stage_ref, turned_ref,
    b_send, b_recv, i_send, i_recv, x_send, x_recv, m_send, m_recv, r_send, r_recv, local_sem, w_sem, v_send, v_recv, y_send, y_recv, grads_sem, near_sem, out_sem,
):
    count = 2 * LINE
    me = lax.axis_index("expert")
    place = me // 2
    side = me - 2 * place
    mate = me + 1 - 2 * side
    barrier = pltpu.get_barrier_semaphore()

    def greet(k, carry):
        pl.semaphore_signal(
            barrier,
            inc=1,
            device_id={"expert": lax.rem(me + k, count)},
            device_id_type=pl.DeviceIdType.MESH,
        )
        return carry

    lax.fori_loop(1, count, greet, 0)
    core = flipped(lax.axis_index("tensor"), 1, 4)
    pl.semaphore_signal(
        barrier, inc=1, device_id={"tensor": core}, device_id_type=pl.DeviceIdType.MESH
    )
    away = flipped(lax.axis_index("tensor"), 2, 4)
    pl.semaphore_signal(
        barrier, inc=1, device_id={"tensor": away}, device_id_type=pl.DeviceIdType.MESH
    )
    pl.semaphore_wait(barrier, count + 1)

    def along(block, step):
        return (
            mesh_copy(
                info_ref.at[block],
                info_ref.at[block],
                i_send.at[(step + 1) // 2, block],
                i_recv.at[block],
                me + 2 * step,
            ),
            mesh_copy(
                block_ref.at[block],
                block_ref.at[block],
                b_send.at[(step + 1) // 2, block],
                b_recv.at[block],
                me + 2 * step,
            ),
        )

    def across(block):
        return (
            mesh_copy(ms_ref.at[block], meta_ref.at[1, block], m_send.at[block], m_recv.at[block], mate),
            mesh_copy(xs_ref.at[block], x_ref.at[1, block], x_send.at[block], x_recv.at[block], mate),
        )

    def rows_of(number):
        return pl.ds(pl.multiple_of(number * cap, cap), cap)

    def origin(part, block):
        return 2 * block + side + part * (1 - 2 * side)

    def give_back(part, block):
        return mesh_copy(
            x_ref.at[part, block],
            came_ref.at[rows_of(me)],
            r_send.at[part, block],
            r_recv.at[me],
            origin(part, block),
        )

    def each(pair, act):
        for one in pair:
            act(one)

    own = (
        pltpu.make_async_copy(info_in, info_ref.at[place], local_sem.at[0]),
        pltpu.make_async_copy(normed_ref, block_ref.at[place], local_sem.at[1]),
    )
    each(own, lambda c: c.start())
    rest = D // 4 * 3
    far_down = tensor_copy(down_ref.at[rest:], w_ref.at[1, D + rest :], y_send, y_recv, away)
    far_down.start()
    grads_load = pltpu.make_async_copy(grads_in, grads_ref, grads_sem)
    grads_load.start()
    near = [
        (
            pltpu.make_async_copy(near_info_ref.at[i], info_ref.at[place + 2 * i - 1], near_sem.at[i]),
            pltpu.make_async_copy(near_ref.at[i], block_ref.at[place + 2 * i - 1], near_sem.at[i + 2]),
        )
        for i in range(2)
    ]
    inside = [place > 0, place < LINE - 1]
    for i in range(2):

        @pl.when(inside[i])
        def _():
            each(near[i], lambda c: c.start())

    weights = (
        (up_ref, 0, 0, D), (down_ref, 0, D, D), (far_up_ref, 1, 0, D), (far_half_ref, 1, D, rest),
        (w_ref.at[1, D + rest :], 1, D + rest, D - rest),
    )

    def load(i):
        source, q, start, size = weights[i]
        return pltpu.make_async_copy(source, w_ref.at[q, start : start + size], w_sem.at[i])

    def lend(i):
        source, q, start, size = weights[i]
        return tensor_copy(source, w_ref.at[2 + q, start : start + size], v_send.at[i], v_recv.at[i], core)

    for i in range(2):

        @pl.when(inside[i])
        def _():
            each(near[i], lambda c: c.wait())

            @pl.when(inside[1 - i])
            def _():
                each(along(place + 2 * i - 1, 1 - 2 * i), lambda c: c.start())

    for i in range(4):
        load(i).start()
        lend(i).start()
    each(own, lambda c: c.wait())
    experts = router_ref.shape[0]
    rows = normed_ref.shape[0]

    def select(block):
        info = info_ref[block]
        slots = info[0:2].astype(jnp.int32)
        lines0 = meta_lines(info[2:3], info[5:6])
        lines1 = meta_lines(info[3:4], info[4:5])
        for part, expert in ((1, mate), (0, me)):
            where = iota((cap, rows), 0) + expert * cap
            pick0 = where == slots[0:1]
            pick1 = where == slots[1:2]
            taken = dot((pick0 | pick1).astype(BF), block_ref[block]).astype(BF)
            meta = dot(lines0, pick0.astype(BF), 1, 1) + dot(lines1, pick1.astype(BF), 1, 1)
            if part:
                xs_ref[block] = taken
                ms_ref[block] = meta
                each(across(block), lambda c: c.start())
            else:
                x_ref[0, block] = taken
                meta_ref[0, block] = meta

    select(place)
    grouter_ref[...] = jnp.zeros_like(grouter_ref)
    mirror = place // 2
    inward = place + mirror * (LINE - 1 - 2 * place)

    def block_at(i):
        step = i + inward * (1 - i // 2 - 2 * (i // 2 - i // (LINE - 1)))
        return step + mirror * (LINE - 1 - 2 * step)

    outer = sum(d * 8**i for i, d in enumerate((0, 1, 4, 2, 5, 3, 6, 7)))
    inner = sum(d * 8**i for i, d in enumerate((0, 1, 4, 2, 5, 3, 6, 7)))
    chunks = outer + inward * (inner - outer)

    def chunk_at(power):
        digit = lax.rem(chunks // power, 8)
        return digit // 4, block_at(lax.rem(digit, 4))

    for i in range(2):

        @pl.when(inside[i])
        def _():
            select(place + 2 * i - 1)

    grads_load.wait()
    for i in range(2):
        load(i).wait()
        lend(i).wait_recv()

    def far_ready(c):
        @pl.when(c == 0)
        def _():
            far_down.wait_recv()
            lend(4).start()
            for i in (2, 3):
                load(i).wait()
                lend(i).wait_recv()
            lend(4).wait_recv()


    def chunk(c, power):
        for distance in range(2, LINE):

            @pl.when(c == 4 * distance - 7)
            def _():
                line_accept(place, distance, along, select)

        part, block = chunk_at(power)

        @pl.when(part == 1)
        def _():
            each(across(block), lambda c: c.wait_recv())

        here = pl.ds(pl.multiple_of(c * cap, cap), cap)
        meta = meta_ref[part, block].T
        gate = meta[:, 0:1] + meta[:, 1:2] + meta[:, 2:3]
        code = meta[:, 3:4].astype(jnp.int32)
        geo = (gate * grads_ref[part, block].astype(F32)).astype(BF)
        x = x_ref[part, block]
        worth = expert_rows(lambda: far_ready(c), x, geo, here, w_ref, xt_ref, geot_ref, act_ref, gi_ref, acc_ref)
        ids = iota((cap, experts), 1)
        signs = (ids == me).astype(F32) - (ids + 1 == code).astype(F32)
        share = jnp.where(code > 0, (1.0 - gate) * worth, 0.0) * signs
        high = share.astype(BF)
        low = (share - high.astype(F32)).astype(BF)
        grouter_ref[...] += dot(high.T, x) + dot(low.T, x)
        x_ref[part, block] = (acc_ref[...] + dot(high, router_ref[...])).astype(BF)

        @pl.when(origin(part, block) != me)
        def _():
            give_back(part, block).start()

        return power * 8

    lax.fori_loop(0, count, chunk, jnp.int32(1))
    own_back = pltpu.make_async_copy(x_ref.at[0, place], came_ref.at[rows_of(me)], local_sem.at[0])
    own_back.start()

    def results(step, carry):
        first = step // (D // TILE) * LINE
        cols, total = expert_outs(first * cap, LINE * cap, lax.rem(step, D // TILE), act_ref, w_ref)
        for i in range(LINE):
            part, block = chunk_at((1 + first // LINE * (8**LINE - 1)) * 8**i)
            meta = meta_ref[part, block].T
            gate = meta[:, 0:1] + meta[:, 1:2] + meta[:, 2:3]
            result_ref[rows_of(origin(part, block)), cols] = (
                gate * total[i * cap : (i + 1) * cap]
            ).astype(BF)
        return carry

    lax.fori_loop(0, 2 * (D // TILE), results, 0)
    leave = pltpu.make_async_copy(result_ref, result_out, local_sem.at[1])
    leave.start()
    weight_grads(xt_ref, geot_ref, act_ref, gi_ref, stage_ref, turned_ref, stay_ref, away_ref, go_ref, out_sem)
    own_back.wait()
    leave.wait()
    for i in range(5):
        lend(i).wait_send()
    far_down.wait_send()
    line_sent(place, along, 1)
    for block in range(LINE):
        each(across(block), lambda c: c.wait_send())
        for part in (0, 1):

            @pl.when(origin(part, block) != me)
            def _():
                give_back(part, block).wait_send()

    for number in range(count):

        @pl.when(number != me)
        def _():
            mesh_copy(
                x_ref.at[0, 0], came_ref.at[rows_of(number)], r_send.at[0, 0], r_recv.at[number], mate
            ).wait_recv()


def turn_kernel(lengths_ref, came_ref, slots_ref, hidden_ref, gain_ref, grad_ref, gh_ref, ga_ref, gain_out):
    gn = dot(back_matrix(slots_ref, came_ref.shape[0]), came_ref[...])
    hidden = hidden_ref[...]
    scale = rms(hidden)
    unit = hidden * scale
    gain_out[...] = jnp.broadcast_to(jnp.sum(gn * unit, axis=0, keepdims=True), gain_out.shape)
    g = gn * as_row(gain_ref)
    valid = (iota((hidden.shape[0], 1), 0) < own_valid(lengths_ref, hidden.shape[0])).astype(F32)
    gh = scale * (g - unit * jnp.mean(g * unit, axis=1, keepdims=True)) + valid * grad_ref[...].astype(F32)
    gh_ref[...] = gh
    ga_ref[...] = gh.astype(BF)


def output_kernel(lengths_ref, came_ref, slots_ref, hidden_ref, out_ref):
    mix = dot(back_matrix(slots_ref, came_ref.shape[0]), came_ref[...])
    hidden = hidden_ref[...]
    valid = (iota((hidden.shape[0], 1), 0) < own_valid(lengths_ref, hidden.shape[0])).astype(F32)
    out_ref[...] = (valid * (hidden + mix)).astype(BF)


def last_kernel(x_ref, keep_ref, got_ref, gain_ref, gh_ref, out_ref, gain_out):
    x = x_ref[...].astype(F32)
    scale = rms(x)
    unit = x * scale
    gn = keep_ref[...] + got_ref[...].astype(F32)
    gain_out[...] = jnp.broadcast_to(jnp.sum(gn * unit, axis=0, keepdims=True), gain_out.shape)
    g = gn * as_row(gain_ref)
    out_ref[...] = (
        gh_ref[...] + scale * (g - unit * jnp.mean(g * unit, axis=1, keepdims=True))
    ).astype(BF)


def moe(experts, cap, packed, meta, grads, router, quarters):
    spots = experts * cap
    anyspec = pl.BlockSpec(memory_space=pl.ANY)
    dma = pltpu.SemaphoreType.DMA
    return pl.pallas_call(
        functools.partial(expert_kernel, experts, cap),
        out_shape=[
            jax.ShapeDtypeStruct((spots, D), BF),
            jax.ShapeDtypeStruct((spots, D), BF),
            jax.ShapeDtypeStruct((2 * D, D), BF),
            jax.ShapeDtypeStruct((2 * D, D), BF),
            jax.ShapeDtypeStruct((2, 2 * D, D), BF),
            jax.ShapeDtypeStruct((experts, D), F32),
        ],
        in_specs=[anyspec, VM, VM, VM] + [anyspec] * 4,
        out_specs=[anyspec, VM, anyspec, anyspec, anyspec, VM],
        scratch_shapes=[
            pltpu.VMEM((4, 2 * D, D), BF),
            pltpu.VMEM((spots, D), BF),
            pltpu.VMEM((D, spots), BF),
            pltpu.VMEM((D, spots), BF),
            pltpu.VMEM((4, spots, D), BF),
            pltpu.VMEM((4, spots, D), BF),
            pltpu.VMEM((spots, D), BF),
            pltpu.VMEM((experts, 8, cap), F32),
            pltpu.VMEM((CHUNK, D), F32),
            pltpu.VMEM((2, D, TILE), BF),
            pltpu.VMEM((2, TILE, D), BF),
            dma((experts,)),
            dma((experts,)),
            dma((experts,)),
            dma((experts,)),
            dma((experts,)),
            dma((experts,)),
            dma((2,)),
            dma((4,)),
            dma((2,)),
        ],
        compiler_params=pltpu.CompilerParams(
            collective_id=1, has_side_effects=True, vmem_limit_bytes=60 * MIB
        ),
        cost_estimate=pl.CostEstimate(flops=12 * spots * D * 4 * D, bytes_accessed=60 * MIB, transcendentals=0),
        name="experts",
    )(packed, meta, grads, router, *quarters)


def moe_line(experts, cap, normed, info, router, others):
    rows = normed.shape[0]
    spots = experts * cap
    anyspec = pl.BlockSpec(memory_space=pl.ANY)
    dma = pltpu.SemaphoreType.DMA
    return pl.pallas_call(
        functools.partial(expert_line_kernel, cap),
        out_shape=[
            jax.ShapeDtypeStruct((spots, D), BF),
            jax.ShapeDtypeStruct((spots, D), BF),
            jax.ShapeDtypeStruct((2 * D, D), BF),
            jax.ShapeDtypeStruct((2 * D, D), BF),
            jax.ShapeDtypeStruct((2, 2 * D, D), BF),
            jax.ShapeDtypeStruct((experts, D), F32),
        ],
        in_specs=[VM, VM, VM] + [anyspec] * 7,
        out_specs=[anyspec, anyspec, anyspec, anyspec, anyspec, VM],
        scratch_shapes=[
            pltpu.VMEM((spots, D), BF),
            pltpu.VMEM((2, LINE, cap, D), BF),
            pltpu.VMEM((4, 2 * D, D), BF),
            pltpu.VMEM((LINE, rows, D), BF),
            pltpu.VMEM((LINE, 8, rows), F32),
            pltpu.VMEM((2, LINE, cap, D), BF),
            pltpu.VMEM((LINE, cap, D), BF),
            pltpu.VMEM((2, LINE, 8, cap), F32),
            pltpu.VMEM((LINE, 8, cap), F32),
            pltpu.VMEM((D, spots), BF),
            pltpu.VMEM((D, spots), BF),
            pltpu.VMEM((4, spots, D), BF),
            pltpu.VMEM((4, spots, D), BF),
            pltpu.VMEM((cap, D), F32),
            pltpu.VMEM((2, D, TILE), BF),
            pltpu.VMEM((2, TILE, D), BF),
            dma((2, LINE)),
            dma((LINE,)),
            dma((2, LINE)),
            dma((LINE,)),
            dma((LINE,)),
            dma((LINE,)),
            dma((LINE,)),
            dma((LINE,)),
            dma((2, LINE)),
            dma((experts,)),
            dma((2,)),
            dma((4,)),
            dma((5,)),
            dma((5,)),
            dma,
            dma,
            dma,
            dma((4,)),
            dma((2,)),
        ],
        compiler_params=pltpu.CompilerParams(
            collective_id=2, has_side_effects=True, vmem_limit_bytes=62 * MIB
        ),
        cost_estimate=pl.CostEstimate(flops=12 * spots * D * 4 * D, bytes_accessed=60 * MIB, transcendentals=0),
        name="experts_line",
    )(normed, info, router, *others)


def tensor_copy(src, dst, send_sem, recv_sem, target):
    return pltpu.make_async_remote_copy(
        src_ref=src,
        dst_ref=dst,
        send_sem=send_sem,
        recv_sem=recv_sem,
        device_id={"tensor": target},
        device_id_type=pl.DeviceIdType.MESH,
    )


def sums(
    pair_done, beside, gw_ref, pair_ref, keep_ref, send_ref, x_in, gain_ref, gh_ref, moe_ref, router_ref, bias0_ref, bias1_ref,
    gwt_out, gow_out, gin_out, attn_out, moe_out, router_out, bias_out,
    small_out, part_ref, cross_ref, line_ref, from_ref, all_ref, got_ref, lines_ref, few_ref, ranks_ref,
    a_send, a_recv, b_send, b_recv, c_send, c_recv, d_send, d_recv, s_send, s_recv, f_send, f_recv, t_send, t_recv, g_send, g_recv,
):
    count = 2 * LINE
    me = lax.axis_index("expert")
    rank = lax.axis_index("tensor")
    place = me // 2
    side = me - 2 * place
    mate = me + 1 - 2 * side
    size = part_ref.shape[0] // count
    def slab(which, number):
        return pl.ds(pl.multiple_of((which * LINE + number) * size, size), size)

    swap = tensor_copy(send_ref, got_ref, s_send, s_recv, flipped(rank, 1, 4))
    swap.start()
    pair_done()
    part_ref[...] = (gw_ref[...] + pair_ref[...].astype(F32)).astype(BF)
    rows = gwt_out.shape[0]

    def cross(number):
        return mesh_copy(
            part_ref.at[slab(1 - side, number)], cross_ref.at[number], a_send.at[number], a_recv.at[number], mate
        )

    def along(number):
        return mesh_copy(
            line_ref.at[number], from_ref.at[place], b_send.at[number], b_recv.at[place], 2 * number + side
        )

    def spread(number):
        return mesh_copy(
            all_ref.at[slab(side, place)],
            all_ref.at[slab(side, place)],
            c_send.at[number],
            c_recv.at[place],
            2 * number + side,
        )

    def over(number):
        return mesh_copy(
            all_ref.at[slab(side, number)], all_ref.at[slab(side, number)], d_send.at[number], d_recv.at[number], mate
        )

    for number in range(LINE):
        cross(number).start()

    swap.wait()
    x = x_in[...].astype(F32)
    scale = rms(x)
    unit = x * scale
    gn = keep_ref[...] + got_ref[...].astype(F32)
    attn = jnp.sum(gn * unit, axis=0, keepdims=True)
    g = gn * as_row(gain_ref)
    gin_out[...] = (gh_ref[...] + scale * (g - unit * jnp.mean(g * unit, axis=1, keepdims=True))).astype(BF)

    heads = gow_out.shape[0] // HD
    blank = jnp.zeros((1, 128), F32)

    def flat(bias_ref):
        line = [bias_ref[h : h + 1, :NB] for h in range(heads)]
        return jnp.concatenate(line + [jnp.zeros((1, 128 - heads * NB), F32)], axis=1)

    own_bias, pair_bias = flat(bias0_ref), flat(bias1_ref)
    other = flipped(rank, 2, 4)
    for j in range(D // 128):
        lines_ref[j] = router_ref[:, j * 128 : (j + 1) * 128]
    for j, row in ((6, attn), (7, moe_ref[0:1])):
        places = [2 * (j - 6), 2 * (j - 6) + 1]
        bias = [
            jnp.where(rank == p, own_bias, blank) + jnp.where(other == p, pair_bias, blank) for p in places
        ]
        lines_ref[j] = jnp.concatenate([row[:, i * 128 : (i + 1) * 128] for i in range(6)] + bias, axis=0)

    def small(k):
        return mesh_copy(
            lines_ref.at[flipped(me, k, count)], few_ref.at[k], f_send.at[k], f_recv.at[k], flipped(me, k, count)
        )

    def rank_copy(k):
        return tensor_copy(
            ranks_ref.at[rank], ranks_ref.at[rank], t_send.at[k], t_recv.at[k], flipped(rank, k, 4)
        )

    def rank_from(k):
        return tensor_copy(
            ranks_ref.at[rank], ranks_ref.at[flipped(rank, k, 4)], t_send.at[k], t_recv.at[k], flipped(rank, k, 4)
        )

    def small_spread(k):
        return mesh_copy(
            small_out.at[me], small_out.at[me], g_send.at[k], g_recv.at[k], flipped(me, k, count)
        )

    def small_from(k):
        return mesh_copy(
            small_out.at[me], small_out.at[flipped(me, k, count)], g_send.at[k], g_recv.at[k], flipped(me, k, count)
        )

    for k in range(1, count):
        small(k).start()

    for number in range(LINE):

        @pl.when(number != place)
        def _():
            cross(number).wait_recv()
            line_ref[number] = (
                part_ref[slab(side, number)].astype(F32) + cross_ref[number].astype(F32)
            ).astype(BF)
            along(number).start()

    total = lines_ref[me]
    for k in range(1, count):
        small(k).wait_recv()
        total = total + few_ref[k]
    ranks_ref[rank] = total
    for k in range(1, 4):
        rank_copy(k).start()

    for number in range(LINE):

        @pl.when(number == place)
        def _():
            cross(number).wait_recv()

    beside()
    whole = part_ref[slab(side, place)].astype(F32) + cross_ref[place].astype(F32)
    from_ref[place] = whole.astype(BF)
    for k in range(1, LINE):
        number = lax.rem(place + k, LINE)
        mesh_copy(
            line_ref.at[number], from_ref.at[number], b_send.at[number], b_recv.at[number], mate
        ).wait_recv()
        whole = whole + from_ref[number].astype(F32)
    all_ref[slab(side, place)] = whole.astype(BF)
    over(place).start()
    for number in range(LINE):

        @pl.when(number != place)
        def _():
            spread(number).start()

    for k in range(1, 4):
        rank_from(k).wait_recv()
    small_out[me] = ranks_ref[0] + ranks_ref[1] + ranks_ref[2] + ranks_ref[3]
    for k in range(1, count):
        small_spread(k).start()

    for k in range(1, LINE):
        number = lax.rem(place + k, LINE)
        mesh_copy(
            all_ref.at[slab(side, number)], all_ref.at[slab(side, number)], c_send.at[number], c_recv.at[number], mate
        ).wait_recv()
        over(number).start()
    for k in range(1, count):
        small_from(k).wait_recv()
    for number in range(LINE):
        mesh_copy(
            all_ref.at[slab(1 - side, number)],
            all_ref.at[slab(1 - side, number)],
            d_send.at[number],
            d_recv.at[number],
            mate,
        ).wait_recv()
    attn_out[...] = jnp.concatenate([small_out[6, i : i + 1] for i in range(6)], axis=1).reshape(D)
    moe_out[...] = jnp.concatenate([small_out[7, i : i + 1] for i in range(6)], axis=1).reshape(D)
    router_out[...] = jnp.concatenate([small_out[j] for j in range(D // 128)], axis=1)
    bias = functools.reduce(
        jnp.add,
        [jnp.where(rank == p, small_out[6 + p // 2, 6 + p % 2 : 7 + p % 2], blank) for p in range(4)],
    )
    bias_out[...] = jnp.concatenate([bias[:, h * NB : (h + 1) * NB] for h in range(heads)], axis=0)
    gwt_out[...] = all_ref[:rows].astype(F32)
    gow_out[...] = all_ref[rows:].astype(F32)
    for number in range(LINE):
        cross(number).wait_send()
        over(number).wait_send()

        @pl.when(number != place)
        def _():
            along(number).wait_send()
            spread(number).wait_send()

    for k in range(1, count):
        small(k).wait_send()
        small_spread(k).wait_send()
    for k in range(1, 4):
        rank_copy(k).wait_send()


PARTS = 6


def finish_kernel(
    heads, cap, lengths_ref,
    table0_ref, table1_ref, slots_ref, gain2_ref, gain1_ref, router_ref,
    came_in, hidden_in, grad_in, result_in, go_in, away_in, x_in, normed_in, wt_in, ow_in, pw_in, qkvt0_in, mixt0_in, lse0_in, qkvt1_in, mixt1_in, lse1_in,
    out_ref, gin_out, gwt_out, gow_out, attn_out, moe_out, router_out, bias_out, came_go_ref, came_away_ref,
    came_ref, hidden_ref, grad_ref, outs_ref, gorecv_ref, away_ref, x_ref, normed_ref, wt_ref, ow_ref, pw_ref, qkvt0_ref, mixt0_ref, lse0_ref, qkvt1_ref, mixt1_ref, lse1_ref,
    gh_ref, ga_ref, other_ref, moe_ref, gpart_ref, gpair_ref, gown_ref, bias0_ref, bias1_ref, keep_ref, send_ref,
    all_ga_ref, got_ref, gt_ref, d0_ref, d1_ref, npart_ref,
    o_send, o_recv, v_send, v_recv, y_send, y_recv, w_send, w_recv, e_send, e_recv, load_sem, *tail_refs,
):
    count = 2 * LINE
    me = lax.axis_index("expert")
    rank = lax.axis_index("tensor")
    core = flipped(rank, 1, 4)
    away_rank = flipped(rank, 2, 4)
    places = (
        (came_in, came_ref),
        (hidden_in, hidden_ref),
        (grad_in, grad_ref),
        (normed_in, normed_ref),
        (pw_in, pw_ref),
        (qkvt1_in, qkvt1_ref),
        (mixt1_in, mixt1_ref),
        (lse1_in, lse1_ref),
        (wt_in, wt_ref),
        (ow_in, ow_ref),
        (qkvt0_in, qkvt0_ref),
        (mixt0_in, mixt0_ref),
        (lse0_in, lse0_ref),
        (x_in, x_ref),
    )
    loads = [pltpu.make_async_copy(a, b, load_sem.at[i + 2]) for i, (a, b) in enumerate(places)]
    for load in loads:
        load.start()
    barrier = pltpu.get_barrier_semaphore()
    for k in range(1, count):
        pl.semaphore_signal(
            barrier, inc=1, device_id={"expert": flipped(me, k, count)}, device_id_type=pl.DeviceIdType.MESH
        )
    for k in range(1, 4):
        pl.semaphore_signal(
            barrier, inc=1, device_id={"tensor": flipped(rank, k, 4)}, device_id_type=pl.DeviceIdType.MESH
        )
    pl.semaphore_wait(barrier, count + 2)

    def rows_of(number):
        return pl.ds(pl.multiple_of(number * cap, cap), cap)

    def result(k):
        return mesh_copy(
            result_in.at[rows_of(flipped(me, k, count))],
            outs_ref.at[rows_of(me)],
            o_send.at[k],
            o_recv.at[k],
            flipped(me, k, count),
        )

    order = list(range(LINE, count)) + list(range(1, LINE))
    for k in order:
        result(k).start()
    own_result = pltpu.make_async_copy(result_in.at[rows_of(me)], outs_ref.at[rows_of(me)], load_sem.at[0])
    own_result.start()
    away_load = pltpu.make_async_copy(away_in, away_ref, load_sem.at[1])
    away_load.start()
    go_away = tensor_copy(go_in.at[1], gorecv_ref, v_send.at[0], v_recv.at[0], core)
    go_away.start()
    go_stay = tensor_copy(go_in.at[0], came_go_ref, v_send.at[1], v_recv.at[1], core)
    for load in loads[:3]:
        load.wait()
    turn_kernel(lengths_ref, came_ref, slots_ref, hidden_ref, gain2_ref, grad_ref, gh_ref, ga_ref, moe_ref)
    ga_swap = tensor_copy(ga_ref, other_ref, w_send, w_recv, core)
    ga_swap.start()
    away_load.wait()
    go_away.wait_recv()
    size = away_ref.shape[0] // PARTS

    def lines(i):
        return pl.ds(i * size, size)

    def away(i):
        return tensor_copy(
            away_ref.at[lines(i)], came_away_ref.at[lines(i)], y_send.at[i], y_recv.at[i], away_rank
        )

    for i in range(PARTS):
        away_ref[lines(i)] = (
            away_ref[lines(i)].astype(F32) + gorecv_ref[lines(i)].astype(F32)
        ).astype(BF)
        if i < 1:
            away(i).start()
    ga_swap.wait()
    go_stay.start()
    for load in loads[3:]:
        load.wait()
    inner = heads * HD
    split = ((slice(3 * inner, 4 * inner), 0), (slice(0, 3 * inner), 1))
    pair = [
        tensor_copy(gpart_ref.at[lines_of], gpair_ref.at[lines_of], e_send.at[i], e_recv.at[i], away_rank)
        for lines_of, i in split
    ]
    attn_bwd_kernel(
        pair[0].start, False, heads, lengths_ref, table1_ref,
        normed_ref, pw_ref.at[: 3 * inner], pw_ref.at[3 * inner :], qkvt1_ref, mixt1_ref, lse1_ref, ga_ref, other_ref,
        gpart_ref, bias1_ref, npart_ref, all_ga_ref, got_ref, gt_ref, d0_ref, d1_ref,
    )
    pair[1].start()
    attn_bwd_kernel(
        None, True, heads, lengths_ref, table0_ref,
        normed_ref, wt_ref, ow_ref, qkvt0_ref, mixt0_ref, lse0_ref, ga_ref, other_ref, npart_ref,
        gown_ref, bias0_ref, keep_ref, send_ref, all_ga_ref, got_ref, gt_ref, d0_ref, d1_ref, npart_ref,
    )

    def pair_done():
        for one in pair:
            one.wait_recv()
        for i in range(1, PARTS):
            away(i).start()

    def beside():
        own_result.wait()
        for k in order:
            result(k).wait_recv()
        output_kernel(lengths_ref, outs_ref, slots_ref, hidden_ref, out_ref)

    sums(
        pair_done, beside, gown_ref, gpair_ref, keep_ref, send_ref, x_ref, gain1_ref, gh_ref, moe_ref, router_ref,
        bias0_ref, bias1_ref, gwt_out, gow_out, gin_out, attn_out, moe_out, router_out, bias_out, *tail_refs,
    )
    for k in order:
        result(k).wait_send()
    for one in pair:
        one.wait_send()
    go_away.wait_send()
    go_stay.wait()
    for i in range(PARTS):
        away(i).wait()


def finish(heads, cap, scalars, arrays, others):
    dma = pltpu.SemaphoreType.DMA
    count = 2 * LINE
    spots = count * cap
    rows = others[1].shape[0]
    local = heads * HD
    part = 4 * local // count
    anyspec = pl.BlockSpec(memory_space=pl.ANY)
    half = (rows, D)
    tail_sems = [dma((LINE,))] * 8 + [dma, dma] + [dma((count,))] * 2 + [dma((4,))] * 2 + [dma((count,))] * 2
    shapes = [
        ((spots, D), BF), (half, F32), (half, BF),
        ((spots, D), BF), ((2 * D, D), BF), ((2 * D, D), BF), (half, BF), ((SEQ, D), BF), ((3 * local, D), BF),
        ((local, D), BF), ((4 * local, D), BF), ((3 * local, SEQ), BF), ((local, SEQ), BF), ((8, SEQ), F32),
        ((3 * local, SEQ), BF), ((local, SEQ), BF), ((8, SEQ), F32),
        (half, F32), (half, BF), (half, BF), ((8, D), F32), ((4 * local, D), BF), ((4 * local, D), BF),
        ((4 * local, D), F32), ((8, 128), F32), ((8, 128), F32), (half, F32), (half, BF),
        ((SEQ, D), BF), ((local, SEQ), BF), ((3 * local, SEQ), BF), ((TILE, TILE), F32), ((TILE, TILE), F32), ((SEQ, D), F32),
    ]
    tail_shapes = [
        ((count, 8, 128), F32),
        ((4 * local, D), BF), ((LINE, part, D), BF), ((LINE, part, D), BF), ((LINE, part, D), BF), ((4 * local, D), BF),
        (half, BF), ((count, 8, 128), F32), ((count, 8, 128), F32), ((4, 8, 128), F32),
    ]
    return pl.pallas_call(
        functools.partial(finish_kernel, heads, cap),
        out_shape=[
            jax.ShapeDtypeStruct(half, BF),
            jax.ShapeDtypeStruct(half, BF),
            jax.ShapeDtypeStruct((3 * local, D), F32),
            jax.ShapeDtypeStruct((local, D), F32),
            jax.ShapeDtypeStruct((D,), F32),
            jax.ShapeDtypeStruct((D,), F32),
            jax.ShapeDtypeStruct((count, D), F32),
            jax.ShapeDtypeStruct((heads, NB), F32),
            jax.ShapeDtypeStruct((2 * D, D), BF),
            jax.ShapeDtypeStruct((2 * D, D), BF),
        ],
        in_specs=[SM] * len(scalars) + [VM] * len(arrays) + [anyspec] * len(others),
        out_specs=[VM] * 8 + [anyspec] * 2,
        scratch_shapes=[pltpu.VMEM(*v) for v in shapes]
        + [dma((count,)), dma((count,)), dma((2,)), dma((2,)), dma((PARTS,)), dma((PARTS,)), dma, dma, dma((2,)), dma((2,)), dma((16,))]
        + [pltpu.VMEM(*v) for v in tail_shapes]
        + tail_sems,
        compiler_params=pltpu.CompilerParams(
            collective_id=3, has_side_effects=True, vmem_limit_bytes=62 * MIB
        ),
        cost_estimate=pl.CostEstimate(flops=0, bytes_accessed=200 * MIB, transcendentals=0),
        name="finish",
    )(*scalars, *arrays, *others)


def line_accept(place, distance, copies, take):
    for step in (-1, 1):
        block = place + step * distance

        @pl.when((block >= 0) & (block < LINE))
        def _():
            for one in copies(block, -step):
                one.wait_recv()
            ahead = place - step

            @pl.when((ahead >= 0) & (ahead < LINE))
            def _():
                for one in copies(block, -step):
                    one.start()

    for step in (-1, 1):
        block = place + step * distance

        @pl.when((block >= 0) & (block < LINE))
        def _():
            take(block)


def line_sent(place, copies, least):
    for block in range(LINE):
        for step in (-1, 1):

            @pl.when((place + step >= 0) & (place + step < LINE) & ((place - block) * step >= least))
            def _():
                for one in copies(block, step):
                    one.wait_send()


def begin_kernel(
    heads, cap, lengths_ref,
    table_ref, x_ref, gain1_ref, wt_ref, ow_ref, routes_ref, grad_ref, router_ref, gain2_ref, up_ref, down_ref,
    normed_out, qkvt0_out, mixt0_out, lse0_out, qkvt1_out, mixt1_out, lse1_out, hidden_ref, normed2_ref, info_ref, slots_ref,
    pw_ref, table1_ref, gy_ref, far_up_ref, far_half_ref, near_ref, near_info_ref,
    other_ref, got_ref, part_ref, keep_ref, send_ref, block_ref, places_ref, gsend_ref, gkeep_ref,
    normed_ref, qkvt0_ref, mixt0_ref, lse0_ref, qkvt1_ref, mixt1_ref, lse1_ref,
    b_send, b_recv, i_send, i_recv, x_send, x_recv, v_send, v_recv, y_send, y_recv, n_send, n_recv, keep_sem, store_sem,
):
    count = 2 * LINE
    me = lax.axis_index("expert")
    rank = lax.axis_index("tensor")
    place = me // 2
    side = me - 2 * place
    mate = me + 1 - 2 * side
    core = flipped(rank, 1, 4)
    away = flipped(rank, 2, 4)
    inner = heads * HD
    barrier = pltpu.get_barrier_semaphore()
    for k in range(1, count):
        pl.semaphore_signal(
            barrier, inc=1, device_id={"expert": flipped(me, k, count)}, device_id_type=pl.DeviceIdType.MESH
        )
    for target in (core, away):
        pl.semaphore_signal(
            barrier, inc=1, device_id={"tensor": target}, device_id_type=pl.DeviceIdType.MESH
        )
    pl.semaphore_wait(barrier, count + 1)

    swap = tensor_copy(x_ref, other_ref, v_send.at[0], v_recv.at[0], core)
    swap.start()
    pair = (
        tensor_copy(ow_ref, pw_ref.at[3 * inner :], y_send.at[0], y_recv.at[0], away),
        tensor_copy(wt_ref, pw_ref.at[: 3 * inner], y_send.at[1], y_recv.at[1], away),
        tensor_copy(table_ref, table1_ref, y_send.at[2], y_recv.at[2], away),
    )
    for one in pair:
        one.start()
    far = (
        tensor_copy(up_ref, far_up_ref, y_send.at[3], y_recv.at[3], away),
        tensor_copy(down_ref.at[: D // 4 * 3], far_half_ref, y_send.at[4], y_recv.at[4], away),
    )

    def along(block, step):
        return (
            mesh_copy(
                places_ref.at[block], places_ref.at[block], i_send.at[(step + 1) // 2, block], i_recv.at[block], me + 2 * step
            ),
            mesh_copy(
                block_ref.at[block], block_ref.at[block], b_send.at[(step + 1) // 2, block], b_recv.at[block], me + 2 * step
            ),
        )

    def across(block):
        return mesh_copy(gsend_ref.at[block], gy_ref.at[1, block], x_send.at[block], x_recv.at[block], mate)

    def keep(block):
        return pltpu.make_async_copy(gkeep_ref.at[block], gy_ref.at[0, block], keep_sem.at[block])

    rows = grad_ref.shape[0]

    def take(block):
        slots = places_ref[block, 0:2].astype(jnp.int32)
        for part, expert in ((1, mate), (0, me)):
            where = iota((cap, rows), 0) + expert * cap
            picks = ((where == slots[0:1]) | (where == slots[1:2])).astype(BF)
            taken = dot(picks, block_ref[block]).astype(BF)
            if part:
                gsend_ref[block] = taken
                across(block).start()
            else:
                gkeep_ref[block] = taken
                keep(block).start()

    block_ref[place] = grad_ref[...]
    slots_kernel(count, cap, lengths_ref, routes_ref, slots_ref)
    places_ref[place] = slots_ref[...]
    for step in (-1, 1):

        @pl.when((place + step >= 0) & (place + step < LINE))
        def _():
            for one in along(place, step):
                one.start()

    take(place)
    swap.wait()
    attn_fwd_kernel(
        True, heads, lengths_ref, table_ref, x_ref, other_ref, gain1_ref, wt_ref, ow_ref,
        normed_ref, qkvt0_ref, mixt0_ref, lse0_ref, part_ref,
    )
    first = (
        (normed_ref, normed_out), (qkvt0_ref, qkvt0_out), (mixt0_ref, mixt0_out), (lse0_ref, lse0_out),
    )
    second = ((qkvt1_ref, qkvt1_out), (mixt1_ref, mixt1_out), (lse1_ref, lse1_out))
    stores = [pltpu.make_async_copy(a, b, store_sem.at[i]) for i, (a, b) in enumerate(first + second)]
    for store in stores[:4]:
        store.start()
    line_accept(place, 1, along, take)
    for one in pair:
        one.wait_recv()
    for one in far:
        one.start()
    attn_fwd_kernel(
        False, heads, lengths_ref, table1_ref, normed_ref, pw_ref.at[: 3 * inner], pw_ref.at[3 * inner :], part_ref,
        qkvt1_ref, mixt1_ref, lse1_ref, keep_ref, send_ref, part_ref,
    )
    back = tensor_copy(send_ref, got_ref, v_send.at[1], v_recv.at[1], core)
    back.start()
    for store in stores[4:]:
        store.start()
    line_accept(place, 2, along, take)
    back.wait()
    middle_line_kernel(
        count, x_ref, keep_ref, got_ref, gain2_ref, router_ref, routes_ref, slots_ref, hidden_ref, normed2_ref, info_ref
    )
    inside = [place > 0, place < LINE - 1]

    def neighbour(i):
        target = me + 2 * (1 - 2 * i)
        return (
            mesh_copy(info_ref, near_info_ref.at[i], n_send.at[i], n_recv.at[i], target),
            mesh_copy(normed2_ref, near_ref.at[i], n_send.at[i + 2], n_recv.at[i + 2], target),
        )

    line_sent(place, along, 0)
    for i in range(2):

        @pl.when(inside[1 - i])
        def _():
            for one in neighbour(i):
                one.start()

    line_accept(place, 3, along, take)
    for block in range(LINE):
        keep(block).wait()
        across(block).wait()
    for store in stores:
        store.wait()
    for one in pair:
        one.wait_send()
    for one in far:
        one.wait()
    for i in range(2):

        @pl.when(inside[i])
        def _():
            for one in neighbour(1 - i):
                one.wait_send()
            for one in neighbour(i):
                one.wait_recv()


def begin(heads, cap, scalars, arrays, others):
    dma = pltpu.SemaphoreType.DMA
    rows = arrays[1].shape[0]
    local = heads * HD
    anyspec = pl.BlockSpec(memory_space=pl.ANY)
    half = (rows, D)
    kept = [
        ((SEQ, D), BF), ((3 * local, SEQ), BF), ((local, SEQ), BF), ((8, SEQ), F32),
        ((3 * local, SEQ), BF), ((local, SEQ), BF), ((8, SEQ), F32),
    ]
    outs = kept + [
        (half, F32), (half, BF), ((8, rows), F32), ((8, rows), F32), ((4 * local, D), BF), ((heads, NB), F32),
        ((2, LINE, cap, D), BF), ((D, D), BF), ((D // 4 * 3, D), BF), ((2, rows, D), BF), ((2, 8, rows), F32),
    ]
    shapes = [
        (half, BF), (half, BF), ((SEQ, D), F32), (half, F32), (half, BF), ((LINE, rows, D), BF), ((LINE, 8, rows), F32),
        ((LINE, cap, D), BF), ((LINE, cap, D), BF),
    ] + kept
    return pl.pallas_call(
        functools.partial(begin_kernel, heads, cap),
        out_shape=[jax.ShapeDtypeStruct(*v) for v in outs],
        in_specs=[SM] * len(scalars) + [VM] * len(arrays) + [anyspec] * len(others),
        out_specs=[anyspec] * 7 + [VM] * 6 + [anyspec] * 5,
        scratch_shapes=[pltpu.VMEM(*v) for v in shapes]
        + [dma((2, LINE)), dma((LINE,)), dma((2, LINE)), dma((LINE,)), dma((LINE,)), dma((LINE,))]
        + [dma((2,)), dma((2,)), dma((5,)), dma((5,)), dma((4,)), dma((4,)), dma((LINE,)), dma((7,))],
        compiler_params=pltpu.CompilerParams(
            collective_id=4, has_side_effects=True, vmem_limit_bytes=56 * MIB
        ),
        cost_estimate=pl.CostEstimate(flops=0, bytes_accessed=200 * MIB, transcendentals=0),
        name="begin",
    )(*scalars, *arrays, *others)


def shards(
    inputs,
    lengths,
    routes,
    attn_gain,
    qkv_weight,
    out_weight,
    rel_bias,
    moe_gain,
    router_weight,
    up_weight,
    down_weight,
    out_grad,
):
    rows = inputs.shape[0]
    rank = lax.axis_index("tensor")
    expert = lax.axis_index("expert")
    heads = rel_bias.shape[1]
    inner = heads * HD
    experts = router_weight.shape[1]
    cap = 4 * rows // experts
    spots = experts * cap
    table = jnp.transpose(rel_bias)

    def swap(x, bit):
        return lax.ppermute(x, "tensor", [(i, i ^ bit) for i in range(4)])

    gain1, gain2 = attn_gain, moe_gain
    wt = jnp.transpose(qkv_weight.reshape(D, 3 * inner))
    routes_t = jnp.transpose(routes)
    up, down = up_weight[0], down_weight[0]
    line = experts == 2 * LINE and cap == TILE
    if line:
        router_t = jnp.transpose(router_weight)
        (
            normed, qkvt0, mixt0, lse0, qkvt1, mixt1, lse1, hidden, normed_two, info, slots, pair_w, pair_table, grads_in, far_up, far_half, near, near_info,
        ) = begin(
            heads,
            cap,
            (lengths,),
            (table, inputs, gain1, wt, out_weight, routes_t, out_grad, router_t, gain2),
            (up, down),
        )
        came, result, stay, away, go, grad_router = moe_line(
            experts, cap, normed_two, info, router_t, (grads_in, near, near_info, up, down, far_up, far_half)
        )
    else:
        other = swap(inputs, 1)
        pair_w = swap(jnp.concatenate([wt, out_weight], axis=0), 2)
        pair_table = swap(table, 2)

        packed_grad, slots = call(
            functools.partial(route_kernel, experts, cap),
            [((spots, D), BF), ((8, rows), F32)],
            (lengths, routes_t, out_grad),
            [SM, VM, VM],
            flops=2 * spots * rows * D,
            moved=4 * MIB,
            name="route",
        )

        def exchange(x):
            return lax.all_to_all(
                x.reshape(experts, cap, x.shape[-1]), "expert", split_axis=0, concat_axis=0, tiled=True
            ).reshape(x.shape)

        grads_in = exchange(packed_grad)
        up, down, pair_w, pair_table = lax.optimization_barrier((up, down, pair_w, pair_table))
        far_up, far_down = swap(up, 2), swap(down, 2)

        attn_cost = dict(
            flops=2 * SEQ * D * 4 * inner + heads * SEQ * SEQ * 160, moved=6 * MIB, exps=heads * SEQ * SEQ
        )
        normed, qkvt0, mixt0, lse0, part0 = call(
            functools.partial(attn_fwd_kernel, True, heads),
            [((SEQ, D), BF), ((3 * inner, SEQ), BF), ((inner, SEQ), BF), ((8, SEQ), F32), ((SEQ, D), F32)],
            (lengths, table, inputs, other, gain1, wt, out_weight),
            [SM] + [VM] * 1 + [VM] * 5,
            name="attend_own",
            **attn_cost,
        )
        wt1, ow1 = pair_w[: 3 * inner], pair_w[3 * inner :]
        qkvt1, mixt1, lse1, keep, send = call(
            functools.partial(attn_fwd_kernel, False, heads),
            [((3 * inner, SEQ), BF), ((inner, SEQ), BF), ((8, SEQ), F32), ((rows, D), F32), ((rows, D), BF)],
            (lengths, pair_table, normed, wt1, ow1, part0),
            [SM] + [VM] * 1 + [VM] * 4,
            scratch=[pltpu.VMEM((SEQ, D), F32)],
            name="attend_pair",
            **attn_cost,
        )
        got = swap(send, 1)
        middle_args = (inputs, keep, got, gain2, jnp.transpose(router_weight), routes_t, slots)
        mine = jnp.concatenate([up, down], axis=0)
        far = jnp.concatenate([far_up, far_down], axis=0)
        quarters = [mine, far, swap(mine, 1), swap(far, 1)]
        hidden, packed_rows, meta = call(
            functools.partial(middle_kernel, experts, cap),
            [((rows, D), F32), ((spots, D), BF), ((experts, 8, cap), F32)],
            middle_args,
            flops=2 * spots * rows * D,
            moved=8 * MIB,
            name="middle",
        )
        came, result, stay, away, go, grad_router = moe(
            experts, cap, packed_rows, meta, grads_in, router_weight, quarters
        )
    if line:
        outputs, grad_inputs, gwt, gow, attn_sum, moe_sum, router_sum, bias_sum, go_stay, came_away = finish(
            heads,
            cap,
            (lengths,),
            (table, pair_table, slots, gain2, gain1, grad_router),
            (came, hidden, out_grad, result, go, away, inputs, normed, wt, out_weight, pair_w, qkvt0, mixt0, lse0, qkvt1, mixt1, lse1),
        )
    else:
        came_out = exchange(result)
        came_go = swap(go, 1)
        grad_hidden, grad_attended, moe_part = call(
            turn_kernel,
            [((rows, D), F32), ((rows, D), BF), ((8, D), F32)],
            (lengths, came, slots, hidden, gain2, out_grad),
            [SM] + [VM] * 5,
            flops=2 * spots * rows * D,
            moved=8 * MIB,
            name="turn",
        )
        other_grad = swap(grad_attended, 1)
        away = (away.astype(F32) + came_go[1].astype(F32)).astype(BF)
        bwd_cost = dict(
            flops=2 * SEQ * D * 10 * inner + heads * SEQ * SEQ * 400, moved=9 * MIB, exps=heads * SEQ * SEQ
        )
        work = [
            pltpu.VMEM((SEQ, D), BF),
            pltpu.VMEM((inner, SEQ), BF),
            pltpu.VMEM((3 * inner, SEQ), BF),
            pltpu.VMEM((TILE, TILE), F32),
            pltpu.VMEM((TILE, TILE), F32),
        ]
        gpart, gbias1, npart = call(
            functools.partial(attn_bwd_kernel, None, False, heads),
            [((4 * inner, D), BF), ((8, 128), F32), ((SEQ, D), F32)],
            (lengths, pair_table, normed, wt1, ow1, qkvt1, mixt1, lse1, grad_attended, other_grad),
            [SM] + [VM] * 1 + [VM] * 8,
            scratch=work,
            name="attend_pair_back",
            **bwd_cost,
        )
        gpair = swap(gpart, 2)
        gown, gbias0, keep_n, send_n = call(
            functools.partial(attn_bwd_kernel, None, True, heads),
            [((4 * inner, D), F32), ((8, 128), F32), ((rows, D), F32), ((rows, D), BF)],
            (lengths, table, normed, wt, out_weight, qkvt0, mixt0, lse0, grad_attended, other_grad, npart),
            [SM] + [VM] * 1 + [VM] * 9,
            scratch=work + [pltpu.VMEM((SEQ, D), F32)],
            name="attend_own_back",
            **bwd_cost,
        )
        away, gpair, gown = lax.optimization_barrier((away, gpair, gown))
        came_away = swap(away, 2)
        got_n = swap(send_n, 1)
        grad_inputs, attn_part = call(
            last_kernel,
            [((rows, D), BF), ((8, D), F32)],
            (inputs, keep_n, got_n, gain1, grad_hidden),
            moved=6 * MIB,
            name="last",
        )
        wide = (gown + gpair.astype(F32)).astype(BF)
        wide = lax.psum(wide, "expert").astype(F32)
        outputs = call(
            output_kernel,
            [((rows, D), BF)],
            (lengths, came_out, slots, hidden),
            [SM] + [VM] * 3,
            flops=2 * spots * rows * D,
            moved=8 * MIB,
            name="outputs",
        )[0]
        go_stay = came_go[0]

    if line:
        router_sum = jnp.transpose(router_sum)
    else:
        gwt, gow = wide[: 3 * inner], wide[3 * inner :]
        own_bias = gbias0[:heads, :NB].reshape(1, -1)
        pair_bias = gbias1[:heads, :NB].reshape(1, -1)
        ranks = jnp.arange(4, dtype=jnp.int32)[:, None]
        bias_parts = jnp.where(ranks == rank, own_bias, 0.0) + jnp.where(
            ranks == (rank ^ 2), pair_bias, 0.0
        )
        small = jnp.concatenate(
            [attn_part[0], moe_part[0], jnp.transpose(grad_router).reshape(-1), bias_parts.reshape(-1)]
        )
        small = lax.psum(small, ("expert", "tensor"))
        attn_sum, moe_sum = small[:D], small[D : 2 * D]
        router_sum = small[2 * D : 2 * D + experts * D].reshape(D, experts)
        bias_sum = lax.dynamic_slice(
            small[2 * D + experts * D :].reshape(4, heads * NB), (rank, 0), (1, heads * NB)
        )
    grad_up, grad_down = (
        stay[rows_of].astype(F32) + go_stay[rows_of].astype(F32) + came_away[rows_of].astype(F32)
        for rows_of in (slice(0, D), slice(D, 2 * D))
    )
    return (
        outputs,
        grad_inputs,
        attn_sum,
        jnp.transpose(gwt).reshape(D, 3, inner),
        gow,
        jnp.transpose(bias_sum.reshape(heads, NB)),
        moe_sum,
        router_sum,
        grad_up[None],
        grad_down[None],
    )


def solution(mesh):
    return jax.shard_map(
        shards,
        mesh=mesh,
        in_specs=(
            P(("expert", "tensor"), None),
            P("expert"),
            P(("expert", "tensor"), None),
            P(),
            P(None, None, "tensor"),
            P("tensor", None),
            P(None, "tensor"),
            P(),
            P(),
            P("expert", None, "tensor"),
            P("expert", "tensor", None),
            P(("expert", "tensor"), None),
        ),
        out_specs=(
            P(("expert", "tensor"), None),
            P(("expert", "tensor"), None),
            P(),
            P(None, None, "tensor"),
            P("tensor", None),
            P(None, "tensor"),
            P(),
            P(),
            P("expert", None, "tensor"),
            P("expert", "tensor", None),
        ),
        check_vma=False,
    )
```

```python
import functools

import jax
import jax.numpy as jnp
from jax import lax
from jax.experimental import pallas as pl
from jax.experimental.pallas import tpu as pltpu
from jax.sharding import PartitionSpec as P

D = 768
HD = 64
NB = 32
MAXDIST = 128
SEQ = 1024
EPSILON = 1e-06
NEGATIVE = -1e30
TILE = 256
BF = jnp.bfloat16
F32 = jnp.float32
MIB = 2**20
CHUNK = 256
GELU = 0.7978845608028654
CUBIC = 0.044715


def bucket_edges():
    half_count = NB // 2
    short_edges = list(range(1, half_count))
    long_edges = [
        int(half_count * (MAXDIST / half_count) ** (step_index / half_count))
        for step_index in range(half_count)
    ]
    return short_edges + long_edges


EDGES = bucket_edges()


def dot(a, b, ca=1, cb=0, precision=None):
    return lax.dot_general(
        a, b, (((ca,), (cb,)), ((), ())), preferred_element_type=F32, precision=precision
    )


def iota(shape, dim):
    return lax.broadcasted_iota(jnp.int32, shape, dim)


def rms(v):
    return lax.rsqrt(jnp.mean(v * v, axis=-1, keepdims=True) + EPSILON)


def call(kernel, outs, args, specs=None, scratch=(), flops=0, moved=0, exps=0, vmem=56, name=None):
    vm = pl.BlockSpec(memory_space=pltpu.VMEM)
    return pl.pallas_call(
        kernel,
        out_shape=[jax.ShapeDtypeStruct(s, d) for s, d in outs],
        in_specs=specs or [vm] * len(args),
        out_specs=[vm] * len(outs),
        scratch_shapes=list(scratch),
        compiler_params=pltpu.CompilerParams(vmem_limit_bytes=vmem * MIB),
        cost_estimate=pl.CostEstimate(flops=flops, bytes_accessed=moved, transcendentals=exps),
        name=name,
    )(*args)


def own_length(lengths_ref):
    return lengths_ref[lax.axis_index("tensor") // 2]


def own_valid(lengths_ref, rows):
    half = lax.rem(lax.axis_index("tensor"), 2)
    return jnp.clip(own_length(lengths_ref) - half * rows, 0, rows)


def as_row(ref):
    return ref[...].reshape(1, D)


VM = pl.BlockSpec(memory_space=pltpu.VMEM)
SM = pl.BlockSpec(memory_space=pltpu.SMEM)


def slot_lines(experts, cap, valid_count, routes):
    rows = routes.shape[1]
    valid = iota((1, rows), 1) < valid_count
    ids = iota((experts, rows), 0)
    hot0 = ((ids == routes[0:1]) & valid).astype(F32)
    hot1 = ((ids == routes[1:2]) & valid).astype(F32)
    before = (iota((rows, rows), 0) < iota((rows, rows), 1)).astype(BF)
    rank = dot((hot0 + hot1).astype(BF), before)
    place = ids.astype(F32) * cap + rank
    bad = jnp.where(valid, 0.0, 1.0)
    slot0 = jnp.sum(hot0 * place, axis=0, keepdims=True) - bad
    slot1 = jnp.sum(hot1 * place, axis=0, keepdims=True) - bad
    return slot0, slot1


def route_kernel(experts, cap, lengths_ref, routes_ref, grad_ref, packed_ref, slots_ref):
    rows = grad_ref.shape[0]
    slot0, slot1 = slot_lines(experts, cap, own_valid(lengths_ref, routes_ref.shape[1]), routes_ref[...])
    spots = iota((experts * cap, rows), 0)
    pick0 = spots == slot0.astype(jnp.int32)
    pick1 = spots == slot1.astype(jnp.int32)
    packed_ref[...] = dot((pick0 | pick1).astype(BF), grad_ref[...]).astype(BF)
    slots_ref[...] = jnp.concatenate([slot0, slot1, jnp.zeros((6, rows), F32)], axis=0)


def slots_kernel(experts, cap, lengths_ref, routes_ref, slots_ref):
    rows = routes_ref.shape[1]
    slot0, slot1 = slot_lines(experts, cap, own_valid(lengths_ref, routes_ref.shape[1]), routes_ref[...])
    slots_ref[...] = jnp.concatenate([slot0, slot1, jnp.zeros((6, rows), F32)], axis=0)


def back_matrix(slots_ref, spots):
    rows = slots_ref.shape[1]
    where = iota((rows, spots), 1)
    slots = slots_ref[...].T.astype(jnp.int32)
    return ((where == slots[:, 0:1]) | (where == slots[:, 1:2])).astype(BF)


def bias_tiles(table_ref, head):
    dist = iota((8, TILE), 1)
    line = table_ref[head : head + 1, :]
    line = line - line[:, NB - 1 :]
    curve = jnp.broadcast_to(line[:, 0:1], (8, TILE))
    for number, edge in enumerate(EDGES):
        curve = jnp.where(dist >= edge, line[:, number + 1 : number + 2], curve)
    spread = jnp.broadcast_to(curve[0:1], (TILE, TILE))
    ring = pltpu.roll(spread, 0, 1, stride=1, stride_axis=0)
    ahead = iota((TILE, TILE), 1) >= iota((TILE, TILE), 0)
    return jnp.where(ahead, ring, NEGATIVE), jnp.where(ahead, 0.0, ring)


def head_pieces(qkvt_ref, mask_rows, head, local_inner):
    start = pl.multiple_of(head * HD, HD)
    q = qkvt_ref[pl.ds(start, HD), :] * jnp.asarray(HD**-0.5, BF)
    k = qkvt_ref[pl.ds(local_inner + start, HD), :]
    v = qkvt_ref[pl.ds(2 * local_inner + start, HD), :]
    ones = jnp.ones((16, SEQ), BF)
    return jnp.concatenate([q, ones], 0), jnp.concatenate([k, mask_rows], 0), v, ones


def mask_block(length):
    keep = (iota((16, SEQ), 1) < length) | (iota((16, SEQ), 0) > 0)
    return jnp.where(keep, 0.0, NEGATIVE).astype(BF)


def score_pieces(k, q, block, near, below):
    cols = slice(block * TILE, (block + 1) * TILE)
    qb = q[:, cols]
    pieces = []
    if block >= 2:
        pieces.append((0, (block - 1) * TILE, dot(k[: (block - 1) * TILE], qb)))
    if block >= 1:
        lo = (block - 1) * TILE
        pieces.append((lo, block * TILE, dot(k[lo : lo + TILE], qb) + below))
    lo = block * TILE
    pieces.append((lo, lo + TILE, dot(k[lo : lo + TILE], qb) + near))
    return cols, pieces


def attn_fwd_kernel(first, heads, lengths_ref, table_ref, *refs):
    if first:
        own_ref, other_ref, gain_ref, w_ref, ow_ref = refs[:5]
        normed_ref, qkvt_ref, mixt_ref, lse_ref, part_ref = refs[5:]
        half = own_ref.shape[0]
        core = lax.rem(lax.axis_index("tensor"), 2)
        for source, place in ((own_ref, core), (other_ref, 1 - core)):
            x = source[...].astype(F32)
            normed_ref[pl.ds(pl.multiple_of(place * half, half), half), :] = (
                x * rms(x) * as_row(gain_ref)
            ).astype(BF)
    else:
        normed_ref, w_ref, ow_ref, part_in = refs[:4]
        qkvt_ref, mixt_ref, lse_ref, keep_ref, send_ref, part_ref = refs[4:]
    local_inner = heads * HD
    qkvt_ref[...] = dot(w_ref[...], normed_ref[...], 1, 1).astype(BF)
    masks = mask_block(own_length(lengths_ref))
    lse_ref[...] = jnp.zeros_like(lse_ref)

    for head in range(heads):
        near, below = bias_tiles(table_ref, head)
        q, kt, v, ones = head_pieces(qkvt_ref, masks, head, local_inner)
        k = kt.T
        vx = jnp.concatenate([v, ones], 0)
        for block in range(SEQ // TILE):
            cols, pieces = score_pieces(k, q, block, near, below)
            top = functools.reduce(
                jnp.maximum, [jnp.max(s, axis=0, keepdims=True) for _, _, s in pieces]
            )
            total = None
            for lo, hi, s in pieces:
                term = dot(vx[:, lo:hi], jnp.exp(s - top).astype(BF))
                total = term if total is None else total + term
            weight = total[HD : HD + 1]
            mixt_ref[head * HD : (head + 1) * HD, cols] = (total[:HD] / weight).astype(BF)
            lse_ref[head : head + 1, cols] = top + jnp.log(weight)
    part = dot(mixt_ref[...], ow_ref[...], 0, 0)
    if first:
        part_ref[...] = part
    else:
        part_ref[...] = part + part_in[...]
        half = keep_ref.shape[0]
        core = lax.rem(lax.axis_index("tensor"), 2)
        keep_ref[...] = part_ref[pl.ds(pl.multiple_of(core * half, half), half), :]
        send_ref[...] = part_ref[pl.ds(pl.multiple_of((1 - core) * half, half), half), :].astype(BF)


def attn_bwd_kernel(early, last, heads, lengths_ref, table_ref, *refs):
    if last:
        (normed_ref, w_ref, ow_ref, qkvt_ref, mixt_ref, lse_ref, own_ref, other_ref, part_in) = refs[:9]
        gw_ref, gbias_ref, keep_ref, send_ref, ga_ref, got_ref, gt_ref, d0_ref, d1_ref, part_ref = refs[9:]
    else:
        (normed_ref, w_ref, ow_ref, qkvt_ref, mixt_ref, lse_ref, own_ref, other_ref) = refs[:8]
        gw_ref, gbias_ref, part_ref, ga_ref, got_ref, gt_ref, d0_ref, d1_ref = refs[8:]
    local_inner = heads * HD
    half = own_ref.shape[0]
    core = lax.rem(lax.axis_index("tensor"), 2)
    ga_ref[pl.ds(pl.multiple_of(core * half, half), half), :] = own_ref[...]
    ga_ref[pl.ds(pl.multiple_of((1 - core) * half, half), half), :] = other_ref[...]
    got_ref[...] = dot(ow_ref[...], ga_ref[...], 1, 1).astype(BF)
    gw_ref[3 * local_inner :] = dot(mixt_ref[...], ga_ref[...]).astype(gw_ref.dtype)
    if early is not None:
        early()
    masks = mask_block(own_length(lengths_ref))
    gbias_ref[...] = jnp.zeros_like(gbias_ref)
    ahead = iota((TILE, TILE), 1) >= iota((TILE, TILE), 0)
    spot = (iota((TILE, 128), 0) + 1) % TILE
    flip = (iota((TILE, TILE), 0) + iota((TILE, TILE), 1) == TILE - 1).astype(F32)
    bucket = jnp.zeros((TILE, 128), jnp.int32)
    for edge in EDGES:
        bucket = bucket + (spot >= edge).astype(jnp.int32)
    hot = (bucket == iota((TILE, 128), 1)).astype(F32)

    for head in range(heads):
        near, below = bias_tiles(table_ref, head)
        q, kt, vt, _ = head_pieces(qkvt_ref, masks, head, local_inner)
        k = kt.T
        v = vt.T
        rows = slice(head * HD, (head + 1) * HD)
        gt = got_ref[rows, :]
        delta = jnp.sum(gt.astype(F32) * mixt_ref[rows, :].astype(F32), axis=0, keepdims=True)
        gk = [None] * (SEQ // TILE)
        gv = [None] * (SEQ // TILE)
        far = jnp.zeros((8, TILE), F32)
        for block in range(SEQ // TILE):
            cols, pieces = score_pieces(k, q, block, near, below)
            gb = gt[:, cols]
            qb = q[:HD, cols]
            lse = lse_ref[head : head + 1, cols]
            db = delta[:, cols]
            gq = None
            for lo, hi, s in pieces:
                p = jnp.exp(s - lse)
                ds = p * (dot(v[lo:hi], gb) - db)
                pb = p.astype(BF)
                dsb = ds.astype(BF)
                term = dot(kt[:HD, lo:hi], dsb)
                gq = term if gq is None else gq + term
                tv = dot(pb, gb, 1, 1)
                tk = dot(dsb, qb, 1, 1)
                for tile in range(lo // TILE, hi // TILE):
                    part = slice(tile * TILE - lo, (tile + 1) * TILE - lo)
                    gv[tile] = tv[part] if gv[tile] is None else gv[tile] + tv[part]
                    gk[tile] = tk[part] if gk[tile] is None else gk[tile] + tk[part]
                if hi == (block + 1) * TILE:
                    d0_ref[...] = ds if block == 0 else d0_ref[...] + ds
                elif hi == block * TILE and lo == (block - 1) * TILE:
                    d1_ref[...] = ds if block == 1 else d1_ref[...] + ds
                else:
                    far = far + jnp.sum(ds.reshape((hi - lo) // 8, 8, TILE), axis=0)
            gt_ref[rows, cols] = (gq * HD**-0.5).astype(BF)
        for tile in range(SEQ // TILE):
            cols = slice(tile * TILE, (tile + 1) * TILE)
            gt_ref[local_inner + head * HD : local_inner + (head + 1) * HD, cols] = (
                gk[tile].T.astype(BF)
            )
            gt_ref[2 * local_inner + head * HD : 2 * local_inner + (head + 1) * HD, cols] = (
                gv[tile].T.astype(BF)
            )
        d1 = d1_ref[...]
        ring = jnp.where(ahead, d0_ref[...], d1)
        turned = pltpu.roll(
            dot(flip, ring, 1, 0, lax.Precision.HIGHEST), 0, 1, stride=1, stride_axis=0
        )
        far = far + jnp.sum(jnp.where(ahead, d1, 0.0).reshape(TILE // 8, 8, TILE), axis=0)
        line = jnp.sum(turned, axis=0, keepdims=True)
        sums = dot(
            jnp.broadcast_to(line, (8, TILE)), hot, 1, 0, lax.Precision.HIGHEST
        )
        sums = sums + jnp.where(iota((8, 128), 1) == NB - 1, jnp.sum(far), 0.0)
        gbias_ref[head : head + 1, :] = sums[0:1]
    gw_ref[: 3 * local_inner] = dot(gt_ref[...], normed_ref[...]).astype(gw_ref.dtype)
    part = dot(gt_ref[...], w_ref[...], 0, 0)
    if last:
        part_ref[...] = part + part_in[...]
        keep_ref[...] = part_ref[pl.ds(pl.multiple_of(core * half, half), half), :]
        send_ref[...] = part_ref[pl.ds(pl.multiple_of((1 - core) * half, half), half), :].astype(BF)
    else:
        part_ref[...] = part


def gates_of(experts, normed, router_t, routes):
    rows = normed.shape[0]
    logits = dot(router_t, normed, 1, 1)
    ids = iota((experts, rows), 0)
    signs = (ids == routes[0:1]).astype(F32) - (ids == routes[1:2]).astype(F32)
    gap = jnp.sum(logits * signs, axis=0, keepdims=True)
    return 1.0 / (1.0 + jnp.exp(-gap)), 1.0 / (1.0 + jnp.exp(gap))


def meta_lines(gate, code):
    rows = gate.shape[1]
    line = iota((8, rows), 0)
    high = gate.astype(BF).astype(F32)
    mid = (gate - high).astype(BF).astype(F32)
    low = gate - high - mid
    picked = jnp.where(line == 0, high, jnp.where(line == 1, mid, jnp.where(line == 2, low, 0.0)))
    return jnp.where(line == 3, code, picked).astype(BF)


def hidden_rows(x_ref, keep_ref, got_ref, gain_ref, hidden_ref):
    hidden = x_ref[...].astype(F32) + keep_ref[...] + got_ref[...].astype(F32)
    hidden_ref[...] = hidden
    return (hidden * rms(hidden) * as_row(gain_ref)).astype(BF)


def middle_kernel(
    experts, cap, x_ref, keep_ref, got_ref, gain_ref, router_ref, routes_ref, slots_ref, hidden_ref, packed_ref, meta_ref
):
    normed = hidden_rows(x_ref, keep_ref, got_ref, gain_ref, hidden_ref)
    slots = slots_ref[...].astype(jnp.int32)
    routes = routes_ref[...]
    where = iota((experts * cap, normed.shape[0]), 0)
    pick0 = where == slots[0:1]
    pick1 = where == slots[1:2]
    packed_ref[...] = dot((pick0 | pick1).astype(BF), normed).astype(BF)
    gate0, gate1 = gates_of(experts, normed, router_ref[...], routes)
    codes = (routes + 1).astype(F32)
    meta = dot(meta_lines(gate0, codes[1:2]), pick0.astype(BF), 1, 1) + dot(
        meta_lines(gate1, codes[0:1]), pick1.astype(BF), 1, 1
    )
    for number in range(experts):
        meta_ref[number] = meta[:, number * cap : (number + 1) * cap]


def middle_line_kernel(
    experts, x_ref, keep_ref, got_ref, gain_ref, router_ref, routes_ref, slots_ref, hidden_ref, normed_ref, info_ref
):
    normed = hidden_rows(x_ref, keep_ref, got_ref, gain_ref, hidden_ref)
    normed_ref[...] = normed
    routes = routes_ref[...]
    gate0, gate1 = gates_of(experts, normed, router_ref[...], routes)
    codes = (routes + 1).astype(F32)
    info_ref[...] = jnp.concatenate(
        [slots_ref[0:2], gate0, gate1, codes, jnp.zeros((2, normed.shape[0]), F32)], axis=0
    )


def gelu_pair(v):
    squared = v * v
    slope = GELU * (1.0 + 3 * CUBIC * squared)
    t = jnp.tanh(v * (GELU + GELU * CUBIC * squared))
    half = 0.5 + 0.5 * t
    return v * half, half + 0.5 * v * (1.0 - t * t) * slope


def flipped(me, k, count):
    total, bit = 0, 1
    while bit < count:
        total = total + lax.rem(me // bit + k // bit, 2) * bit
        bit *= 2
    return total


def weight_grads(xt_ref, geot_ref, act_ref, gi_ref, stage_ref, turned_ref, stay_ref, away_ref, go_ref, out_sem):
    tiles = D // TILE
    steps = 8 * tiles

    def columns(step):
        return pl.ds(pl.multiple_of(lax.rem(step, tiles) * TILE, TILE), TILE)

    def store(step, slot, out_ref, half):
        if half:
            there = pl.ds(pl.multiple_of(D + lax.rem(step, tiles) * TILE, TILE), TILE)
            return pltpu.make_async_copy(turned_ref.at[slot], out_ref.at[there], out_sem.at[slot])
        return pltpu.make_async_copy(stage_ref.at[slot], out_ref.at[:D, columns(step)], out_sem.at[slot])

    def weights(step, carry):
        q = step // (2 * tiles)
        half = lax.rem(step, 2 * tiles) // tiles
        slot = lax.rem(step, 2)

        outs = (stay_ref, away_ref, go_ref.at[0], go_ref.at[1])

        @pl.when(step >= 2)
        def _():
            store(step - 2, slot, stay_ref, 0).wait()

        @pl.when(half == 0)
        def _():
            stage_ref[slot] = dot(xt_ref[...], gi_ref[q, :, columns(step)]).astype(BF)

        @pl.when(half == 1)
        def _():
            turned_ref[slot] = dot(geot_ref[...], act_ref[q, :, columns(step)]).astype(BF).T

        for number, out_ref in enumerate(outs):
            for kind in range(2):

                @pl.when((q == number) & (half == kind))
                def _():
                    store(step, slot, out_ref, kind).start()

        return carry

    lax.fori_loop(0, steps, weights, 0)
    for step in (steps - 2, steps - 1):
        store(step, step % 2, stay_ref, 1).wait()


def expert_rows(ready, x, geo, here, w_ref, xt_ref, geot_ref, act_ref, gi_ref, acc_ref):
    xt_ref[:, here] = x.T
    geot_ref[:, here] = geo.T
    worth = 0.0
    for q in (0, 2, 1, 3):
        if q == 1:
            ready()
        inner = dot(x, w_ref[q, :D])
        grad_active = dot(geo, w_ref[q, D:], 1, 1)
        act, slope = gelu_pair(inner)
        gi = (slope * grad_active).astype(BF)
        act_ref[q, here] = act.astype(BF)
        gi_ref[q, here] = gi
        back = dot(gi, w_ref[q, :D], 1, 1)
        if q == 0:
            acc_ref[...] = back
        else:
            acc_ref[...] += back
        worth = worth + jnp.sum(act * grad_active, axis=1, keepdims=True)
    return worth


def expert_outs(start, size, column, act_ref, w_ref):
    here = pl.ds(pl.multiple_of(start, size), size)
    cols = pl.ds(pl.multiple_of(column * TILE, TILE), TILE)
    total = None
    for q in range(4):
        term = dot(act_ref[q, here], w_ref[q, D:, cols])
        total = term if total is None else total + term
    return cols, total


def expert_kernel(
    count, cap, packed_ref, send_meta_ref, grads_ref, router_ref, w0, w1, w2, w3,
    came_ref, result_ref, stay_ref, away_ref, go_ref, grouter_ref,
    w_ref, x_ref, xt_ref, geot_ref, act_ref, gi_ref, gsend_ref, meta_ref, acc_ref, stage_ref, turned_ref,
    x_send, x_recv, m_send, m_recv, r_send, r_recv, local_sem, w_sem, out_sem,
):
    me = lax.axis_index("expert")
    barrier = pltpu.get_barrier_semaphore()

    def peer(k):
        return flipped(me, k, count)

    source = peer

    def greet(k, carry):
        pl.semaphore_signal(
            barrier, inc=1, device_id={"expert": peer(k)}, device_id_type=pl.DeviceIdType.MESH
        )
        return carry

    lax.fori_loop(1, count, greet, 0)
    pl.semaphore_wait(barrier, count - 1)

    def rows_of(k):
        return pl.ds(pl.multiple_of(k * cap, cap), cap)

    def send_rows(k):
        return pltpu.make_async_remote_copy(
            src_ref=packed_ref.at[rows_of(peer(k))],
            dst_ref=x_ref.at[rows_of(k)],
            send_sem=x_send.at[k],
            recv_sem=x_recv.at[k],
            device_id={"expert": peer(k)},
            device_id_type=pl.DeviceIdType.MESH,
        )

    def send_meta(k):
        return pltpu.make_async_remote_copy(
            src_ref=send_meta_ref.at[peer(k)],
            dst_ref=meta_ref.at[k],
            send_sem=m_send.at[k],
            recv_sem=m_recv.at[k],
            device_id={"expert": peer(k)},
            device_id_type=pl.DeviceIdType.MESH,
        )

    def send_back(k):
        return pltpu.make_async_remote_copy(
            src_ref=gsend_ref.at[rows_of(k)],
            dst_ref=came_ref.at[rows_of(me)],
            send_sem=r_send.at[k],
            recv_sem=r_recv.at[k],
            device_id={"expert": source(k)},
            device_id_type=pl.DeviceIdType.MESH,
        )

    def start_sends(k, carry):
        send_meta(k).start()
        send_rows(k).start()
        return carry

    lax.fori_loop(count // 2, count, start_sends, 0)
    lax.fori_loop(1, count // 2, start_sends, 0)
    own_rows = pltpu.make_async_copy(packed_ref.at[rows_of(me)], x_ref.at[rows_of(0)], local_sem.at[0])
    own_rows.start()
    own_meta = pltpu.make_async_copy(send_meta_ref.at[me], meta_ref.at[0], local_sem.at[1])
    own_meta.start()
    loads = [
        pltpu.make_async_copy(w, w_ref.at[i], w_sem.at[i]) for i, w in enumerate((w0, w1, w2, w3))
    ]
    for load in loads:
        load.start()
    grouter_ref[...] = jnp.zeros_like(grouter_ref)
    experts = router_ref.shape[1]
    own_rows.wait()
    own_meta.wait()
    for load in loads:
        load.wait()
    group = max(1, CHUNK // cap)
    span = group * cap

    def chunk(j, carry):
        for i in range(group):
            k = j * group + i

            @pl.when(k > 0)
            def _():
                send_rows(k).wait_recv()
                send_meta(k).wait_recv()

        here = pl.ds(pl.multiple_of(j * span, span), span)
        meta = jnp.concatenate([meta_ref[j * group + i].T for i in range(group)], axis=0)
        gate = meta[:, 0:1] + meta[:, 1:2] + meta[:, 2:3]
        code = meta[:, 3:4].astype(jnp.int32)
        gy = jnp.concatenate([grads_ref[rows_of(source(j * group + i)), :] for i in range(group)], axis=0)
        geo = (gate * gy.astype(F32)).astype(BF)
        x = x_ref[here, :]
        worth = expert_rows(lambda: None, x, geo, here, w_ref, xt_ref, geot_ref, act_ref, gi_ref, acc_ref)
        ids = iota((span, experts), 1)
        signs = (ids == me).astype(F32) - (ids + 1 == code).astype(F32)
        share = jnp.where(code > 0, (1.0 - gate) * worth, 0.0) * signs
        high = share.astype(BF)
        low = (share - high.astype(F32)).astype(BF)
        gsend_ref[here, :] = (acc_ref[...] + dot(high, router_ref[...], 1, 1)).astype(BF)
        grouter_ref[...] += dot(high.T, x) + dot(low.T, x)
        for i in range(group):
            k = j * group + i

            @pl.when(k > 0)
            def _():
                send_back(k).start()

        return carry

    lax.fori_loop(0, count // group, chunk, 0)
    own_back = pltpu.make_async_copy(gsend_ref.at[rows_of(0)], came_ref.at[rows_of(me)], local_sem.at[0])
    own_back.start()

    def results(step, carry):
        j = step // (D // TILE)
        meta = jnp.concatenate([meta_ref[j * group + i].T for i in range(group)], axis=0)
        gate = meta[:, 0:1] + meta[:, 1:2] + meta[:, 2:3]
        cols, total = expert_outs(j * span, span, lax.rem(step, D // TILE), act_ref, w_ref)
        out = (gate * total).astype(BF)
        for i in range(group):
            result_ref[rows_of(source(j * group + i)), cols] = out[i * cap : (i + 1) * cap]
        return carry

    lax.fori_loop(0, count // group * (D // TILE), results, 0)
    weight_grads(xt_ref, geot_ref, act_ref, gi_ref, stage_ref, turned_ref, stay_ref, away_ref, go_ref, out_sem)
    own_back.wait()

    def finish(k, carry):
        send_rows(k).wait_send()
        send_meta(k).wait_send()
        send_back(k).wait()
        return carry

    lax.fori_loop(1, count, finish, 0)


def mesh_copy(src, dst, send_sem, recv_sem, target):
    return pltpu.make_async_remote_copy(
        src_ref=src,
        dst_ref=dst,
        send_sem=send_sem,
        recv_sem=recv_sem,
        device_id={"expert": target},
        device_id_type=pl.DeviceIdType.MESH,
    )


LINE = 4


def expert_line_kernel(
    cap, normed_ref, info_in, router_ref, grads_in, near_ref, near_info_ref, up_ref, down_ref, far_up_ref, far_half_ref,
    came_ref, result_out, stay_ref, away_ref, go_ref, grouter_ref,
    result_ref, grads_ref, w_ref, block_ref, info_ref, x_ref, xs_ref, meta_ref, ms_ref, xt_ref, geot_ref, act_ref, gi_ref, acc_ref, stage_ref, turned_ref,
    b_send, b_recv, i_send, i_recv, x_send, x_recv, m_send, m_recv, r_send, r_recv, local_sem, w_sem, v_send, v_recv, y_send, y_recv, grads_sem, near_sem, out_sem,
):
    count = 2 * LINE
    me = lax.axis_index("expert")
    place = me // 2
    side = me - 2 * place
    mate = me + 1 - 2 * side
    barrier = pltpu.get_barrier_semaphore()

    def greet(k, carry):
        pl.semaphore_signal(
            barrier,
            inc=1,
            device_id={"expert": lax.rem(me + k, count)},
            device_id_type=pl.DeviceIdType.MESH,
        )
        return carry

    lax.fori_loop(1, count, greet, 0)
    core = flipped(lax.axis_index("tensor"), 1, 4)
    pl.semaphore_signal(
        barrier, inc=1, device_id={"tensor": core}, device_id_type=pl.DeviceIdType.MESH
    )
    away = flipped(lax.axis_index("tensor"), 2, 4)
    pl.semaphore_signal(
        barrier, inc=1, device_id={"tensor": away}, device_id_type=pl.DeviceIdType.MESH
    )
    pl.semaphore_wait(barrier, count + 1)

    def along(block, step):
        return (
            mesh_copy(
                info_ref.at[block],
                info_ref.at[block],
                i_send.at[(step + 1) // 2, block],
                i_recv.at[block],
                me + 2 * step,
            ),
            mesh_copy(
                block_ref.at[block],
                block_ref.at[block],
                b_send.at[(step + 1) // 2, block],
                b_recv.at[block],
                me + 2 * step,
            ),
        )

    def across(block):
        return (
            mesh_copy(ms_ref.at[block], meta_ref.at[1, block], m_send.at[block], m_recv.at[block], mate),
            mesh_copy(xs_ref.at[block], x_ref.at[1, block], x_send.at[block], x_recv.at[block], mate),
        )

    def rows_of(number):
        return pl.ds(pl.multiple_of(number * cap, cap), cap)

    def origin(part, block):
        return 2 * block + side + part * (1 - 2 * side)

    def give_back(part, block):
        return mesh_copy(
            x_ref.at[part, block],
            came_ref.at[rows_of(me)],
            r_send.at[part, block],
            r_recv.at[me],
            origin(part, block),
        )

    def each(pair, act):
        for one in pair:
            act(one)

    own = (
        pltpu.make_async_copy(info_in, info_ref.at[place], local_sem.at[0]),
        pltpu.make_async_copy(normed_ref, block_ref.at[place], local_sem.at[1]),
    )
    each(own, lambda c: c.start())
    rest = D // 8 * 5
    far_down = tensor_copy(down_ref.at[rest:], w_ref.at[1, D + rest :], y_send, y_recv, away)
    far_down.start()
    grads_load = pltpu.make_async_copy(grads_in, grads_ref, grads_sem)
    grads_load.start()
    near = [
        (
            pltpu.make_async_copy(near_info_ref.at[i], info_ref.at[place + 2 * i - 1], near_sem.at[i]),
            pltpu.make_async_copy(near_ref.at[i], block_ref.at[place + 2 * i - 1], near_sem.at[i + 2]),
        )
        for i in range(2)
    ]
    inside = [place > 0, place < LINE - 1]
    for i in range(2):

        @pl.when(inside[i])
        def _():
            each(near[i], lambda c: c.start())

    weights = (
        (up_ref, 0, 0, D), (down_ref, 0, D, D), (far_up_ref, 1, 0, D), (far_half_ref, 1, D, rest),
        (w_ref.at[1, D + rest :], 1, D + rest, D - rest),
    )

    def load(i):
        source, q, start, size = weights[i]
        return pltpu.make_async_copy(source, w_ref.at[q, start : start + size], w_sem.at[i])

    def lend(i):
        source, q, start, size = weights[i]
        return tensor_copy(source, w_ref.at[2 + q, start : start + size], v_send.at[i], v_recv.at[i], core)

    for i in range(2):

        @pl.when(inside[i])
        def _():
            each(near[i], lambda c: c.wait())

            @pl.when(inside[1 - i])
            def _():
                each(along(place + 2 * i - 1, 1 - 2 * i), lambda c: c.start())

    for i in range(4):
        load(i).start()
        lend(i).start()
    each(own, lambda c: c.wait())
    experts = router_ref.shape[0]
    rows = normed_ref.shape[0]

    def select(block):
        info = info_ref[block]
        slots = info[0:2].astype(jnp.int32)
        lines0 = meta_lines(info[2:3], info[5:6])
        lines1 = meta_lines(info[3:4], info[4:5])
        for part, expert in ((1, mate), (0, me)):
            where = iota((cap, rows), 0) + expert * cap
            pick0 = where == slots[0:1]
            pick1 = where == slots[1:2]
            taken = dot((pick0 | pick1).astype(BF), block_ref[block]).astype(BF)
            meta = dot(lines0, pick0.astype(BF), 1, 1) + dot(lines1, pick1.astype(BF), 1, 1)
            if part:
                xs_ref[block] = taken
                ms_ref[block] = meta
                each(across(block), lambda c: c.start())
            else:
                x_ref[0, block] = taken
                meta_ref[0, block] = meta

    select(place)
    grouter_ref[...] = jnp.zeros_like(grouter_ref)
    mirror = place // 2
    inward = place + mirror * (LINE - 1 - 2 * place)

    def block_at(i):
        step = i + inward * (1 - i // 2 - 2 * (i // 2 - i // (LINE - 1)))
        return step + mirror * (LINE - 1 - 2 * step)

    outer = sum(d * 8**i for i, d in enumerate((0, 1, 4, 2, 5, 3, 6, 7)))
    inner = sum(d * 8**i for i, d in enumerate((0, 1, 4, 2, 5, 3, 6, 7)))
    chunks = outer + inward * (inner - outer)

    def chunk_at(power):
        digit = lax.rem(chunks // power, 8)
        return digit // 4, block_at(lax.rem(digit, 4))

    for i in range(2):

        @pl.when(inside[i])
        def _():
            select(place + 2 * i - 1)

    grads_load.wait()
    for i in range(2):
        load(i).wait()
        lend(i).wait_recv()

    def far_ready(c):
        @pl.when(c == 0)
        def _():
            far_down.wait_recv()
            lend(4).start()
            for i in (2, 3):
                load(i).wait()
                lend(i).wait_recv()
            lend(4).wait_recv()


    def chunk(c, power):
        for distance in range(2, LINE):

            @pl.when(c == 4 * distance - 7)
            def _():
                line_accept(place, distance, along, select)

        part, block = chunk_at(power)

        @pl.when(part == 1)
        def _():
            each(across(block), lambda c: c.wait_recv())

        here = pl.ds(pl.multiple_of(c * cap, cap), cap)
        meta = meta_ref[part, block].T
        gate = meta[:, 0:1] + meta[:, 1:2] + meta[:, 2:3]
        code = meta[:, 3:4].astype(jnp.int32)
        geo = (gate * grads_ref[part, block].astype(F32)).astype(BF)
        x = x_ref[part, block]
        worth = expert_rows(lambda: far_ready(c), x, geo, here, w_ref, xt_ref, geot_ref, act_ref, gi_ref, acc_ref)
        ids = iota((cap, experts), 1)
        signs = (ids == me).astype(F32) - (ids + 1 == code).astype(F32)
        share = jnp.where(code > 0, (1.0 - gate) * worth, 0.0) * signs
        high = share.astype(BF)
        low = (share - high.astype(F32)).astype(BF)
        grouter_ref[...] += dot(high.T, x) + dot(low.T, x)
        x_ref[part, block] = (acc_ref[...] + dot(high, router_ref[...])).astype(BF)

        @pl.when(origin(part, block) != me)
        def _():
            give_back(part, block).start()

        return power * 8

    lax.fori_loop(0, count, chunk, jnp.int32(1))
    own_back = pltpu.make_async_copy(x_ref.at[0, place], came_ref.at[rows_of(me)], local_sem.at[0])
    own_back.start()

    def results(step, carry):
        first = step // (D // TILE) * LINE
        cols, total = expert_outs(first * cap, LINE * cap, lax.rem(step, D // TILE), act_ref, w_ref)
        for i in range(LINE):
            part, block = chunk_at((1 + first // LINE * (8**LINE - 1)) * 8**i)
            meta = meta_ref[part, block].T
            gate = meta[:, 0:1] + meta[:, 1:2] + meta[:, 2:3]
            result_ref[rows_of(origin(part, block)), cols] = (
                gate * total[i * cap : (i + 1) * cap]
            ).astype(BF)
        return carry

    lax.fori_loop(0, 2 * (D // TILE), results, 0)
    leave = pltpu.make_async_copy(result_ref, result_out, local_sem.at[1])
    leave.start()
    weight_grads(xt_ref, geot_ref, act_ref, gi_ref, stage_ref, turned_ref, stay_ref, away_ref, go_ref, out_sem)
    own_back.wait()
    leave.wait()
    for i in range(5):
        lend(i).wait_send()
    far_down.wait_send()
    line_sent(place, along, 1)
    for block in range(LINE):
        each(across(block), lambda c: c.wait_send())
        for part in (0, 1):

            @pl.when(origin(part, block) != me)
            def _():
                give_back(part, block).wait_send()

    for number in range(count):

        @pl.when(number != me)
        def _():
            mesh_copy(
                x_ref.at[0, 0], came_ref.at[rows_of(number)], r_send.at[0, 0], r_recv.at[number], mate
            ).wait_recv()


def turn_kernel(lengths_ref, came_ref, slots_ref, hidden_ref, gain_ref, grad_ref, gh_ref, ga_ref, gain_out):
    gn = dot(back_matrix(slots_ref, came_ref.shape[0]), came_ref[...])
    hidden = hidden_ref[...]
    scale = rms(hidden)
    unit = hidden * scale
    gain_out[...] = jnp.broadcast_to(jnp.sum(gn * unit, axis=0, keepdims=True), gain_out.shape)
    g = gn * as_row(gain_ref)
    valid = (iota((hidden.shape[0], 1), 0) < own_valid(lengths_ref, hidden.shape[0])).astype(F32)
    gh = scale * (g - unit * jnp.mean(g * unit, axis=1, keepdims=True)) + valid * grad_ref[...].astype(F32)
    gh_ref[...] = gh
    ga_ref[...] = gh.astype(BF)


def output_kernel(lengths_ref, came_ref, slots_ref, hidden_ref, out_ref):
    mix = dot(back_matrix(slots_ref, came_ref.shape[0]), came_ref[...])
    hidden = hidden_ref[...]
    valid = (iota((hidden.shape[0], 1), 0) < own_valid(lengths_ref, hidden.shape[0])).astype(F32)
    out_ref[...] = (valid * (hidden + mix)).astype(BF)


def last_kernel(x_ref, keep_ref, got_ref, gain_ref, gh_ref, out_ref, gain_out):
    x = x_ref[...].astype(F32)
    scale = rms(x)
    unit = x * scale
    gn = keep_ref[...] + got_ref[...].astype(F32)
    gain_out[...] = jnp.broadcast_to(jnp.sum(gn * unit, axis=0, keepdims=True), gain_out.shape)
    g = gn * as_row(gain_ref)
    out_ref[...] = (
        gh_ref[...] + scale * (g - unit * jnp.mean(g * unit, axis=1, keepdims=True))
    ).astype(BF)


def moe(experts, cap, packed, meta, grads, router, quarters):
    spots = experts * cap
    anyspec = pl.BlockSpec(memory_space=pl.ANY)
    dma = pltpu.SemaphoreType.DMA
    return pl.pallas_call(
        functools.partial(expert_kernel, experts, cap),
        out_shape=[
            jax.ShapeDtypeStruct((spots, D), BF),
            jax.ShapeDtypeStruct((spots, D), BF),
            jax.ShapeDtypeStruct((2 * D, D), BF),
            jax.ShapeDtypeStruct((2 * D, D), BF),
            jax.ShapeDtypeStruct((2, 2 * D, D), BF),
            jax.ShapeDtypeStruct((experts, D), F32),
        ],
        in_specs=[anyspec, VM, VM, VM] + [anyspec] * 4,
        out_specs=[anyspec, VM, anyspec, anyspec, anyspec, VM],
        scratch_shapes=[
            pltpu.VMEM((4, 2 * D, D), BF),
            pltpu.VMEM((spots, D), BF),
            pltpu.VMEM((D, spots), BF),
            pltpu.VMEM((D, spots), BF),
            pltpu.VMEM((4, spots, D), BF),
            pltpu.VMEM((4, spots, D), BF),
            pltpu.VMEM((spots, D), BF),
            pltpu.VMEM((experts, 8, cap), F32),
            pltpu.VMEM((CHUNK, D), F32),
            pltpu.VMEM((2, D, TILE), BF),
            pltpu.VMEM((2, TILE, D), BF),
            dma((experts,)),
            dma((experts,)),
            dma((experts,)),
            dma((experts,)),
            dma((experts,)),
            dma((experts,)),
            dma((2,)),
            dma((4,)),
            dma((2,)),
        ],
        compiler_params=pltpu.CompilerParams(
            collective_id=1, has_side_effects=True, vmem_limit_bytes=60 * MIB
        ),
        cost_estimate=pl.CostEstimate(flops=12 * spots * D * 4 * D, bytes_accessed=60 * MIB, transcendentals=0),
        name="experts",
    )(packed, meta, grads, router, *quarters)


def moe_line(experts, cap, normed, info, router, others):
    rows = normed.shape[0]
    spots = experts * cap
    anyspec = pl.BlockSpec(memory_space=pl.ANY)
    dma = pltpu.SemaphoreType.DMA
    return pl.pallas_call(
        functools.partial(expert_line_kernel, cap),
        out_shape=[
            jax.ShapeDtypeStruct((spots, D), BF),
            jax.ShapeDtypeStruct((spots, D), BF),
            jax.ShapeDtypeStruct((2 * D, D), BF),
            jax.ShapeDtypeStruct((2 * D, D), BF),
            jax.ShapeDtypeStruct((2, 2 * D, D), BF),
            jax.ShapeDtypeStruct((experts, D), F32),
        ],
        in_specs=[VM, VM, VM] + [anyspec] * 7,
        out_specs=[anyspec, anyspec, anyspec, anyspec, anyspec, VM],
        scratch_shapes=[
            pltpu.VMEM((spots, D), BF),
            pltpu.VMEM((2, LINE, cap, D), BF),
            pltpu.VMEM((4, 2 * D, D), BF),
            pltpu.VMEM((LINE, rows, D), BF),
            pltpu.VMEM((LINE, 8, rows), F32),
            pltpu.VMEM((2, LINE, cap, D), BF),
            pltpu.VMEM((LINE, cap, D), BF),
            pltpu.VMEM((2, LINE, 8, cap), F32),
            pltpu.VMEM((LINE, 8, cap), F32),
            pltpu.VMEM((D, spots), BF),
            pltpu.VMEM((D, spots), BF),
            pltpu.VMEM((4, spots, D), BF),
            pltpu.VMEM((4, spots, D), BF),
            pltpu.VMEM((cap, D), F32),
            pltpu.VMEM((2, D, TILE), BF),
            pltpu.VMEM((2, TILE, D), BF),
            dma((2, LINE)),
            dma((LINE,)),
            dma((2, LINE)),
            dma((LINE,)),
            dma((LINE,)),
            dma((LINE,)),
            dma((LINE,)),
            dma((LINE,)),
            dma((2, LINE)),
            dma((experts,)),
            dma((2,)),
            dma((4,)),
            dma((5,)),
            dma((5,)),
            dma,
            dma,
            dma,
            dma((4,)),
            dma((2,)),
        ],
        compiler_params=pltpu.CompilerParams(
            collective_id=2, has_side_effects=True, vmem_limit_bytes=62 * MIB
        ),
        cost_estimate=pl.CostEstimate(flops=12 * spots * D * 4 * D, bytes_accessed=60 * MIB, transcendentals=0),
        name="experts_line",
    )(normed, info, router, *others)


def tensor_copy(src, dst, send_sem, recv_sem, target):
    return pltpu.make_async_remote_copy(
        src_ref=src,
        dst_ref=dst,
        send_sem=send_sem,
        recv_sem=recv_sem,
        device_id={"tensor": target},
        device_id_type=pl.DeviceIdType.MESH,
    )


def sums(
    pair_done, beside, gw_ref, pair_ref, keep_ref, send_ref, x_in, gain_ref, gh_ref, moe_ref, router_ref, bias0_ref, bias1_ref,
    gwt_out, gow_out, gin_out, attn_out, moe_out, router_out, bias_out,
    small_out, part_ref, cross_ref, line_ref, from_ref, all_ref, got_ref, lines_ref, few_ref, ranks_ref,
    a_send, a_recv, b_send, b_recv, c_send, c_recv, d_send, d_recv, s_send, s_recv, f_send, f_recv, t_send, t_recv, g_send, g_recv,
):
    count = 2 * LINE
    me = lax.axis_index("expert")
    rank = lax.axis_index("tensor")
    place = me // 2
    side = me - 2 * place
    mate = me + 1 - 2 * side
    size = part_ref.shape[0] // count
    def slab(which, number):
        return pl.ds(pl.multiple_of((which * LINE + number) * size, size), size)

    swap = tensor_copy(send_ref, got_ref, s_send, s_recv, flipped(rank, 1, 4))
    swap.start()
    pair_done()
    part_ref[...] = (gw_ref[...] + pair_ref[...].astype(F32)).astype(BF)
    rows = gwt_out.shape[0]

    def cross(number):
        return mesh_copy(
            part_ref.at[slab(1 - side, number)], cross_ref.at[number], a_send.at[number], a_recv.at[number], mate
        )

    def along(number):
        return mesh_copy(
            line_ref.at[number], from_ref.at[place], b_send.at[number], b_recv.at[place], 2 * number + side
        )

    def spread(number):
        return mesh_copy(
            all_ref.at[slab(side, place)],
            all_ref.at[slab(side, place)],
            c_send.at[number],
            c_recv.at[place],
            2 * number + side,
        )

    def over(number):
        return mesh_copy(
            all_ref.at[slab(side, number)], all_ref.at[slab(side, number)], d_send.at[number], d_recv.at[number], mate
        )

    for number in range(LINE):
        cross(number).start()

    swap.wait()
    x = x_in[...].astype(F32)
    scale = rms(x)
    unit = x * scale
    gn = keep_ref[...] + got_ref[...].astype(F32)
    attn = jnp.sum(gn * unit, axis=0, keepdims=True)
    g = gn * as_row(gain_ref)
    gin_out[...] = (gh_ref[...] + scale * (g - unit * jnp.mean(g * unit, axis=1, keepdims=True))).astype(BF)

    heads = gow_out.shape[0] // HD
    blank = jnp.zeros((1, 128), F32)

    def flat(bias_ref):
        line = [bias_ref[h : h + 1, :NB] for h in range(heads)]
        return jnp.concatenate(line + [jnp.zeros((1, 128 - heads * NB), F32)], axis=1)

    own_bias, pair_bias = flat(bias0_ref), flat(bias1_ref)
    other = flipped(rank, 2, 4)
    for j in range(D // 128):
        lines_ref[j] = router_ref[:, j * 128 : (j + 1) * 128]
    for j, row in ((6, attn), (7, moe_ref[0:1])):
        places = [2 * (j - 6), 2 * (j - 6) + 1]
        bias = [
            jnp.where(rank == p, own_bias, blank) + jnp.where(other == p, pair_bias, blank) for p in places
        ]
        lines_ref[j] = jnp.concatenate([row[:, i * 128 : (i + 1) * 128] for i in range(6)] + bias, axis=0)

    def small(k):
        return mesh_copy(
            lines_ref.at[flipped(me, k, count)], few_ref.at[k], f_send.at[k], f_recv.at[k], flipped(me, k, count)
        )

    def rank_copy(k):
        return tensor_copy(
            ranks_ref.at[rank], ranks_ref.at[rank], t_send.at[k], t_recv.at[k], flipped(rank, k, 4)
        )

    def rank_from(k):
        return tensor_copy(
            ranks_ref.at[rank], ranks_ref.at[flipped(rank, k, 4)], t_send.at[k], t_recv.at[k], flipped(rank, k, 4)
        )

    def small_spread(k):
        return mesh_copy(
            small_out.at[me], small_out.at[me], g_send.at[k], g_recv.at[k], flipped(me, k, count)
        )

    def small_from(k):
        return mesh_copy(
            small_out.at[me], small_out.at[flipped(me, k, count)], g_send.at[k], g_recv.at[k], flipped(me, k, count)
        )

    for k in range(1, count):
        small(k).start()

    for number in range(LINE):

        @pl.when(number != place)
        def _():
            cross(number).wait_recv()
            line_ref[number] = (
                part_ref[slab(side, number)].astype(F32) + cross_ref[number].astype(F32)
            ).astype(BF)
            along(number).start()

    total = lines_ref[me]
    for k in range(1, count):
        small(k).wait_recv()
        total = total + few_ref[k]
    ranks_ref[rank] = total
    for k in range(1, 4):
        rank_copy(k).start()

    for number in range(LINE):

        @pl.when(number == place)
        def _():
            cross(number).wait_recv()

    beside()
    whole = part_ref[slab(side, place)].astype(F32) + cross_ref[place].astype(F32)
    from_ref[place] = whole.astype(BF)
    for k in range(1, LINE):
        number = lax.rem(place + k, LINE)
        mesh_copy(
            line_ref.at[number], from_ref.at[number], b_send.at[number], b_recv.at[number], mate
        ).wait_recv()
        whole = whole + from_ref[number].astype(F32)
    all_ref[slab(side, place)] = whole.astype(BF)
    over(place).start()
    for number in range(LINE):

        @pl.when(number != place)
        def _():
            spread(number).start()

    for k in range(1, 4):
        rank_from(k).wait_recv()
    small_out[me] = ranks_ref[0] + ranks_ref[1] + ranks_ref[2] + ranks_ref[3]
    for k in range(1, count):
        small_spread(k).start()

    for k in range(1, LINE):
        number = lax.rem(place + k, LINE)
        mesh_copy(
            all_ref.at[slab(side, number)], all_ref.at[slab(side, number)], c_send.at[number], c_recv.at[number], mate
        ).wait_recv()
        over(number).start()
    for k in range(1, count):
        small_from(k).wait_recv()
    for number in range(LINE):
        mesh_copy(
            all_ref.at[slab(1 - side, number)],
            all_ref.at[slab(1 - side, number)],
            d_send.at[number],
            d_recv.at[number],
            mate,
        ).wait_recv()
    attn_out[...] = jnp.concatenate([small_out[6, i : i + 1] for i in range(6)], axis=1).reshape(D)
    moe_out[...] = jnp.concatenate([small_out[7, i : i + 1] for i in range(6)], axis=1).reshape(D)
    router_out[...] = jnp.concatenate([small_out[j] for j in range(D // 128)], axis=1)
    bias = functools.reduce(
        jnp.add,
        [jnp.where(rank == p, small_out[6 + p // 2, 6 + p % 2 : 7 + p % 2], blank) for p in range(4)],
    )
    bias_out[...] = jnp.concatenate([bias[:, h * NB : (h + 1) * NB] for h in range(heads)], axis=0)
    gwt_out[...] = all_ref[:rows].astype(F32)
    gow_out[...] = all_ref[rows:].astype(F32)
    for number in range(LINE):
        cross(number).wait_send()
        over(number).wait_send()

        @pl.when(number != place)
        def _():
            along(number).wait_send()
            spread(number).wait_send()

    for k in range(1, count):
        small(k).wait_send()
        small_spread(k).wait_send()
    for k in range(1, 4):
        rank_copy(k).wait_send()


PARTS = 6


def finish_kernel(
    heads, cap, lengths_ref,
    table0_ref, table1_ref, slots_ref, gain2_ref, gain1_ref, router_ref,
    came_in, hidden_in, grad_in, result_in, go_in, away_in, x_in, normed_in, wt_in, ow_in, pw_in, qkvt0_in, mixt0_in, lse0_in, qkvt1_in, mixt1_in, lse1_in,
    out_ref, gin_out, gwt_out, gow_out, attn_out, moe_out, router_out, bias_out, came_go_ref, came_away_ref,
    came_ref, hidden_ref, grad_ref, outs_ref, gorecv_ref, away_ref, x_ref, normed_ref, wt_ref, ow_ref, pw_ref, qkvt0_ref, mixt0_ref, lse0_ref, qkvt1_ref, mixt1_ref, lse1_ref,
    gh_ref, ga_ref, other_ref, moe_ref, gpart_ref, gpair_ref, gown_ref, bias0_ref, bias1_ref, keep_ref, send_ref,
    all_ga_ref, got_ref, gt_ref, d0_ref, d1_ref, npart_ref,
    o_send, o_recv, v_send, v_recv, y_send, y_recv, w_send, w_recv, e_send, e_recv, load_sem, *tail_refs,
):
    count = 2 * LINE
    me = lax.axis_index("expert")
    rank = lax.axis_index("tensor")
    core = flipped(rank, 1, 4)
    away_rank = flipped(rank, 2, 4)
    places = (
        (came_in, came_ref),
        (hidden_in, hidden_ref),
        (grad_in, grad_ref),
        (normed_in, normed_ref),
        (pw_in, pw_ref),
        (qkvt1_in, qkvt1_ref),
        (mixt1_in, mixt1_ref),
        (lse1_in, lse1_ref),
        (wt_in, wt_ref),
        (ow_in, ow_ref),
        (qkvt0_in, qkvt0_ref),
        (mixt0_in, mixt0_ref),
        (lse0_in, lse0_ref),
        (x_in, x_ref),
    )
    loads = [pltpu.make_async_copy(a, b, load_sem.at[i + 2]) for i, (a, b) in enumerate(places)]
    for load in loads:
        load.start()
    barrier = pltpu.get_barrier_semaphore()
    for k in range(1, count):
        pl.semaphore_signal(
            barrier, inc=1, device_id={"expert": flipped(me, k, count)}, device_id_type=pl.DeviceIdType.MESH
        )
    for k in range(1, 4):
        pl.semaphore_signal(
            barrier, inc=1, device_id={"tensor": flipped(rank, k, 4)}, device_id_type=pl.DeviceIdType.MESH
        )
    pl.semaphore_wait(barrier, count + 2)

    def rows_of(number):
        return pl.ds(pl.multiple_of(number * cap, cap), cap)

    def result(k):
        return mesh_copy(
            result_in.at[rows_of(flipped(me, k, count))],
            outs_ref.at[rows_of(me)],
            o_send.at[k],
            o_recv.at[k],
            flipped(me, k, count),
        )

    order = list(range(LINE, count)) + list(range(1, LINE))
    for k in order:
        result(k).start()
    own_result = pltpu.make_async_copy(result_in.at[rows_of(me)], outs_ref.at[rows_of(me)], load_sem.at[0])
    own_result.start()
    away_load = pltpu.make_async_copy(away_in, away_ref, load_sem.at[1])
    away_load.start()
    go_away = tensor_copy(go_in.at[1], gorecv_ref, v_send.at[0], v_recv.at[0], core)
    go_away.start()
    go_stay = tensor_copy(go_in.at[0], came_go_ref, v_send.at[1], v_recv.at[1], core)
    for load in loads[:3]:
        load.wait()
    turn_kernel(lengths_ref, came_ref, slots_ref, hidden_ref, gain2_ref, grad_ref, gh_ref, ga_ref, moe_ref)
    ga_swap = tensor_copy(ga_ref, other_ref, w_send, w_recv, core)
    ga_swap.start()
    away_load.wait()
    go_away.wait_recv()
    size = away_ref.shape[0] // PARTS

    def lines(i):
        return pl.ds(i * size, size)

    def away(i):
        return tensor_copy(
            away_ref.at[lines(i)], came_away_ref.at[lines(i)], y_send.at[i], y_recv.at[i], away_rank
        )

    for i in range(PARTS):
        away_ref[lines(i)] = (
            away_ref[lines(i)].astype(F32) + gorecv_ref[lines(i)].astype(F32)
        ).astype(BF)
        if i < 1:
            away(i).start()
    ga_swap.wait()
    go_stay.start()
    for load in loads[3:]:
        load.wait()
    inner = heads * HD
    split = ((slice(3 * inner, 4 * inner), 0), (slice(0, 3 * inner), 1))
    pair = [
        tensor_copy(gpart_ref.at[lines_of], gpair_ref.at[lines_of], e_send.at[i], e_recv.at[i], away_rank)
        for lines_of, i in split
    ]
    attn_bwd_kernel(
        pair[0].start, False, heads, lengths_ref, table1_ref,
        normed_ref, pw_ref.at[: 3 * inner], pw_ref.at[3 * inner :], qkvt1_ref, mixt1_ref, lse1_ref, ga_ref, other_ref,
        gpart_ref, bias1_ref, npart_ref, all_ga_ref, got_ref, gt_ref, d0_ref, d1_ref,
    )
    pair[1].start()
    attn_bwd_kernel(
        None, True, heads, lengths_ref, table0_ref,
        normed_ref, wt_ref, ow_ref, qkvt0_ref, mixt0_ref, lse0_ref, ga_ref, other_ref, npart_ref,
        gown_ref, bias0_ref, keep_ref, send_ref, all_ga_ref, got_ref, gt_ref, d0_ref, d1_ref, npart_ref,
    )

    def pair_done():
        for one in pair:
            one.wait_recv()
        for i in range(1, PARTS):
            away(i).start()

    def beside():
        own_result.wait()
        for k in order:
            result(k).wait_recv()
        output_kernel(lengths_ref, outs_ref, slots_ref, hidden_ref, out_ref)

    sums(
        pair_done, beside, gown_ref, gpair_ref, keep_ref, send_ref, x_ref, gain1_ref, gh_ref, moe_ref, router_ref,
        bias0_ref, bias1_ref, gwt_out, gow_out, gin_out, attn_out, moe_out, router_out, bias_out, *tail_refs,
    )
    for k in order:
        result(k).wait_send()
    for one in pair:
        one.wait_send()
    go_away.wait_send()
    go_stay.wait()
    for i in range(PARTS):
        away(i).wait()


def finish(heads, cap, scalars, arrays, others):
    dma = pltpu.SemaphoreType.DMA
    count = 2 * LINE
    spots = count * cap
    rows = others[1].shape[0]
    local = heads * HD
    part = 4 * local // count
    anyspec = pl.BlockSpec(memory_space=pl.ANY)
    half = (rows, D)
    tail_sems = [dma((LINE,))] * 8 + [dma, dma] + [dma((count,))] * 2 + [dma((4,))] * 2 + [dma((count,))] * 2
    shapes = [
        ((spots, D), BF), (half, F32), (half, BF),
        ((spots, D), BF), ((2 * D, D), BF), ((2 * D, D), BF), (half, BF), ((SEQ, D), BF), ((3 * local, D), BF),
        ((local, D), BF), ((4 * local, D), BF), ((3 * local, SEQ), BF), ((local, SEQ), BF), ((8, SEQ), F32),
        ((3 * local, SEQ), BF), ((local, SEQ), BF), ((8, SEQ), F32),
        (half, F32), (half, BF), (half, BF), ((8, D), F32), ((4 * local, D), BF), ((4 * local, D), BF),
        ((4 * local, D), F32), ((8, 128), F32), ((8, 128), F32), (half, F32), (half, BF),
        ((SEQ, D), BF), ((local, SEQ), BF), ((3 * local, SEQ), BF), ((TILE, TILE), F32), ((TILE, TILE), F32), ((SEQ, D), F32),
    ]
    tail_shapes = [
        ((count, 8, 128), F32),
        ((4 * local, D), BF), ((LINE, part, D), BF), ((LINE, part, D), BF), ((LINE, part, D), BF), ((4 * local, D), BF),
        (half, BF), ((count, 8, 128), F32), ((count, 8, 128), F32), ((4, 8, 128), F32),
    ]
    return pl.pallas_call(
        functools.partial(finish_kernel, heads, cap),
        out_shape=[
            jax.ShapeDtypeStruct(half, BF),
            jax.ShapeDtypeStruct(half, BF),
            jax.ShapeDtypeStruct((3 * local, D), F32),
            jax.ShapeDtypeStruct((local, D), F32),
            jax.ShapeDtypeStruct((D,), F32),
            jax.ShapeDtypeStruct((D,), F32),
            jax.ShapeDtypeStruct((count, D), F32),
            jax.ShapeDtypeStruct((heads, NB), F32),
            jax.ShapeDtypeStruct((2 * D, D), BF),
            jax.ShapeDtypeStruct((2 * D, D), BF),
        ],
        in_specs=[SM] * len(scalars) + [VM] * len(arrays) + [anyspec] * len(others),
        out_specs=[VM] * 8 + [anyspec] * 2,
        scratch_shapes=[pltpu.VMEM(*v) for v in shapes]
        + [dma((count,)), dma((count,)), dma((2,)), dma((2,)), dma((PARTS,)), dma((PARTS,)), dma, dma, dma((2,)), dma((2,)), dma((16,))]
        + [pltpu.VMEM(*v) for v in tail_shapes]
        + tail_sems,
        compiler_params=pltpu.CompilerParams(
            collective_id=3, has_side_effects=True, vmem_limit_bytes=62 * MIB
        ),
        cost_estimate=pl.CostEstimate(flops=0, bytes_accessed=200 * MIB, transcendentals=0),
        name="finish",
    )(*scalars, *arrays, *others)


def line_accept(place, distance, copies, take):
    for step in (-1, 1):
        block = place + step * distance

        @pl.when((block >= 0) & (block < LINE))
        def _():
            for one in copies(block, -step):
                one.wait_recv()
            ahead = place - step

            @pl.when((ahead >= 0) & (ahead < LINE))
            def _():
                for one in copies(block, -step):
                    one.start()

    for step in (-1, 1):
        block = place + step * distance

        @pl.when((block >= 0) & (block < LINE))
        def _():
            take(block)


def line_sent(place, copies, least):
    for block in range(LINE):
        for step in (-1, 1):

            @pl.when((place + step >= 0) & (place + step < LINE) & ((place - block) * step >= least))
            def _():
                for one in copies(block, step):
                    one.wait_send()


def begin_kernel(
    heads, cap, lengths_ref,
    table_ref, x_ref, gain1_ref, wt_ref, ow_ref, routes_ref, grad_ref, router_ref, gain2_ref, up_ref, down_ref,
    normed_out, qkvt0_out, mixt0_out, lse0_out, qkvt1_out, mixt1_out, lse1_out, hidden_ref, normed2_ref, info_ref, slots_ref,
    pw_ref, table1_ref, gy_ref, far_up_ref, far_half_ref, near_ref, near_info_ref,
    other_ref, got_ref, part_ref, keep_ref, send_ref, block_ref, places_ref, gsend_ref, gkeep_ref,
    normed_ref, qkvt0_ref, mixt0_ref, lse0_ref, qkvt1_ref, mixt1_ref, lse1_ref,
    b_send, b_recv, i_send, i_recv, x_send, x_recv, v_send, v_recv, y_send, y_recv, n_send, n_recv, keep_sem, store_sem,
):
    count = 2 * LINE
    me = lax.axis_index("expert")
    rank = lax.axis_index("tensor")
    place = me // 2
    side = me - 2 * place
    mate = me + 1 - 2 * side
    core = flipped(rank, 1, 4)
    away = flipped(rank, 2, 4)
    inner = heads * HD
    barrier = pltpu.get_barrier_semaphore()
    for k in range(1, count):
        pl.semaphore_signal(
            barrier, inc=1, device_id={"expert": flipped(me, k, count)}, device_id_type=pl.DeviceIdType.MESH
        )
    for target in (core, away):
        pl.semaphore_signal(
            barrier, inc=1, device_id={"tensor": target}, device_id_type=pl.DeviceIdType.MESH
        )
    pl.semaphore_wait(barrier, count + 1)

    swap = tensor_copy(x_ref, other_ref, v_send.at[0], v_recv.at[0], core)
    swap.start()
    pair = (
        tensor_copy(ow_ref, pw_ref.at[3 * inner :], y_send.at[0], y_recv.at[0], away),
        tensor_copy(wt_ref, pw_ref.at[: 3 * inner], y_send.at[1], y_recv.at[1], away),
        tensor_copy(table_ref, table1_ref, y_send.at[2], y_recv.at[2], away),
    )
    for one in pair:
        one.start()
    far = (
        tensor_copy(up_ref, far_up_ref, y_send.at[3], y_recv.at[3], away),
        tensor_copy(down_ref.at[: D // 8 * 5], far_half_ref, y_send.at[4], y_recv.at[4], away),
    )

    def along(block, step):
        return (
            mesh_copy(
                places_ref.at[block], places_ref.at[block], i_send.at[(step + 1) // 2, block], i_recv.at[block], me + 2 * step
            ),
            mesh_copy(
                block_ref.at[block], block_ref.at[block], b_send.at[(step + 1) // 2, block], b_recv.at[block], me + 2 * step
            ),
        )

    def across(block):
        return mesh_copy(gsend_ref.at[block], gy_ref.at[1, block], x_send.at[block], x_recv.at[block], mate)

    def keep(block):
        return pltpu.make_async_copy(gkeep_ref.at[block], gy_ref.at[0, block], keep_sem.at[block])

    rows = grad_ref.shape[0]

    def take(block):
        slots = places_ref[block, 0:2].astype(jnp.int32)
        for part, expert in ((1, mate), (0, me)):
            where = iota((cap, rows), 0) + expert * cap
            picks = ((where == slots[0:1]) | (where == slots[1:2])).astype(BF)
            taken = dot(picks, block_ref[block]).astype(BF)
            if part:
                gsend_ref[block] = taken
                across(block).start()
            else:
                gkeep_ref[block] = taken
                keep(block).start()

    block_ref[place] = grad_ref[...]
    slots_kernel(count, cap, lengths_ref, routes_ref, slots_ref)
    places_ref[place] = slots_ref[...]
    for step in (-1, 1):

        @pl.when((place + step >= 0) & (place + step < LINE))
        def _():
            for one in along(place, step):
                one.start()

    take(place)
    swap.wait()
    attn_fwd_kernel(
        True, heads, lengths_ref, table_ref, x_ref, other_ref, gain1_ref, wt_ref, ow_ref,
        normed_ref, qkvt0_ref, mixt0_ref, lse0_ref, part_ref,
    )
    first = (
        (normed_ref, normed_out), (qkvt0_ref, qkvt0_out), (mixt0_ref, mixt0_out), (lse0_ref, lse0_out),
    )
    second = ((qkvt1_ref, qkvt1_out), (mixt1_ref, mixt1_out), (lse1_ref, lse1_out))
    stores = [pltpu.make_async_copy(a, b, store_sem.at[i]) for i, (a, b) in enumerate(first + second)]
    for store in stores[:4]:
        store.start()
    line_accept(place, 1, along, take)
    for one in pair:
        one.wait_recv()
    for one in far:
        one.start()
    attn_fwd_kernel(
        False, heads, lengths_ref, table1_ref, normed_ref, pw_ref.at[: 3 * inner], pw_ref.at[3 * inner :], part_ref,
        qkvt1_ref, mixt1_ref, lse1_ref, keep_ref, send_ref, part_ref,
    )
    back = tensor_copy(send_ref, got_ref, v_send.at[1], v_recv.at[1], core)
    back.start()
    for store in stores[4:]:
        store.start()
    line_accept(place, 2, along, take)
    back.wait()
    middle_line_kernel(
        count, x_ref, keep_ref, got_ref, gain2_ref, router_ref, routes_ref, slots_ref, hidden_ref, normed2_ref, info_ref
    )
    inside = [place > 0, place < LINE - 1]

    def neighbour(i):
        target = me + 2 * (1 - 2 * i)
        return (
            mesh_copy(info_ref, near_info_ref.at[i], n_send.at[i], n_recv.at[i], target),
            mesh_copy(normed2_ref, near_ref.at[i], n_send.at[i + 2], n_recv.at[i + 2], target),
        )

    line_sent(place, along, 0)
    for i in range(2):

        @pl.when(inside[1 - i])
        def _():
            for one in neighbour(i):
                one.start()

    line_accept(place, 3, along, take)
    for block in range(LINE):
        keep(block).wait()
        across(block).wait()
    for store in stores:
        store.wait()
    for one in pair:
        one.wait_send()
    for one in far:
        one.wait()
    for i in range(2):

        @pl.when(inside[i])
        def _():
            for one in neighbour(1 - i):
                one.wait_send()
            for one in neighbour(i):
                one.wait_recv()


def begin(heads, cap, scalars, arrays, others):
    dma = pltpu.SemaphoreType.DMA
    rows = arrays[1].shape[0]
    local = heads * HD
    anyspec = pl.BlockSpec(memory_space=pl.ANY)
    half = (rows, D)
    kept = [
        ((SEQ, D), BF), ((3 * local, SEQ), BF), ((local, SEQ), BF), ((8, SEQ), F32),
        ((3 * local, SEQ), BF), ((local, SEQ), BF), ((8, SEQ), F32),
    ]
    outs = kept + [
        (half, F32), (half, BF), ((8, rows), F32), ((8, rows), F32), ((4 * local, D), BF), ((heads, NB), F32),
        ((2, LINE, cap, D), BF), ((D, D), BF), ((D // 8 * 5, D), BF), ((2, rows, D), BF), ((2, 8, rows), F32),
    ]
    shapes = [
        (half, BF), (half, BF), ((SEQ, D), F32), (half, F32), (half, BF), ((LINE, rows, D), BF), ((LINE, 8, rows), F32),
        ((LINE, cap, D), BF), ((LINE, cap, D), BF),
    ] + kept
    return pl.pallas_call(
        functools.partial(begin_kernel, heads, cap),
        out_shape=[jax.ShapeDtypeStruct(*v) for v in outs],
        in_specs=[SM] * len(scalars) + [VM] * len(arrays) + [anyspec] * len(others),
        out_specs=[anyspec] * 7 + [VM] * 6 + [anyspec] * 5,
        scratch_shapes=[pltpu.VMEM(*v) for v in shapes]
        + [dma((2, LINE)), dma((LINE,)), dma((2, LINE)), dma((LINE,)), dma((LINE,)), dma((LINE,))]
        + [dma((2,)), dma((2,)), dma((5,)), dma((5,)), dma((4,)), dma((4,)), dma((LINE,)), dma((7,))],
        compiler_params=pltpu.CompilerParams(
            collective_id=4, has_side_effects=True, vmem_limit_bytes=56 * MIB
        ),
        cost_estimate=pl.CostEstimate(flops=0, bytes_accessed=200 * MIB, transcendentals=0),
        name="begin",
    )(*scalars, *arrays, *others)


def shards(
    inputs,
    lengths,
    routes,
    attn_gain,
    qkv_weight,
    out_weight,
    rel_bias,
    moe_gain,
    router_weight,
    up_weight,
    down_weight,
    out_grad,
):
    rows = inputs.shape[0]
    rank = lax.axis_index("tensor")
    expert = lax.axis_index("expert")
    heads = rel_bias.shape[1]
    inner = heads * HD
    experts = router_weight.shape[1]
    cap = 4 * rows // experts
    spots = experts * cap
    table = jnp.transpose(rel_bias)

    def swap(x, bit):
        return lax.ppermute(x, "tensor", [(i, i ^ bit) for i in range(4)])

    gain1, gain2 = attn_gain, moe_gain
    wt = jnp.transpose(qkv_weight.reshape(D, 3 * inner))
    routes_t = jnp.transpose(routes)
    up, down = up_weight[0], down_weight[0]
    line = experts == 2 * LINE and cap == TILE
    if line:
        router_t = jnp.transpose(router_weight)
        (
            normed, qkvt0, mixt0, lse0, qkvt1, mixt1, lse1, hidden, normed_two, info, slots, pair_w, pair_table, grads_in, far_up, far_half, near, near_info,
        ) = begin(
            heads,
            cap,
            (lengths,),
            (table, inputs, gain1, wt, out_weight, routes_t, out_grad, router_t, gain2),
            (up, down),
        )
        came, result, stay, away, go, grad_router = moe_line(
            experts, cap, normed_two, info, router_t, (grads_in, near, near_info, up, down, far_up, far_half)
        )
    else:
        other = swap(inputs, 1)
        pair_w = swap(jnp.concatenate([wt, out_weight], axis=0), 2)
        pair_table = swap(table, 2)

        packed_grad, slots = call(
            functools.partial(route_kernel, experts, cap),
            [((spots, D), BF), ((8, rows), F32)],
            (lengths, routes_t, out_grad),
            [SM, VM, VM],
            flops=2 * spots * rows * D,
            moved=4 * MIB,
            name="route",
        )

        def exchange(x):
            return lax.all_to_all(
                x.reshape(experts, cap, x.shape[-1]), "expert", split_axis=0, concat_axis=0, tiled=True
            ).reshape(x.shape)

        grads_in = exchange(packed_grad)
        up, down, pair_w, pair_table = lax.optimization_barrier((up, down, pair_w, pair_table))
        far_up, far_down = swap(up, 2), swap(down, 2)

        attn_cost = dict(
            flops=2 * SEQ * D * 4 * inner + heads * SEQ * SEQ * 160, moved=6 * MIB, exps=heads * SEQ * SEQ
        )
        normed, qkvt0, mixt0, lse0, part0 = call(
            functools.partial(attn_fwd_kernel, True, heads),
            [((SEQ, D), BF), ((3 * inner, SEQ), BF), ((inner, SEQ), BF), ((8, SEQ), F32), ((SEQ, D), F32)],
            (lengths, table, inputs, other, gain1, wt, out_weight),
            [SM] + [VM] * 1 + [VM] * 5,
            name="attend_own",
            **attn_cost,
        )
        wt1, ow1 = pair_w[: 3 * inner], pair_w[3 * inner :]
        qkvt1, mixt1, lse1, keep, send = call(
            functools.partial(attn_fwd_kernel, False, heads),
            [((3 * inner, SEQ), BF), ((inner, SEQ), BF), ((8, SEQ), F32), ((rows, D), F32), ((rows, D), BF)],
            (lengths, pair_table, normed, wt1, ow1, part0),
            [SM] + [VM] * 1 + [VM] * 4,
            scratch=[pltpu.VMEM((SEQ, D), F32)],
            name="attend_pair",
            **attn_cost,
        )
        got = swap(send, 1)
        middle_args = (inputs, keep, got, gain2, jnp.transpose(router_weight), routes_t, slots)
        mine = jnp.concatenate([up, down], axis=0)
        far = jnp.concatenate([far_up, far_down], axis=0)
        quarters = [mine, far, swap(mine, 1), swap(far, 1)]
        hidden, packed_rows, meta = call(
            functools.partial(middle_kernel, experts, cap),
            [((rows, D), F32), ((spots, D), BF), ((experts, 8, cap), F32)],
            middle_args,
            flops=2 * spots * rows * D,
            moved=8 * MIB,
            name="middle",
        )
        came, result, stay, away, go, grad_router = moe(
            experts, cap, packed_rows, meta, grads_in, router_weight, quarters
        )
    if line:
        outputs, grad_inputs, gwt, gow, attn_sum, moe_sum, router_sum, bias_sum, go_stay, came_away = finish(
            heads,
            cap,
            (lengths,),
            (table, pair_table, slots, gain2, gain1, grad_router),
            (came, hidden, out_grad, result, go, away, inputs, normed, wt, out_weight, pair_w, qkvt0, mixt0, lse0, qkvt1, mixt1, lse1),
        )
    else:
        came_out = exchange(result)
        came_go = swap(go, 1)
        grad_hidden, grad_attended, moe_part = call(
            turn_kernel,
            [((rows, D), F32), ((rows, D), BF), ((8, D), F32)],
            (lengths, came, slots, hidden, gain2, out_grad),
            [SM] + [VM] * 5,
            flops=2 * spots * rows * D,
            moved=8 * MIB,
            name="turn",
        )
        other_grad = swap(grad_attended, 1)
        away = (away.astype(F32) + came_go[1].astype(F32)).astype(BF)
        bwd_cost = dict(
            flops=2 * SEQ * D * 10 * inner + heads * SEQ * SEQ * 400, moved=9 * MIB, exps=heads * SEQ * SEQ
        )
        work = [
            pltpu.VMEM((SEQ, D), BF),
            pltpu.VMEM((inner, SEQ), BF),
            pltpu.VMEM((3 * inner, SEQ), BF),
            pltpu.VMEM((TILE, TILE), F32),
            pltpu.VMEM((TILE, TILE), F32),
        ]
        gpart, gbias1, npart = call(
            functools.partial(attn_bwd_kernel, None, False, heads),
            [((4 * inner, D), BF), ((8, 128), F32), ((SEQ, D), F32)],
            (lengths, pair_table, normed, wt1, ow1, qkvt1, mixt1, lse1, grad_attended, other_grad),
            [SM] + [VM] * 1 + [VM] * 8,
            scratch=work,
            name="attend_pair_back",
            **bwd_cost,
        )
        gpair = swap(gpart, 2)
        gown, gbias0, keep_n, send_n = call(
            functools.partial(attn_bwd_kernel, None, True, heads),
            [((4 * inner, D), F32), ((8, 128), F32), ((rows, D), F32), ((rows, D), BF)],
            (lengths, table, normed, wt, out_weight, qkvt0, mixt0, lse0, grad_attended, other_grad, npart),
            [SM] + [VM] * 1 + [VM] * 9,
            scratch=work + [pltpu.VMEM((SEQ, D), F32)],
            name="attend_own_back",
            **bwd_cost,
        )
        away, gpair, gown = lax.optimization_barrier((away, gpair, gown))
        came_away = swap(away, 2)
        got_n = swap(send_n, 1)
        grad_inputs, attn_part = call(
            last_kernel,
            [((rows, D), BF), ((8, D), F32)],
            (inputs, keep_n, got_n, gain1, grad_hidden),
            moved=6 * MIB,
            name="last",
        )
        wide = (gown + gpair.astype(F32)).astype(BF)
        wide = lax.psum(wide, "expert").astype(F32)
        outputs = call(
            output_kernel,
            [((rows, D), BF)],
            (lengths, came_out, slots, hidden),
            [SM] + [VM] * 3,
            flops=2 * spots * rows * D,
            moved=8 * MIB,
            name="outputs",
        )[0]
        go_stay = came_go[0]

    if line:
        router_sum = jnp.transpose(router_sum)
    else:
        gwt, gow = wide[: 3 * inner], wide[3 * inner :]
        own_bias = gbias0[:heads, :NB].reshape(1, -1)
        pair_bias = gbias1[:heads, :NB].reshape(1, -1)
        ranks = jnp.arange(4, dtype=jnp.int32)[:, None]
        bias_parts = jnp.where(ranks == rank, own_bias, 0.0) + jnp.where(
            ranks == (rank ^ 2), pair_bias, 0.0
        )
        small = jnp.concatenate(
            [attn_part[0], moe_part[0], jnp.transpose(grad_router).reshape(-1), bias_parts.reshape(-1)]
        )
        small = lax.psum(small, ("expert", "tensor"))
        attn_sum, moe_sum = small[:D], small[D : 2 * D]
        router_sum = small[2 * D : 2 * D + experts * D].reshape(D, experts)
        bias_sum = lax.dynamic_slice(
            small[2 * D + experts * D :].reshape(4, heads * NB), (rank, 0), (1, heads * NB)
        )
    grad_up, grad_down = (
        stay[rows_of].astype(F32) + go_stay[rows_of].astype(F32) + came_away[rows_of].astype(F32)
        for rows_of in (slice(0, D), slice(D, 2 * D))
    )
    return (
        outputs,
        grad_inputs,
        attn_sum,
        jnp.transpose(gwt).reshape(D, 3, inner),
        gow,
        jnp.transpose(bias_sum.reshape(heads, NB)),
        moe_sum,
        router_sum,
        grad_up[None],
        grad_down[None],
    )


def solution(mesh):
    return jax.shard_map(
        shards,
        mesh=mesh,
        in_specs=(
            P(("expert", "tensor"), None),
            P("expert"),
            P(("expert", "tensor"), None),
            P(),
            P(None, None, "tensor"),
            P("tensor", None),
            P(None, "tensor"),
            P(),
            P(),
            P("expert", None, "tensor"),
            P("expert", "tensor", None),
            P(("expert", "tensor"), None),
        ),
        out_specs=(
            P(("expert", "tensor"), None),
            P(("expert", "tensor"), None),
            P(),
            P(None, None, "tensor"),
            P("tensor", None),
            P(None, "tensor"),
            P(),
            P(),
            P("expert", None, "tensor"),
            P("expert", "tensor", None),
        ),
        check_vma=False,
    )
```

```python
import functools

import jax
import jax.numpy as jnp
from jax import lax
from jax.experimental import pallas as pl
from jax.experimental.pallas import tpu as pltpu
from jax.sharding import PartitionSpec as P

D = 768
HD = 64
NB = 32
MAXDIST = 128
SEQ = 1024
EPSILON = 1e-06
NEGATIVE = -1e30
TILE = 256
BF = jnp.bfloat16
F32 = jnp.float32
MIB = 2**20
CHUNK = 256
GELU = 0.7978845608028654
CUBIC = 0.044715


def bucket_edges():
    half_count = NB // 2
    short_edges = list(range(1, half_count))
    long_edges = [
        int(half_count * (MAXDIST / half_count) ** (step_index / half_count))
        for step_index in range(half_count)
    ]
    return short_edges + long_edges


EDGES = bucket_edges()


def dot(a, b, ca=1, cb=0, precision=None):
    return lax.dot_general(
        a, b, (((ca,), (cb,)), ((), ())), preferred_element_type=F32, precision=precision
    )


def iota(shape, dim):
    return lax.broadcasted_iota(jnp.int32, shape, dim)


def rms(v):
    return lax.rsqrt(jnp.mean(v * v, axis=-1, keepdims=True) + EPSILON)


def call(kernel, outs, args, specs=None, scratch=(), flops=0, moved=0, exps=0, vmem=56, name=None):
    vm = pl.BlockSpec(memory_space=pltpu.VMEM)
    return pl.pallas_call(
        kernel,
        out_shape=[jax.ShapeDtypeStruct(s, d) for s, d in outs],
        in_specs=specs or [vm] * len(args),
        out_specs=[vm] * len(outs),
        scratch_shapes=list(scratch),
        compiler_params=pltpu.CompilerParams(vmem_limit_bytes=vmem * MIB),
        cost_estimate=pl.CostEstimate(flops=flops, bytes_accessed=moved, transcendentals=exps),
        name=name,
    )(*args)


def own_length(lengths_ref):
    return lengths_ref[lax.axis_index("tensor") // 2]


def own_valid(lengths_ref, rows):
    half = lax.rem(lax.axis_index("tensor"), 2)
    return jnp.clip(own_length(lengths_ref) - half * rows, 0, rows)


def as_row(ref):
    return ref[...].reshape(1, D)


VM = pl.BlockSpec(memory_space=pltpu.VMEM)
SM = pl.BlockSpec(memory_space=pltpu.SMEM)


def slot_lines(experts, cap, valid_count, routes):
    rows = routes.shape[1]
    valid = iota((1, rows), 1) < valid_count
    ids = iota((experts, rows), 0)
    hot0 = ((ids == routes[0:1]) & valid).astype(F32)
    hot1 = ((ids == routes[1:2]) & valid).astype(F32)
    before = (iota((rows, rows), 0) < iota((rows, rows), 1)).astype(BF)
    rank = dot((hot0 + hot1).astype(BF), before)
    place = ids.astype(F32) * cap + rank
    bad = jnp.where(valid, 0.0, 1.0)
    slot0 = jnp.sum(hot0 * place, axis=0, keepdims=True) - bad
    slot1 = jnp.sum(hot1 * place, axis=0, keepdims=True) - bad
    return slot0, slot1


def route_kernel(experts, cap, lengths_ref, routes_ref, grad_ref, packed_ref, slots_ref):
    rows = grad_ref.shape[0]
    slot0, slot1 = slot_lines(experts, cap, own_valid(lengths_ref, routes_ref.shape[1]), routes_ref[...])
    spots = iota((experts * cap, rows), 0)
    pick0 = spots == slot0.astype(jnp.int32)
    pick1 = spots == slot1.astype(jnp.int32)
    packed_ref[...] = dot((pick0 | pick1).astype(BF), grad_ref[...]).astype(BF)
    slots_ref[...] = jnp.concatenate([slot0, slot1, jnp.zeros((6, rows), F32)], axis=0)


def slots_kernel(experts, cap, lengths_ref, routes_ref, slots_ref):
    rows = routes_ref.shape[1]
    slot0, slot1 = slot_lines(experts, cap, own_valid(lengths_ref, routes_ref.shape[1]), routes_ref[...])
    slots_ref[...] = jnp.concatenate([slot0, slot1, jnp.zeros((6, rows), F32)], axis=0)


def back_matrix(slots_ref, spots):
    rows = slots_ref.shape[1]
    where = iota((rows, spots), 1)
    slots = slots_ref[...].T.astype(jnp.int32)
    return ((where == slots[:, 0:1]) | (where == slots[:, 1:2])).astype(BF)


def bias_tiles(table_ref, head):
    dist = iota((8, TILE), 1)
    line = table_ref[head : head + 1, :]
    line = line - line[:, NB - 1 :]
    curve = jnp.broadcast_to(line[:, 0:1], (8, TILE))
    for number, edge in enumerate(EDGES):
        curve = jnp.where(dist >= edge, line[:, number + 1 : number + 2], curve)
    spread = jnp.broadcast_to(curve[0:1], (TILE, TILE))
    ring = pltpu.roll(spread, 0, 1, stride=1, stride_axis=0)
    ahead = iota((TILE, TILE), 1) >= iota((TILE, TILE), 0)
    return jnp.where(ahead, ring, NEGATIVE), jnp.where(ahead, 0.0, ring)


def head_pieces(qkvt_ref, mask_rows, head, local_inner):
    start = pl.multiple_of(head * HD, HD)
    q = qkvt_ref[pl.ds(start, HD), :] * jnp.asarray(HD**-0.5, BF)
    k = qkvt_ref[pl.ds(local_inner + start, HD), :]
    v = qkvt_ref[pl.ds(2 * local_inner + start, HD), :]
    ones = jnp.ones((16, SEQ), BF)
    return jnp.concatenate([q, ones], 0), jnp.concatenate([k, mask_rows], 0), v, ones


def mask_block(length):
    keep = (iota((16, SEQ), 1) < length) | (iota((16, SEQ), 0) > 0)
    return jnp.where(keep, 0.0, NEGATIVE).astype(BF)


def score_pieces(k, q, block, near, below):
    cols = slice(block * TILE, (block + 1) * TILE)
    qb = q[:, cols]
    pieces = []
    if block >= 2:
        pieces.append((0, (block - 1) * TILE, dot(k[: (block - 1) * TILE], qb)))
    if block >= 1:
        lo = (block - 1) * TILE
        pieces.append((lo, block * TILE, dot(k[lo : lo + TILE], qb) + below))
    lo = block * TILE
    pieces.append((lo, lo + TILE, dot(k[lo : lo + TILE], qb) + near))
    return cols, pieces


def attn_fwd_kernel(first, heads, lengths_ref, table_ref, *refs):
    if first:
        own_ref, other_ref, gain_ref, w_ref, ow_ref = refs[:5]
        normed_ref, qkvt_ref, mixt_ref, lse_ref, part_ref = refs[5:]
        half = own_ref.shape[0]
        core = lax.rem(lax.axis_index("tensor"), 2)
        for source, place in ((own_ref, core), (other_ref, 1 - core)):
            x = source[...].astype(F32)
            normed_ref[pl.ds(pl.multiple_of(place * half, half), half), :] = (
                x * rms(x) * as_row(gain_ref)
            ).astype(BF)
    else:
        normed_ref, w_ref, ow_ref, part_in = refs[:4]
        qkvt_ref, mixt_ref, lse_ref, keep_ref, send_ref, part_ref = refs[4:]
    local_inner = heads * HD
    qkvt_ref[...] = dot(w_ref[...], normed_ref[...], 1, 1).astype(BF)
    masks = mask_block(own_length(lengths_ref))
    lse_ref[...] = jnp.zeros_like(lse_ref)

    for head in range(heads):
        near, below = bias_tiles(table_ref, head)
        q, kt, v, ones = head_pieces(qkvt_ref, masks, head, local_inner)
        k = kt.T
        vx = jnp.concatenate([v, ones], 0)
        for block in range(SEQ // TILE):
            cols, pieces = score_pieces(k, q, block, near, below)
            top = functools.reduce(
                jnp.maximum, [jnp.max(s, axis=0, keepdims=True) for _, _, s in pieces]
            )
            total = None
            for lo, hi, s in pieces:
                term = dot(vx[:, lo:hi], jnp.exp(s - top).astype(BF))
                total = term if total is None else total + term
            weight = total[HD : HD + 1]
            mixt_ref[head * HD : (head + 1) * HD, cols] = (total[:HD] / weight).astype(BF)
            lse_ref[head : head + 1, cols] = top + jnp.log(weight)
    part = dot(mixt_ref[...], ow_ref[...], 0, 0)
    if first:
        part_ref[...] = part
    else:
        part_ref[...] = part + part_in[...]
        half = keep_ref.shape[0]
        core = lax.rem(lax.axis_index("tensor"), 2)
        keep_ref[...] = part_ref[pl.ds(pl.multiple_of(core * half, half), half), :]
        send_ref[...] = part_ref[pl.ds(pl.multiple_of((1 - core) * half, half), half), :].astype(BF)


def attn_bwd_kernel(early, last, heads, lengths_ref, table_ref, *refs):
    if last:
        (normed_ref, w_ref, ow_ref, qkvt_ref, mixt_ref, lse_ref, own_ref, other_ref, part_in) = refs[:9]
        gw_ref, gbias_ref, keep_ref, send_ref, ga_ref, got_ref, gt_ref, d0_ref, d1_ref, part_ref = refs[9:]
    else:
        (normed_ref, w_ref, ow_ref, qkvt_ref, mixt_ref, lse_ref, own_ref, other_ref) = refs[:8]
        gw_ref, gbias_ref, part_ref, ga_ref, got_ref, gt_ref, d0_ref, d1_ref = refs[8:]
    local_inner = heads * HD
    half = own_ref.shape[0]
    core = lax.rem(lax.axis_index("tensor"), 2)
    ga_ref[pl.ds(pl.multiple_of(core * half, half), half), :] = own_ref[...]
    ga_ref[pl.ds(pl.multiple_of((1 - core) * half, half), half), :] = other_ref[...]
    got_ref[...] = dot(ow_ref[...], ga_ref[...], 1, 1).astype(BF)
    gw_ref[3 * local_inner :] = dot(mixt_ref[...], ga_ref[...]).astype(gw_ref.dtype)
    if early is not None:
        early()
    masks = mask_block(own_length(lengths_ref))
    gbias_ref[...] = jnp.zeros_like(gbias_ref)
    ahead = iota((TILE, TILE), 1) >= iota((TILE, TILE), 0)
    spot = (iota((TILE, 128), 0) + 1) % TILE
    flip = (iota((TILE, TILE), 0) + iota((TILE, TILE), 1) == TILE - 1).astype(F32)
    bucket = jnp.zeros((TILE, 128), jnp.int32)
    for edge in EDGES:
        bucket = bucket + (spot >= edge).astype(jnp.int32)
    hot = (bucket == iota((TILE, 128), 1)).astype(F32)

    for head in range(heads):
        near, below = bias_tiles(table_ref, head)
        q, kt, vt, _ = head_pieces(qkvt_ref, masks, head, local_inner)
        k = kt.T
        v = vt.T
        rows = slice(head * HD, (head + 1) * HD)
        gt = got_ref[rows, :]
        delta = jnp.sum(gt.astype(F32) * mixt_ref[rows, :].astype(F32), axis=0, keepdims=True)
        gk = [None] * (SEQ // TILE)
        gv = [None] * (SEQ // TILE)
        far = jnp.zeros((8, TILE), F32)
        for block in range(SEQ // TILE):
            cols, pieces = score_pieces(k, q, block, near, below)
            gb = gt[:, cols]
            qb = q[:HD, cols]
            lse = lse_ref[head : head + 1, cols]
            db = delta[:, cols]
            gq = None
            for lo, hi, s in pieces:
                p = jnp.exp(s - lse)
                ds = p * (dot(v[lo:hi], gb) - db)
                pb = p.astype(BF)
                dsb = ds.astype(BF)
                term = dot(kt[:HD, lo:hi], dsb)
                gq = term if gq is None else gq + term
                tv = dot(pb, gb, 1, 1)
                tk = dot(dsb, qb, 1, 1)
                for tile in range(lo // TILE, hi // TILE):
                    part = slice(tile * TILE - lo, (tile + 1) * TILE - lo)
                    gv[tile] = tv[part] if gv[tile] is None else gv[tile] + tv[part]
                    gk[tile] = tk[part] if gk[tile] is None else gk[tile] + tk[part]
                if hi == (block + 1) * TILE:
                    d0_ref[...] = ds if block == 0 else d0_ref[...] + ds
                elif hi == block * TILE and lo == (block - 1) * TILE:
                    d1_ref[...] = ds if block == 1 else d1_ref[...] + ds
                else:
                    far = far + jnp.sum(ds.reshape((hi - lo) // 8, 8, TILE), axis=0)
            gt_ref[rows, cols] = (gq * HD**-0.5).astype(BF)
        for tile in range(SEQ // TILE):
            cols = slice(tile * TILE, (tile + 1) * TILE)
            gt_ref[local_inner + head * HD : local_inner + (head + 1) * HD, cols] = (
                gk[tile].T.astype(BF)
            )
            gt_ref[2 * local_inner + head * HD : 2 * local_inner + (head + 1) * HD, cols] = (
                gv[tile].T.astype(BF)
            )
        d1 = d1_ref[...]
        ring = jnp.where(ahead, d0_ref[...], d1)
        turned = pltpu.roll(
            dot(flip, ring, 1, 0, lax.Precision.HIGHEST), 0, 1, stride=1, stride_axis=0
        )
        far = far + jnp.sum(jnp.where(ahead, d1, 0.0).reshape(TILE // 8, 8, TILE), axis=0)
        line = jnp.sum(turned, axis=0, keepdims=True)
        sums = dot(
            jnp.broadcast_to(line, (8, TILE)), hot, 1, 0, lax.Precision.HIGHEST
        )
        sums = sums + jnp.where(iota((8, 128), 1) == NB - 1, jnp.sum(far), 0.0)
        gbias_ref[head : head + 1, :] = sums[0:1]
    gw_ref[: 3 * local_inner] = dot(gt_ref[...], normed_ref[...]).astype(gw_ref.dtype)
    part = dot(gt_ref[...], w_ref[...], 0, 0)
    if last:
        part_ref[...] = part + part_in[...]
        keep_ref[...] = part_ref[pl.ds(pl.multiple_of(core * half, half), half), :]
        send_ref[...] = part_ref[pl.ds(pl.multiple_of((1 - core) * half, half), half), :].astype(BF)
    else:
        part_ref[...] = part


def gates_of(experts, normed, router_t, routes):
    rows = normed.shape[0]
    logits = dot(router_t, normed, 1, 1)
    ids = iota((experts, rows), 0)
    signs = (ids == routes[0:1]).astype(F32) - (ids == routes[1:2]).astype(F32)
    gap = jnp.sum(logits * signs, axis=0, keepdims=True)
    return 1.0 / (1.0 + jnp.exp(-gap)), 1.0 / (1.0 + jnp.exp(gap))


def meta_lines(gate, code):
    rows = gate.shape[1]
    line = iota((8, rows), 0)
    high = gate.astype(BF).astype(F32)
    mid = (gate - high).astype(BF).astype(F32)
    low = gate - high - mid
    picked = jnp.where(line == 0, high, jnp.where(line == 1, mid, jnp.where(line == 2, low, 0.0)))
    return jnp.where(line == 3, code, picked).astype(BF)


def hidden_rows(x_ref, keep_ref, got_ref, gain_ref, hidden_ref):
    hidden = x_ref[...].astype(F32) + keep_ref[...] + got_ref[...].astype(F32)
    hidden_ref[...] = hidden
    return (hidden * rms(hidden) * as_row(gain_ref)).astype(BF)


def middle_kernel(
    experts, cap, x_ref, keep_ref, got_ref, gain_ref, router_ref, routes_ref, slots_ref, hidden_ref, packed_ref, meta_ref
):
    normed = hidden_rows(x_ref, keep_ref, got_ref, gain_ref, hidden_ref)
    slots = slots_ref[...].astype(jnp.int32)
    routes = routes_ref[...]
    where = iota((experts * cap, normed.shape[0]), 0)
    pick0 = where == slots[0:1]
    pick1 = where == slots[1:2]
    packed_ref[...] = dot((pick0 | pick1).astype(BF), normed).astype(BF)
    gate0, gate1 = gates_of(experts, normed, router_ref[...], routes)
    codes = (routes + 1).astype(F32)
    meta = dot(meta_lines(gate0, codes[1:2]), pick0.astype(BF), 1, 1) + dot(
        meta_lines(gate1, codes[0:1]), pick1.astype(BF), 1, 1
    )
    for number in range(experts):
        meta_ref[number] = meta[:, number * cap : (number + 1) * cap]


def middle_line_kernel(
    experts, x_ref, keep_ref, got_ref, gain_ref, router_ref, routes_ref, slots_ref, hidden_ref, normed_ref, info_ref
):
    normed = hidden_rows(x_ref, keep_ref, got_ref, gain_ref, hidden_ref)
    normed_ref[...] = normed
    routes = routes_ref[...]
    gate0, gate1 = gates_of(experts, normed, router_ref[...], routes)
    codes = (routes + 1).astype(F32)
    info_ref[...] = jnp.concatenate(
        [slots_ref[0:2], gate0, gate1, codes, jnp.zeros((2, normed.shape[0]), F32)], axis=0
    )


def gelu_pair(v):
    squared = v * v
    slope = GELU * (1.0 + 3 * CUBIC * squared)
    t = jnp.tanh(v * (GELU + GELU * CUBIC * squared))
    half = 0.5 + 0.5 * t
    return v * half, half + 0.5 * v * (1.0 - t * t) * slope


def flipped(me, k, count):
    total, bit = 0, 1
    while bit < count:
        total = total + lax.rem(me // bit + k // bit, 2) * bit
        bit *= 2
    return total


def weight_grads(xt_ref, geot_ref, act_ref, gi_ref, stage_ref, turned_ref, stay_ref, away_ref, go_ref, out_sem):
    tiles = D // TILE
    steps = 8 * tiles

    def columns(step):
        return pl.ds(pl.multiple_of(lax.rem(step, tiles) * TILE, TILE), TILE)

    def store(step, slot, out_ref, half):
        if half:
            there = pl.ds(pl.multiple_of(D + lax.rem(step, tiles) * TILE, TILE), TILE)
            return pltpu.make_async_copy(turned_ref.at[slot], out_ref.at[there], out_sem.at[slot])
        return pltpu.make_async_copy(stage_ref.at[slot], out_ref.at[:D, columns(step)], out_sem.at[slot])

    def weights(step, carry):
        q = step // (2 * tiles)
        half = lax.rem(step, 2 * tiles) // tiles
        slot = lax.rem(step, 2)

        outs = (stay_ref, away_ref, go_ref.at[0], go_ref.at[1])

        @pl.when(step >= 2)
        def _():
            store(step - 2, slot, stay_ref, 0).wait()

        @pl.when(half == 0)
        def _():
            stage_ref[slot] = dot(xt_ref[...], gi_ref[q, :, columns(step)]).astype(BF)

        @pl.when(half == 1)
        def _():
            turned_ref[slot] = dot(geot_ref[...], act_ref[q, :, columns(step)]).astype(BF).T

        for number, out_ref in enumerate(outs):
            for kind in range(2):

                @pl.when((q == number) & (half == kind))
                def _():
                    store(step, slot, out_ref, kind).start()

        return carry

    lax.fori_loop(0, steps, weights, 0)
    for step in (steps - 2, steps - 1):
        store(step, step % 2, stay_ref, 1).wait()


def expert_rows(ready, x, geo, here, w_ref, xt_ref, geot_ref, act_ref, gi_ref, acc_ref):
    xt_ref[:, here] = x.T
    geot_ref[:, here] = geo.T
    worth = 0.0
    for q in (0, 2, 1, 3):
        if q == 1:
            ready()
        inner = dot(x, w_ref[q, :D])
        grad_active = dot(geo, w_ref[q, D:], 1, 1)
        act, slope = gelu_pair(inner)
        gi = (slope * grad_active).astype(BF)
        act_ref[q, here] = act.astype(BF)
        gi_ref[q, here] = gi
        back = dot(gi, w_ref[q, :D], 1, 1)
        if q == 0:
            acc_ref[...] = back
        else:
            acc_ref[...] += back
        worth = worth + jnp.sum(act * grad_active, axis=1, keepdims=True)
    return worth


def expert_outs(start, size, column, act_ref, w_ref):
    here = pl.ds(pl.multiple_of(start, size), size)
    cols = pl.ds(pl.multiple_of(column * TILE, TILE), TILE)
    total = None
    for q in range(4):
        term = dot(act_ref[q, here], w_ref[q, D:, cols])
        total = term if total is None else total + term
    return cols, total


def expert_kernel(
    count, cap, packed_ref, send_meta_ref, grads_ref, router_ref, w0, w1, w2, w3,
    came_ref, result_ref, stay_ref, away_ref, go_ref, grouter_ref,
    w_ref, x_ref, xt_ref, geot_ref, act_ref, gi_ref, gsend_ref, meta_ref, acc_ref, stage_ref, turned_ref,
    x_send, x_recv, m_send, m_recv, r_send, r_recv, local_sem, w_sem, out_sem,
):
    me = lax.axis_index("expert")
    barrier = pltpu.get_barrier_semaphore()

    def peer(k):
        return flipped(me, k, count)

    source = peer

    def greet(k, carry):
        pl.semaphore_signal(
            barrier, inc=1, device_id={"expert": peer(k)}, device_id_type=pl.DeviceIdType.MESH
        )
        return carry

    lax.fori_loop(1, count, greet, 0)
    pl.semaphore_wait(barrier, count - 1)

    def rows_of(k):
        return pl.ds(pl.multiple_of(k * cap, cap), cap)

    def send_rows(k):
        return pltpu.make_async_remote_copy(
            src_ref=packed_ref.at[rows_of(peer(k))],
            dst_ref=x_ref.at[rows_of(k)],
            send_sem=x_send.at[k],
            recv_sem=x_recv.at[k],
            device_id={"expert": peer(k)},
            device_id_type=pl.DeviceIdType.MESH,
        )

    def send_meta(k):
        return pltpu.make_async_remote_copy(
            src_ref=send_meta_ref.at[peer(k)],
            dst_ref=meta_ref.at[k],
            send_sem=m_send.at[k],
            recv_sem=m_recv.at[k],
            device_id={"expert": peer(k)},
            device_id_type=pl.DeviceIdType.MESH,
        )

    def send_back(k):
        return pltpu.make_async_remote_copy(
            src_ref=gsend_ref.at[rows_of(k)],
            dst_ref=came_ref.at[rows_of(me)],
            send_sem=r_send.at[k],
            recv_sem=r_recv.at[k],
            device_id={"expert": source(k)},
            device_id_type=pl.DeviceIdType.MESH,
        )

    def start_sends(k, carry):
        send_meta(k).start()
        send_rows(k).start()
        return carry

    lax.fori_loop(count // 2, count, start_sends, 0)
    lax.fori_loop(1, count // 2, start_sends, 0)
    own_rows = pltpu.make_async_copy(packed_ref.at[rows_of(me)], x_ref.at[rows_of(0)], local_sem.at[0])
    own_rows.start()
    own_meta = pltpu.make_async_copy(send_meta_ref.at[me], meta_ref.at[0], local_sem.at[1])
    own_meta.start()
    loads = [
        pltpu.make_async_copy(w, w_ref.at[i], w_sem.at[i]) for i, w in enumerate((w0, w1, w2, w3))
    ]
    for load in loads:
        load.start()
    grouter_ref[...] = jnp.zeros_like(grouter_ref)
    experts = router_ref.shape[1]
    own_rows.wait()
    own_meta.wait()
    for load in loads:
        load.wait()
    group = max(1, CHUNK // cap)
    span = group * cap

    def chunk(j, carry):
        for i in range(group):
            k = j * group + i

            @pl.when(k > 0)
            def _():
                send_rows(k).wait_recv()
                send_meta(k).wait_recv()

        here = pl.ds(pl.multiple_of(j * span, span), span)
        meta = jnp.concatenate([meta_ref[j * group + i].T for i in range(group)], axis=0)
        gate = meta[:, 0:1] + meta[:, 1:2] + meta[:, 2:3]
        code = meta[:, 3:4].astype(jnp.int32)
        gy = jnp.concatenate([grads_ref[rows_of(source(j * group + i)), :] for i in range(group)], axis=0)
        geo = (gate * gy.astype(F32)).astype(BF)
        x = x_ref[here, :]
        worth = expert_rows(lambda: None, x, geo, here, w_ref, xt_ref, geot_ref, act_ref, gi_ref, acc_ref)
        ids = iota((span, experts), 1)
        signs = (ids == me).astype(F32) - (ids + 1 == code).astype(F32)
        share = jnp.where(code > 0, (1.0 - gate) * worth, 0.0) * signs
        high = share.astype(BF)
        low = (share - high.astype(F32)).astype(BF)
        gsend_ref[here, :] = (acc_ref[...] + dot(high, router_ref[...], 1, 1)).astype(BF)
        grouter_ref[...] += dot(high.T, x) + dot(low.T, x)
        for i in range(group):
            k = j * group + i

            @pl.when(k > 0)
            def _():
                send_back(k).start()

        return carry

    lax.fori_loop(0, count // group, chunk, 0)
    own_back = pltpu.make_async_copy(gsend_ref.at[rows_of(0)], came_ref.at[rows_of(me)], local_sem.at[0])
    own_back.start()

    def results(step, carry):
        j = step // (D // TILE)
        meta = jnp.concatenate([meta_ref[j * group + i].T for i in range(group)], axis=0)
        gate = meta[:, 0:1] + meta[:, 1:2] + meta[:, 2:3]
        cols, total = expert_outs(j * span, span, lax.rem(step, D // TILE), act_ref, w_ref)
        out = (gate * total).astype(BF)
        for i in range(group):
            result_ref[rows_of(source(j * group + i)), cols] = out[i * cap : (i + 1) * cap]
        return carry

    lax.fori_loop(0, count // group * (D // TILE), results, 0)
    weight_grads(xt_ref, geot_ref, act_ref, gi_ref, stage_ref, turned_ref, stay_ref, away_ref, go_ref, out_sem)
    own_back.wait()

    def finish(k, carry):
        send_rows(k).wait_send()
        send_meta(k).wait_send()
        send_back(k).wait()
        return carry

    lax.fori_loop(1, count, finish, 0)


def mesh_copy(src, dst, send_sem, recv_sem, target):
    return pltpu.make_async_remote_copy(
        src_ref=src,
        dst_ref=dst,
        send_sem=send_sem,
        recv_sem=recv_sem,
        device_id={"expert": target},
        device_id_type=pl.DeviceIdType.MESH,
    )


LINE = 4


def expert_line_kernel(
    cap, normed_ref, info_in, router_ref, grads_in, near_ref, near_info_ref, up_ref, down_ref, far_up_ref, far_half_ref,
    came_ref, result_out, stay_ref, away_ref, go_ref, grouter_ref,
    result_ref, grads_ref, w_ref, block_ref, info_ref, x_ref, xs_ref, meta_ref, ms_ref, xt_ref, geot_ref, act_ref, gi_ref, acc_ref, stage_ref, turned_ref,
    b_send, b_recv, i_send, i_recv, x_send, x_recv, m_send, m_recv, r_send, r_recv, local_sem, w_sem, v_send, v_recv, y_send, y_recv, grads_sem, near_sem, out_sem,
):
    count = 2 * LINE
    me = lax.axis_index("expert")
    place = me // 2
    side = me - 2 * place
    mate = me + 1 - 2 * side
    barrier = pltpu.get_barrier_semaphore()

    def greet(k, carry):
        pl.semaphore_signal(
            barrier,
            inc=1,
            device_id={"expert": lax.rem(me + k, count)},
            device_id_type=pl.DeviceIdType.MESH,
        )
        return carry

    lax.fori_loop(1, count, greet, 0)
    core = flipped(lax.axis_index("tensor"), 1, 4)
    pl.semaphore_signal(
        barrier, inc=1, device_id={"tensor": core}, device_id_type=pl.DeviceIdType.MESH
    )
    away = flipped(lax.axis_index("tensor"), 2, 4)
    pl.semaphore_signal(
        barrier, inc=1, device_id={"tensor": away}, device_id_type=pl.DeviceIdType.MESH
    )
    pl.semaphore_wait(barrier, count + 1)

    def along(block, step):
        return (
            mesh_copy(
                info_ref.at[block],
                info_ref.at[block],
                i_send.at[(step + 1) // 2, block],
                i_recv.at[block],
                me + 2 * step,
            ),
            mesh_copy(
                block_ref.at[block],
                block_ref.at[block],
                b_send.at[(step + 1) // 2, block],
                b_recv.at[block],
                me + 2 * step,
            ),
        )

    def across(block):
        return (
            mesh_copy(ms_ref.at[block], meta_ref.at[1, block], m_send.at[block], m_recv.at[block], mate),
            mesh_copy(xs_ref.at[block], x_ref.at[1, block], x_send.at[block], x_recv.at[block], mate),
        )

    def rows_of(number):
        return pl.ds(pl.multiple_of(number * cap, cap), cap)

    def origin(part, block):
        return 2 * block + side + part * (1 - 2 * side)

    def give_back(part, block):
        return mesh_copy(
            x_ref.at[part, block],
            came_ref.at[rows_of(me)],
            r_send.at[part, block],
            r_recv.at[me],
            origin(part, block),
        )

    def each(pair, act):
        for one in pair:
            act(one)

    own = (
        pltpu.make_async_copy(info_in, info_ref.at[place], local_sem.at[0]),
        pltpu.make_async_copy(normed_ref, block_ref.at[place], local_sem.at[1]),
    )
    each(own, lambda c: c.start())
    rest = D // 2
    far_down = tensor_copy(down_ref.at[rest:], w_ref.at[1, D + rest :], y_send, y_recv, away)
    far_down.start()
    grads_load = pltpu.make_async_copy(grads_in, grads_ref, grads_sem)
    grads_load.start()
    near = [
        (
            pltpu.make_async_copy(near_info_ref.at[i], info_ref.at[place + 2 * i - 1], near_sem.at[i]),
            pltpu.make_async_copy(near_ref.at[i], block_ref.at[place + 2 * i - 1], near_sem.at[i + 2]),
        )
        for i in range(2)
    ]
    inside = [place > 0, place < LINE - 1]
    for i in range(2):

        @pl.when(inside[i])
        def _():
            each(near[i], lambda c: c.start())

    weights = (
        (up_ref, 0, 0, D), (down_ref, 0, D, D), (far_up_ref, 1, 0, D), (far_half_ref, 1, D, rest),
        (w_ref.at[1, D + rest :], 1, D + rest, D - rest),
    )

    def load(i):
        source, q, start, size = weights[i]
        return pltpu.make_async_copy(source, w_ref.at[q, start : start + size], w_sem.at[i])

    def lend(i):
        source, q, start, size = weights[i]
        return tensor_copy(source, w_ref.at[2 + q, start : start + size], v_send.at[i], v_recv.at[i], core)

    for i in range(2):

        @pl.when(inside[i])
        def _():
            each(near[i], lambda c: c.wait())

            @pl.when(inside[1 - i])
            def _():
                each(along(place + 2 * i - 1, 1 - 2 * i), lambda c: c.start())

    for i in range(4):
        load(i).start()
        lend(i).start()
    each(own, lambda c: c.wait())
    experts = router_ref.shape[0]
    rows = normed_ref.shape[0]

    def select(block):
        info = info_ref[block]
        slots = info[0:2].astype(jnp.int32)
        lines0 = meta_lines(info[2:3], info[5:6])
        lines1 = meta_lines(info[3:4], info[4:5])
        for part, expert in ((1, mate), (0, me)):
            where = iota((cap, rows), 0) + expert * cap
            pick0 = where == slots[0:1]
            pick1 = where == slots[1:2]
            taken = dot((pick0 | pick1).astype(BF), block_ref[block]).astype(BF)
            meta = dot(lines0, pick0.astype(BF), 1, 1) + dot(lines1, pick1.astype(BF), 1, 1)
            if part:
                xs_ref[block] = taken
                ms_ref[block] = meta
                each(across(block), lambda c: c.start())
            else:
                x_ref[0, block] = taken
                meta_ref[0, block] = meta

    select(place)
    grouter_ref[...] = jnp.zeros_like(grouter_ref)
    mirror = place // 2
    inward = place + mirror * (LINE - 1 - 2 * place)

    def block_at(i):
        step = i + inward * (1 - i // 2 - 2 * (i // 2 - i // (LINE - 1)))
        return step + mirror * (LINE - 1 - 2 * step)

    outer = sum(d * 8**i for i, d in enumerate((0, 1, 4, 2, 5, 3, 6, 7)))
    inner = sum(d * 8**i for i, d in enumerate((0, 1, 4, 2, 5, 3, 6, 7)))
    chunks = outer + inward * (inner - outer)

    def chunk_at(power):
        digit = lax.rem(chunks // power, 8)
        return digit // 4, block_at(lax.rem(digit, 4))

    for i in range(2):

        @pl.when(inside[i])
        def _():
            select(place + 2 * i - 1)

    grads_load.wait()
    for i in range(2):
        load(i).wait()
        lend(i).wait_recv()

    def far_ready(c):
        @pl.when(c == 0)
        def _():
            far_down.wait_recv()
            lend(4).start()
            for i in (2, 3):
                load(i).wait()
                lend(i).wait_recv()
            lend(4).wait_recv()


    def chunk(c, power):
        for distance in range(2, LINE):

            @pl.when(c == 4 * distance - 7)
            def _():
                line_accept(place, distance, along, select)

        part, block = chunk_at(power)

        @pl.when(part == 1)
        def _():
            each(across(block), lambda c: c.wait_recv())

        here = pl.ds(pl.multiple_of(c * cap, cap), cap)
        meta = meta_ref[part, block].T
        gate = meta[:, 0:1] + meta[:, 1:2] + meta[:, 2:3]
        code = meta[:, 3:4].astype(jnp.int32)
        geo = (gate * grads_ref[part, block].astype(F32)).astype(BF)
        x = x_ref[part, block]
        worth = expert_rows(lambda: far_ready(c), x, geo, here, w_ref, xt_ref, geot_ref, act_ref, gi_ref, acc_ref)
        ids = iota((cap, experts), 1)
        signs = (ids == me).astype(F32) - (ids + 1 == code).astype(F32)
        share = jnp.where(code > 0, (1.0 - gate) * worth, 0.0) * signs
        high = share.astype(BF)
        low = (share - high.astype(F32)).astype(BF)
        grouter_ref[...] += dot(high.T, x) + dot(low.T, x)
        x_ref[part, block] = (acc_ref[...] + dot(high, router_ref[...])).astype(BF)

        @pl.when(origin(part, block) != me)
        def _():
            give_back(part, block).start()

        return power * 8

    lax.fori_loop(0, count, chunk, jnp.int32(1))
    own_back = pltpu.make_async_copy(x_ref.at[0, place], came_ref.at[rows_of(me)], local_sem.at[0])
    own_back.start()

    def results(step, carry):
        first = step // (D // TILE) * LINE
        cols, total = expert_outs(first * cap, LINE * cap, lax.rem(step, D // TILE), act_ref, w_ref)
        for i in range(LINE):
            part, block = chunk_at((1 + first // LINE * (8**LINE - 1)) * 8**i)
            meta = meta_ref[part, block].T
            gate = meta[:, 0:1] + meta[:, 1:2] + meta[:, 2:3]
            result_ref[rows_of(origin(part, block)), cols] = (
                gate * total[i * cap : (i + 1) * cap]
            ).astype(BF)
        return carry

    lax.fori_loop(0, 2 * (D // TILE), results, 0)
    leave = pltpu.make_async_copy(result_ref, result_out, local_sem.at[1])
    leave.start()
    weight_grads(xt_ref, geot_ref, act_ref, gi_ref, stage_ref, turned_ref, stay_ref, away_ref, go_ref, out_sem)
    own_back.wait()
    leave.wait()
    for i in range(5):
        lend(i).wait_send()
    far_down.wait_send()
    line_sent(place, along, 1)
    for block in range(LINE):
        each(across(block), lambda c: c.wait_send())
        for part in (0, 1):

            @pl.when(origin(part, block) != me)
            def _():
                give_back(part, block).wait_send()

    for number in range(count):

        @pl.when(number != me)
        def _():
            mesh_copy(
                x_ref.at[0, 0], came_ref.at[rows_of(number)], r_send.at[0, 0], r_recv.at[number], mate
            ).wait_recv()


def turn_kernel(lengths_ref, came_ref, slots_ref, hidden_ref, gain_ref, grad_ref, gh_ref, ga_ref, gain_out):
    gn = dot(back_matrix(slots_ref, came_ref.shape[0]), came_ref[...])
    hidden = hidden_ref[...]
    scale = rms(hidden)
    unit = hidden * scale
    gain_out[...] = jnp.broadcast_to(jnp.sum(gn * unit, axis=0, keepdims=True), gain_out.shape)
    g = gn * as_row(gain_ref)
    valid = (iota((hidden.shape[0], 1), 0) < own_valid(lengths_ref, hidden.shape[0])).astype(F32)
    gh = scale * (g - unit * jnp.mean(g * unit, axis=1, keepdims=True)) + valid * grad_ref[...].astype(F32)
    gh_ref[...] = gh
    ga_ref[...] = gh.astype(BF)


def output_kernel(lengths_ref, came_ref, slots_ref, hidden_ref, out_ref):
    mix = dot(back_matrix(slots_ref, came_ref.shape[0]), came_ref[...])
    hidden = hidden_ref[...]
    valid = (iota((hidden.shape[0], 1), 0) < own_valid(lengths_ref, hidden.shape[0])).astype(F32)
    out_ref[...] = (valid * (hidden + mix)).astype(BF)


def last_kernel(x_ref, keep_ref, got_ref, gain_ref, gh_ref, out_ref, gain_out):
    x = x_ref[...].astype(F32)
    scale = rms(x)
    unit = x * scale
    gn = keep_ref[...] + got_ref[...].astype(F32)
    gain_out[...] = jnp.broadcast_to(jnp.sum(gn * unit, axis=0, keepdims=True), gain_out.shape)
    g = gn * as_row(gain_ref)
    out_ref[...] = (
        gh_ref[...] + scale * (g - unit * jnp.mean(g * unit, axis=1, keepdims=True))
    ).astype(BF)


def moe(experts, cap, packed, meta, grads, router, quarters):
    spots = experts * cap
    anyspec = pl.BlockSpec(memory_space=pl.ANY)
    dma = pltpu.SemaphoreType.DMA
    return pl.pallas_call(
        functools.partial(expert_kernel, experts, cap),
        out_shape=[
            jax.ShapeDtypeStruct((spots, D), BF),
            jax.ShapeDtypeStruct((spots, D), BF),
            jax.ShapeDtypeStruct((2 * D, D), BF),
            jax.ShapeDtypeStruct((2 * D, D), BF),
            jax.ShapeDtypeStruct((2, 2 * D, D), BF),
            jax.ShapeDtypeStruct((experts, D), F32),
        ],
        in_specs=[anyspec, VM, VM, VM] + [anyspec] * 4,
        out_specs=[anyspec, VM, anyspec, anyspec, anyspec, VM],
        scratch_shapes=[
            pltpu.VMEM((4, 2 * D, D), BF),
            pltpu.VMEM((spots, D), BF),
            pltpu.VMEM((D, spots), BF),
            pltpu.VMEM((D, spots), BF),
            pltpu.VMEM((4, spots, D), BF),
            pltpu.VMEM((4, spots, D), BF),
            pltpu.VMEM((spots, D), BF),
            pltpu.VMEM((experts, 8, cap), F32),
            pltpu.VMEM((CHUNK, D), F32),
            pltpu.VMEM((2, D, TILE), BF),
            pltpu.VMEM((2, TILE, D), BF),
            dma((experts,)),
            dma((experts,)),
            dma((experts,)),
            dma((experts,)),
            dma((experts,)),
            dma((experts,)),
            dma((2,)),
            dma((4,)),
            dma((2,)),
        ],
        compiler_params=pltpu.CompilerParams(
            collective_id=1, has_side_effects=True, vmem_limit_bytes=60 * MIB
        ),
        cost_estimate=pl.CostEstimate(flops=12 * spots * D * 4 * D, bytes_accessed=60 * MIB, transcendentals=0),
        name="experts",
    )(packed, meta, grads, router, *quarters)


def moe_line(experts, cap, normed, info, router, others):
    rows = normed.shape[0]
    spots = experts * cap
    anyspec = pl.BlockSpec(memory_space=pl.ANY)
    dma = pltpu.SemaphoreType.DMA
    return pl.pallas_call(
        functools.partial(expert_line_kernel, cap),
        out_shape=[
            jax.ShapeDtypeStruct((spots, D), BF),
            jax.ShapeDtypeStruct((spots, D), BF),
            jax.ShapeDtypeStruct((2 * D, D), BF),
            jax.ShapeDtypeStruct((2 * D, D), BF),
            jax.ShapeDtypeStruct((2, 2 * D, D), BF),
            jax.ShapeDtypeStruct((experts, D), F32),
        ],
        in_specs=[VM, VM, VM] + [anyspec] * 7,
        out_specs=[anyspec, anyspec, anyspec, anyspec, anyspec, VM],
        scratch_shapes=[
            pltpu.VMEM((spots, D), BF),
            pltpu.VMEM((2, LINE, cap, D), BF),
            pltpu.VMEM((4, 2 * D, D), BF),
            pltpu.VMEM((LINE, rows, D), BF),
            pltpu.VMEM((LINE, 8, rows), F32),
            pltpu.VMEM((2, LINE, cap, D), BF),
            pltpu.VMEM((LINE, cap, D), BF),
            pltpu.VMEM((2, LINE, 8, cap), F32),
            pltpu.VMEM((LINE, 8, cap), F32),
            pltpu.VMEM((D, spots), BF),
            pltpu.VMEM((D, spots), BF),
            pltpu.VMEM((4, spots, D), BF),
            pltpu.VMEM((4, spots, D), BF),
            pltpu.VMEM((cap, D), F32),
            pltpu.VMEM((2, D, TILE), BF),
            pltpu.VMEM((2, TILE, D), BF),
            dma((2, LINE)),
            dma((LINE,)),
            dma((2, LINE)),
            dma((LINE,)),
            dma((LINE,)),
            dma((LINE,)),
            dma((LINE,)),
            dma((LINE,)),
            dma((2, LINE)),
            dma((experts,)),
            dma((2,)),
            dma((4,)),
            dma((5,)),
            dma((5,)),
            dma,
            dma,
            dma,
            dma((4,)),
            dma((2,)),
        ],
        compiler_params=pltpu.CompilerParams(
            collective_id=2, has_side_effects=True, vmem_limit_bytes=62 * MIB
        ),
        cost_estimate=pl.CostEstimate(flops=12 * spots * D * 4 * D, bytes_accessed=60 * MIB, transcendentals=0),
        name="experts_line",
    )(normed, info, router, *others)


def tensor_copy(src, dst, send_sem, recv_sem, target):
    return pltpu.make_async_remote_copy(
        src_ref=src,
        dst_ref=dst,
        send_sem=send_sem,
        recv_sem=recv_sem,
        device_id={"tensor": target},
        device_id_type=pl.DeviceIdType.MESH,
    )


def sums(
    pair_done, beside, gw_ref, pair_ref, keep_ref, send_ref, x_in, gain_ref, gh_ref, moe_ref, router_ref, bias0_ref, bias1_ref,
    gwt_out, gow_out, gin_out, attn_out, moe_out, router_out, bias_out,
    small_out, part_ref, cross_ref, line_ref, from_ref, all_ref, got_ref, lines_ref, few_ref, ranks_ref,
    a_send, a_recv, b_send, b_recv, c_send, c_recv, d_send, d_recv, s_send, s_recv, f_send, f_recv, t_send, t_recv, g_send, g_recv,
):
    count = 2 * LINE
    me = lax.axis_index("expert")
    rank = lax.axis_index("tensor")
    place = me // 2
    side = me - 2 * place
    mate = me + 1 - 2 * side
    size = part_ref.shape[0] // count
    def slab(which, number):
        return pl.ds(pl.multiple_of((which * LINE + number) * size, size), size)

    swap = tensor_copy(send_ref, got_ref, s_send, s_recv, flipped(rank, 1, 4))
    swap.start()
    pair_done()
    part_ref[...] = (gw_ref[...] + pair_ref[...].astype(F32)).astype(BF)
    rows = gwt_out.shape[0]

    def cross(number):
        return mesh_copy(
            part_ref.at[slab(1 - side, number)], cross_ref.at[number], a_send.at[number], a_recv.at[number], mate
        )

    def along(number):
        return mesh_copy(
            line_ref.at[number], from_ref.at[place], b_send.at[number], b_recv.at[place], 2 * number + side
        )

    def spread(number):
        return mesh_copy(
            all_ref.at[slab(side, place)],
            all_ref.at[slab(side, place)],
            c_send.at[number],
            c_recv.at[place],
            2 * number + side,
        )

    def over(number):
        return mesh_copy(
            all_ref.at[slab(side, number)], all_ref.at[slab(side, number)], d_send.at[number], d_recv.at[number], mate
        )

    for number in range(LINE):
        cross(number).start()

    swap.wait()
    x = x_in[...].astype(F32)
    scale = rms(x)
    unit = x * scale
    gn = keep_ref[...] + got_ref[...].astype(F32)
    attn = jnp.sum(gn * unit, axis=0, keepdims=True)
    g = gn * as_row(gain_ref)
    gin_out[...] = (gh_ref[...] + scale * (g - unit * jnp.mean(g * unit, axis=1, keepdims=True))).astype(BF)

    heads = gow_out.shape[0] // HD
    blank = jnp.zeros((1, 128), F32)

    def flat(bias_ref):
        line = [bias_ref[h : h + 1, :NB] for h in range(heads)]
        return jnp.concatenate(line + [jnp.zeros((1, 128 - heads * NB), F32)], axis=1)

    own_bias, pair_bias = flat(bias0_ref), flat(bias1_ref)
    other = flipped(rank, 2, 4)
    for j in range(D // 128):
        lines_ref[j] = router_ref[:, j * 128 : (j + 1) * 128]
    for j, row in ((6, attn), (7, moe_ref[0:1])):
        places = [2 * (j - 6), 2 * (j - 6) + 1]
        bias = [
            jnp.where(rank == p, own_bias, blank) + jnp.where(other == p, pair_bias, blank) for p in places
        ]
        lines_ref[j] = jnp.concatenate([row[:, i * 128 : (i + 1) * 128] for i in range(6)] + bias, axis=0)

    def small(k):
        return mesh_copy(
            lines_ref.at[flipped(me, k, count)], few_ref.at[k], f_send.at[k], f_recv.at[k], flipped(me, k, count)
        )

    def rank_copy(k):
        return tensor_copy(
            ranks_ref.at[rank], ranks_ref.at[rank], t_send.at[k], t_recv.at[k], flipped(rank, k, 4)
        )

    def rank_from(k):
        return tensor_copy(
            ranks_ref.at[rank], ranks_ref.at[flipped(rank, k, 4)], t_send.at[k], t_recv.at[k], flipped(rank, k, 4)
        )

    def small_spread(k):
        return mesh_copy(
            small_out.at[me], small_out.at[me], g_send.at[k], g_recv.at[k], flipped(me, k, count)
        )

    def small_from(k):
        return mesh_copy(
            small_out.at[me], small_out.at[flipped(me, k, count)], g_send.at[k], g_recv.at[k], flipped(me, k, count)
        )

    for k in range(1, count):
        small(k).start()

    for number in range(LINE):

        @pl.when(number != place)
        def _():
            cross(number).wait_recv()
            line_ref[number] = (
                part_ref[slab(side, number)].astype(F32) + cross_ref[number].astype(F32)
            ).astype(BF)
            along(number).start()

    total = lines_ref[me]
    for k in range(1, count):
        small(k).wait_recv()
        total = total + few_ref[k]
    ranks_ref[rank] = total
    for k in range(1, 4):
        rank_copy(k).start()

    for number in range(LINE):

        @pl.when(number == place)
        def _():
            cross(number).wait_recv()

    beside()
    whole = part_ref[slab(side, place)].astype(F32) + cross_ref[place].astype(F32)
    from_ref[place] = whole.astype(BF)
    for k in range(1, LINE):
        number = lax.rem(place + k, LINE)
        mesh_copy(
            line_ref.at[number], from_ref.at[number], b_send.at[number], b_recv.at[number], mate
        ).wait_recv()
        whole = whole + from_ref[number].astype(F32)
    all_ref[slab(side, place)] = whole.astype(BF)
    over(place).start()
    for number in range(LINE):

        @pl.when(number != place)
        def _():
            spread(number).start()

    for k in range(1, 4):
        rank_from(k).wait_recv()
    small_out[me] = ranks_ref[0] + ranks_ref[1] + ranks_ref[2] + ranks_ref[3]
    for k in range(1, count):
        small_spread(k).start()

    for k in range(1, LINE):
        number = lax.rem(place + k, LINE)
        mesh_copy(
            all_ref.at[slab(side, number)], all_ref.at[slab(side, number)], c_send.at[number], c_recv.at[number], mate
        ).wait_recv()
        over(number).start()
    for k in range(1, count):
        small_from(k).wait_recv()
    for number in range(LINE):
        mesh_copy(
            all_ref.at[slab(1 - side, number)],
            all_ref.at[slab(1 - side, number)],
            d_send.at[number],
            d_recv.at[number],
            mate,
        ).wait_recv()
    attn_out[...] = jnp.concatenate([small_out[6, i : i + 1] for i in range(6)], axis=1).reshape(D)
    moe_out[...] = jnp.concatenate([small_out[7, i : i + 1] for i in range(6)], axis=1).reshape(D)
    router_out[...] = jnp.concatenate([small_out[j] for j in range(D // 128)], axis=1)
    bias = functools.reduce(
        jnp.add,
        [jnp.where(rank == p, small_out[6 + p // 2, 6 + p % 2 : 7 + p % 2], blank) for p in range(4)],
    )
    bias_out[...] = jnp.concatenate([bias[:, h * NB : (h + 1) * NB] for h in range(heads)], axis=0)
    gwt_out[...] = all_ref[:rows].astype(F32)
    gow_out[...] = all_ref[rows:].astype(F32)
    for number in range(LINE):
        cross(number).wait_send()
        over(number).wait_send()

        @pl.when(number != place)
        def _():
            along(number).wait_send()
            spread(number).wait_send()

    for k in range(1, count):
        small(k).wait_send()
        small_spread(k).wait_send()
    for k in range(1, 4):
        rank_copy(k).wait_send()


PARTS = 6


def finish_kernel(
    heads, cap, lengths_ref,
    table0_ref, table1_ref, slots_ref, gain2_ref, gain1_ref, router_ref,
    came_in, hidden_in, grad_in, result_in, go_in, away_in, x_in, normed_in, wt_in, ow_in, pw_in, qkvt0_in, mixt0_in, lse0_in, qkvt1_in, mixt1_in, lse1_in,
    out_ref, gin_out, gwt_out, gow_out, attn_out, moe_out, router_out, bias_out, came_go_ref, came_away_ref,
    came_ref, hidden_ref, grad_ref, outs_ref, gorecv_ref, away_ref, x_ref, normed_ref, wt_ref, ow_ref, pw_ref, qkvt0_ref, mixt0_ref, lse0_ref, qkvt1_ref, mixt1_ref, lse1_ref,
    gh_ref, ga_ref, other_ref, moe_ref, gpart_ref, gpair_ref, gown_ref, bias0_ref, bias1_ref, keep_ref, send_ref,
    all_ga_ref, got_ref, gt_ref, d0_ref, d1_ref, npart_ref,
    o_send, o_recv, v_send, v_recv, y_send, y_recv, w_send, w_recv, e_send, e_recv, load_sem, *tail_refs,
):
    count = 2 * LINE
    me = lax.axis_index("expert")
    rank = lax.axis_index("tensor")
    core = flipped(rank, 1, 4)
    away_rank = flipped(rank, 2, 4)
    places = (
        (came_in, came_ref),
        (hidden_in, hidden_ref),
        (grad_in, grad_ref),
        (normed_in, normed_ref),
        (pw_in, pw_ref),
        (qkvt1_in, qkvt1_ref),
        (mixt1_in, mixt1_ref),
        (lse1_in, lse1_ref),
        (wt_in, wt_ref),
        (ow_in, ow_ref),
        (qkvt0_in, qkvt0_ref),
        (mixt0_in, mixt0_ref),
        (lse0_in, lse0_ref),
        (x_in, x_ref),
    )
    loads = [pltpu.make_async_copy(a, b, load_sem.at[i + 2]) for i, (a, b) in enumerate(places)]
    for load in loads:
        load.start()
    barrier = pltpu.get_barrier_semaphore()
    for k in range(1, count):
        pl.semaphore_signal(
            barrier, inc=1, device_id={"expert": flipped(me, k, count)}, device_id_type=pl.DeviceIdType.MESH
        )
    for k in range(1, 4):
        pl.semaphore_signal(
            barrier, inc=1, device_id={"tensor": flipped(rank, k, 4)}, device_id_type=pl.DeviceIdType.MESH
        )
    pl.semaphore_wait(barrier, count + 2)

    def rows_of(number):
        return pl.ds(pl.multiple_of(number * cap, cap), cap)

    def result(k):
        return mesh_copy(
            result_in.at[rows_of(flipped(me, k, count))],
            outs_ref.at[rows_of(me)],
            o_send.at[k],
            o_recv.at[k],
            flipped(me, k, count),
        )

    order = list(range(LINE, count)) + list(range(1, LINE))
    for k in order:
        result(k).start()
    own_result = pltpu.make_async_copy(result_in.at[rows_of(me)], outs_ref.at[rows_of(me)], load_sem.at[0])
    own_result.start()
    away_load = pltpu.make_async_copy(away_in, away_ref, load_sem.at[1])
    away_load.start()
    go_away = tensor_copy(go_in.at[1], gorecv_ref, v_send.at[0], v_recv.at[0], core)
    go_away.start()
    go_stay = tensor_copy(go_in.at[0], came_go_ref, v_send.at[1], v_recv.at[1], core)
    for load in loads[:3]:
        load.wait()
    turn_kernel(lengths_ref, came_ref, slots_ref, hidden_ref, gain2_ref, grad_ref, gh_ref, ga_ref, moe_ref)
    ga_swap = tensor_copy(ga_ref, other_ref, w_send, w_recv, core)
    ga_swap.start()
    away_load.wait()
    go_away.wait_recv()
    size = away_ref.shape[0] // PARTS

    def lines(i):
        return pl.ds(i * size, size)

    def away(i):
        return tensor_copy(
            away_ref.at[lines(i)], came_away_ref.at[lines(i)], y_send.at[i], y_recv.at[i], away_rank
        )

    for i in range(PARTS):
        away_ref[lines(i)] = (
            away_ref[lines(i)].astype(F32) + gorecv_ref[lines(i)].astype(F32)
        ).astype(BF)
        if i < 1:
            away(i).start()
    ga_swap.wait()
    go_stay.start()
    for load in loads[3:]:
        load.wait()
    inner = heads * HD
    split = ((slice(3 * inner, 4 * inner), 0), (slice(0, 3 * inner), 1))
    pair = [
        tensor_copy(gpart_ref.at[lines_of], gpair_ref.at[lines_of], e_send.at[i], e_recv.at[i], away_rank)
        for lines_of, i in split
    ]
    attn_bwd_kernel(
        pair[0].start, False, heads, lengths_ref, table1_ref,
        normed_ref, pw_ref.at[: 3 * inner], pw_ref.at[3 * inner :], qkvt1_ref, mixt1_ref, lse1_ref, ga_ref, other_ref,
        gpart_ref, bias1_ref, npart_ref, all_ga_ref, got_ref, gt_ref, d0_ref, d1_ref,
    )
    pair[1].start()
    attn_bwd_kernel(
        None, True, heads, lengths_ref, table0_ref,
        normed_ref, wt_ref, ow_ref, qkvt0_ref, mixt0_ref, lse0_ref, ga_ref, other_ref, npart_ref,
        gown_ref, bias0_ref, keep_ref, send_ref, all_ga_ref, got_ref, gt_ref, d0_ref, d1_ref, npart_ref,
    )

    def pair_done():
        for one in pair:
            one.wait_recv()
        for i in range(1, PARTS):
            away(i).start()

    def beside():
        own_result.wait()
        for k in order:
            result(k).wait_recv()
        output_kernel(lengths_ref, outs_ref, slots_ref, hidden_ref, out_ref)

    sums(
        pair_done, beside, gown_ref, gpair_ref, keep_ref, send_ref, x_ref, gain1_ref, gh_ref, moe_ref, router_ref,
        bias0_ref, bias1_ref, gwt_out, gow_out, gin_out, attn_out, moe_out, router_out, bias_out, *tail_refs,
    )
    for k in order:
        result(k).wait_send()
    for one in pair:
        one.wait_send()
    go_away.wait_send()
    go_stay.wait()
    for i in range(PARTS):
        away(i).wait()


def finish(heads, cap, scalars, arrays, others):
    dma = pltpu.SemaphoreType.DMA
    count = 2 * LINE
    spots = count * cap
    rows = others[1].shape[0]
    local = heads * HD
    part = 4 * local // count
    anyspec = pl.BlockSpec(memory_space=pl.ANY)
    half = (rows, D)
    tail_sems = [dma((LINE,))] * 8 + [dma, dma] + [dma((count,))] * 2 + [dma((4,))] * 2 + [dma((count,))] * 2
    shapes = [
        ((spots, D), BF), (half, F32), (half, BF),
        ((spots, D), BF), ((2 * D, D), BF), ((2 * D, D), BF), (half, BF), ((SEQ, D), BF), ((3 * local, D), BF),
        ((local, D), BF), ((4 * local, D), BF), ((3 * local, SEQ), BF), ((local, SEQ), BF), ((8, SEQ), F32),
        ((3 * local, SEQ), BF), ((local, SEQ), BF), ((8, SEQ), F32),
        (half, F32), (half, BF), (half, BF), ((8, D), F32), ((4 * local, D), BF), ((4 * local, D), BF),
        ((4 * local, D), F32), ((8, 128), F32), ((8, 128), F32), (half, F32), (half, BF),
        ((SEQ, D), BF), ((local, SEQ), BF), ((3 * local, SEQ), BF), ((TILE, TILE), F32), ((TILE, TILE), F32), ((SEQ, D), F32),
    ]
    tail_shapes = [
        ((count, 8, 128), F32),
        ((4 * local, D), BF), ((LINE, part, D), BF), ((LINE, part, D), BF), ((LINE, part, D), BF), ((4 * local, D), BF),
        (half, BF), ((count, 8, 128), F32), ((count, 8, 128), F32), ((4, 8, 128), F32),
    ]
    return pl.pallas_call(
        functools.partial(finish_kernel, heads, cap),
        out_shape=[
            jax.ShapeDtypeStruct(half, BF),
            jax.ShapeDtypeStruct(half, BF),
            jax.ShapeDtypeStruct((3 * local, D), F32),
            jax.ShapeDtypeStruct((local, D), F32),
            jax.ShapeDtypeStruct((D,), F32),
            jax.ShapeDtypeStruct((D,), F32),
            jax.ShapeDtypeStruct((count, D), F32),
            jax.ShapeDtypeStruct((heads, NB), F32),
            jax.ShapeDtypeStruct((2 * D, D), BF),
            jax.ShapeDtypeStruct((2 * D, D), BF),
        ],
        in_specs=[SM] * len(scalars) + [VM] * len(arrays) + [anyspec] * len(others),
        out_specs=[VM] * 8 + [anyspec] * 2,
        scratch_shapes=[pltpu.VMEM(*v) for v in shapes]
        + [dma((count,)), dma((count,)), dma((2,)), dma((2,)), dma((PARTS,)), dma((PARTS,)), dma, dma, dma((2,)), dma((2,)), dma((16,))]
        + [pltpu.VMEM(*v) for v in tail_shapes]
        + tail_sems,
        compiler_params=pltpu.CompilerParams(
            collective_id=3, has_side_effects=True, vmem_limit_bytes=62 * MIB
        ),
        cost_estimate=pl.CostEstimate(flops=0, bytes_accessed=200 * MIB, transcendentals=0),
        name="finish",
    )(*scalars, *arrays, *others)


def line_accept(place, distance, copies, take):
    for step in (-1, 1):
        block = place + step * distance

        @pl.when((block >= 0) & (block < LINE))
        def _():
            for one in copies(block, -step):
                one.wait_recv()
            ahead = place - step

            @pl.when((ahead >= 0) & (ahead < LINE))
            def _():
                for one in copies(block, -step):
                    one.start()

    for step in (-1, 1):
        block = place + step * distance

        @pl.when((block >= 0) & (block < LINE))
        def _():
            take(block)


def line_sent(place, copies, least):
    for block in range(LINE):
        for step in (-1, 1):

            @pl.when((place + step >= 0) & (place + step < LINE) & ((place - block) * step >= least))
            def _():
                for one in copies(block, step):
                    one.wait_send()


def begin_kernel(
    heads, cap, lengths_ref,
    table_ref, x_ref, gain1_ref, wt_ref, ow_ref, routes_ref, grad_ref, router_ref, gain2_ref, up_ref, down_ref,
    normed_out, qkvt0_out, mixt0_out, lse0_out, qkvt1_out, mixt1_out, lse1_out, hidden_ref, normed2_ref, info_ref, slots_ref,
    pw_ref, table1_ref, gy_ref, far_up_ref, far_half_ref, near_ref, near_info_ref,
    other_ref, got_ref, part_ref, keep_ref, send_ref, block_ref, places_ref, gsend_ref, gkeep_ref,
    normed_ref, qkvt0_ref, mixt0_ref, lse0_ref, qkvt1_ref, mixt1_ref, lse1_ref,
    b_send, b_recv, i_send, i_recv, x_send, x_recv, v_send, v_recv, y_send, y_recv, n_send, n_recv, keep_sem, store_sem,
):
    count = 2 * LINE
    me = lax.axis_index("expert")
    rank = lax.axis_index("tensor")
    place = me // 2
    side = me - 2 * place
    mate = me + 1 - 2 * side
    core = flipped(rank, 1, 4)
    away = flipped(rank, 2, 4)
    inner = heads * HD
    barrier = pltpu.get_barrier_semaphore()
    for k in range(1, count):
        pl.semaphore_signal(
            barrier, inc=1, device_id={"expert": flipped(me, k, count)}, device_id_type=pl.DeviceIdType.MESH
        )
    for target in (core, away):
        pl.semaphore_signal(
            barrier, inc=1, device_id={"tensor": target}, device_id_type=pl.DeviceIdType.MESH
        )
    pl.semaphore_wait(barrier, count + 1)

    swap = tensor_copy(x_ref, other_ref, v_send.at[0], v_recv.at[0], core)
    swap.start()
    pair = (
        tensor_copy(ow_ref, pw_ref.at[3 * inner :], y_send.at[0], y_recv.at[0], away),
        tensor_copy(wt_ref, pw_ref.at[: 3 * inner], y_send.at[1], y_recv.at[1], away),
        tensor_copy(table_ref, table1_ref, y_send.at[2], y_recv.at[2], away),
    )
    for one in pair:
        one.start()
    far = (
        tensor_copy(up_ref, far_up_ref, y_send.at[3], y_recv.at[3], away),
        tensor_copy(down_ref.at[: D // 2], far_half_ref, y_send.at[4], y_recv.at[4], away),
    )

    def along(block, step):
        return (
            mesh_copy(
                places_ref.at[block], places_ref.at[block], i_send.at[(step + 1) // 2, block], i_recv.at[block], me + 2 * step
            ),
            mesh_copy(
                block_ref.at[block], block_ref.at[block], b_send.at[(step + 1) // 2, block], b_recv.at[block], me + 2 * step
            ),
        )

    def across(block):
        return mesh_copy(gsend_ref.at[block], gy_ref.at[1, block], x_send.at[block], x_recv.at[block], mate)

    def keep(block):
        return pltpu.make_async_copy(gkeep_ref.at[block], gy_ref.at[0, block], keep_sem.at[block])

    rows = grad_ref.shape[0]

    def take(block):
        slots = places_ref[block, 0:2].astype(jnp.int32)
        for part, expert in ((1, mate), (0, me)):
            where = iota((cap, rows), 0) + expert * cap
            picks = ((where == slots[0:1]) | (where == slots[1:2])).astype(BF)
            taken = dot(picks, block_ref[block]).astype(BF)
            if part:
                gsend_ref[block] = taken
                across(block).start()
            else:
                gkeep_ref[block] = taken
                keep(block).start()

    block_ref[place] = grad_ref[...]
    slots_kernel(count, cap, lengths_ref, routes_ref, slots_ref)
    places_ref[place] = slots_ref[...]
    for step in (-1, 1):

        @pl.when((place + step >= 0) & (place + step < LINE))
        def _():
            for one in along(place, step):
                one.start()

    take(place)
    swap.wait()
    attn_fwd_kernel(
        True, heads, lengths_ref, table_ref, x_ref, other_ref, gain1_ref, wt_ref, ow_ref,
        normed_ref, qkvt0_ref, mixt0_ref, lse0_ref, part_ref,
    )
    first = (
        (normed_ref, normed_out), (qkvt0_ref, qkvt0_out), (mixt0_ref, mixt0_out), (lse0_ref, lse0_out),
    )
    second = ((qkvt1_ref, qkvt1_out), (mixt1_ref, mixt1_out), (lse1_ref, lse1_out))
    stores = [pltpu.make_async_copy(a, b, store_sem.at[i]) for i, (a, b) in enumerate(first + second)]
    for store in stores[:4]:
        store.start()
    line_accept(place, 1, along, take)
    for one in pair:
        one.wait_recv()
    for one in far:
        one.start()
    attn_fwd_kernel(
        False, heads, lengths_ref, table1_ref, normed_ref, pw_ref.at[: 3 * inner], pw_ref.at[3 * inner :], part_ref,
        qkvt1_ref, mixt1_ref, lse1_ref, keep_ref, send_ref, part_ref,
    )
    back = tensor_copy(send_ref, got_ref, v_send.at[1], v_recv.at[1], core)
    back.start()
    for store in stores[4:]:
        store.start()
    line_accept(place, 2, along, take)
    back.wait()
    middle_line_kernel(
        count, x_ref, keep_ref, got_ref, gain2_ref, router_ref, routes_ref, slots_ref, hidden_ref, normed2_ref, info_ref
    )
    inside = [place > 0, place < LINE - 1]

    def neighbour(i):
        target = me + 2 * (1 - 2 * i)
        return (
            mesh_copy(info_ref, near_info_ref.at[i], n_send.at[i], n_recv.at[i], target),
            mesh_copy(normed2_ref, near_ref.at[i], n_send.at[i + 2], n_recv.at[i + 2], target),
        )

    line_sent(place, along, 0)
    for i in range(2):

        @pl.when(inside[1 - i])
        def _():
            for one in neighbour(i):
                one.start()

    line_accept(place, 3, along, take)
    for block in range(LINE):
        keep(block).wait()
        across(block).wait()
    for store in stores:
        store.wait()
    for one in pair:
        one.wait_send()
    for one in far:
        one.wait()
    for i in range(2):

        @pl.when(inside[i])
        def _():
            for one in neighbour(1 - i):
                one.wait_send()
            for one in neighbour(i):
                one.wait_recv()


def begin(heads, cap, scalars, arrays, others):
    dma = pltpu.SemaphoreType.DMA
    rows = arrays[1].shape[0]
    local = heads * HD
    anyspec = pl.BlockSpec(memory_space=pl.ANY)
    half = (rows, D)
    kept = [
        ((SEQ, D), BF), ((3 * local, SEQ), BF), ((local, SEQ), BF), ((8, SEQ), F32),
        ((3 * local, SEQ), BF), ((local, SEQ), BF), ((8, SEQ), F32),
    ]
    outs = kept + [
        (half, F32), (half, BF), ((8, rows), F32), ((8, rows), F32), ((4 * local, D), BF), ((heads, NB), F32),
        ((2, LINE, cap, D), BF), ((D, D), BF), ((D // 2, D), BF), ((2, rows, D), BF), ((2, 8, rows), F32),
    ]
    shapes = [
        (half, BF), (half, BF), ((SEQ, D), F32), (half, F32), (half, BF), ((LINE, rows, D), BF), ((LINE, 8, rows), F32),
        ((LINE, cap, D), BF), ((LINE, cap, D), BF),
    ] + kept
    return pl.pallas_call(
        functools.partial(begin_kernel, heads, cap),
        out_shape=[jax.ShapeDtypeStruct(*v) for v in outs],
        in_specs=[SM] * len(scalars) + [VM] * len(arrays) + [anyspec] * len(others),
        out_specs=[anyspec] * 7 + [VM] * 6 + [anyspec] * 5,
        scratch_shapes=[pltpu.VMEM(*v) for v in shapes]
        + [dma((2, LINE)), dma((LINE,)), dma((2, LINE)), dma((LINE,)), dma((LINE,)), dma((LINE,))]
        + [dma((2,)), dma((2,)), dma((5,)), dma((5,)), dma((4,)), dma((4,)), dma((LINE,)), dma((7,))],
        compiler_params=pltpu.CompilerParams(
            collective_id=4, has_side_effects=True, vmem_limit_bytes=56 * MIB
        ),
        cost_estimate=pl.CostEstimate(flops=0, bytes_accessed=200 * MIB, transcendentals=0),
        name="begin",
    )(*scalars, *arrays, *others)


def shards(
    inputs,
    lengths,
    routes,
    attn_gain,
    qkv_weight,
    out_weight,
    rel_bias,
    moe_gain,
    router_weight,
    up_weight,
    down_weight,
    out_grad,
):
    rows = inputs.shape[0]
    rank = lax.axis_index("tensor")
    expert = lax.axis_index("expert")
    heads = rel_bias.shape[1]
    inner = heads * HD
    experts = router_weight.shape[1]
    cap = 4 * rows // experts
    spots = experts * cap
    table = jnp.transpose(rel_bias)

    def swap(x, bit):
        return lax.ppermute(x, "tensor", [(i, i ^ bit) for i in range(4)])

    gain1, gain2 = attn_gain, moe_gain
    wt = jnp.transpose(qkv_weight.reshape(D, 3 * inner))
    routes_t = jnp.transpose(routes)
    up, down = up_weight[0], down_weight[0]
    line = experts == 2 * LINE and cap == TILE
    if line:
        router_t = jnp.transpose(router_weight)
        (
            normed, qkvt0, mixt0, lse0, qkvt1, mixt1, lse1, hidden, normed_two, info, slots, pair_w, pair_table, grads_in, far_up, far_half, near, near_info,
        ) = begin(
            heads,
            cap,
            (lengths,),
            (table, inputs, gain1, wt, out_weight, routes_t, out_grad, router_t, gain2),
            (up, down),
        )
        came, result, stay, away, go, grad_router = moe_line(
            experts, cap, normed_two, info, router_t, (grads_in, near, near_info, up, down, far_up, far_half)
        )
    else:
        other = swap(inputs, 1)
        pair_w = swap(jnp.concatenate([wt, out_weight], axis=0), 2)
        pair_table = swap(table, 2)

        packed_grad, slots = call(
            functools.partial(route_kernel, experts, cap),
            [((spots, D), BF), ((8, rows), F32)],
            (lengths, routes_t, out_grad),
            [SM, VM, VM],
            flops=2 * spots * rows * D,
            moved=4 * MIB,
            name="route",
        )

        def exchange(x):
            return lax.all_to_all(
                x.reshape(experts, cap, x.shape[-1]), "expert", split_axis=0, concat_axis=0, tiled=True
            ).reshape(x.shape)

        grads_in = exchange(packed_grad)
        up, down, pair_w, pair_table = lax.optimization_barrier((up, down, pair_w, pair_table))
        far_up, far_down = swap(up, 2), swap(down, 2)

        attn_cost = dict(
            flops=2 * SEQ * D * 4 * inner + heads * SEQ * SEQ * 160, moved=6 * MIB, exps=heads * SEQ * SEQ
        )
        normed, qkvt0, mixt0, lse0, part0 = call(
            functools.partial(attn_fwd_kernel, True, heads),
            [((SEQ, D), BF), ((3 * inner, SEQ), BF), ((inner, SEQ), BF), ((8, SEQ), F32), ((SEQ, D), F32)],
            (lengths, table, inputs, other, gain1, wt, out_weight),
            [SM] + [VM] * 1 + [VM] * 5,
            name="attend_own",
            **attn_cost,
        )
        wt1, ow1 = pair_w[: 3 * inner], pair_w[3 * inner :]
        qkvt1, mixt1, lse1, keep, send = call(
            functools.partial(attn_fwd_kernel, False, heads),
            [((3 * inner, SEQ), BF), ((inner, SEQ), BF), ((8, SEQ), F32), ((rows, D), F32), ((rows, D), BF)],
            (lengths, pair_table, normed, wt1, ow1, part0),
            [SM] + [VM] * 1 + [VM] * 4,
            scratch=[pltpu.VMEM((SEQ, D), F32)],
            name="attend_pair",
            **attn_cost,
        )
        got = swap(send, 1)
        middle_args = (inputs, keep, got, gain2, jnp.transpose(router_weight), routes_t, slots)
        mine = jnp.concatenate([up, down], axis=0)
        far = jnp.concatenate([far_up, far_down], axis=0)
        quarters = [mine, far, swap(mine, 1), swap(far, 1)]
        hidden, packed_rows, meta = call(
            functools.partial(middle_kernel, experts, cap),
            [((rows, D), F32), ((spots, D), BF), ((experts, 8, cap), F32)],
            middle_args,
            flops=2 * spots * rows * D,
            moved=8 * MIB,
            name="middle",
        )
        came, result, stay, away, go, grad_router = moe(
            experts, cap, packed_rows, meta, grads_in, router_weight, quarters
        )
    if line:
        outputs, grad_inputs, gwt, gow, attn_sum, moe_sum, router_sum, bias_sum, go_stay, came_away = finish(
            heads,
            cap,
            (lengths,),
            (table, pair_table, slots, gain2, gain1, grad_router),
            (came, hidden, out_grad, result, go, away, inputs, normed, wt, out_weight, pair_w, qkvt0, mixt0, lse0, qkvt1, mixt1, lse1),
        )
    else:
        came_out = exchange(result)
        came_go = swap(go, 1)
        grad_hidden, grad_attended, moe_part = call(
            turn_kernel,
            [((rows, D), F32), ((rows, D), BF), ((8, D), F32)],
            (lengths, came, slots, hidden, gain2, out_grad),
            [SM] + [VM] * 5,
            flops=2 * spots * rows * D,
            moved=8 * MIB,
            name="turn",
        )
        other_grad = swap(grad_attended, 1)
        away = (away.astype(F32) + came_go[1].astype(F32)).astype(BF)
        bwd_cost = dict(
            flops=2 * SEQ * D * 10 * inner + heads * SEQ * SEQ * 400, moved=9 * MIB, exps=heads * SEQ * SEQ
        )
        work = [
            pltpu.VMEM((SEQ, D), BF),
            pltpu.VMEM((inner, SEQ), BF),
            pltpu.VMEM((3 * inner, SEQ), BF),
            pltpu.VMEM((TILE, TILE), F32),
            pltpu.VMEM((TILE, TILE), F32),
        ]
        gpart, gbias1, npart = call(
            functools.partial(attn_bwd_kernel, None, False, heads),
            [((4 * inner, D), BF), ((8, 128), F32), ((SEQ, D), F32)],
            (lengths, pair_table, normed, wt1, ow1, qkvt1, mixt1, lse1, grad_attended, other_grad),
            [SM] + [VM] * 1 + [VM] * 8,
            scratch=work,
            name="attend_pair_back",
            **bwd_cost,
        )
        gpair = swap(gpart, 2)
        gown, gbias0, keep_n, send_n = call(
            functools.partial(attn_bwd_kernel, None, True, heads),
            [((4 * inner, D), F32), ((8, 128), F32), ((rows, D), F32), ((rows, D), BF)],
            (lengths, table, normed, wt, out_weight, qkvt0, mixt0, lse0, grad_attended, other_grad, npart),
            [SM] + [VM] * 1 + [VM] * 9,
            scratch=work + [pltpu.VMEM((SEQ, D), F32)],
            name="attend_own_back",
            **bwd_cost,
        )
        away, gpair, gown = lax.optimization_barrier((away, gpair, gown))
        came_away = swap(away, 2)
        got_n = swap(send_n, 1)
        grad_inputs, attn_part = call(
            last_kernel,
            [((rows, D), BF), ((8, D), F32)],
            (inputs, keep_n, got_n, gain1, grad_hidden),
            moved=6 * MIB,
            name="last",
        )
        wide = (gown + gpair.astype(F32)).astype(BF)
        wide = lax.psum(wide, "expert").astype(F32)
        outputs = call(
            output_kernel,
            [((rows, D), BF)],
            (lengths, came_out, slots, hidden),
            [SM] + [VM] * 3,
            flops=2 * spots * rows * D,
            moved=8 * MIB,
            name="outputs",
        )[0]
        go_stay = came_go[0]

    if line:
        router_sum = jnp.transpose(router_sum)
    else:
        gwt, gow = wide[: 3 * inner], wide[3 * inner :]
        own_bias = gbias0[:heads, :NB].reshape(1, -1)
        pair_bias = gbias1[:heads, :NB].reshape(1, -1)
        ranks = jnp.arange(4, dtype=jnp.int32)[:, None]
        bias_parts = jnp.where(ranks == rank, own_bias, 0.0) + jnp.where(
            ranks == (rank ^ 2), pair_bias, 0.0
        )
        small = jnp.concatenate(
            [attn_part[0], moe_part[0], jnp.transpose(grad_router).reshape(-1), bias_parts.reshape(-1)]
        )
        small = lax.psum(small, ("expert", "tensor"))
        attn_sum, moe_sum = small[:D], small[D : 2 * D]
        router_sum = small[2 * D : 2 * D + experts * D].reshape(D, experts)
        bias_sum = lax.dynamic_slice(
            small[2 * D + experts * D :].reshape(4, heads * NB), (rank, 0), (1, heads * NB)
        )
    grad_up, grad_down = (
        stay[rows_of].astype(F32) + go_stay[rows_of].astype(F32) + came_away[rows_of].astype(F32)
        for rows_of in (slice(0, D), slice(D, 2 * D))
    )
    return (
        outputs,
        grad_inputs,
        attn_sum,
        jnp.transpose(gwt).reshape(D, 3, inner),
        gow,
        jnp.transpose(bias_sum.reshape(heads, NB)),
        moe_sum,
        router_sum,
        grad_up[None],
        grad_down[None],
    )


def solution(mesh):
    return jax.shard_map(
        shards,
        mesh=mesh,
        in_specs=(
            P(("expert", "tensor"), None),
            P("expert"),
            P(("expert", "tensor"), None),
            P(),
            P(None, None, "tensor"),
            P("tensor", None),
            P(None, "tensor"),
            P(),
            P(),
            P("expert", None, "tensor"),
            P("expert", "tensor", None),
            P(("expert", "tensor"), None),
        ),
        out_specs=(
            P(("expert", "tensor"), None),
            P(("expert", "tensor"), None),
            P(),
            P(None, None, "tensor"),
            P("tensor", None),
            P(None, "tensor"),
            P(),
            P(),
            P("expert", None, "tensor"),
            P("expert", "tensor", None),
        ),
        check_vma=False,
    )
```
